32 devices in a mesh: section: 4 (over y, x), lat: 8 (over z, core).
Axes of the slice: x: 2, y: 2, z: 4, core: 2. Of those that a mesh axis runs over, the one named last changes fastest.
Arguments:
- grad_out: bfloat16 [4, 8, 180, 384], P('section', 'lat'), may hold values from -6 to 6
- spec_saved: bfloat16 [4, 8, 2, 27648], P('section', None, None, 'lat'), may hold values from -6 to 6
- w1: bfloat16 [4, 2, 96, 384], P('section'), may hold values from -0.4375 to 0.4375
- w2: bfloat16 [4, 2, 96, 384], P('section'), may hold values from -0.4375 to 0.4375
- b1: bfloat16 [4, 2, 384], P('section'), may hold values from -5 to 5
- mode_counts: int32 [8], replicated, may hold values from 1 to 72, as said below
- assignment: int32 [8], replicated, may hold values from 0 to 7, each once
Outputs:
- grad_input: bfloat16 [4, 8, 180, 384], P('section', 'lat')
- grad_w1: float32 [4, 2, 96, 384], P('section', None, None, 'lat')
- grad_w2: float32 [4, 2, 96, 384], P('section', None, None, 'lat')
- grad_b1: float32 [4, 2, 384], P('section', None, 'lat')
The draws below stay inside these ranges and needn't reach their ends.
Inputs may be any that keep to these rules, and one draw needn't show every extreme that they name: `mode_counts`: active modes shrink from the middle band toward both ends; the middle band keeps all 72. `assignment`: A permutation of the latitude bands.
All inputs are finite; a program needn't handle non-finite values.
Results may differ from the reference program's by a relative error of at most 0.018.
Values may be sent and summed in bfloat16 or wider, within the bound.
No kernel may reach another device: no remote copies, remote signals or barrier semaphores. Data moves between devices by JAX's collectives and lax.ppermute only.
A program may use at most 64 MiB of HBM per device.

```python
import math
import jax
import jax.numpy as jnp
from jax import lax

NB = 4
BS = 96
KM = 72
LON = 180
D = 384
LAT_ROWS = 8
SECTIONS = 4


def draw_mode_counts(key, part):
    bands = jnp.arange(LAT_ROWS, dtype=jnp.int32)
    spread = jnp.abs(2 * bands - (LAT_ROWS - 1))
    base = KM - spread * KM // (2 * LAT_ROWS)
    jitter = jax.random.randint(key, (LAT_ROWS,), -(KM // 8), 1)
    counts = jnp.clip(base + jitter, 1, KM)
    counts = jnp.where(bands == LAT_ROWS // 2, KM, counts)
    return counts.astype(jnp.int32)


def shard_levels(own_key, dims, split, low, top_value):
    level = 1.0
    for position, blocks in split:
        draws = jax.random.uniform(jax.random.fold_in(jax.random.fold_in(own_key, 6), position), (blocks,), jnp.float32, low / len(split), top_value / len(split))
        level = level * jnp.repeat(jnp.exp(draws), dims[position] // blocks).reshape((-1,) + (1,) * (len(dims) - 1 - position))
    return level


def bell_draw(stream_key, shape, deviation, bound, split=(), kind=jnp.bfloat16):
    values = jax.random.normal(stream_key, shape, jnp.float32) * deviation
    if len(split) > 0:
        values = shard_levels(stream_key, shape, split, -0.22, 0.18) * values
    return jnp.clip(values, min=-bound, max=bound).astype(kind)


def setup_inputs(seed: int = 0) -> dict:
    splits = jax.random.split(jax.random.key(seed), 8)
    return {
        "grad_out": bell_draw(splits[0], (SECTIONS, LAT_ROWS, LON, D), 1.0, 6.0, ((0, 4), (1, 8))),
        "spec_saved": bell_draw(splits[1], (SECTIONS, LAT_ROWS, 2, KM * NB * BS), 1.0, 6.0, ((0, 4), (3, 8))),
        "w1": bell_draw(splits[2], (SECTIONS, 2, BS, D), (2 * BS) ** -0.5, 0.4375, ((0, 4),)),
        "w2": bell_draw(splits[3], (SECTIONS, 2, BS, D), (2 * BS) ** -0.5, 0.4375, ((0, 4),)),
        "b1": bell_draw(splits[4], (SECTIONS, 2, D), 1.0, 5.0, ((0, 4),)),
        "mode_counts": draw_mode_counts(jax.random.fold_in(splits[7], 71), 0),
        "assignment": jax.random.permutation(splits[6], LAT_ROWS).astype(jnp.int32),
    }


def lon_tables(n_modes, length):
    modes = jnp.arange(n_modes, dtype=jnp.int32)
    cells = jnp.arange(length, dtype=jnp.int32)
    phase = modes[:, None] * cells[None, :] % length
    angle = phase.astype(jnp.float32) * (2.0 * math.pi / length)
    factor = 1.0 / math.sqrt(length)
    cosine = jnp.cos(angle) * factor
    sine = jnp.sin(angle) * factor
    weight = jnp.where(modes == 0, 1.0, 2.0).astype(jnp.float32)[:, None]
    forward = jnp.stack([cosine, -sine]).astype(jnp.bfloat16)
    inverse = jnp.stack([cosine * weight, -sine * weight]).astype(jnp.bfloat16)
    return (forward, inverse)

def lat_table(latitude, n_rows):
    freqs = jnp.arange(n_rows, dtype=jnp.int32)
    phase = freqs[:, None] * latitude[None, :] % n_rows
    angle = phase.astype(jnp.float32) * (2.0 * math.pi / n_rows)
    factor = 1.0 / math.sqrt(n_rows)
    cosine = jnp.cos(angle) * factor
    sine = jnp.sin(angle) * factor
    upper = jnp.stack([cosine, sine], axis=-1)
    lower = jnp.stack([-sine, cosine], axis=-1)
    return jnp.stack([upper, lower], axis=1).astype(jnp.bfloat16)

def silu_slope(pre):
    sig = jax.nn.sigmoid(pre)
    return sig * (1.0 + pre * (1.0 - sig))

def apply_mat(vec, mat):
    return jnp.einsum('knmi,inj->knmj', vec, mat)

def adjoint_mat(vec, mat):
    return jnp.einsum('knmj,inj->knmi', vec, mat)

def outer_sum(left, right):
    return jnp.einsum('knmi,knmj->inj', left, right)

def section_grad(cotan, saved, w_first, w_second, bias, active, fwd_table, inv_table, table):
    f32 = jnp.float32
    bf16 = jnp.bfloat16
    cot = cotan.reshape(LAT_ROWS, LON, NB, BS).astype(f32)
    spec = jnp.einsum('cml,rlni->rcnmi', inv_table.astype(f32), cot)
    spec = (spec * active[:, None, None, :, None]).astype(bf16)
    grad_y = jnp.einsum('kerc,rcnmi->kenmi', table.astype(f32), spec.astype(f32)).astype(bf16)
    vin = saved.reshape(LAT_ROWS, 2, KM, NB, BS).astype(f32)
    vin = jnp.transpose(vin, (0, 1, 3, 2, 4))
    first = w_first.reshape(2, BS, NB, BS).astype(f32)
    second = w_second.reshape(2, BS, NB, BS).astype(f32)
    shift_b = bias.reshape(2, NB, BS).astype(f32)
    v_r = vin[:, 0]
    v_i = vin[:, 1]
    pre_r = apply_mat(v_r, first[0]) - apply_mat(v_i, first[1]) + shift_b[0][None, :, None, :]
    pre_i = apply_mat(v_i, first[0]) + apply_mat(v_r, first[1]) + shift_b[1][None, :, None, :]
    hid_r = jax.nn.silu(pre_r).astype(bf16).astype(f32)
    hid_i = jax.nn.silu(pre_i).astype(bf16).astype(f32)
    dy_r = grad_y[:, 0].astype(f32)
    dy_i = grad_y[:, 1].astype(f32)
    dh_r = adjoint_mat(dy_r, second[0]) + adjoint_mat(dy_i, second[1])
    dh_i = adjoint_mat(dy_i, second[0]) - adjoint_mat(dy_r, second[1])
    dp_r = (dh_r * silu_slope(pre_r)).astype(bf16).astype(f32)
    dp_i = (dh_i * silu_slope(pre_i)).astype(bf16).astype(f32)
    gw2 = jnp.stack([outer_sum(hid_r, dy_r) + outer_sum(hid_i, dy_i), outer_sum(hid_r, dy_i) - outer_sum(hid_i, dy_r)])
    gw1 = jnp.stack([outer_sum(v_r, dp_r) + outer_sum(v_i, dp_i), outer_sum(v_r, dp_i) - outer_sum(v_i, dp_r)])
    gb1 = jnp.stack([lax.optimization_barrier(jnp.sum(dp_r, axis=(0, 2))), lax.optimization_barrier(jnp.sum(dp_i, axis=(0, 2)))])
    dv_r = adjoint_mat(dp_r, first[0]) + adjoint_mat(dp_i, first[1])
    dv_i = adjoint_mat(dp_i, first[0]) - adjoint_mat(dp_r, first[1])
    grad_v = jnp.stack([dv_r, dv_i], axis=1).astype(bf16)
    band = jnp.einsum('kerc,kenmi->rcnmi', table.astype(f32), grad_v.astype(f32)).astype(bf16)
    band = band.astype(f32) * active[:, None, None, :, None]
    mixed = jnp.einsum('cml,rcnmi->rlni', fwd_table.astype(f32), band).astype(bf16)
    mixed = mixed.reshape(LAT_ROWS, LON, D)
    total = (cotan.astype(f32) + mixed.astype(f32)).astype(bf16)
    return (total, gw1.reshape(2, BS, D), gw2.reshape(2, BS, D), gb1.reshape(2, D))

def reference(grad_out, spec_saved, w1, w2, b1, mode_counts, assignment):
    fwd_table, inv_table = lon_tables(KM, LON)
    table = lat_table(assignment.astype(jnp.int32), LAT_ROWS)
    row_counts = mode_counts[assignment]
    active = (jnp.arange(KM, dtype=jnp.int32)[None, :] < row_counts[:, None]).astype(jnp.float32)

    def one_section(items):
        cotan, saved, w_first, w_second, bias = items
        return section_grad(cotan, saved, w_first, w_second, bias, active, fwd_table, inv_table, table)
    total, gw1, gw2, gb1 = lax.map(one_section, (grad_out, spec_saved, w1, w2, b1))
    zeros = jnp.zeros((1, LAT_ROWS, LON, D), dtype=jnp.bfloat16)
    grad_input = jnp.concatenate([total[1:], zeros], axis=0)
    return (grad_input, gw1, gw2, gb1)
```

```python
import functools
import math

import jax
import jax.numpy as jnp
import numpy as np
from jax import lax
from jax.experimental import pallas as pl
from jax.experimental.pallas import tpu as pltpu
from jax.sharding import PartitionSpec as P

NB = 4
BS = 96
KM = 72
LANES = 128
F32 = jnp.float32
BF16 = jnp.bfloat16


def from_behind(value, axis, by):
    length = lax.axis_size(axis)
    pairs = [(i, i + by) for i in range(length) if 0 <= i + by < length]
    return lax.ppermute(value, axis, pairs)


def lon_tables(n_modes, length):
    modes = np.arange(n_modes)
    phase = modes[:, None] * np.arange(length)[None, :] % length
    angle = phase * (2.0 * math.pi / length)
    forward = np.stack([np.cos(angle), -np.sin(angle)]) / math.sqrt(length)
    weight = np.where(modes == 0, 1.0, 2.0)[None, :, None]
    return forward, forward * weight


def lat_waves(n_rows):
    freqs = np.arange(n_rows)
    angle = (freqs[:, None] * freqs[None, :] % n_rows) * (2.0 * math.pi / n_rows)
    factor = 1.0 / math.sqrt(n_rows)
    return np.cos(angle) * factor, np.sin(angle) * factor


def silu_slope(pre):
    sig = jax.nn.sigmoid(pre)
    return sig * (1.0 + pre * (1.0 - sig))


def window(x, start):
    low = start // LANES * LANES
    shift = start - low
    if shift == 0:
        return x[:, low : low + LANES]
    if shift + BS <= LANES:
        return pltpu.roll(x[:, low : low + LANES], LANES - shift, 1)
    return pltpu.roll(x[:, low : low + 2 * LANES], 2 * LANES - shift, 1)[:, :LANES]


def dense(parts):
    lane = lax.broadcasted_iota(jnp.int32, parts[0].shape, 1)
    first = pltpu.roll(parts[1], 96, 1)
    second = pltpu.roll(parts[2], 64, 1)
    third = pltpu.roll(parts[3], 32, 1)
    return jnp.concatenate(
        [
            jnp.where(lane < 96, parts[0], first),
            jnp.where(lane < 64, first, second),
            jnp.where(lane < 32, second, third),
        ],
        axis=1,
    )


def dot(a, b, contract):
    return lax.dot_general(a, b, ((contract[:1], contract[1:]), ((), ())), preferred_element_type=F32)


def own_count(counts, assign):
    return counts[assign[lax.axis_index("lat")]]


def analyse_kernel(q, counts, assign, field, table, out):
    n_dev, pad, width = out.shape
    active = own_count(counts, assign)
    spectral = jnp.dot(table[...], field[...], preferred_element_type=F32)
    row = lax.broadcasted_iota(jnp.int32, (pad, width), 0)
    mode = jnp.where(row >= q, row - q, row)
    for d in range(n_dev):
        part = spectral[d * pad : (d + 1) * pad]
        out[d] = jnp.where(mode < active - q * d, part, 0.0).astype(BF16)


def filter_kernel(q, split, assign, pencil, saved, w1, w2, b1, lat, out, by_lat, mat1, mat2):
    n_rows, pad, width = pencil.shape
    points = q * n_rows
    cols = BS // split
    for r in range(n_rows):
        by_lat[assign[r]] = pencil[r].astype(F32)
    field = by_lat[...].reshape(n_rows * pad, width).astype(BF16)
    grad_y = dot(lat[...], field, (1, 0)).astype(BF16).astype(F32)
    parts = [saved[:, c, :].astype(F32) for c in range(2)]
    shift_b = b1[...].astype(F32)
    lane = lax.broadcasted_iota(jnp.int32, (BS, LANES), 1)
    gap = jnp.zeros((LANES - BS, 2 * LANES), BF16)
    for mat in (mat1, mat2):
        mat[BS:LANES] = gap
        mat[LANES + BS : 2 * LANES] = gap
    inner = []
    for n in range(NB):
        for mat, source in ((mat1, w1), (mat2, w2)):
            real, imag = (
                jnp.where(lane < BS, window(source[c].astype(F32), n * BS), 0.0) for c in range(2)
            )
            mat[0:BS] = jnp.concatenate([real, imag], axis=1).astype(BF16)
            mat[LANES : LANES + BS] = jnp.concatenate([-imag, real], axis=1).astype(BF16)
        bias = window(shift_b, n * BS)
        bias = jnp.concatenate([bias[0:1], bias[1:2]], axis=1)
        v = jnp.concatenate(
            [
                jnp.concatenate([window(part, (mm * NB + n) * BS) for mm in range(q)], axis=0)
                for part in parts
            ],
            axis=1,
        ).astype(BF16)
        dy = jnp.concatenate(
            [window(grad_y[c * points : (c + 1) * points], n * BS) for c in range(2)], axis=1
        ).astype(BF16)
        pre = dot(v, mat1[...], (1, 0)) + bias
        sig = jax.nn.sigmoid(pre)
        hidden = (pre * sig).astype(BF16)
        grad_hidden = dot(dy, mat2[...], (1, 1))
        dp = (grad_hidden * (sig * (1.0 + pre * (1.0 - sig)))).astype(BF16)
        dv = dot(dp, mat1[...], (1, 1))
        inner.append(jnp.concatenate([dv[:, :LANES], dv[:, LANES:]], axis=0))
        columns = []
        for left, right in ((dp, v), (dy, hidden)):
            both = dot(left, right, (0, 0))
            columns.append(both[:BS, :LANES] + both[LANES : LANES + BS, LANES:])
            columns.append(both[LANES : LANES + BS, :LANES] - both[:BS, LANES:])
        weights = dense(columns).astype(BF16)
        grad_b = jnp.sum(dp.astype(F32), axis=0, keepdims=True)
        for h in range(split):
            out[n * split + h, 0:cols] = weights[h * cols : (h + 1) * cols]
        mat_b = jnp.concatenate([grad_b, jnp.zeros((1, width - 2 * LANES), F32)], axis=1)
        inner[n] = (inner[n], mat_b)
    grad_v = dense([item[0] for item in inner]).astype(BF16)
    by_lat[...] = dot(lat[...], grad_v, (0, 0)).reshape(n_rows, pad, width)
    row = lax.broadcasted_iota(jnp.int32, (pad, width), 0)
    for d in range(n_rows):
        band = by_lat[assign[d]]
        out[d, cols : cols + pad] = jnp.where(row == 2 * q, inner[d // split][1], band).astype(BF16)


def compose_kernel(q, cols, counts, assign, back, field, table, out):
    n_dev, rows, width = back.shape
    pad = rows - cols
    active = own_count(counts, assign)
    spectral = back[:, cols:, :].astype(F32)
    row = lax.broadcasted_iota(jnp.int32, (pad, width), 0)
    mode = jnp.where(row >= q, row - q, row)
    held = [jnp.where(mode < active - q * d, spectral[d], 0.0) for d in range(n_dev)]
    held = jnp.concatenate(held, axis=0).astype(BF16)
    mixed = jnp.dot(table[...], held, preferred_element_type=F32).astype(BF16)
    out[...] = (field[...].astype(F32) + mixed.astype(F32)).astype(BF16)


def sum_kernel(q, split, back, gw1, gw2, gb1):
    n_dev, rows, width = back.shape
    cols = BS // split
    total = back[0, 0:cols].astype(F32)
    tail = back[0, cols:rows].astype(F32)
    for d in range(1, n_dev):
        total += back[d, 0:cols].astype(F32)
        tail += back[d, cols:rows].astype(F32)
    turned = total.T
    for w, ref in enumerate((gw1, gw2)):
        for c in range(2):
            start = (2 * w + c) * BS
            ref[c] = turned[start : start + BS]
    half = lax.rem(lax.axis_index("lat"), split)
    for c in range(2):
        line = tail[2 * q : 2 * q + 1, c * LANES : (c + 1) * LANES]
        picked = line[:, 0:cols]
        for h in range(1, split):
            picked = jnp.where(half == h, line[:, h * cols : (h + 1) * cols], picked)
        gb1[c : c + 1] = picked


def call(kernel, outs, scratch, n_scalars, *args):
    whole = pl.BlockSpec(memory_space=pltpu.VMEM)
    scalar = pl.BlockSpec(memory_space=pltpu.SMEM)
    specs = [scalar] * n_scalars + [whole] * (len(args) - n_scalars)
    many = isinstance(outs, tuple)
    return pl.pallas_call(
        kernel,
        out_shape=outs,
        in_specs=specs,
        out_specs=tuple([whole] * len(outs)) if many else whole,
        scratch_shapes=scratch,
        compiler_params=pltpu.CompilerParams(vmem_limit_bytes=32 * 2**20),
    )(*args)


def whole_blocks(grad_out, spec_saved, w1, w2, b1, mode_counts, assignment):
    length, width = grad_out.shape[2:]
    n_rows = assignment.shape[0]
    n_dev = lax.axis_size("lat")
    q = spec_saved.shape[3] // (NB * BS)
    split = n_dev // NB
    cols = BS // split
    pad = (2 * q + 8) // 8 * 8
    forward, inverse = lon_tables(KM, length)

    def by_device(table):
        table = table.reshape(2, n_dev, q, length).transpose(1, 0, 2, 3)
        table = table.reshape(n_dev, 2 * q, length)
        table = np.pad(table, ((0, 0), (0, pad - 2 * q), (0, 0)))
        return table.reshape(n_dev * pad, length).astype(BF16)

    cosine, sine = lat_waves(n_rows)
    eye = np.eye(q)
    rounds = np.array([[cosine, sine], [-sine, cosine]])
    lat = np.einsum("eckr,mv->emkrcv", rounds, eye)
    lat = lat.reshape(2 * q * n_rows, n_rows, 2 * q)
    lat = np.pad(lat, ((0, 0), (0, 0), (0, pad - 2 * q))).reshape(2 * q * n_rows, n_rows * pad)
    lat = jnp.asarray(lat.astype(BF16))
    inverse = jnp.asarray(by_device(inverse))
    forward = jnp.asarray(by_device(forward).T)

    field = grad_out.reshape(length, width)
    spectral = call(
        functools.partial(analyse_kernel, q),
        jax.ShapeDtypeStruct((n_dev, pad, width), BF16),
        [],
        2,
        mode_counts,
        assignment,
        field,
        inverse,
    )
    pencil = lax.all_to_all(spectral, "lat", split_axis=0, concat_axis=0, tiled=True)
    chunks = call(
        functools.partial(filter_kernel, q, split),
        jax.ShapeDtypeStruct((n_dev, cols + pad, width), BF16),
        [
            pltpu.VMEM((n_rows, pad, width), F32),
            pltpu.VMEM((2 * LANES, 2 * LANES), BF16),
            pltpu.VMEM((2 * LANES, 2 * LANES), BF16),
        ],
        1,
        assignment,
        pencil,
        spec_saved[0],
        w1[0],
        w2[0],
        b1[0],
        lat,
    )
    back = lax.all_to_all(chunks, "lat", split_axis=0, concat_axis=0, tiled=True)
    total = call(
        functools.partial(compose_kernel, q, cols),
        jax.ShapeDtypeStruct((length, width), BF16),
        [],
        2,
        mode_counts,
        assignment,
        back,
        field,
        forward,
    )
    received = from_behind(total[None, None], "section", -1)
    gw1, gw2, gb1 = call(
        functools.partial(sum_kernel, q, split),
        (
            jax.ShapeDtypeStruct((2, BS, cols), F32),
            jax.ShapeDtypeStruct((2, BS, cols), F32),
            jax.ShapeDtypeStruct((2, cols), F32),
        ),
        [],
        0,
        back,
    )
    return received, gw1[None], gw2[None], gb1[None]


def apply_mat(vec, mat):
    return jnp.einsum("kpi,ipj->kpj", vec, mat, preferred_element_type=F32)


def adjoint_mat(vec, mat):
    return jnp.einsum("kpj,ipj->kpi", vec, mat, preferred_element_type=F32)


def outer_sum(left, right):
    return jnp.einsum("kpi,kpj->ipj", left, right, preferred_element_type=F32)


def split_blocks(grad_out, spec_saved, w1, w2, b1, mode_counts, assignment):
    rows_dev = grad_out.shape[1]
    length = grad_out.shape[2]
    width = grad_out.shape[3]
    n_rows = assignment.shape[0]
    pairs_dev = spec_saved.shape[3] // BS
    forward, inverse = (jnp.asarray(t.astype(BF16)) for t in lon_tables(KM, length))
    cosine, sine = (jnp.asarray(t.astype(BF16))[:, assignment] for t in lat_waves(n_rows))
    table = jnp.stack(
        [jnp.stack([cosine, sine], axis=-1), jnp.stack([-sine, cosine], axis=-1)], axis=1
    )
    lat_pos = lax.axis_index("lat")
    lat_count = lax.axis_size("lat")
    own_lat = lax.dynamic_slice_in_dim(assignment, lat_pos * rows_dev, rows_dev)
    active = (jnp.arange(KM, dtype=jnp.int32)[None, :] < mode_counts[own_lat][:, None]).astype(F32)
    cotan = grad_out[0]
    spectral = jnp.einsum(
        "cml,rlni->rcmni",
        inverse,
        cotan.reshape(rows_dev, length, NB, BS),
        preferred_element_type=F32,
    )
    spectral = (spectral * active[:, None, :, None, None]).astype(BF16)
    spectral = spectral.reshape(rows_dev, 2, KM * NB * BS)
    pencil = lax.all_to_all(spectral, "lat", split_axis=2, concat_axis=0, tiled=True)
    pencil = pencil.reshape(n_rows, 2, pairs_dev, BS)
    grad_y = jnp.einsum("kerc,rcpi->kepi", table, pencil, preferred_element_type=F32).astype(BF16)
    saved = spec_saved[0].reshape(n_rows, 2, pairs_dev, BS)
    pair_ids = lat_pos * pairs_dev + jnp.arange(pairs_dev, dtype=jnp.int32)
    owner = (pair_ids % NB)[:, None] == jnp.arange(NB, dtype=jnp.int32)[None, :]
    owner = owner.astype(F32)
    first = jnp.take(w1[0].reshape(2, BS, NB, BS), pair_ids % NB, axis=2)
    second = jnp.take(w2[0].reshape(2, BS, NB, BS), pair_ids % NB, axis=2)
    shift_b = jnp.take(b1[0].reshape(2, NB, BS), pair_ids % NB, axis=1).astype(F32)
    v_r = saved[:, 0]
    v_i = saved[:, 1]
    pre_r = apply_mat(v_r, first[0]) - apply_mat(v_i, first[1]) + shift_b[0][None]
    pre_i = apply_mat(v_i, first[0]) + apply_mat(v_r, first[1]) + shift_b[1][None]
    hid_r = jax.nn.silu(pre_r).astype(BF16)
    hid_i = jax.nn.silu(pre_i).astype(BF16)
    dy_r = grad_y[:, 0]
    dy_i = grad_y[:, 1]
    dh_r = adjoint_mat(dy_r, second[0]) + adjoint_mat(dy_i, second[1])
    dh_i = adjoint_mat(dy_i, second[0]) - adjoint_mat(dy_r, second[1])
    dp_r = (dh_r * silu_slope(pre_r)).astype(BF16)
    dp_i = (dh_i * silu_slope(pre_i)).astype(BF16)
    gw2 = jnp.stack(
        [
            outer_sum(hid_r, dy_r) + outer_sum(hid_i, dy_i),
            outer_sum(hid_r, dy_i) - outer_sum(hid_i, dy_r),
        ]
    )
    gw1 = jnp.stack(
        [outer_sum(v_r, dp_r) + outer_sum(v_i, dp_i), outer_sum(v_r, dp_i) - outer_sum(v_i, dp_r)]
    )
    gb1 = jnp.stack([jnp.sum(dp_r.astype(F32), axis=0), jnp.sum(dp_i.astype(F32), axis=0)])
    dv_r = adjoint_mat(dp_r, first[0]) + adjoint_mat(dp_i, first[1])
    dv_i = adjoint_mat(dp_i, first[0]) - adjoint_mat(dp_r, first[1])
    grad_v = jnp.stack([dv_r, dv_i], axis=1).astype(BF16)
    grad_u = jnp.einsum("kerc,kepi->rcpi", table, grad_v, preferred_element_type=F32).astype(BF16)
    grad_u = grad_u.reshape(n_rows, 2, pairs_dev * BS)
    back = lax.all_to_all(grad_u, "lat", split_axis=0, concat_axis=2, tiled=True)
    back = back.reshape(rows_dev, 2, KM, NB, BS) * active[:, None, :, None, None].astype(BF16)
    mixed = jnp.einsum("cml,rcmni->rlni", forward, back, preferred_element_type=F32)
    mixed = mixed.reshape(rows_dev, length, width).astype(BF16)
    block_w1 = jnp.einsum("pn,cipj->cinj", owner, gw1).reshape(1, 2, BS, width)
    block_w2 = jnp.einsum("pn,cipj->cinj", owner, gw2).reshape(1, 2, BS, width)
    block_b1 = jnp.einsum("pn,cpj->cnj", owner, gb1).reshape(1, 2, width)
    columns = width // lat_count
    full_w1, full_w2, full_b1 = lax.psum((block_w1, block_w2, block_b1), "lat")
    sum_w1 = lax.dynamic_slice_in_dim(full_w1, lat_pos * columns, columns, 3)
    sum_w2 = lax.dynamic_slice_in_dim(full_w2, lat_pos * columns, columns, 3)
    sum_b1 = lax.dynamic_slice_in_dim(full_b1, lat_pos * columns, columns, 2)
    whole = (cotan.astype(F32) + mixed.astype(F32)).astype(BF16)
    received = from_behind(whole[None], "section", -1)
    return (received, sum_w1, sum_w2, sum_b1)


def per_device(grad_out, spec_saved, w1, w2, b1, mode_counts, assignment):
    n_dev = lax.axis_size("lat")
    pairs_dev = spec_saved.shape[3] // BS
    even = grad_out.shape[1] == 1 and pairs_dev % NB == 0 and n_dev % NB == 0
    even = even and BS % (n_dev // NB) == 0 and BS // (n_dev // NB) % 16 == 0
    body = whole_blocks if even else split_blocks
    return body(grad_out, spec_saved, w1, w2, b1, mode_counts, assignment)


def solution(mesh):
    return jax.shard_map(
        per_device,
        mesh=mesh,
        in_specs=(
            P("section", "lat", None, None),
            P("section", None, None, "lat"),
            P("section", None, None, None),
            P("section", None, None, None),
            P("section", None, None),
            P(),
            P(),
        ),
        out_specs=(
            P("section", "lat", None, None),
            P("section", None, None, "lat"),
            P("section", None, None, "lat"),
            P("section", None, "lat"),
        ),
        check_vma=False,
    )
```

```python
import functools
import math

import jax
import jax.numpy as jnp
import numpy as np
from jax import lax
from jax.experimental import pallas as pl
from jax.experimental.pallas import tpu as pltpu
from jax.sharding import PartitionSpec as P

NB = 4
BS = 96
KM = 72
LANES = 128
F32 = jnp.float32
BF16 = jnp.bfloat16


def from_behind(value, axis, by):
    length = lax.axis_size(axis)
    pairs = [(i, i + by) for i in range(length) if 0 <= i + by < length]
    return lax.ppermute(value, axis, pairs)


def lon_tables(n_modes, length):
    modes = np.arange(n_modes)
    phase = modes[:, None] * np.arange(length)[None, :] % length
    angle = phase * (2.0 * math.pi / length)
    forward = np.stack([np.cos(angle), -np.sin(angle)]) / math.sqrt(length)
    weight = np.where(modes == 0, 1.0, 2.0)[None, :, None]
    return forward, forward * weight


def lat_waves(n_rows):
    freqs = np.arange(n_rows)
    angle = (freqs[:, None] * freqs[None, :] % n_rows) * (2.0 * math.pi / n_rows)
    factor = 1.0 / math.sqrt(n_rows)
    return np.cos(angle) * factor, np.sin(angle) * factor


def silu_slope(pre):
    sig = jax.nn.sigmoid(pre)
    return sig * (1.0 + pre * (1.0 - sig))


def window(x, start):
    low = start // LANES * LANES
    shift = start - low
    if shift == 0:
        return x[:, low : low + LANES]
    if shift + BS <= LANES:
        return pltpu.roll(x[:, low : low + LANES], LANES - shift, 1)
    return pltpu.roll(x[:, low : low + 2 * LANES], 2 * LANES - shift, 1)[:, :LANES]


def dense(parts):
    lane = lax.broadcasted_iota(jnp.int32, parts[0].shape, 1)
    first = pltpu.roll(parts[1], 96, 1)
    second = pltpu.roll(parts[2], 64, 1)
    third = pltpu.roll(parts[3], 32, 1)
    return jnp.concatenate(
        [
            jnp.where(lane < 96, parts[0], first),
            jnp.where(lane < 64, first, second),
            jnp.where(lane < 32, second, third),
        ],
        axis=1,
    )


def dot(a, b, contract):
    return lax.dot_general(a, b, ((contract[:1], contract[1:]), ((), ())), preferred_element_type=F32)


def keep_active(counts, assign, q, groups):
    active = counts[assign[lax.axis_index("lat")]]
    shape = groups[0].shape
    number = lax.broadcasted_iota(jnp.int32, shape, 0)
    number = jnp.where(number >= NB * q, number - NB * q, number)
    mode = number
    for z in range(1, NB):
        mode = jnp.where(number >= z * q, number + z * q, mode)
    return [jnp.where(mode < active - g * q, value, 0.0) for g, value in enumerate(groups)]


def analyse_kernel(q, counts, assign, field, table, saved, out):
    rows = out.shape[1]
    spectral = jnp.dot(table[...], field[...], preferred_element_type=F32)
    groups = keep_active(counts, assign, q, [spectral[:rows], spectral[rows:]])
    parts = [saved[:, c, :].astype(F32) for c in range(2)]
    for n in range(NB):
        pieces = [window(group, n * BS) for group in groups]
        for part in parts:
            columns = [window(part, (mm * NB + n) * BS) for mm in range(q)]
            pieces.append(jnp.concatenate(columns, axis=0))
        out[n] = dense(pieces).astype(BF16)


def weights_kernel(w1, w2, b1, mat1, mat2, bias):
    block = lax.axis_index("lat") // 2

    def pick(x):
        value = window(x, 0)
        for n in range(1, NB):
            value = jnp.where(block == n, window(x, n * BS), value)
        lane = lax.broadcasted_iota(jnp.int32, value.shape, 1)
        return jnp.where(lane < BS, value, 0.0)

    gap = jnp.zeros((LANES - BS, 2 * LANES), BF16)
    for source, mat in ((w1, mat1), (w2, mat2)):
        real, imag = (pick(source[c].astype(F32)) for c in range(2))
        mat[0:BS] = jnp.concatenate([real, imag], axis=1).astype(BF16)
        mat[BS:LANES] = gap
        mat[LANES : LANES + BS] = jnp.concatenate([-imag, real], axis=1).astype(BF16)
        mat[LANES + BS : 2 * LANES] = gap
    shift_b = pick(b1[...].astype(F32))
    bias[...] = jnp.concatenate([shift_b[0:1], shift_b[1:2]], axis=1)


def filter_kernel(assign, own, other, mat1, mat2, bias, lat, lat_t, out, gw1, gw2, gb1, by_lat):
    n_half, rows, width = own.shape
    core = lax.rem(lax.axis_index("lat"), 2)
    segments = [BS * j for j in range(4)]
    saved = []
    for b, buffer in enumerate((own, other)):
        side = core if b == 0 else 1 - core
        pieces = []
        for z in range(n_half):
            chunk = buffer[z].astype(F32)
            groups = [window(chunk, segments[j]) for j in range(2)]
            by_lat[assign[2 * z + side]] = jnp.concatenate(groups, axis=1)
            parts = [window(chunk, segments[j]) for j in (2, 3)]
            pieces.append(jnp.concatenate(parts, axis=1))
        saved.append(jnp.concatenate(pieces, axis=0).astype(BF16))
    field = by_lat[...].reshape(lat.shape[1], 2 * LANES).astype(BF16)
    grad_y = dot(lat[...], field, (1, 0)).astype(BF16)
    points = grad_y.shape[0] // 2
    first, second = mat1[...], mat2[...]
    both1, both2, sums, inner = 0.0, 0.0, 0.0, []
    for g in range(2):
        v = jnp.where(core == g, saved[0], saved[1])
        dy = [grad_y[c * points : (c + 1) * points, g * LANES : (g + 1) * LANES] for c in range(2)]
        dy = jnp.concatenate(dy, axis=1)
        pre = dot(v, first, (1, 0)) + bias[...]
        sig = jax.nn.sigmoid(pre)
        hidden = (pre * sig).astype(BF16)
        grad_hidden = dot(dy, second, (1, 1))
        dp = (grad_hidden * (sig * (1.0 + pre * (1.0 - sig)))).astype(BF16)
        dv = dot(dp, first, (1, 1)).astype(BF16)
        inner.append(jnp.concatenate([dv[:, :LANES], dv[:, LANES:]], axis=0))
        both1 += dot(dp, v, (0, 0))
        both2 += dot(dy, hidden, (0, 0))
        sums += jnp.sum(dp.astype(F32), axis=0, keepdims=True)
    inner = jnp.concatenate(inner, axis=1)
    for z in range(n_half):
        band = dot(lat_t[assign[2 * z + core]], inner, (1, 0))
        out[z] = band.astype(BF16)
    half = BS // 2
    for both, ref in ((both1, gw1), (both2, gw2)):
        real = both[:BS, :LANES] + both[LANES : LANES + BS, LANES:]
        imag = both[LANES : LANES + BS, :LANES] - both[:BS, LANES:]
        for c, full in enumerate((real, imag)):
            ref[c] = jnp.where(core == 0, full[:half], full[half:])[:, :BS]
    for c in range(2):
        line = sums[:, c * LANES : (c + 1) * LANES]
        gb1[c : c + 1] = jnp.where(core == 0, line[:, :half], line[:, half:BS])


def compose_kernel(q, counts, assign, back, field, table, out):
    chunks = [back[n].astype(F32) for n in range(NB)]
    groups = [
        dense([chunk[:, g * LANES : (g + 1) * LANES] for chunk in chunks]) for g in range(2)
    ]
    held = jnp.concatenate(keep_active(counts, assign, q, groups), axis=0).astype(BF16)
    mixed = jnp.dot(table[...], held, preferred_element_type=F32).astype(BF16)
    out[...] = (field[...].astype(F32) + mixed.astype(F32)).astype(BF16)


def call(kernel, outs, scratch, n_scalars, *args):
    whole = pl.BlockSpec(memory_space=pltpu.VMEM)
    scalar = pl.BlockSpec(memory_space=pltpu.SMEM)
    specs = [scalar] * n_scalars + [whole] * (len(args) - n_scalars)
    many = isinstance(outs, tuple)
    return pl.pallas_call(
        kernel,
        out_shape=outs,
        in_specs=specs,
        out_specs=tuple([whole] * len(outs)) if many else whole,
        scratch_shapes=scratch,
        compiler_params=pltpu.CompilerParams(vmem_limit_bytes=32 * 2**20),
    )(*args)


def paired_blocks(grad_out, spec_saved, w1, w2, b1, mode_counts, assignment):
    length, width = grad_out.shape[2:]
    n_rows = assignment.shape[0]
    q = spec_saved.shape[3] // (NB * BS)
    rows = 2 * NB * q
    forward, inverse = lon_tables(KM, length)

    def by_group(table):
        table = table.reshape(2, NB, 2, q, length).transpose(2, 0, 1, 3, 4)
        return table.reshape(2 * rows, length).astype(BF16)

    cosine, sine = lat_waves(n_rows)
    waves = np.array([[cosine, sine], [-sine, cosine]])
    lat = np.einsum("eckr,uv->eukrcv", waves, np.eye(NB * q))
    lat = lat.reshape(2 * NB * q * n_rows, n_rows * rows).astype(BF16)
    lat_t = np.ascontiguousarray(lat.T).reshape(n_rows, rows, -1)

    field = grad_out.reshape(length, width)
    sent = call(
        functools.partial(analyse_kernel, q),
        jax.ShapeDtypeStruct((NB, rows, width), BF16),
        [],
        2,
        mode_counts,
        assignment,
        field,
        jnp.asarray(by_group(inverse)),
        spec_saved[0],
    )
    cores = [[2 * z + c for z in range(NB)] for c in range(2)]
    exchange = functools.partial(
        lax.all_to_all,
        axis_name="lat",
        split_axis=0,
        concat_axis=0,
        axis_index_groups=cores,
        tiled=True,
    )
    own = exchange(sent)
    wide = (2 * LANES, 2 * LANES)
    mat1, mat2, bias = call(
        weights_kernel,
        (
            jax.ShapeDtypeStruct(wide, BF16),
            jax.ShapeDtypeStruct(wide, BF16),
            jax.ShapeDtypeStruct((1, 2 * LANES), F32),
        ),
        [],
        0,
        w1[0],
        w2[0],
        b1[0],
    )
    other = lax.ppermute(own, "lat", [(i, i ^ 1) for i in range(2 * NB)])
    chunks, gw1, gw2, gb1 = call(
        filter_kernel,
        (
            jax.ShapeDtypeStruct((NB, rows, 2 * LANES), BF16),
            jax.ShapeDtypeStruct((2, BS // 2, BS), F32),
            jax.ShapeDtypeStruct((2, BS // 2, BS), F32),
            jax.ShapeDtypeStruct((2, BS // 2), F32),
        ),
        [pltpu.VMEM((n_rows, rows, 2 * LANES), F32)],
        1,
        assignment,
        own,
        other,
        mat1,
        mat2,
        bias,
        jnp.asarray(lat),
        jnp.asarray(lat_t),
    )
    back = exchange(chunks)
    total = call(
        functools.partial(compose_kernel, q),
        jax.ShapeDtypeStruct((length, width), BF16),
        [],
        2,
        mode_counts,
        assignment,
        back,
        field,
        jnp.asarray(by_group(forward).T),
    )
    received = from_behind(total[None, None], "section", -1)
    return received, gw1.swapaxes(1, 2)[None], gw2.swapaxes(1, 2)[None], gb1[None]


def apply_mat(vec, mat):
    return jnp.einsum("kpi,ipj->kpj", vec, mat, preferred_element_type=F32)


def adjoint_mat(vec, mat):
    return jnp.einsum("kpj,ipj->kpi", vec, mat, preferred_element_type=F32)


def outer_sum(left, right):
    return jnp.einsum("kpi,kpj->ipj", left, right, preferred_element_type=F32)


def split_blocks(grad_out, spec_saved, w1, w2, b1, mode_counts, assignment):
    rows_dev = grad_out.shape[1]
    length = grad_out.shape[2]
    width = grad_out.shape[3]
    n_rows = assignment.shape[0]
    pairs_dev = spec_saved.shape[3] // BS
    forward, inverse = (jnp.asarray(t.astype(BF16)) for t in lon_tables(KM, length))
    cosine, sine = (jnp.asarray(t.astype(BF16))[:, assignment] for t in lat_waves(n_rows))
    table = jnp.stack(
        [jnp.stack([cosine, sine], axis=-1), jnp.stack([-sine, cosine], axis=-1)], axis=1
    )
    lat_pos = lax.axis_index("lat")
    lat_count = lax.axis_size("lat")
    own_lat = lax.dynamic_slice_in_dim(assignment, lat_pos * rows_dev, rows_dev)
    active = (jnp.arange(KM, dtype=jnp.int32)[None, :] < mode_counts[own_lat][:, None]).astype(F32)
    cotan = grad_out[0]
    spectral = jnp.einsum(
        "cml,rlni->rcmni",
        inverse,
        cotan.reshape(rows_dev, length, NB, BS),
        preferred_element_type=F32,
    )
    spectral = (spectral * active[:, None, :, None, None]).astype(BF16)
    spectral = spectral.reshape(rows_dev, 2, KM * NB * BS)
    pencil = lax.all_to_all(spectral, "lat", split_axis=2, concat_axis=0, tiled=True)
    pencil = pencil.reshape(n_rows, 2, pairs_dev, BS)
    grad_y = jnp.einsum("kerc,rcpi->kepi", table, pencil, preferred_element_type=F32).astype(BF16)
    saved = spec_saved[0].reshape(n_rows, 2, pairs_dev, BS)
    pair_ids = lat_pos * pairs_dev + jnp.arange(pairs_dev, dtype=jnp.int32)
    owner = (pair_ids % NB)[:, None] == jnp.arange(NB, dtype=jnp.int32)[None, :]
    owner = owner.astype(F32)
    first = jnp.take(w1[0].reshape(2, BS, NB, BS), pair_ids % NB, axis=2)
    second = jnp.take(w2[0].reshape(2, BS, NB, BS), pair_ids % NB, axis=2)
    shift_b = jnp.take(b1[0].reshape(2, NB, BS), pair_ids % NB, axis=1).astype(F32)
    v_r = saved[:, 0]
    v_i = saved[:, 1]
    pre_r = apply_mat(v_r, first[0]) - apply_mat(v_i, first[1]) + shift_b[0][None]
    pre_i = apply_mat(v_i, first[0]) + apply_mat(v_r, first[1]) + shift_b[1][None]
    hid_r = jax.nn.silu(pre_r).astype(BF16)
    hid_i = jax.nn.silu(pre_i).astype(BF16)
    dy_r = grad_y[:, 0]
    dy_i = grad_y[:, 1]
    dh_r = adjoint_mat(dy_r, second[0]) + adjoint_mat(dy_i, second[1])
    dh_i = adjoint_mat(dy_i, second[0]) - adjoint_mat(dy_r, second[1])
    dp_r = (dh_r * silu_slope(pre_r)).astype(BF16)
    dp_i = (dh_i * silu_slope(pre_i)).astype(BF16)
    gw2 = jnp.stack(
        [
            outer_sum(hid_r, dy_r) + outer_sum(hid_i, dy_i),
            outer_sum(hid_r, dy_i) - outer_sum(hid_i, dy_r),
        ]
    )
    gw1 = jnp.stack(
        [outer_sum(v_r, dp_r) + outer_sum(v_i, dp_i), outer_sum(v_r, dp_i) - outer_sum(v_i, dp_r)]
    )
    gb1 = jnp.stack([jnp.sum(dp_r.astype(F32), axis=0), jnp.sum(dp_i.astype(F32), axis=0)])
    dv_r = adjoint_mat(dp_r, first[0]) + adjoint_mat(dp_i, first[1])
    dv_i = adjoint_mat(dp_i, first[0]) - adjoint_mat(dp_r, first[1])
    grad_v = jnp.stack([dv_r, dv_i], axis=1).astype(BF16)
    grad_u = jnp.einsum("kerc,kepi->rcpi", table, grad_v, preferred_element_type=F32).astype(BF16)
    grad_u = grad_u.reshape(n_rows, 2, pairs_dev * BS)
    back = lax.all_to_all(grad_u, "lat", split_axis=0, concat_axis=2, tiled=True)
    back = back.reshape(rows_dev, 2, KM, NB, BS) * active[:, None, :, None, None].astype(BF16)
    mixed = jnp.einsum("cml,rcmni->rlni", forward, back, preferred_element_type=F32)
    mixed = mixed.reshape(rows_dev, length, width).astype(BF16)
    block_w1 = jnp.einsum("pn,cipj->cinj", owner, gw1).reshape(1, 2, BS, width)
    block_w2 = jnp.einsum("pn,cipj->cinj", owner, gw2).reshape(1, 2, BS, width)
    block_b1 = jnp.einsum("pn,cpj->cnj", owner, gb1).reshape(1, 2, width)
    columns = width // lat_count
    full_w1, full_w2, full_b1 = lax.psum((block_w1, block_w2, block_b1), "lat")
    sum_w1 = lax.dynamic_slice_in_dim(full_w1, lat_pos * columns, columns, 3)
    sum_w2 = lax.dynamic_slice_in_dim(full_w2, lat_pos * columns, columns, 3)
    sum_b1 = lax.dynamic_slice_in_dim(full_b1, lat_pos * columns, columns, 2)
    whole = (cotan.astype(F32) + mixed.astype(F32)).astype(BF16)
    received = from_behind(whole[None], "section", -1)
    return (received, sum_w1, sum_w2, sum_b1)


def per_device(grad_out, spec_saved, w1, w2, b1, mode_counts, assignment):
    n_dev = lax.axis_size("lat")
    pairs_dev = spec_saved.shape[3] // BS
    paired = n_dev == 2 * NB and grad_out.shape[1] == 1 and pairs_dev % NB == 0
    body = paired_blocks if paired else split_blocks
    return body(grad_out, spec_saved, w1, w2, b1, mode_counts, assignment)


def solution(mesh):
    return jax.shard_map(
        per_device,
        mesh=mesh,
        in_specs=(
            P("section", "lat", None, None),
            P("section", None, None, "lat"),
            P("section", None, None, None),
            P("section", None, None, None),
            P("section", None, None),
            P(),
            P(),
        ),
        out_specs=(
            P("section", "lat", None, None),
            P("section", None, None, "lat"),
            P("section", None, None, "lat"),
            P("section", None, "lat"),
        ),
        check_vma=False,
    )
```

```python
import functools
import math

import jax
import jax.numpy as jnp
import numpy as np
from jax import lax
from jax.experimental import pallas as pl
from jax.experimental.pallas import tpu as pltpu
from jax.sharding import PartitionSpec as P

NB = 4
BS = 96
KM = 72
LANES = 128
F32 = jnp.float32
BF16 = jnp.bfloat16


def from_behind(value, axis, by):
    length = lax.axis_size(axis)
    pairs = [(i, i + by) for i in range(length) if 0 <= i + by < length]
    return lax.ppermute(value, axis, pairs)


def lon_tables(n_modes, length):
    modes = np.arange(n_modes)
    phase = modes[:, None] * np.arange(length)[None, :] % length
    angle = phase * (2.0 * math.pi / length)
    forward = np.stack([np.cos(angle), -np.sin(angle)]) / math.sqrt(length)
    weight = np.where(modes == 0, 1.0, 2.0)[None, :, None]
    return forward, forward * weight


def lat_waves(n_rows):
    freqs = np.arange(n_rows)
    angle = (freqs[:, None] * freqs[None, :] % n_rows) * (2.0 * math.pi / n_rows)
    factor = 1.0 / math.sqrt(n_rows)
    return np.cos(angle) * factor, np.sin(angle) * factor


def silu_slope(pre):
    sig = jax.nn.sigmoid(pre)
    return sig * (1.0 + pre * (1.0 - sig))


def window(x, start):
    low = start // LANES * LANES
    shift = start - low
    if shift == 0:
        return x[:, low : low + LANES]
    if shift + BS <= LANES:
        return pltpu.roll(x[:, low : low + LANES], LANES - shift, 1)
    return pltpu.roll(x[:, low : low + 2 * LANES], 2 * LANES - shift, 1)[:, :LANES]


def dense(parts):
    lane = lax.broadcasted_iota(jnp.int32, parts[0].shape, 1)
    first = pltpu.roll(parts[1], 96, 1)
    second = pltpu.roll(parts[2], 64, 1)
    third = pltpu.roll(parts[3], 32, 1)
    return jnp.concatenate(
        [
            jnp.where(lane < 96, parts[0], first),
            jnp.where(lane < 64, first, second),
            jnp.where(lane < 32, second, third),
        ],
        axis=1,
    )


def dot(a, b, contract):
    return lax.dot_general(a, b, ((contract[:1], contract[1:]), ((), ())), preferred_element_type=F32)


def keep_active(counts, assign, q, groups):
    active = counts[assign[lax.axis_index("lat")]]
    shape = groups[0].shape
    number = lax.broadcasted_iota(jnp.int32, shape, 0)
    number = jnp.where(number >= NB * q, number - NB * q, number)
    mode = number
    for z in range(1, NB):
        mode = jnp.where(number >= z * q, number + z * q, mode)
    return [jnp.where(mode < active - g * q, value, 0.0) for g, value in enumerate(groups)]


def fetch(sems, sources, targets):
    copies = [
        pltpu.make_async_copy(source, target, sems.at[i])
        for i, (source, target) in enumerate(zip(sources, targets))
    ]
    for copy in copies:
        copy.start()
    return copies


def wait(copies):
    for copy in copies:
        copy.wait()


def partner(d):
    return jnp.bitwise_xor(lax.axis_index("lat") // 2, d)


def analyse_kernel(q, *refs):
    hbm, outs, held, (by_block, sems) = refs[:5], refs[5:9], refs[9:14], refs[14:]
    counts, assign, field, table, saved = held
    copies = fetch(sems, hbm, held)
    wait(copies[4:])
    parts = [saved[:, c, :].astype(F32) for c in range(2)]
    points = [
        [
            jnp.concatenate([window(part, (mm * NB + n) * BS) for mm in range(q)], axis=0)
            for part in parts
        ]
        for n in range(NB)
    ]
    wait(copies[:4])
    rows = by_block.shape[1]
    spectral = jnp.dot(table[...], field[...], preferred_element_type=F32)
    groups = keep_active(counts, assign, q, [spectral[:rows], spectral[rows:]])
    for n in range(NB):
        pieces = [window(group, n * BS) for group in groups]
        by_block[n] = dense(pieces + points[n]).astype(BF16)
    for d, out in enumerate(outs):
        out[...] = by_block[partner(d)]


def weights_kernel(w1_hbm, w2_hbm, b1_hbm, mat1, mat2, bias, w1, w2, b1, sems):
    wait(fetch(sems, (w1_hbm, w2_hbm, b1_hbm), (w1, w2, b1)))
    block = lax.axis_index("lat") // 2

    def pick(x):
        value = window(x, 0)
        for n in range(1, NB):
            value = jnp.where(block == n, window(x, n * BS), value)
        lane = lax.broadcasted_iota(jnp.int32, value.shape, 1)
        return jnp.where(lane < BS, value, 0.0)

    gap = jnp.zeros((LANES - BS, 2 * LANES), BF16)
    for source, mat in ((w1, mat1), (w2, mat2)):
        real, imag = (pick(source[c].astype(F32)) for c in range(2))
        mat[0:BS] = jnp.concatenate([real, imag], axis=1).astype(BF16)
        mat[BS:LANES] = gap
        mat[LANES : LANES + BS] = jnp.concatenate([-imag, real], axis=1).astype(BF16)
        mat[LANES + BS : 2 * LANES] = gap
    shift_b = pick(b1[...].astype(F32))
    bias[...] = jnp.concatenate([shift_b[0:1], shift_b[1:2]], axis=1)


def join_kernel(*refs):
    out = refs[-1]
    for d, ref in enumerate(refs[:-1]):
        out[d] = ref[...]


def pack(band):
    rows = band.shape[0]
    tail = rows // 2 + 4
    left, right = band[:, :LANES], pltpu.roll(band[:, LANES:], 96, 1)
    lane = lax.broadcasted_iota(jnp.int32, left.shape, 1)
    upper = jnp.where(lane < 96, left, right)
    lower = pltpu.roll(right[rows - tail :], 64, 1)
    lower = jnp.where(lane[:tail] < 64, right[:tail], lower)
    return jnp.concatenate([upper, lower], axis=0)


def unpack(packed, rows):
    tail = rows // 2 + 4
    upper, lower = packed[:rows], packed[rows:]
    rest = jnp.concatenate([lower, pltpu.roll(lower, 64, 1)[2 * tail - rows :]], axis=0)
    lane = lax.broadcasted_iota(jnp.int32, upper.shape, 1)
    right = jnp.where(lane < 32, pltpu.roll(upper, 32, 1), pltpu.roll(rest, 32, 1))
    return [upper, right]


def filter_kernel(*refs):
    own, other, mat1, mat2, bias, assign_hbm, lat_hbm, lat_t_hbm = refs[:8]
    outs, (gw1, gw2, gb1) = refs[8:12], refs[12:15]
    assign, lat, lat_t, by_lat, points_v, sems = refs[15:]
    copies = fetch(sems, (assign_hbm, lat_hbm, lat_t_hbm), (assign, lat, lat_t))
    wait(copies[:1])
    n_half, rows, width = own.shape
    core = lax.rem(lax.axis_index("lat"), 2)
    segments = [BS * j for j in range(4)]
    for b, buffer in enumerate((own, other)):
        side = core if b == 0 else 1 - core
        for d in range(n_half):
            chunk = buffer[d].astype(F32)
            groups = [window(chunk, segments[j]) for j in range(2)]
            by_lat[assign[2 * partner(d) + side]] = jnp.concatenate(groups, axis=1)
            parts = [window(chunk, segments[j]) for j in (2, 3)]
            points_v[side, partner(d)] = jnp.concatenate(parts, axis=1)
    field = by_lat[...].reshape(lat.shape[1], 2 * LANES).astype(BF16)
    wait(copies[1:2])
    grad_y = dot(lat[...], field, (1, 0)).astype(BF16)
    points = grad_y.shape[0] // 2
    first, second = mat1[...], mat2[...]
    both1, both2, sums, inner = 0.0, 0.0, 0.0, []
    for g in range(2):
        v = points_v[g].reshape(points, 2 * LANES).astype(BF16)
        dy = [grad_y[c * points : (c + 1) * points, g * LANES : (g + 1) * LANES] for c in range(2)]
        dy = jnp.concatenate(dy, axis=1)
        pre = dot(v, first, (1, 0)) + bias[...]
        sig = jax.nn.sigmoid(pre)
        hidden = (pre * sig).astype(BF16)
        grad_hidden = dot(dy, second, (1, 1))
        dp = (grad_hidden * (sig * (1.0 + pre * (1.0 - sig)))).astype(BF16)
        dv = dot(dp, first, (1, 1)).astype(BF16)
        inner.append(jnp.concatenate([dv[:, :LANES], dv[:, LANES:]], axis=0))
        both1 += dot(dp, v, (0, 0))
        both2 += dot(dy, hidden, (0, 0))
        sums += jnp.sum(dp.astype(F32), axis=0, keepdims=True)
    inner = jnp.concatenate(inner, axis=1)
    wait(copies[2:])
    for d, out in enumerate(outs):
        band = dot(lat_t[assign[2 * partner(d) + core]], inner, (1, 0))
        out[...] = pack(band).astype(BF16)
    half = BS // 2
    for both, ref in ((both1, gw1), (both2, gw2)):
        real = both[:BS, :LANES] + both[LANES : LANES + BS, LANES:]
        imag = both[LANES : LANES + BS, :LANES] - both[:BS, LANES:]
        for c, full in enumerate((real, imag)):
            ref[c] = jnp.where(core == 0, full[:half], full[half:])[:, :BS]
    for c in range(2):
        line = sums[:, c * LANES : (c + 1) * LANES]
        gb1[c : c + 1] = jnp.where(core == 0, line[:, :half], line[:, half:BS])


def compose_kernel(q, *refs):
    backs, hbm, out, held, (by_block, sems) = refs[:4], refs[4:8], refs[8], refs[9:13], refs[13:]
    counts, assign, field, table = held
    copies = fetch(sems, hbm, held)
    rows = 2 * NB * q
    for d, back in enumerate(backs):
        by_block[partner(d)] = jnp.concatenate(unpack(back[...].astype(F32), rows), axis=1)
    groups = [
        dense([by_block[n, :, g * LANES : (g + 1) * LANES] for n in range(NB)]) for g in range(2)
    ]
    wait(copies)
    masked = jnp.concatenate(keep_active(counts, assign, q, groups), axis=0).astype(BF16)
    mixed = jnp.dot(table[...], masked, preferred_element_type=F32).astype(BF16)
    out[...] = (field[...].astype(F32) + mixed.astype(F32)).astype(BF16)


VMEM = pl.BlockSpec(memory_space=pltpu.VMEM)
HBM = pl.BlockSpec(memory_space=pltpu.HBM)


def call(kernel, outs, scratch, near, far):
    many = isinstance(outs, tuple)
    return pl.pallas_call(
        kernel,
        out_shape=outs,
        in_specs=[VMEM] * len(near) + [HBM] * len(far),
        out_specs=tuple([VMEM] * len(outs)) if many else VMEM,
        scratch_shapes=scratch,
        compiler_params=pltpu.CompilerParams(vmem_limit_bytes=32 * 2**20),
    )(*near, *far)


def scratch_for(*arrays):
    scratch = []
    for x in arrays:
        space = pltpu.SMEM if x.dtype == jnp.int32 else pltpu.VMEM
        scratch.append(space(x.shape, x.dtype))
    return scratch, pltpu.SemaphoreType.DMA((len(arrays),))


def paired_blocks(grad_out, spec_saved, w1, w2, b1, mode_counts, assignment):
    length, width = grad_out.shape[2:]
    n_rows = assignment.shape[0]
    q = spec_saved.shape[3] // (NB * BS)
    rows = 2 * NB * q
    forward, inverse = lon_tables(KM, length)

    def by_group(table):
        table = table.reshape(2, NB, 2, q, length).transpose(2, 0, 1, 3, 4)
        return table.reshape(2 * rows, length).astype(BF16)

    cosine, sine = lat_waves(n_rows)
    waves = np.array([[cosine, sine], [-sine, cosine]])
    lat = np.einsum("eckr,uv->eukrcv", waves, np.eye(NB * q))
    lat = lat.reshape(2 * NB * q * n_rows, n_rows * rows).astype(BF16)
    lat_t = np.ascontiguousarray(lat.T).reshape(n_rows, rows, -1)

    lat, lat_t = jnp.asarray(lat), jnp.asarray(lat_t)
    inverse = jnp.asarray(by_group(inverse))
    forward = jnp.asarray(by_group(forward).T)

    def swap(chunks):
        pairs = [[(i, i ^ (2 * d)) for i in range(2 * NB)] for d in range(NB)]
        return [chunks[0]] + [lax.ppermute(chunks[d], "lat", pairs[d]) for d in (3, 2, 1)][::-1]

    field = grad_out.reshape(length, width)
    shape = jax.ShapeDtypeStruct
    far = (mode_counts, assignment, field, inverse, spec_saved[0])
    scratch, sems = scratch_for(*far)
    sent = call(
        functools.partial(analyse_kernel, q),
        (shape((rows, width), BF16),) * NB,
        scratch + [pltpu.VMEM((NB, rows, width), BF16), sems],
        (),
        far,
    )
    received = swap(sent)
    far = (w1[0], w2[0], b1[0])
    scratch, sems = scratch_for(*far)
    wide = (2 * LANES, 2 * LANES)
    mats = call(
        weights_kernel,
        (shape(wide, BF16), shape(wide, BF16), shape((1, 2 * LANES), F32)),
        scratch + [sems],
        (),
        far,
    )
    own = call(join_kernel, shape((NB, rows, width), BF16), [], received, ())
    other = lax.ppermute(own, "lat", [(i, i ^ 1) for i in range(2 * NB)])
    far = (assignment, lat, lat_t)
    scratch, sems = scratch_for(*far)
    packed = shape((rows + rows // 2 + 4, LANES), BF16)
    matrix = shape((2, BS // 2, BS), F32)
    *chunks, gw1, gw2, gb1 = call(
        filter_kernel,
        (packed,) * NB + (matrix, matrix, shape((2, BS // 2), F32)),
        scratch
        + [
            pltpu.VMEM((n_rows, rows, 2 * LANES), F32),
            pltpu.VMEM((2, NB, rows, 2 * LANES), F32),
            sems,
        ],
        (own, other, *mats),
        far,
    )
    backs = swap(chunks)
    far = (mode_counts, assignment, field, forward)
    scratch, sems = scratch_for(*far)
    total = call(
        functools.partial(compose_kernel, q),
        shape((length, width), BF16),
        scratch + [pltpu.VMEM((NB, rows, 2 * LANES), F32), sems],
        backs,
        far,
    )
    shifted = from_behind(total[None, None], "section", -1)
    return shifted, gw1.swapaxes(1, 2)[None], gw2.swapaxes(1, 2)[None], gb1[None]


def apply_mat(vec, mat):
    return jnp.einsum("kpi,ipj->kpj", vec, mat, preferred_element_type=F32)


def adjoint_mat(vec, mat):
    return jnp.einsum("kpj,ipj->kpi", vec, mat, preferred_element_type=F32)


def outer_sum(left, right):
    return jnp.einsum("kpi,kpj->ipj", left, right, preferred_element_type=F32)


def split_blocks(grad_out, spec_saved, w1, w2, b1, mode_counts, assignment):
    rows_dev = grad_out.shape[1]
    length = grad_out.shape[2]
    width = grad_out.shape[3]
    n_rows = assignment.shape[0]
    pairs_dev = spec_saved.shape[3] // BS
    forward, inverse = (jnp.asarray(t.astype(BF16)) for t in lon_tables(KM, length))
    cosine, sine = (jnp.asarray(t.astype(BF16))[:, assignment] for t in lat_waves(n_rows))
    table = jnp.stack(
        [jnp.stack([cosine, sine], axis=-1), jnp.stack([-sine, cosine], axis=-1)], axis=1
    )
    lat_pos = lax.axis_index("lat")
    lat_count = lax.axis_size("lat")
    own_lat = lax.dynamic_slice_in_dim(assignment, lat_pos * rows_dev, rows_dev)
    active = (jnp.arange(KM, dtype=jnp.int32)[None, :] < mode_counts[own_lat][:, None]).astype(F32)
    cotan = grad_out[0]
    spectral = jnp.einsum(
        "cml,rlni->rcmni",
        inverse,
        cotan.reshape(rows_dev, length, NB, BS),
        preferred_element_type=F32,
    )
    spectral = (spectral * active[:, None, :, None, None]).astype(BF16)
    spectral = spectral.reshape(rows_dev, 2, KM * NB * BS)
    pencil = lax.all_to_all(spectral, "lat", split_axis=2, concat_axis=0, tiled=True)
    pencil = pencil.reshape(n_rows, 2, pairs_dev, BS)
    grad_y = jnp.einsum("kerc,rcpi->kepi", table, pencil, preferred_element_type=F32).astype(BF16)
    saved = spec_saved[0].reshape(n_rows, 2, pairs_dev, BS)
    pair_ids = lat_pos * pairs_dev + jnp.arange(pairs_dev, dtype=jnp.int32)
    owner = (pair_ids % NB)[:, None] == jnp.arange(NB, dtype=jnp.int32)[None, :]
    owner = owner.astype(F32)
    first = jnp.take(w1[0].reshape(2, BS, NB, BS), pair_ids % NB, axis=2)
    second = jnp.take(w2[0].reshape(2, BS, NB, BS), pair_ids % NB, axis=2)
    shift_b = jnp.take(b1[0].reshape(2, NB, BS), pair_ids % NB, axis=1).astype(F32)
    v_r = saved[:, 0]
    v_i = saved[:, 1]
    pre_r = apply_mat(v_r, first[0]) - apply_mat(v_i, first[1]) + shift_b[0][None]
    pre_i = apply_mat(v_i, first[0]) + apply_mat(v_r, first[1]) + shift_b[1][None]
    hid_r = jax.nn.silu(pre_r).astype(BF16)
    hid_i = jax.nn.silu(pre_i).astype(BF16)
    dy_r = grad_y[:, 0]
    dy_i = grad_y[:, 1]
    dh_r = adjoint_mat(dy_r, second[0]) + adjoint_mat(dy_i, second[1])
    dh_i = adjoint_mat(dy_i, second[0]) - adjoint_mat(dy_r, second[1])
    dp_r = (dh_r * silu_slope(pre_r)).astype(BF16)
    dp_i = (dh_i * silu_slope(pre_i)).astype(BF16)
    gw2 = jnp.stack(
        [
            outer_sum(hid_r, dy_r) + outer_sum(hid_i, dy_i),
            outer_sum(hid_r, dy_i) - outer_sum(hid_i, dy_r),
        ]
    )
    gw1 = jnp.stack(
        [outer_sum(v_r, dp_r) + outer_sum(v_i, dp_i), outer_sum(v_r, dp_i) - outer_sum(v_i, dp_r)]
    )
    gb1 = jnp.stack([jnp.sum(dp_r.astype(F32), axis=0), jnp.sum(dp_i.astype(F32), axis=0)])
    dv_r = adjoint_mat(dp_r, first[0]) + adjoint_mat(dp_i, first[1])
    dv_i = adjoint_mat(dp_i, first[0]) - adjoint_mat(dp_r, first[1])
    grad_v = jnp.stack([dv_r, dv_i], axis=1).astype(BF16)
    grad_u = jnp.einsum("kerc,kepi->rcpi", table, grad_v, preferred_element_type=F32).astype(BF16)
    grad_u = grad_u.reshape(n_rows, 2, pairs_dev * BS)
    back = lax.all_to_all(grad_u, "lat", split_axis=0, concat_axis=2, tiled=True)
    back = back.reshape(rows_dev, 2, KM, NB, BS) * active[:, None, :, None, None].astype(BF16)
    mixed = jnp.einsum("cml,rcmni->rlni", forward, back, preferred_element_type=F32)
    mixed = mixed.reshape(rows_dev, length, width).astype(BF16)
    block_w1 = jnp.einsum("pn,cipj->cinj", owner, gw1).reshape(1, 2, BS, width)
    block_w2 = jnp.einsum("pn,cipj->cinj", owner, gw2).reshape(1, 2, BS, width)
    block_b1 = jnp.einsum("pn,cpj->cnj", owner, gb1).reshape(1, 2, width)
    columns = width // lat_count
    full_w1, full_w2, full_b1 = lax.psum((block_w1, block_w2, block_b1), "lat")
    sum_w1 = lax.dynamic_slice_in_dim(full_w1, lat_pos * columns, columns, 3)
    sum_w2 = lax.dynamic_slice_in_dim(full_w2, lat_pos * columns, columns, 3)
    sum_b1 = lax.dynamic_slice_in_dim(full_b1, lat_pos * columns, columns, 2)
    whole = (cotan.astype(F32) + mixed.astype(F32)).astype(BF16)
    received = from_behind(whole[None], "section", -1)
    return (received, sum_w1, sum_w2, sum_b1)


def per_device(grad_out, spec_saved, w1, w2, b1, mode_counts, assignment):
    n_dev = lax.axis_size("lat")
    pairs_dev = spec_saved.shape[3] // BS
    paired = n_dev == 2 * NB and grad_out.shape[1] == 1 and pairs_dev % NB == 0
    body = paired_blocks if paired else split_blocks
    return body(grad_out, spec_saved, w1, w2, b1, mode_counts, assignment)


def solution(mesh):
    return jax.shard_map(
        per_device,
        mesh=mesh,
        in_specs=(
            P("section", "lat", None, None),
            P("section", None, None, "lat"),
            P("section", None, None, None),
            P("section", None, None, None),
            P("section", None, None),
            P(),
            P(),
        ),
        out_specs=(
            P("section", "lat", None, None),
            P("section", None, None, "lat"),
            P("section", None, None, "lat"),
            P("section", None, "lat"),
        ),
        check_vma=False,
    )
```

```python
import functools
import math

import jax
import jax.numpy as jnp
import numpy as np
from jax import lax
from jax.experimental import pallas as pl
from jax.experimental.pallas import tpu as pltpu
from jax.sharding import PartitionSpec as P

NB = 4
BS = 96
KM = 72
LANES = 128
F32 = jnp.float32
BF16 = jnp.bfloat16


def from_behind(value, axis, by):
    length = lax.axis_size(axis)
    pairs = [(i, i + by) for i in range(length) if 0 <= i + by < length]
    return lax.ppermute(value, axis, pairs)


def lon_tables(n_modes, length):
    modes = np.arange(n_modes)
    phase = modes[:, None] * np.arange(length)[None, :] % length
    angle = phase * (2.0 * math.pi / length)
    forward = np.stack([np.cos(angle), -np.sin(angle)]) / math.sqrt(length)
    weight = np.where(modes == 0, 1.0, 2.0)[None, :, None]
    return forward, forward * weight


def lat_waves(n_rows):
    freqs = np.arange(n_rows)
    angle = (freqs[:, None] * freqs[None, :] % n_rows) * (2.0 * math.pi / n_rows)
    factor = 1.0 / math.sqrt(n_rows)
    return np.cos(angle) * factor, np.sin(angle) * factor


def silu_slope(pre):
    sig = jax.nn.sigmoid(pre)
    return sig * (1.0 + pre * (1.0 - sig))


def window(x, start):
    low = start // LANES * LANES
    shift = start - low
    if shift == 0:
        return x[:, low : low + LANES]
    if shift + BS <= LANES:
        return pltpu.roll(x[:, low : low + LANES], LANES - shift, 1)
    return pltpu.roll(x[:, low : low + 2 * LANES], 2 * LANES - shift, 1)[:, :LANES]


def dense(parts):
    lane = lax.broadcasted_iota(jnp.int32, parts[0].shape, 1)
    first = pltpu.roll(parts[1], 96, 1)
    second = pltpu.roll(parts[2], 64, 1)
    third = pltpu.roll(parts[3], 32, 1)
    return jnp.concatenate(
        [
            jnp.where(lane < 96, parts[0], first),
            jnp.where(lane < 64, first, second),
            jnp.where(lane < 32, second, third),
        ],
        axis=1,
    )


def dot(a, b, contract):
    return lax.dot_general(a, b, ((contract[:1], contract[1:]), ((), ())), preferred_element_type=F32)


def keep_active(counts, assign, q, groups):
    active = counts[assign[lax.axis_index("lat")]]
    shape = groups[0].shape
    number = lax.broadcasted_iota(jnp.int32, shape, 0)
    number = jnp.where(number >= NB * q, number - NB * q, number)
    mode = number
    for z in range(1, NB):
        mode = jnp.where(number >= z * q, number + z * q, mode)
    return [jnp.where(mode < active - g * q, value, 0.0) for g, value in enumerate(groups)]


def fetch(sems, sources, targets):
    copies = [
        pltpu.make_async_copy(source, target, sems.at[i])
        for i, (source, target) in enumerate(zip(sources, targets))
    ]
    for copy in copies:
        copy.start()
    return copies


def wait(copies):
    for copy in copies:
        copy.wait()


def partner(d):
    return jnp.bitwise_xor(lax.axis_index("lat") // 2, d)


def analyse_kernel(q, *refs):
    hbm, outs, held, (by_block, sems) = refs[:5], refs[5:9], refs[9:14], refs[14:]
    counts, assign, field, table, saved = held
    copies = fetch(sems, hbm, held)
    wait(copies[4:])
    parts = [saved[:, c, :].astype(F32) for c in range(2)]
    points = [
        [
            jnp.concatenate([window(part, (mm * NB + n) * BS) for mm in range(q)], axis=0)
            for part in parts
        ]
        for n in range(NB)
    ]
    wait(copies[:4])
    rows = by_block.shape[1]
    spectral = jnp.dot(table[...], field[...], preferred_element_type=F32)
    groups = keep_active(counts, assign, q, [spectral[:rows], spectral[rows:]])
    for n in range(NB):
        pieces = [window(group, n * BS) for group in groups]
        by_block[n] = dense(pieces + points[n]).astype(BF16)
    for d, out in enumerate(outs):
        out[...] = by_block[partner(d)]


def weights_kernel(w1_hbm, w2_hbm, b1_hbm, mat1, mat2, bias, w1, w2, b1, sems):
    wait(fetch(sems, (w1_hbm, w2_hbm, b1_hbm), (w1, w2, b1)))
    block = lax.axis_index("lat") // 2

    def pick(x):
        value = window(x, 0)
        for n in range(1, NB):
            value = jnp.where(block == n, window(x, n * BS), value)
        lane = lax.broadcasted_iota(jnp.int32, value.shape, 1)
        return jnp.where(lane < BS, value, 0.0)

    gap = jnp.zeros((LANES - BS, 2 * LANES), BF16)
    for source, mat in ((w1, mat1), (w2, mat2)):
        real, imag = (pick(source[c].astype(F32)) for c in range(2))
        mat[0:BS] = jnp.concatenate([real, imag], axis=1).astype(BF16)
        mat[BS:LANES] = gap
        mat[LANES : LANES + BS] = jnp.concatenate([-imag, real], axis=1).astype(BF16)
        mat[LANES + BS : 2 * LANES] = gap
    shift_b = pick(b1[...].astype(F32))
    bias[...] = jnp.concatenate([shift_b[0:1], shift_b[1:2]], axis=1)


def join_kernel(*refs):
    out = refs[-1]
    for d, ref in enumerate(refs[:-1]):
        out[d] = ref[...]


def pack(band):
    rows = band.shape[0]
    tail = rows // 2 + 4
    left, right = band[:, :LANES], pltpu.roll(band[:, LANES:], 96, 1)
    lane = lax.broadcasted_iota(jnp.int32, left.shape, 1)
    upper = jnp.where(lane < 96, left, right)
    lower = pltpu.roll(right[rows - tail :], 64, 1)
    lower = jnp.where(lane[:tail] < 64, right[:tail], lower)
    return jnp.concatenate([upper, lower], axis=0)


def unpack(packed, rows):
    tail = rows // 2 + 4
    upper, lower = packed[:rows], packed[rows:]
    rest = jnp.concatenate([lower, pltpu.roll(lower, 64, 1)[2 * tail - rows :]], axis=0)
    lane = lax.broadcasted_iota(jnp.int32, upper.shape, 1)
    right = jnp.where(lane < 32, pltpu.roll(upper, 32, 1), pltpu.roll(rest, 32, 1))
    return [upper, right]


def filter_kernel(*refs):
    own, other, mat1, mat2, bias, assign_hbm, lat_hbm, lat_t_hbm = refs[:8]
    outs, (gw1, gw2, gb1) = refs[8:12], refs[12:15]
    assign, lat, lat_t, by_lat, points_v, sems = refs[15:]
    copies = fetch(sems, (assign_hbm, lat_hbm, lat_t_hbm), (assign, lat, lat_t))
    wait(copies[:1])
    n_half, rows, width = own.shape
    core = lax.rem(lax.axis_index("lat"), 2)
    segments = [BS * j for j in range(4)]
    for b, buffer in enumerate((own, other)):
        side = core if b == 0 else 1 - core
        for d in range(n_half):
            chunk = buffer[d].astype(F32)
            groups = [window(chunk, segments[j]) for j in range(2)]
            by_lat[assign[2 * partner(d) + side]] = jnp.concatenate(groups, axis=1)
            parts = [window(chunk, segments[j]) for j in (2, 3)]
            points_v[side, partner(d)] = jnp.concatenate(parts, axis=1)
    field = by_lat[...].reshape(lat.shape[1], 2 * LANES).astype(BF16)
    wait(copies[1:2])
    grad_y = dot(lat[...], field, (1, 0)).astype(BF16)
    points = grad_y.shape[0] // 2
    first, second = mat1[...], mat2[...]
    both1, both2, sums, inner = 0.0, 0.0, 0.0, []
    for g in range(2):
        v = points_v[g].reshape(points, 2 * LANES).astype(BF16)
        dy = [grad_y[c * points : (c + 1) * points, g * LANES : (g + 1) * LANES] for c in range(2)]
        dy = jnp.concatenate(dy, axis=1)
        pre = dot(v, first, (1, 0)) + bias[...]
        sig = jax.nn.sigmoid(pre)
        hidden = (pre * sig).astype(BF16)
        grad_hidden = dot(dy, second, (1, 1))
        dp = (grad_hidden * (sig * (1.0 + pre * (1.0 - sig)))).astype(BF16)
        dv = dot(dp, first, (1, 1)).astype(BF16)
        inner.append(jnp.concatenate([dv[:, :LANES], dv[:, LANES:]], axis=0))
        both1 += dot(dp, v, (0, 0))
        both2 += dot(dy, hidden, (0, 0))
        sums += jnp.sum(dp.astype(F32), axis=0, keepdims=True)
    inner = jnp.concatenate(inner, axis=1)
    wait(copies[2:])
    for d, out in enumerate(outs):
        band = dot(lat_t[assign[2 * partner(d) + core]], inner, (1, 0))
        out[...] = pack(band).astype(BF16)
    half = BS // 2
    for both, ref in ((both1, gw1), (both2, gw2)):
        real = both[:BS, :LANES] + both[LANES : LANES + BS, LANES:]
        imag = both[LANES : LANES + BS, :LANES] - both[:BS, LANES:]
        for c, full in enumerate((real, imag)):
            ref[c] = jnp.where(core == 0, full[:half], full[half:])[:, :BS]
    for c in range(2):
        line = sums[:, c * LANES : (c + 1) * LANES]
        gb1[c : c + 1] = jnp.where(core == 0, line[:, :half], line[:, half:BS])


def compose_kernel(q, *refs):
    backs, hbm, out, held, (by_block, sems) = refs[:4], refs[4:8], refs[8], refs[9:13], refs[13:]
    counts, assign, field, table = held
    copies = fetch(sems, hbm, held)
    rows = 2 * NB * q
    for d, back in enumerate(backs):
        by_block[partner(d)] = jnp.concatenate(unpack(back[...].astype(F32), rows), axis=1)
    groups = [
        dense([by_block[n, :, g * LANES : (g + 1) * LANES] for n in range(NB)]) for g in range(2)
    ]
    wait(copies)
    masked = jnp.concatenate(keep_active(counts, assign, q, groups), axis=0).astype(BF16)
    mixed = jnp.dot(table[...], masked, preferred_element_type=F32).astype(BF16)
    out[...] = (field[...].astype(F32) + mixed.astype(F32)).astype(BF16)


VMEM = pl.BlockSpec(memory_space=pltpu.VMEM)
HBM = pl.BlockSpec(memory_space=pltpu.HBM)


def call(kernel, outs, scratch, near, far):
    many = isinstance(outs, tuple)
    return pl.pallas_call(
        kernel,
        out_shape=outs,
        in_specs=[VMEM] * len(near) + [HBM] * len(far),
        out_specs=tuple([VMEM] * len(outs)) if many else VMEM,
        scratch_shapes=scratch,
        compiler_params=pltpu.CompilerParams(vmem_limit_bytes=32 * 2**20),
    )(*near, *(pltpu.with_memory_space_constraint(x, pltpu.HBM) for x in far))


def scratch_for(*arrays):
    scratch = []
    for x in arrays:
        space = pltpu.SMEM if x.dtype == jnp.int32 else pltpu.VMEM
        scratch.append(space(x.shape, x.dtype))
    return scratch, pltpu.SemaphoreType.DMA((len(arrays),))


def paired_blocks(grad_out, spec_saved, w1, w2, b1, mode_counts, assignment):
    length, width = grad_out.shape[2:]
    n_rows = assignment.shape[0]
    q = spec_saved.shape[3] // (NB * BS)
    rows = 2 * NB * q
    forward, inverse = lon_tables(KM, length)

    def by_group(table):
        table = table.reshape(2, NB, 2, q, length).transpose(2, 0, 1, 3, 4)
        return table.reshape(2 * rows, length).astype(BF16)

    cosine, sine = lat_waves(n_rows)
    waves = np.array([[cosine, sine], [-sine, cosine]])
    lat = np.einsum("eckr,uv->eukrcv", waves, np.eye(NB * q))
    lat = lat.reshape(2 * NB * q * n_rows, n_rows * rows).astype(BF16)
    lat_t = np.ascontiguousarray(lat.T).reshape(n_rows, rows, -1)

    lat, lat_t = jnp.asarray(lat), jnp.asarray(lat_t)
    inverse = jnp.asarray(by_group(inverse))
    forward = jnp.asarray(by_group(forward).T)

    def swap(chunks):
        pairs = [[(i, i ^ (2 * d)) for i in range(2 * NB)] for d in range(NB)]
        return [chunks[0]] + [lax.ppermute(chunks[d], "lat", pairs[d]) for d in (3, 2, 1)][::-1]

    field = grad_out.reshape(length, width)
    shape = jax.ShapeDtypeStruct
    far = (mode_counts, assignment, field, inverse, spec_saved[0])
    scratch, sems = scratch_for(*far)
    sent = call(
        functools.partial(analyse_kernel, q),
        (shape((rows, width), BF16),) * NB,
        scratch + [pltpu.VMEM((NB, rows, width), BF16), sems],
        (),
        far,
    )
    received = swap(sent)
    far = (w1[0], w2[0], b1[0])
    scratch, sems = scratch_for(*far)
    wide = (2 * LANES, 2 * LANES)
    mats = call(
        weights_kernel,
        (shape(wide, BF16), shape(wide, BF16), shape((1, 2 * LANES), F32)),
        scratch + [sems],
        (),
        far,
    )
    own = call(join_kernel, shape((NB, rows, width), BF16), [], received, ())
    other = lax.ppermute(own, "lat", [(i, i ^ 1) for i in range(2 * NB)])
    far = (assignment, lat, lat_t)
    scratch, sems = scratch_for(*far)
    packed = shape((rows + rows // 2 + 4, LANES), BF16)
    matrix = shape((2, BS // 2, BS), F32)
    *chunks, gw1, gw2, gb1 = call(
        filter_kernel,
        (packed,) * NB + (matrix, matrix, shape((2, BS // 2), F32)),
        scratch
        + [
            pltpu.VMEM((n_rows, rows, 2 * LANES), F32),
            pltpu.VMEM((2, NB, rows, 2 * LANES), F32),
            sems,
        ],
        (own, other, *mats),
        far,
    )
    backs = swap(chunks)
    far = (mode_counts, assignment, field, forward)
    scratch, sems = scratch_for(*far)
    total = call(
        functools.partial(compose_kernel, q),
        shape((length, width), BF16),
        scratch + [pltpu.VMEM((NB, rows, 2 * LANES), F32), sems],
        backs,
        far,
    )
    shifted = from_behind(total[None, None], "section", -1)
    return shifted, gw1.swapaxes(1, 2)[None], gw2.swapaxes(1, 2)[None], gb1[None]


def apply_mat(vec, mat):
    return jnp.einsum("kpi,ipj->kpj", vec, mat, preferred_element_type=F32)


def adjoint_mat(vec, mat):
    return jnp.einsum("kpj,ipj->kpi", vec, mat, preferred_element_type=F32)


def outer_sum(left, right):
    return jnp.einsum("kpi,kpj->ipj", left, right, preferred_element_type=F32)


def split_blocks(grad_out, spec_saved, w1, w2, b1, mode_counts, assignment):
    rows_dev = grad_out.shape[1]
    length = grad_out.shape[2]
    width = grad_out.shape[3]
    n_rows = assignment.shape[0]
    pairs_dev = spec_saved.shape[3] // BS
    forward, inverse = (jnp.asarray(t.astype(BF16)) for t in lon_tables(KM, length))
    cosine, sine = (jnp.asarray(t.astype(BF16))[:, assignment] for t in lat_waves(n_rows))
    table = jnp.stack(
        [jnp.stack([cosine, sine], axis=-1), jnp.stack([-sine, cosine], axis=-1)], axis=1
    )
    lat_pos = lax.axis_index("lat")
    lat_count = lax.axis_size("lat")
    own_lat = lax.dynamic_slice_in_dim(assignment, lat_pos * rows_dev, rows_dev)
    active = (jnp.arange(KM, dtype=jnp.int32)[None, :] < mode_counts[own_lat][:, None]).astype(F32)
    cotan = grad_out[0]
    spectral = jnp.einsum(
        "cml,rlni->rcmni",
        inverse,
        cotan.reshape(rows_dev, length, NB, BS),
        preferred_element_type=F32,
    )
    spectral = (spectral * active[:, None, :, None, None]).astype(BF16)
    spectral = spectral.reshape(rows_dev, 2, KM * NB * BS)
    pencil = lax.all_to_all(spectral, "lat", split_axis=2, concat_axis=0, tiled=True)
    pencil = pencil.reshape(n_rows, 2, pairs_dev, BS)
    grad_y = jnp.einsum("kerc,rcpi->kepi", table, pencil, preferred_element_type=F32).astype(BF16)
    saved = spec_saved[0].reshape(n_rows, 2, pairs_dev, BS)
    pair_ids = lat_pos * pairs_dev + jnp.arange(pairs_dev, dtype=jnp.int32)
    owner = (pair_ids % NB)[:, None] == jnp.arange(NB, dtype=jnp.int32)[None, :]
    owner = owner.astype(F32)
    first = jnp.take(w1[0].reshape(2, BS, NB, BS), pair_ids % NB, axis=2)
    second = jnp.take(w2[0].reshape(2, BS, NB, BS), pair_ids % NB, axis=2)
    shift_b = jnp.take(b1[0].reshape(2, NB, BS), pair_ids % NB, axis=1).astype(F32)
    v_r = saved[:, 0]
    v_i = saved[:, 1]
    pre_r = apply_mat(v_r, first[0]) - apply_mat(v_i, first[1]) + shift_b[0][None]
    pre_i = apply_mat(v_i, first[0]) + apply_mat(v_r, first[1]) + shift_b[1][None]
    hid_r = jax.nn.silu(pre_r).astype(BF16)
    hid_i = jax.nn.silu(pre_i).astype(BF16)
    dy_r = grad_y[:, 0]
    dy_i = grad_y[:, 1]
    dh_r = adjoint_mat(dy_r, second[0]) + adjoint_mat(dy_i, second[1])
    dh_i = adjoint_mat(dy_i, second[0]) - adjoint_mat(dy_r, second[1])
    dp_r = (dh_r * silu_slope(pre_r)).astype(BF16)
    dp_i = (dh_i * silu_slope(pre_i)).astype(BF16)
    gw2 = jnp.stack(
        [
            outer_sum(hid_r, dy_r) + outer_sum(hid_i, dy_i),
            outer_sum(hid_r, dy_i) - outer_sum(hid_i, dy_r),
        ]
    )
    gw1 = jnp.stack(
        [outer_sum(v_r, dp_r) + outer_sum(v_i, dp_i), outer_sum(v_r, dp_i) - outer_sum(v_i, dp_r)]
    )
    gb1 = jnp.stack([jnp.sum(dp_r.astype(F32), axis=0), jnp.sum(dp_i.astype(F32), axis=0)])
    dv_r = adjoint_mat(dp_r, first[0]) + adjoint_mat(dp_i, first[1])
    dv_i = adjoint_mat(dp_i, first[0]) - adjoint_mat(dp_r, first[1])
    grad_v = jnp.stack([dv_r, dv_i], axis=1).astype(BF16)
    grad_u = jnp.einsum("kerc,kepi->rcpi", table, grad_v, preferred_element_type=F32).astype(BF16)
    grad_u = grad_u.reshape(n_rows, 2, pairs_dev * BS)
    back = lax.all_to_all(grad_u, "lat", split_axis=0, concat_axis=2, tiled=True)
    back = back.reshape(rows_dev, 2, KM, NB, BS) * active[:, None, :, None, None].astype(BF16)
    mixed = jnp.einsum("cml,rcmni->rlni", forward, back, preferred_element_type=F32)
    mixed = mixed.reshape(rows_dev, length, width).astype(BF16)
    block_w1 = jnp.einsum("pn,cipj->cinj", owner, gw1).reshape(1, 2, BS, width)
    block_w2 = jnp.einsum("pn,cipj->cinj", owner, gw2).reshape(1, 2, BS, width)
    block_b1 = jnp.einsum("pn,cpj->cnj", owner, gb1).reshape(1, 2, width)
    columns = width // lat_count
    full_w1, full_w2, full_b1 = lax.psum((block_w1, block_w2, block_b1), "lat")
    sum_w1 = lax.dynamic_slice_in_dim(full_w1, lat_pos * columns, columns, 3)
    sum_w2 = lax.dynamic_slice_in_dim(full_w2, lat_pos * columns, columns, 3)
    sum_b1 = lax.dynamic_slice_in_dim(full_b1, lat_pos * columns, columns, 2)
    whole = (cotan.astype(F32) + mixed.astype(F32)).astype(BF16)
    received = from_behind(whole[None], "section", -1)
    return (received, sum_w1, sum_w2, sum_b1)


def per_device(grad_out, spec_saved, w1, w2, b1, mode_counts, assignment):
    n_dev = lax.axis_size("lat")
    pairs_dev = spec_saved.shape[3] // BS
    paired = n_dev == 2 * NB and grad_out.shape[1] == 1 and pairs_dev % NB == 0
    body = paired_blocks if paired else split_blocks
    return body(grad_out, spec_saved, w1, w2, b1, mode_counts, assignment)


def solution(mesh):
    return jax.shard_map(
        per_device,
        mesh=mesh,
        in_specs=(
            P("section", "lat", None, None),
            P("section", None, None, "lat"),
            P("section", None, None, None),
            P("section", None, None, None),
            P("section", None, None),
            P(),
            P(),
        ),
        out_specs=(
            P("section", "lat", None, None),
            P("section", None, None, "lat"),
            P("section", None, None, "lat"),
            P("section", None, "lat"),
        ),
        check_vma=False,
    )
```

```python
import functools
import math

import jax
import jax.numpy as jnp
import numpy as np
from jax import lax
from jax.experimental import pallas as pl
from jax.experimental.pallas import tpu as pltpu
from jax.sharding import PartitionSpec as P

NB = 4
BS = 96
KM = 72
LANES = 128
F32 = jnp.float32
BF16 = jnp.bfloat16


def from_behind(value, axis, by):
    length = lax.axis_size(axis)
    pairs = [(i, i + by) for i in range(length) if 0 <= i + by < length]
    return lax.ppermute(value, axis, pairs)


def lon_tables(n_modes, length):
    modes = np.arange(n_modes)
    phase = modes[:, None] * np.arange(length)[None, :] % length
    angle = phase * (2.0 * math.pi / length)
    forward = np.stack([np.cos(angle), -np.sin(angle)]) / math.sqrt(length)
    weight = np.where(modes == 0, 1.0, 2.0)[None, :, None]
    return forward, forward * weight


def lat_waves(n_rows):
    freqs = np.arange(n_rows)
    angle = (freqs[:, None] * freqs[None, :] % n_rows) * (2.0 * math.pi / n_rows)
    factor = 1.0 / math.sqrt(n_rows)
    return np.cos(angle) * factor, np.sin(angle) * factor


def silu_slope(pre):
    sig = jax.nn.sigmoid(pre)
    return sig * (1.0 + pre * (1.0 - sig))


def window(x, start):
    low = start // LANES * LANES
    shift = start - low
    if shift == 0:
        return x[:, low : low + LANES]
    if shift + BS <= LANES:
        return pltpu.roll(x[:, low : low + LANES], LANES - shift, 1)
    return pltpu.roll(x[:, low : low + 2 * LANES], 2 * LANES - shift, 1)[:, :LANES]


def dense(parts):
    lane = lax.broadcasted_iota(jnp.int32, parts[0].shape, 1)
    first = pltpu.roll(parts[1], 96, 1)
    second = pltpu.roll(parts[2], 64, 1)
    third = pltpu.roll(parts[3], 32, 1)
    return jnp.concatenate(
        [
            jnp.where(lane < 96, parts[0], first),
            jnp.where(lane < 64, first, second),
            jnp.where(lane < 32, second, third),
        ],
        axis=1,
    )


def dot(a, b, contract):
    return lax.dot_general(a, b, ((contract[:1], contract[1:]), ((), ())), preferred_element_type=F32)


def fetch(sems, sources, targets):
    copies = [
        pltpu.make_async_copy(source, target, sems.at[i])
        for i, (source, target) in enumerate(zip(sources, targets))
    ]
    for copy in copies:
        copy.start()
    return copies


def wait(copies):
    for copy in copies:
        copy.wait()


def partner(d):
    return jnp.bitwise_xor(lax.axis_index("lat") // 2, d)


def place():
    device = lax.axis_index("lat")
    return device // 2, lax.rem(device, 2)


def row_modes(shape, q):
    row = lax.broadcasted_iota(jnp.int32, shape, 0)
    twin = row >= 2 * q
    row = jnp.where(twin, row - 2 * q, row)
    return twin, jnp.where(row >= q, row - q, row)


def analyse_kernel(q, *refs):
    other, hbm, outs, held, (by_pair, sems) = refs[0], refs[1:5], refs[5:9], refs[9:13], refs[13:]
    counts, assign, field, table = held
    z, core = place()
    copies = fetch(sems, hbm[:3] + (hbm[3].at[core],), held)
    wait(copies)
    pad, width = by_pair.shape[1:]
    spectral = jnp.dot(table[0], field[...], preferred_element_type=F32)
    spectral += jnp.dot(table[1], other[...], preferred_element_type=F32)
    twin, mode = row_modes((pad, width), q)
    active = [counts[assign[2 * z + side]] for side in (core, 1 - core)]
    limit = jnp.where(twin, active[1], active[0])
    for n in range(NB):
        part = spectral[n * pad : (n + 1) * pad]
        by_pair[n] = jnp.where(mode < limit - q * (2 * n + core), part, 0.0).astype(BF16)
    for d, out in enumerate(outs):
        out[...] = by_pair[partner(d)]


def silu_kernel(q, *refs):
    hbm, outs, held, sems = refs[:6], refs[6:12], refs[12:18], refs[18]
    mats1, mats2, points, hidden, slope, lat = outs
    assign, saved, w1, w2, b1, base = held
    copies = fetch(sems, hbm, held)
    z, core = place()
    wait(copies)
    shift_b = b1[...].astype(F32)
    parts = [saved[:, c, :].astype(F32) for c in range(2)]
    lane = lax.broadcasted_iota(jnp.int32, (BS, LANES), 1)
    gap = jnp.zeros((LANES - BS, 2 * LANES), BF16)
    for n in range(NB):
        for source, mats in ((w1, mats1), (w2, mats2)):
            real, imag = (
                jnp.where(lane < BS, window(source[c].astype(F32), n * BS), 0.0) for c in range(2)
            )
            mats[n, 0:BS] = jnp.concatenate([real, imag], axis=1).astype(BF16)
            mats[n, BS:LANES] = gap
            mats[n, LANES : LANES + BS] = jnp.concatenate([-imag, real], axis=1).astype(BF16)
            mats[n, LANES + BS : 2 * LANES] = gap
        bias = window(shift_b, n * BS)
        bias = jnp.concatenate([bias[0:1], bias[1:2]], axis=1)
        columns = [
            jnp.concatenate([window(part, (mm * NB + n) * BS) for mm in range(q)], axis=0)
            for part in parts
        ]
        v = jnp.concatenate(columns, axis=1).astype(BF16)
        points[n] = v
        pre = dot(v, mats1[n], (1, 0)) + bias
        sig = jax.nn.sigmoid(pre)
        hidden[n] = (pre * sig).astype(BF16)
        slope[n] = sig * (1.0 + pre * (1.0 - sig))
    pad = lat.shape[1] // NB
    row = lax.broadcasted_iota(jnp.int32, (base.shape[1], lat.shape[1]), 0)
    column = lax.broadcasted_iota(jnp.int32, row.shape, 1)
    row_lat = sum((row >= 2 * q * i).astype(jnp.int32) for i in range(1, 2 * NB))
    column_lat = jnp.full(row.shape, -1, jnp.int32)
    inside = column
    for d in range(NB):
        for twin, side in enumerate((core, 1 - core)):
            start = d * pad + twin * 2 * q
            here = jnp.logical_and(column >= start, column < start + 2 * q)
            column_lat = jnp.where(here, assign[2 * partner(d) + side], column_lat)
            inside = jnp.where(here, column - start, inside)
    same = jnp.logical_and(row_lat == column_lat, row - 2 * q * row_lat == inside)
    lat[...] = dot(base[...], same.astype(F32).astype(BF16), (1, 0)).astype(BF16)


def filter_kernel(q, *refs):
    chunks, (mats1, mats2, points, hidden, slope, lat) = refs[:4], refs[4:10]
    outs, kept, sent, by_block = refs[10:14], refs[14], refs[15], refs[16]
    z, core = place()
    pad, width = chunks[0].shape
    rows = points.shape[1]
    half = BS // 2
    field = jnp.concatenate([chunk[...].astype(F32) for chunk in chunks], axis=0).astype(BF16)
    grad_y = dot(lat[...], field, (1, 0)).astype(BF16).astype(F32)
    inner = []
    for n in range(NB):
        dy = [window(grad_y[c * rows : (c + 1) * rows], n * BS) for c in range(2)]
        dy = jnp.concatenate(dy, axis=1).astype(BF16)
        dp = (dot(dy, mats2[n], (1, 1)) * slope[n]).astype(BF16)
        dv = dot(dp, mats1[n], (1, 1))
        inner.append(jnp.concatenate([dv[:, :LANES], dv[:, LANES:]], axis=0))
        columns = []
        for left, right in ((dp, points[n]), (dy, hidden[n])):
            both = dot(left, right, (0, 0))
            columns.append(both[:BS, :LANES] + both[LANES : LANES + BS, LANES:])
            columns.append(both[LANES : LANES + BS, :LANES] - both[:BS, LANES:])
        by_block[n, 0:BS] = dense(columns)
        sums = jnp.sum(dp.astype(F32), axis=0, keepdims=True)
        sums = jnp.concatenate([sums, jnp.zeros((1, width - 2 * LANES), F32)], axis=1)
        by_block[n, BS : BS + 8] = jnp.broadcast_to(sums, (8, width))
    grad_v = dense(inner).astype(BF16)
    band = dot(lat[...], grad_v, (0, 0))
    for d, out in enumerate(outs):
        out[...] = band[d * pad : (d + 1) * pad].astype(BF16)
    for d in range(NB):
        block = by_block[partner(d)]
        upper, lower, sums = block[:half], block[half:BS], block[BS:]
        own = jnp.where(core == 0, upper, lower)
        other = jnp.where(core == 0, lower, upper)
        kept[d] = jnp.concatenate([own, sums], axis=0)
        sent[d] = jnp.concatenate([other, sums], axis=0).astype(BF16)


def halve_kernel(kept, got, keep, send):
    count = keep.shape[0]
    for d in range(count):
        keep[d] = kept[d] + got[d].astype(F32)
        send[d] = (kept[count + d] + got[count + d].astype(F32)).astype(BF16)


def weights_kernel(kept, got, gw1, gw2, gb1):
    total = kept[0] + got[0].astype(F32)
    half = BS // 2
    for w, ref in enumerate((gw1, gw2)):
        for c in range(2):
            ref[c] = window(total[:half], (2 * w + c) * BS)[:, :BS]
    core = place()[1]
    for c in range(2):
        line = total[half : half + 1, c * LANES : (c + 1) * LANES]
        gb1[c : c + 1] = jnp.where(core == 0, line[:, :half], line[:, half:BS])


def part_kernel(q, *refs):
    backs, out = refs[:4], refs[4]
    pad = backs[0].shape[0]
    rows = out.shape[0] // NB
    twin = [pltpu.roll(back[...].astype(F32), pad - 2 * q, 0)[:rows] for back in backs]
    out[...] = jnp.concatenate(twin, axis=0).astype(BF16)


def compose_kernel(q, *refs):
    backs, got, hbm, out, held, (by_device, sems) = (
        refs[:4],
        refs[4],
        refs[5:9],
        refs[9],
        refs[10:14],
        refs[14:],
    )
    counts, assign, field, table = held
    copies = fetch(sems, hbm, held)
    z, core = place()
    rows, width = by_device.shape[2:]
    other = got[...].astype(F32)
    for d, back in enumerate(backs):
        by_device[core, partner(d)] = back[...].astype(F32)[:rows]
        by_device[1 - core, partner(d)] = other[d * rows : (d + 1) * rows]
    wait(copies)
    active = counts[assign[2 * z + core]]
    mode = row_modes((rows, width), q)[1]
    held_rows = [
        jnp.where(mode < active - q * (2 * n + c), by_device[c, n], 0.0)
        for c in range(2)
        for n in range(NB)
    ]
    held_rows = jnp.concatenate(held_rows, axis=0).astype(BF16)
    mixed = jnp.dot(table[...], held_rows, preferred_element_type=F32).astype(BF16)
    out[...] = (field[...].astype(F32) + mixed.astype(F32)).astype(BF16)


VMEM = pl.BlockSpec(memory_space=pltpu.VMEM)
HBM = pl.BlockSpec(memory_space=pltpu.HBM)


def call(kernel, outs, scratch, near, far):
    many = isinstance(outs, tuple)
    return pl.pallas_call(
        kernel,
        out_shape=outs,
        in_specs=[VMEM] * len(near) + [HBM] * len(far),
        out_specs=tuple([VMEM] * len(outs)) if many else VMEM,
        scratch_shapes=scratch,
        compiler_params=pltpu.CompilerParams(vmem_limit_bytes=32 * 2**20),
    )(*near, *(pltpu.with_memory_space_constraint(x, pltpu.HBM) for x in far))


def scratch_for(*arrays):
    scratch = []
    for x in arrays:
        space = pltpu.SMEM if x.dtype == jnp.int32 else pltpu.VMEM
        scratch.append(space(x.shape, x.dtype))
    return scratch, pltpu.SemaphoreType.DMA((len(arrays),))


def paired_blocks(grad_out, spec_saved, w1, w2, b1, mode_counts, assignment):
    length, width = grad_out.shape[2:]
    n_rows = assignment.shape[0]
    q = spec_saved.shape[3] // (NB * BS)
    rows = q * n_rows
    pad = (4 * q + 7) // 8 * 8
    short = (2 * q + 7) // 8 * 8
    forward, inverse = lon_tables(KM, length)

    inverse, forward = (
        t.reshape(2, NB, 2, q, length).transpose(2, 1, 0, 3, 4).reshape(2, NB, 2 * q, length)
        for t in (inverse, forward)
    )
    analysis = np.zeros((2, 2, NB, pad, length))
    analysis[:, 0, :, : 2 * q] = inverse
    analysis[:, 1, :, 2 * q : 4 * q] = inverse
    analysis = jnp.asarray(analysis.reshape(2, 2, NB * pad, length).astype(BF16))
    synthesis = np.zeros((2, NB, short, length))
    synthesis[:, :, : 2 * q] = forward
    synthesis = jnp.asarray(synthesis.reshape(2 * NB * short, length).T.astype(BF16))
    cosine, sine = lat_waves(n_rows)
    waves = np.array([[cosine, sine], [-sine, cosine]])
    base = np.einsum("eckr,uv->eukrcv", waves, np.eye(q))
    base = jnp.asarray(base.reshape(2 * rows, n_rows * 2 * q).astype(BF16))

    def across(value, d):
        return lax.ppermute(value, "lat", [(i, i ^ (2 * d)) for i in range(2 * NB)])

    def twin(value):
        return lax.ppermute(value, "lat", [(i, i ^ 1) for i in range(2 * NB)])

    def swap(chunks):
        return [chunks[0]] + [across(chunks[d], d) for d in (3, 2, 1)][::-1]

    shape = jax.ShapeDtypeStruct
    field = grad_out.reshape(length, width)
    other = twin(field)
    far = (mode_counts, assignment, field, analysis)
    scratch, sems = scratch_for(mode_counts, assignment, field, shape(analysis.shape[1:], BF16))
    sent = call(
        functools.partial(analyse_kernel, q),
        (shape((pad, width), BF16),) * NB,
        scratch + [pltpu.VMEM((NB, pad, width), BF16), sems],
        (other,),
        far,
    )
    received = swap(sent)
    far = (assignment, spec_saved[0], w1[0], w2[0], b1[0], base)
    scratch, sems = scratch_for(*far)
    wide = 2 * LANES
    ready = call(
        functools.partial(silu_kernel, q),
        (
            shape((NB, wide, wide), BF16),
            shape((NB, wide, wide), BF16),
            shape((NB, rows, wide), BF16),
            shape((NB, rows, wide), BF16),
            shape((NB, rows, wide), F32),
            shape((2 * rows, NB * pad), BF16),
        ),
        scratch + [sems],
        (),
        far,
    )
    tall = BS // 2 + 8
    *chunks, kept, given = call(
        functools.partial(filter_kernel, q),
        (shape((pad, width), BF16),) * NB
        + (shape((NB, tall, width), F32), shape((NB, tall, width), BF16)),
        [pltpu.VMEM((NB, BS + 8, width), F32)],
        (*received, *ready),
        (),
    )
    backs = swap(chunks)
    got = twin(
        call(
            functools.partial(part_kernel, q), shape((NB * short, width), BF16), [], backs, ()
        )
    )
    far = (mode_counts, assignment, field, synthesis)
    scratch, sems = scratch_for(*far)
    total = call(
        functools.partial(compose_kernel, q),
        shape((length, width), BF16),
        scratch + [pltpu.VMEM((2, NB, short, width), F32), sems],
        (*backs, got),
        far,
    )
    shifted = from_behind(total[None, None], "section", -1)

    added = twin(given)
    for d in (2, 1):
        halves = (shape((d, tall, width), F32), shape((d, tall, width), BF16))
        kept, given = call(halve_kernel, halves, [], (kept, added), ())
        added = across(given, d)
    matrix = shape((2, BS // 2, BS), F32)
    gw1, gw2, gb1 = call(
        weights_kernel, (matrix, matrix, shape((2, BS // 2), F32)), [], (kept, added), ()
    )
    return shifted, gw1.swapaxes(1, 2)[None], gw2.swapaxes(1, 2)[None], gb1[None]


def apply_mat(vec, mat):
    return jnp.einsum("kpi,ipj->kpj", vec, mat, preferred_element_type=F32)


def adjoint_mat(vec, mat):
    return jnp.einsum("kpj,ipj->kpi", vec, mat, preferred_element_type=F32)


def outer_sum(left, right):
    return jnp.einsum("kpi,kpj->ipj", left, right, preferred_element_type=F32)


def split_blocks(grad_out, spec_saved, w1, w2, b1, mode_counts, assignment):
    rows_dev = grad_out.shape[1]
    length = grad_out.shape[2]
    width = grad_out.shape[3]
    n_rows = assignment.shape[0]
    pairs_dev = spec_saved.shape[3] // BS
    forward, inverse = (jnp.asarray(t.astype(BF16)) for t in lon_tables(KM, length))
    cosine, sine = (jnp.asarray(t.astype(BF16))[:, assignment] for t in lat_waves(n_rows))
    table = jnp.stack(
        [jnp.stack([cosine, sine], axis=-1), jnp.stack([-sine, cosine], axis=-1)], axis=1
    )
    lat_pos = lax.axis_index("lat")
    lat_count = lax.axis_size("lat")
    own_lat = lax.dynamic_slice_in_dim(assignment, lat_pos * rows_dev, rows_dev)
    active = (jnp.arange(KM, dtype=jnp.int32)[None, :] < mode_counts[own_lat][:, None]).astype(F32)
    cotan = grad_out[0]
    spectral = jnp.einsum(
        "cml,rlni->rcmni",
        inverse,
        cotan.reshape(rows_dev, length, NB, BS),
        preferred_element_type=F32,
    )
    spectral = (spectral * active[:, None, :, None, None]).astype(BF16)
    spectral = spectral.reshape(rows_dev, 2, KM * NB * BS)
    pencil = lax.all_to_all(spectral, "lat", split_axis=2, concat_axis=0, tiled=True)
    pencil = pencil.reshape(n_rows, 2, pairs_dev, BS)
    grad_y = jnp.einsum("kerc,rcpi->kepi", table, pencil, preferred_element_type=F32).astype(BF16)
    saved = spec_saved[0].reshape(n_rows, 2, pairs_dev, BS)
    pair_ids = lat_pos * pairs_dev + jnp.arange(pairs_dev, dtype=jnp.int32)
    owner = (pair_ids % NB)[:, None] == jnp.arange(NB, dtype=jnp.int32)[None, :]
    owner = owner.astype(F32)
    first = jnp.take(w1[0].reshape(2, BS, NB, BS), pair_ids % NB, axis=2)
    second = jnp.take(w2[0].reshape(2, BS, NB, BS), pair_ids % NB, axis=2)
    shift_b = jnp.take(b1[0].reshape(2, NB, BS), pair_ids % NB, axis=1).astype(F32)
    v_r = saved[:, 0]
    v_i = saved[:, 1]
    pre_r = apply_mat(v_r, first[0]) - apply_mat(v_i, first[1]) + shift_b[0][None]
    pre_i = apply_mat(v_i, first[0]) + apply_mat(v_r, first[1]) + shift_b[1][None]
    hid_r = jax.nn.silu(pre_r).astype(BF16)
    hid_i = jax.nn.silu(pre_i).astype(BF16)
    dy_r = grad_y[:, 0]
    dy_i = grad_y[:, 1]
    dh_r = adjoint_mat(dy_r, second[0]) + adjoint_mat(dy_i, second[1])
    dh_i = adjoint_mat(dy_i, second[0]) - adjoint_mat(dy_r, second[1])
    dp_r = (dh_r * silu_slope(pre_r)).astype(BF16)
    dp_i = (dh_i * silu_slope(pre_i)).astype(BF16)
    gw2 = jnp.stack(
        [
            outer_sum(hid_r, dy_r) + outer_sum(hid_i, dy_i),
            outer_sum(hid_r, dy_i) - outer_sum(hid_i, dy_r),
        ]
    )
    gw1 = jnp.stack(
        [outer_sum(v_r, dp_r) + outer_sum(v_i, dp_i), outer_sum(v_r, dp_i) - outer_sum(v_i, dp_r)]
    )
    gb1 = jnp.stack([jnp.sum(dp_r.astype(F32), axis=0), jnp.sum(dp_i.astype(F32), axis=0)])
    dv_r = adjoint_mat(dp_r, first[0]) + adjoint_mat(dp_i, first[1])
    dv_i = adjoint_mat(dp_i, first[0]) - adjoint_mat(dp_r, first[1])
    grad_v = jnp.stack([dv_r, dv_i], axis=1).astype(BF16)
    grad_u = jnp.einsum("kerc,kepi->rcpi", table, grad_v, preferred_element_type=F32).astype(BF16)
    grad_u = grad_u.reshape(n_rows, 2, pairs_dev * BS)
    back = lax.all_to_all(grad_u, "lat", split_axis=0, concat_axis=2, tiled=True)
    back = back.reshape(rows_dev, 2, KM, NB, BS) * active[:, None, :, None, None].astype(BF16)
    mixed = jnp.einsum("cml,rcmni->rlni", forward, back, preferred_element_type=F32)
    mixed = mixed.reshape(rows_dev, length, width).astype(BF16)
    block_w1 = jnp.einsum("pn,cipj->cinj", owner, gw1).reshape(1, 2, BS, width)
    block_w2 = jnp.einsum("pn,cipj->cinj", owner, gw2).reshape(1, 2, BS, width)
    block_b1 = jnp.einsum("pn,cpj->cnj", owner, gb1).reshape(1, 2, width)
    columns = width // lat_count
    full_w1, full_w2, full_b1 = lax.psum((block_w1, block_w2, block_b1), "lat")
    sum_w1 = lax.dynamic_slice_in_dim(full_w1, lat_pos * columns, columns, 3)
    sum_w2 = lax.dynamic_slice_in_dim(full_w2, lat_pos * columns, columns, 3)
    sum_b1 = lax.dynamic_slice_in_dim(full_b1, lat_pos * columns, columns, 2)
    whole = (cotan.astype(F32) + mixed.astype(F32)).astype(BF16)
    received = from_behind(whole[None], "section", -1)
    return (received, sum_w1, sum_w2, sum_b1)


def per_device(grad_out, spec_saved, w1, w2, b1, mode_counts, assignment):
    n_dev = lax.axis_size("lat")
    pairs_dev = spec_saved.shape[3] // BS
    paired = n_dev == 2 * NB and grad_out.shape[1] == 1 and pairs_dev % NB == 0
    body = paired_blocks if paired else split_blocks
    return body(grad_out, spec_saved, w1, w2, b1, mode_counts, assignment)


def solution(mesh):
    return jax.shard_map(
        per_device,
        mesh=mesh,
        in_specs=(
            P("section", "lat", None, None),
            P("section", None, None, "lat"),
            P("section", None, None, None),
            P("section", None, None, None),
            P("section", None, None),
            P(),
            P(),
        ),
        out_specs=(
            P("section", "lat", None, None),
            P("section", None, None, "lat"),
            P("section", None, None, "lat"),
            P("section", None, "lat"),
        ),
        check_vma=False,
    )
```

```python
import functools
import math

import jax
import jax.numpy as jnp
import numpy as np
from jax import lax
from jax.experimental import pallas as pl
from jax.experimental.pallas import tpu as pltpu
from jax.sharding import PartitionSpec as P

NB = 4
BS = 96
KM = 72
LANES = 128
F32 = jnp.float32
BF16 = jnp.bfloat16


def from_behind(value, axis, by):
    length = lax.axis_size(axis)
    pairs = [(i, i + by) for i in range(length) if 0 <= i + by < length]
    return lax.ppermute(value, axis, pairs)


def lon_tables(n_modes, length):
    modes = np.arange(n_modes)
    phase = modes[:, None] * np.arange(length)[None, :] % length
    angle = phase * (2.0 * math.pi / length)
    forward = np.stack([np.cos(angle), -np.sin(angle)]) / math.sqrt(length)
    weight = np.where(modes == 0, 1.0, 2.0)[None, :, None]
    return forward, forward * weight


def lat_waves(n_rows):
    freqs = np.arange(n_rows)
    angle = (freqs[:, None] * freqs[None, :] % n_rows) * (2.0 * math.pi / n_rows)
    factor = 1.0 / math.sqrt(n_rows)
    return np.cos(angle) * factor, np.sin(angle) * factor


def silu_slope(pre):
    sig = jax.nn.sigmoid(pre)
    return sig * (1.0 + pre * (1.0 - sig))


def window(x, start):
    low = start // LANES * LANES
    shift = start - low
    if shift == 0:
        return x[:, low : low + LANES]
    if shift + BS <= LANES:
        return pltpu.roll(x[:, low : low + LANES], LANES - shift, 1)
    return pltpu.roll(x[:, low : low + 2 * LANES], 2 * LANES - shift, 1)[:, :LANES]


def dense(parts):
    lane = lax.broadcasted_iota(jnp.int32, parts[0].shape, 1)
    first = pltpu.roll(parts[1], 96, 1)
    second = pltpu.roll(parts[2], 64, 1)
    third = pltpu.roll(parts[3], 32, 1)
    return jnp.concatenate(
        [
            jnp.where(lane < 96, parts[0], first),
            jnp.where(lane < 64, first, second),
            jnp.where(lane < 32, second, third),
        ],
        axis=1,
    )


def dot(a, b, contract):
    return lax.dot_general(a, b, ((contract[:1], contract[1:]), ((), ())), preferred_element_type=F32)


def fetch(sems, sources, targets):
    copies = [
        pltpu.make_async_copy(source, target, sems.at[i])
        for i, (source, target) in enumerate(zip(sources, targets))
    ]
    for copy in copies:
        copy.start()
    return copies


def wait(copies):
    for copy in copies:
        copy.wait()


def partner(d):
    return jnp.bitwise_xor(lax.axis_index("lat") // 2, d)


def place():
    device = lax.axis_index("lat")
    return device // 2, lax.rem(device, 2)


def active_rows(rows, limit, q):
    row = lax.broadcasted_iota(jnp.int32, rows.shape, 0)
    return jnp.where(jnp.where(row >= q, row - q, row) < limit, rows, 0.0)


def analyse_kernel(q, *refs):
    hbm, out, held, sems = refs[:4], refs[4], refs[5:9], refs[9]
    counts, assign, field, table = held
    wait(fetch(sems, hbm, held))
    n_dev, pad, width = out.shape
    active = counts[assign[lax.axis_index("lat")]]
    spectral = jnp.dot(table[...], field[...], preferred_element_type=F32)
    for i in range(n_dev):
        part = spectral[i * pad : (i + 1) * pad]
        out[i] = active_rows(part, active - q * i, q).astype(BF16)


def silu_kernel(q, *refs):
    hbm, outs, held, sems = refs[:6], refs[6:12], refs[12:18], refs[18]
    mats1, mats2, points, hidden, slope, lat = outs
    assign, saved, w1, w2, b1, base = held
    copies = fetch(sems, hbm, held)
    z, core = place()
    wait(copies)
    shift_b = b1[...].astype(F32)
    parts = [saved[:, c, :].astype(F32) for c in range(2)]
    lane = lax.broadcasted_iota(jnp.int32, (BS, LANES), 1)
    gap = jnp.zeros((LANES - BS, 2 * LANES), BF16)
    for n in range(NB):
        for source, mats in ((w1, mats1), (w2, mats2)):
            real, imag = (
                jnp.where(lane < BS, window(source[c].astype(F32), n * BS), 0.0) for c in range(2)
            )
            mats[n, 0:BS] = jnp.concatenate([real, imag], axis=1).astype(BF16)
            mats[n, BS:LANES] = gap
            mats[n, LANES : LANES + BS] = jnp.concatenate([-imag, real], axis=1).astype(BF16)
            mats[n, LANES + BS : 2 * LANES] = gap
        bias = window(shift_b, n * BS)
        bias = jnp.concatenate([bias[0:1], bias[1:2]], axis=1)
        columns = [
            jnp.concatenate([window(part, (mm * NB + n) * BS) for mm in range(q)], axis=0)
            for part in parts
        ]
        v = jnp.concatenate(columns, axis=1).astype(BF16)
        points[n] = v
        pre = dot(v, mats1[n], (1, 0)) + bias
        sig = jax.nn.sigmoid(pre)
        hidden[n] = (pre * sig).astype(BF16)
        slope[n] = sig * (1.0 + pre * (1.0 - sig))
    n_rows = base.shape[1] // (2 * q)
    pad = lat.shape[1] // n_rows
    row = lax.broadcasted_iota(jnp.int32, (base.shape[1], lat.shape[1]), 0)
    column = lax.broadcasted_iota(jnp.int32, row.shape, 1)
    row_lat = sum((row >= 2 * q * i).astype(jnp.int32) for i in range(1, n_rows))
    column_lat = jnp.full(row.shape, -1, jnp.int32)
    inside = column
    for r in range(n_rows):
        here = jnp.logical_and(column >= r * pad, column < r * pad + 2 * q)
        column_lat = jnp.where(here, assign[r], column_lat)
        inside = jnp.where(here, column - r * pad, inside)
    same = jnp.logical_and(row_lat == column_lat, row - 2 * q * row_lat == inside)
    lat[...] = dot(base[...], same.astype(F32).astype(BF16), (1, 0)).astype(BF16)


def filter_kernel(pencil, mats1, mats2, slope, lat, out, grad_pre, grad_out):
    n_rows, pad, width = pencil.shape
    rows = slope.shape[1]
    field = pencil[...].astype(F32).reshape(n_rows * pad, width).astype(BF16)
    grad_y = dot(lat[...], field, (1, 0)).astype(BF16).astype(F32)
    inner = []
    for n in range(NB):
        dy = [window(grad_y[c * rows : (c + 1) * rows], n * BS) for c in range(2)]
        dy = jnp.concatenate(dy, axis=1).astype(BF16)
        dp = (dot(dy, mats2[n], (1, 1)) * slope[n]).astype(BF16)
        dv = dot(dp, mats1[n], (1, 1))
        inner.append(jnp.concatenate([dv[:, :LANES], dv[:, LANES:]], axis=0))
        grad_out[n] = dy
        grad_pre[n] = dp
    grad_v = dense(inner).astype(BF16)
    band = dot(lat[...], grad_v, (0, 0))
    for r in range(n_rows):
        out[r] = band[r * pad : (r + 1) * pad].astype(BF16)


def products_kernel(points, hidden, grad_pre, grad_out, kept, sent, by_block):
    core = place()[1]
    width = kept.shape[2]
    half = BS // 2
    for n in range(NB):
        columns = []
        for left, right in ((grad_pre, points), (grad_out, hidden)):
            both = dot(left[n], right[n], (0, 0))
            columns.append(both[:BS, :LANES] + both[LANES : LANES + BS, LANES:])
            columns.append(both[LANES : LANES + BS, :LANES] - both[:BS, LANES:])
        by_block[n, 0:BS] = dense(columns)
        sums = jnp.sum(grad_pre[n].astype(F32), axis=0, keepdims=True)
        sums = jnp.concatenate([sums, jnp.zeros((1, width - 2 * LANES), F32)], axis=1)
        by_block[n, BS : BS + 8] = jnp.broadcast_to(sums, (8, width))
    for i, d in enumerate((0, 2, 1, 3)):
        block = by_block[partner(d)]
        upper, lower, sums = block[:half], block[half:BS], block[BS:]
        own = jnp.where(core == 0, upper, lower)
        other = jnp.where(core == 0, lower, upper)
        kept[i] = jnp.concatenate([own, sums], axis=0)
        sent[i] = jnp.concatenate([other, sums], axis=0).astype(BF16)


def halve_kernel(kept, got, keep, send):
    count = keep.shape[0]
    for d in range(count):
        keep[d] = kept[d] + got[d].astype(F32)
        send[d] = (kept[count + d] + got[count + d].astype(F32)).astype(BF16)


def weights_kernel(kept, got, gw1, gw2, gb1):
    total = kept[0] + got[0].astype(F32)
    half = BS // 2
    for w, ref in enumerate((gw1, gw2)):
        for c in range(2):
            ref[c] = window(total[:half], (2 * w + c) * BS)[:, :BS]
    core = place()[1]
    for c in range(2):
        line = total[half : half + 1, c * LANES : (c + 1) * LANES]
        gb1[c : c + 1] = jnp.where(core == 0, line[:, :half], line[:, half:BS])


def compose_kernel(q, *refs):
    back, hbm, out, held, sems = refs[0], refs[1:5], refs[5], refs[6:10], refs[10]
    counts, assign, field, table = held
    copies = fetch(sems, hbm, held)
    wait(copies)
    active = counts[assign[lax.axis_index("lat")]]
    rows = [active_rows(back[i].astype(F32), active - q * i, q) for i in range(back.shape[0])]
    rows = jnp.concatenate(rows, axis=0).astype(BF16)
    mixed = jnp.dot(table[...], rows, preferred_element_type=F32).astype(BF16)
    out[...] = (field[...].astype(F32) + mixed.astype(F32)).astype(BF16)


VMEM = pl.BlockSpec(memory_space=pltpu.VMEM)
HBM = pl.BlockSpec(memory_space=pltpu.HBM)


def call(kernel, outs, scratch, near, far, flops=1 * 10**8):
    cost = pl.CostEstimate(flops=flops, bytes_accessed=10**6, transcendentals=0)
    many = isinstance(outs, tuple)
    return pl.pallas_call(
        kernel,
        out_shape=outs,
        in_specs=[VMEM] * len(near) + [HBM] * len(far),
        out_specs=tuple([VMEM] * len(outs)) if many else VMEM,
        scratch_shapes=scratch,
        cost_estimate=cost,
        compiler_params=pltpu.CompilerParams(vmem_limit_bytes=32 * 2**20),
    )(*near, *(pltpu.with_memory_space_constraint(x, pltpu.HBM) for x in far))


def scratch_for(*arrays):
    scratch = []
    for x in arrays:
        space = pltpu.SMEM if x.dtype == jnp.int32 else pltpu.VMEM
        scratch.append(space(x.shape, x.dtype))
    return scratch, pltpu.SemaphoreType.DMA((len(arrays),))


def paired_blocks(grad_out, spec_saved, w1, w2, b1, mode_counts, assignment):
    length, width = grad_out.shape[2:]
    n_rows = assignment.shape[0]
    q = spec_saved.shape[3] // (NB * BS)
    rows = q * n_rows
    pad = (2 * q + 7) // 8 * 8
    forward, inverse = lon_tables(KM, length)

    def by_device(table):
        table = table.reshape(2, n_rows, q, length).transpose(1, 0, 2, 3)
        table = table.reshape(n_rows, 2 * q, length)
        table = np.pad(table, ((0, 0), (0, pad - 2 * q), (0, 0)))
        return table.reshape(n_rows * pad, length).astype(BF16)

    analysis = jnp.asarray(by_device(inverse))
    synthesis = jnp.asarray(by_device(forward).T)
    cosine, sine = lat_waves(n_rows)
    waves = np.array([[cosine, sine], [-sine, cosine]])
    base = np.einsum("eckr,uv->eukrcv", waves, np.eye(q))
    base = jnp.asarray(base.reshape(2 * rows, n_rows * 2 * q).astype(BF16))

    def across(value, d):
        return lax.ppermute(value, "lat", [(i, i ^ (2 * d)) for i in range(2 * NB)])

    def twin(value):
        return lax.ppermute(value, "lat", [(i, i ^ 1) for i in range(2 * NB)])

    def exchange(value):
        return lax.all_to_all(value, "lat", split_axis=0, concat_axis=0, tiled=True)

    shape = jax.ShapeDtypeStruct
    field = grad_out.reshape(length, width)
    far = (mode_counts, assignment, field, analysis)
    scratch, sems = scratch_for(*far)
    chunks = shape((n_rows, pad, width), BF16)
    sent = call(functools.partial(analyse_kernel, q), chunks, scratch + [sems], (), far)
    pencil = exchange(sent)
    far = (assignment, spec_saved[0], w1[0], w2[0], b1[0], base)
    scratch, sems = scratch_for(*far)
    wide = 2 * LANES
    matrices, vectors = shape((NB, wide, wide), BF16), shape((NB, rows, wide), BF16)
    mats1, mats2, points, hidden, slope, lat = call(
        functools.partial(silu_kernel, q),
        (
            matrices,
            matrices,
            vectors,
            vectors,
            shape((NB, rows, wide), F32),
            shape((2 * rows, n_rows * pad), BF16),
        ),
        scratch + [sems],
        (),
        far,
        5 * 10**9,
    )
    band, grad_pre, grad_y = call(
        filter_kernel,
        (chunks, vectors, vectors),
        [],
        (pencil, mats1, mats2, slope, lat),
        (),
    )
    back = exchange(band)
    tall = BS // 2 + 8
    kept, given = call(
        products_kernel,
        (shape((NB, tall, width), F32), shape((NB, tall, width), BF16)),
        [pltpu.VMEM((NB, BS + 8, width), F32)],
        (points, hidden, grad_pre, grad_y),
        (),
        5 * 10**9,
    )
    far = (mode_counts, assignment, field, synthesis)
    scratch, sems = scratch_for(*far)
    total = call(
        functools.partial(compose_kernel, q),
        shape((length, width), BF16),
        scratch + [sems],
        (back,),
        far,
    )
    shifted = from_behind(total[None, None], "section", -1)

    added = twin(given)
    for d in (1, 2):
        halves = (
            shape((NB // (2 * d), tall, width), F32),
            shape((NB // (2 * d), tall, width), BF16),
        )
        kept, given = call(halve_kernel, halves, [], (kept, added), ())
        added = across(given, d)
    matrix = shape((2, BS // 2, BS), F32)
    gw1, gw2, gb1 = call(
        weights_kernel, (matrix, matrix, shape((2, BS // 2), F32)), [], (kept, added), ()
    )
    return shifted, gw1.swapaxes(1, 2)[None], gw2.swapaxes(1, 2)[None], gb1[None]


def apply_mat(vec, mat):
    return jnp.einsum("kpi,ipj->kpj", vec, mat, preferred_element_type=F32)


def adjoint_mat(vec, mat):
    return jnp.einsum("kpj,ipj->kpi", vec, mat, preferred_element_type=F32)


def outer_sum(left, right):
    return jnp.einsum("kpi,kpj->ipj", left, right, preferred_element_type=F32)


def split_blocks(grad_out, spec_saved, w1, w2, b1, mode_counts, assignment):
    rows_dev = grad_out.shape[1]
    length = grad_out.shape[2]
    width = grad_out.shape[3]
    n_rows = assignment.shape[0]
    pairs_dev = spec_saved.shape[3] // BS
    forward, inverse = (jnp.asarray(t.astype(BF16)) for t in lon_tables(KM, length))
    cosine, sine = (jnp.asarray(t.astype(BF16))[:, assignment] for t in lat_waves(n_rows))
    table = jnp.stack(
        [jnp.stack([cosine, sine], axis=-1), jnp.stack([-sine, cosine], axis=-1)], axis=1
    )
    lat_pos = lax.axis_index("lat")
    lat_count = lax.axis_size("lat")
    own_lat = lax.dynamic_slice_in_dim(assignment, lat_pos * rows_dev, rows_dev)
    active = (jnp.arange(KM, dtype=jnp.int32)[None, :] < mode_counts[own_lat][:, None]).astype(F32)
    cotan = grad_out[0]
    spectral = jnp.einsum(
        "cml,rlni->rcmni",
        inverse,
        cotan.reshape(rows_dev, length, NB, BS),
        preferred_element_type=F32,
    )
    spectral = (spectral * active[:, None, :, None, None]).astype(BF16)
    spectral = spectral.reshape(rows_dev, 2, KM * NB * BS)
    pencil = lax.all_to_all(spectral, "lat", split_axis=2, concat_axis=0, tiled=True)
    pencil = pencil.reshape(n_rows, 2, pairs_dev, BS)
    grad_y = jnp.einsum("kerc,rcpi->kepi", table, pencil, preferred_element_type=F32).astype(BF16)
    saved = spec_saved[0].reshape(n_rows, 2, pairs_dev, BS)
    pair_ids = lat_pos * pairs_dev + jnp.arange(pairs_dev, dtype=jnp.int32)
    owner = (pair_ids % NB)[:, None] == jnp.arange(NB, dtype=jnp.int32)[None, :]
    owner = owner.astype(F32)
    first = jnp.take(w1[0].reshape(2, BS, NB, BS), pair_ids % NB, axis=2)
    second = jnp.take(w2[0].reshape(2, BS, NB, BS), pair_ids % NB, axis=2)
    shift_b = jnp.take(b1[0].reshape(2, NB, BS), pair_ids % NB, axis=1).astype(F32)
    v_r = saved[:, 0]
    v_i = saved[:, 1]
    pre_r = apply_mat(v_r, first[0]) - apply_mat(v_i, first[1]) + shift_b[0][None]
    pre_i = apply_mat(v_i, first[0]) + apply_mat(v_r, first[1]) + shift_b[1][None]
    hid_r = jax.nn.silu(pre_r).astype(BF16)
    hid_i = jax.nn.silu(pre_i).astype(BF16)
    dy_r = grad_y[:, 0]
    dy_i = grad_y[:, 1]
    dh_r = adjoint_mat(dy_r, second[0]) + adjoint_mat(dy_i, second[1])
    dh_i = adjoint_mat(dy_i, second[0]) - adjoint_mat(dy_r, second[1])
    dp_r = (dh_r * silu_slope(pre_r)).astype(BF16)
    dp_i = (dh_i * silu_slope(pre_i)).astype(BF16)
    gw2 = jnp.stack(
        [
            outer_sum(hid_r, dy_r) + outer_sum(hid_i, dy_i),
            outer_sum(hid_r, dy_i) - outer_sum(hid_i, dy_r),
        ]
    )
    gw1 = jnp.stack(
        [outer_sum(v_r, dp_r) + outer_sum(v_i, dp_i), outer_sum(v_r, dp_i) - outer_sum(v_i, dp_r)]
    )
    gb1 = jnp.stack([jnp.sum(dp_r.astype(F32), axis=0), jnp.sum(dp_i.astype(F32), axis=0)])
    dv_r = adjoint_mat(dp_r, first[0]) + adjoint_mat(dp_i, first[1])
    dv_i = adjoint_mat(dp_i, first[0]) - adjoint_mat(dp_r, first[1])
    grad_v = jnp.stack([dv_r, dv_i], axis=1).astype(BF16)
    grad_u = jnp.einsum("kerc,kepi->rcpi", table, grad_v, preferred_element_type=F32).astype(BF16)
    grad_u = grad_u.reshape(n_rows, 2, pairs_dev * BS)
    back = lax.all_to_all(grad_u, "lat", split_axis=0, concat_axis=2, tiled=True)
    back = back.reshape(rows_dev, 2, KM, NB, BS) * active[:, None, :, None, None].astype(BF16)
    mixed = jnp.einsum("cml,rcmni->rlni", forward, back, preferred_element_type=F32)
    mixed = mixed.reshape(rows_dev, length, width).astype(BF16)
    block_w1 = jnp.einsum("pn,cipj->cinj", owner, gw1).reshape(1, 2, BS, width)
    block_w2 = jnp.einsum("pn,cipj->cinj", owner, gw2).reshape(1, 2, BS, width)
    block_b1 = jnp.einsum("pn,cpj->cnj", owner, gb1).reshape(1, 2, width)
    columns = width // lat_count
    full_w1, full_w2, full_b1 = lax.psum((block_w1, block_w2, block_b1), "lat")
    sum_w1 = lax.dynamic_slice_in_dim(full_w1, lat_pos * columns, columns, 3)
    sum_w2 = lax.dynamic_slice_in_dim(full_w2, lat_pos * columns, columns, 3)
    sum_b1 = lax.dynamic_slice_in_dim(full_b1, lat_pos * columns, columns, 2)
    whole = (cotan.astype(F32) + mixed.astype(F32)).astype(BF16)
    received = from_behind(whole[None], "section", -1)
    return (received, sum_w1, sum_w2, sum_b1)


def per_device(grad_out, spec_saved, w1, w2, b1, mode_counts, assignment):
    n_dev = lax.axis_size("lat")
    pairs_dev = spec_saved.shape[3] // BS
    paired = n_dev == 2 * NB and grad_out.shape[1] == 1 and pairs_dev % NB == 0
    body = paired_blocks if paired else split_blocks
    return body(grad_out, spec_saved, w1, w2, b1, mode_counts, assignment)


def solution(mesh):
    return jax.shard_map(
        per_device,
        mesh=mesh,
        in_specs=(
            P("section", "lat", None, None),
            P("section", None, None, "lat"),
            P("section", None, None, None),
            P("section", None, None, None),
            P("section", None, None),
            P(),
            P(),
        ),
        out_specs=(
            P("section", "lat", None, None),
            P("section", None, None, "lat"),
            P("section", None, None, "lat"),
            P("section", None, "lat"),
        ),
        check_vma=False,
    )
```

```python
import functools
import math

import jax
import jax.numpy as jnp
import numpy as np
from jax import lax
from jax.experimental import pallas as pl
from jax.experimental.pallas import tpu as pltpu
from jax.sharding import PartitionSpec as P

NB = 4
BS = 96
KM = 72
LANES = 128
F32 = jnp.float32
BF16 = jnp.bfloat16


def from_behind(value, axis, by):
    length = lax.axis_size(axis)
    pairs = [(i, i + by) for i in range(length) if 0 <= i + by < length]
    return lax.ppermute(value, axis, pairs)


def from_next(value, axis):
    length = lax.axis_size(axis)
    odd = lax.ppermute(value, axis, [(i, i - 1) for i in range(2, length, 2)])
    even = lax.ppermute(value, axis, [(i, i - 1) for i in range(1, length, 2)])
    return jnp.where(lax.axis_index(axis) % 2 == 1, odd, even)


def lon_tables(n_modes, length):
    modes = np.arange(n_modes)
    phase = modes[:, None] * np.arange(length)[None, :] % length
    angle = phase * (2.0 * math.pi / length)
    forward = np.stack([np.cos(angle), -np.sin(angle)]) / math.sqrt(length)
    weight = np.where(modes == 0, 1.0, 2.0)[None, :, None]
    return forward, forward * weight


def lat_waves(n_rows):
    freqs = np.arange(n_rows)
    angle = (freqs[:, None] * freqs[None, :] % n_rows) * (2.0 * math.pi / n_rows)
    factor = 1.0 / math.sqrt(n_rows)
    return np.cos(angle) * factor, np.sin(angle) * factor


def silu_slope(pre):
    sig = jax.nn.sigmoid(pre)
    return sig * (1.0 + pre * (1.0 - sig))


def window(x, start):
    low = start // LANES * LANES
    shift = start - low
    if shift == 0:
        return x[:, low : low + LANES]
    if shift + BS <= LANES:
        return pltpu.roll(x[:, low : low + LANES], LANES - shift, 1)
    return pltpu.roll(x[:, low : low + 2 * LANES], 2 * LANES - shift, 1)[:, :LANES]


def dense(parts):
    lane = lax.broadcasted_iota(jnp.int32, parts[0].shape, 1)
    first = pltpu.roll(parts[1], 96, 1)
    second = pltpu.roll(parts[2], 64, 1)
    third = pltpu.roll(parts[3], 32, 1)
    return jnp.concatenate(
        [
            jnp.where(lane < 96, parts[0], first),
            jnp.where(lane < 64, first, second),
            jnp.where(lane < 32, second, third),
        ],
        axis=1,
    )


def dot(a, b, contract):
    return lax.dot_general(a, b, ((contract[:1], contract[1:]), ((), ())), preferred_element_type=F32)


def mode_numbers(shape, axis, q):
    number = lax.broadcasted_iota(jnp.int32, shape, axis)
    number = jnp.where(number >= NB * q, number - NB * q, number)
    mode = number
    for z in range(1, NB):
        mode = jnp.where(number >= z * q, number + z * q, mode)
    return mode


def fetch(sems, sources, targets):
    copies = [
        pltpu.make_async_copy(source, target, sems.at[i])
        for i, (source, target) in enumerate(zip(sources, targets))
    ]
    for copy in copies:
        copy.start()
    return copies


def wait(copies):
    for copy in copies:
        copy.wait()


def partner(d):
    return jnp.bitwise_xor(lax.axis_index("lat") // 2, d)


def analyse_kernel(q, *refs):
    hbm, outs, held, (by_block, sems) = refs[:5], refs[5:9], refs[9:14], refs[14:]
    counts, assign, field, table, saved = held
    copies = fetch(sems, hbm, held)
    wait(copies[4:])
    parts = [saved[:, c, :].astype(F32) for c in range(2)]
    points = [
        [
            jnp.concatenate([window(part, (mm * NB + n) * BS) for mm in range(q)], axis=0)
            for part in parts
        ]
        for n in range(NB)
    ]
    wait(copies[:4])
    rows = by_block.shape[1]
    spectral = jnp.dot(table[...], field[...], preferred_element_type=F32)
    active = counts[assign[lax.axis_index("lat")]]
    mode = mode_numbers((rows, spectral.shape[1]), 0, q)
    groups = [
        jnp.where(mode < active - g * q, spectral[g * rows : (g + 1) * rows], 0.0)
        for g in range(2)
    ]
    for n in range(NB):
        pieces = [window(group, n * BS) for group in groups]
        by_block[n] = dense(pieces + points[n]).astype(BF16)
    for d, out in enumerate(outs):
        out[...] = by_block[partner(d)]


def ready_kernel(q, *refs):
    hbm, (mat1, mat2, bias, lat, lat_t, own_field, own_table) = refs[:9], refs[9:16]
    counts, assign, w1, w2, b1, table, sems = refs[16:]
    copies = fetch(sems, hbm, (counts, assign, w1, w2, b1, table, lat, lat_t, own_field))
    wait(copies[:6])
    active = counts[assign[lax.axis_index("lat")]]
    rows = table.shape[1] // 2
    mode = mode_numbers((table.shape[0], rows), 1, q)
    for g in range(2):
        part = table[:, g * rows : (g + 1) * rows].astype(F32)
        part = jnp.where(mode < active - g * q, part, 0.0)
        own_table[:, g * rows : (g + 1) * rows] = part.astype(BF16)
    block = lax.axis_index("lat") // 2

    def pick(x):
        value = window(x, 0)
        for n in range(1, NB):
            value = jnp.where(block == n, window(x, n * BS), value)
        lane = lax.broadcasted_iota(jnp.int32, value.shape, 1)
        return jnp.where(lane < BS, value, 0.0)

    gap = jnp.zeros((LANES - BS, 2 * LANES), BF16)
    for source, mat in ((w1, mat1), (w2, mat2)):
        real, imag = (pick(source[c].astype(F32)) for c in range(2))
        mat[0:BS] = jnp.concatenate([real, imag], axis=1).astype(BF16)
        mat[BS:LANES] = gap
        mat[LANES : LANES + BS] = jnp.concatenate([-imag, real], axis=1).astype(BF16)
        mat[LANES + BS : 2 * LANES] = gap
    shift_b = pick(b1[...].astype(F32))
    bias[...] = jnp.concatenate([shift_b[0:1], shift_b[1:2]], axis=1)
    wait(copies[6:])


def join_kernel(*refs):
    out = refs[-1]
    for d, ref in enumerate(refs[:-1]):
        out[d] = ref[...]


def pack(band):
    rows = band.shape[0]
    tail = rows // 2 + 4
    left, right = band[:, :LANES], pltpu.roll(band[:, LANES:], 96, 1)
    lane = lax.broadcasted_iota(jnp.int32, left.shape, 1)
    upper = jnp.where(lane < 96, left, right)
    lower = pltpu.roll(right[rows - tail :], 64, 1)
    lower = jnp.where(lane[:tail] < 64, right[:tail], lower)
    return jnp.concatenate([upper, lower], axis=0)


def unpack(packed, rows):
    tail = rows // 2 + 4
    upper, lower = packed[:rows], packed[rows:]
    rest = jnp.concatenate([lower, pltpu.roll(lower, 64, 1)[2 * tail - rows :]], axis=0)
    lane = lax.broadcasted_iota(jnp.int32, upper.shape, 1)
    right = jnp.where(lane < 32, pltpu.roll(upper, 32, 1), pltpu.roll(rest, 32, 1))
    return [upper, right]


def silu_points(chunks, mat, bias, by_pair, points, hidden, slope):
    for d, chunk in enumerate(chunks):
        parts = [window(chunk, j * BS) for j in (2, 3)]
        by_pair[partner(d)] = jnp.concatenate(parts, axis=1)
    v = by_pair[...].reshape(points.shape).astype(BF16)
    pre = dot(v, mat[...], (1, 0)) + bias[...]
    sig = jax.nn.sigmoid(pre)
    points[...] = v
    hidden[...] = (pre * sig).astype(BF16)
    slope[...] = sig * (1.0 + pre * (1.0 - sig))


def own_kernel(*refs):
    chunks, (mat1, bias), (points, hidden, slope), by_pair = refs[:4], refs[4:6], refs[6:9], refs[9]
    silu_points([chunk[...].astype(F32) for chunk in chunks], mat1, bias, by_pair, points, hidden, slope)


def filter_kernel(*refs):
    owns, (other, slope_own, mat1, mat2, bias, lat, lat_t, assign_hbm) = refs[:4], refs[4:12]
    outs, (points, hidden, grad_pre, grad_y) = refs[12:16], refs[16:20]
    assign, by_lat, by_pair, slope, sems = refs[20:]
    copies = fetch(sems, (assign_hbm,), (assign,))
    core = lax.rem(lax.axis_index("lat"), 2)
    sides = [[own[...].astype(F32) for own in owns], [other[d].astype(F32) for d in range(NB)]]
    silu_points(sides[1], mat1, bias, by_pair, points, hidden, slope)
    wait(copies)
    for side, chunks in zip((core, 1 - core), sides):
        for d, chunk in enumerate(chunks):
            groups = [window(chunk, j * BS) for j in range(2)]
            by_lat[assign[2 * partner(d) + side]] = jnp.concatenate(groups, axis=1)
    field = by_lat[...].reshape(lat.shape[1], 2 * LANES).astype(BF16)
    waves = dot(lat[...], field, (1, 0)).astype(BF16)
    rows = waves.shape[0] // 2
    inner = []
    for side, slopes in enumerate((slope_own, slope)):
        dy = []
        for c in range(2):
            part = waves[c * rows : (c + 1) * rows]
            flip = core == 0 if side == 0 else core == 1
            dy.append(jnp.where(flip, part[:, :LANES], part[:, LANES:]))
        dy = jnp.concatenate(dy, axis=1)
        dp = (dot(dy, mat2[...], (1, 1)) * slopes[...]).astype(BF16)
        dv = dot(dp, mat1[...], (1, 1))
        grad_y[side] = dy
        grad_pre[side] = dp
        inner.append(jnp.concatenate([dv[:, :LANES], dv[:, LANES:]], axis=0))
    left = jnp.where(core == 0, inner[0], inner[1])
    right = jnp.where(core == 0, inner[1], inner[0])
    inner = jnp.concatenate([left, right], axis=1).astype(BF16)
    for d, out in enumerate(outs):
        band = dot(lat_t[assign[2 * partner(d) + core]], inner, (1, 0))
        out[...] = pack(band).astype(BF16)


def products_kernel(points0, hidden0, points1, hidden1, grad_pre, grad_y, gw1, gw2, gb1):
    core = lax.rem(lax.axis_index("lat"), 2)
    half = BS // 2
    for ref, grads, values in ((gw1, grad_pre, (points0, points1)), (gw2, grad_y, (hidden0, hidden1))):
        both = dot(grads[0], values[0][...], (0, 0)) + dot(grads[1], values[1][...], (0, 0))
        real = both[:BS, :LANES] + both[LANES : LANES + BS, LANES:]
        imag = both[LANES : LANES + BS, :LANES] - both[:BS, LANES:]
        for c, full in enumerate((real, imag)):
            ref[c] = jnp.where(core == 0, full[:half], full[half:])[:, :BS]
    sums = sum(jnp.sum(grad_pre[side].astype(F32), axis=0, keepdims=True) for side in range(2))
    for c in range(2):
        line = sums[:, c * LANES : (c + 1) * LANES]
        gb1[c : c + 1] = jnp.where(core == 0, line[:, :half], line[:, half:BS])


def compose_kernel(*refs):
    backs, (field, table, out, by_block) = refs[:4], refs[4:]
    rows = by_block.shape[1]
    for d, back in enumerate(backs):
        by_block[partner(d)] = jnp.concatenate(unpack(back[...].astype(F32), rows), axis=1)
    groups = [
        dense([by_block[n, :, g * LANES : (g + 1) * LANES] for n in range(NB)]) for g in range(2)
    ]
    groups = jnp.concatenate(groups, axis=0).astype(BF16)
    mixed = jnp.dot(table[...], groups, preferred_element_type=F32).astype(BF16)
    out[...] = (field[...].astype(F32) + mixed.astype(F32)).astype(BF16)


VMEM = pl.BlockSpec(memory_space=pltpu.VMEM)
HBM = pl.BlockSpec(memory_space=pltpu.HBM)


def call(kernel, outs, scratch, near, far, flops=10**8):
    many = isinstance(outs, tuple)
    many = isinstance(outs, tuple)
    return pl.pallas_call(
        kernel,
        out_shape=outs,
        in_specs=[VMEM] * len(near) + [HBM] * len(far),
        out_specs=tuple([VMEM] * len(outs)) if many else VMEM,
        scratch_shapes=scratch,
        cost_estimate=pl.CostEstimate(flops=flops, bytes_accessed=10**6, transcendentals=0),
        compiler_params=pltpu.CompilerParams(vmem_limit_bytes=32 * 2**20),
    )(*near, *(pltpu.with_memory_space_constraint(x, pltpu.HBM) for x in far))


def scratch_for(*arrays):
    scratch = []
    for x in arrays:
        space = pltpu.SMEM if x.dtype == jnp.int32 else pltpu.VMEM
        scratch.append(space(x.shape, x.dtype))
    return scratch, pltpu.SemaphoreType.DMA((len(arrays),))


def paired_blocks(grad_out, spec_saved, w1, w2, b1, mode_counts, assignment):
    length, width = grad_out.shape[2:]
    n_rows = assignment.shape[0]
    q = spec_saved.shape[3] // (NB * BS)
    rows = 2 * NB * q
    forward, inverse = lon_tables(KM, length)

    def by_group(table):
        table = table.reshape(2, NB, 2, q, length).transpose(2, 0, 1, 3, 4)
        return table.reshape(2 * rows, length).astype(BF16)

    cosine, sine = lat_waves(n_rows)
    waves = np.array([[cosine, sine], [-sine, cosine]])
    lat = np.einsum("eckr,uv->eukrcv", waves, np.eye(NB * q))
    lat = lat.reshape(2 * NB * q * n_rows, n_rows * rows).astype(BF16)
    lat_t = np.ascontiguousarray(lat.T).reshape(n_rows, rows, -1)

    lat, lat_t = jnp.asarray(lat), jnp.asarray(lat_t)
    inverse = jnp.asarray(by_group(inverse))
    forward = jnp.asarray(by_group(forward).T)

    def swap(chunks):
        pairs = [[(i, i ^ (2 * d)) for i in range(2 * NB)] for d in range(NB)]
        return [chunks[0]] + [lax.ppermute(chunks[d], "lat", pairs[d]) for d in (3, 2, 1)][::-1]

    field = grad_out.reshape(length, width)
    shape = jax.ShapeDtypeStruct
    far = (mode_counts, assignment, field, inverse, spec_saved[0])
    scratch, sems = scratch_for(*far)
    sent = call(
        functools.partial(analyse_kernel, q),
        (shape((rows, width), BF16),) * NB,
        scratch + [pltpu.VMEM((NB, rows, width), BF16), sems],
        (),
        far,
    )
    received = swap(sent)
    far = (mode_counts, assignment, w1[0], w2[0], b1[0], forward)
    scratch, _ = scratch_for(*far)
    far = (*far, lat, lat_t, field)
    wide = 2 * LANES
    mat1, mat2, bias, lat, lat_t, field, forward = call(
        functools.partial(ready_kernel, q),
        (
            shape((wide, wide), BF16),
            shape((wide, wide), BF16),
            shape((1, wide), F32),
            shape(lat.shape, BF16),
            shape(lat_t.shape, BF16),
            shape(field.shape, BF16),
            shape(forward.shape, BF16),
        ),
        scratch + [pltpu.SemaphoreType.DMA((len(far),))],
        (),
        far,
        2 * 10**9,
    )
    own = call(join_kernel, shape((NB, rows, width), BF16), [], received, ())
    other = lax.ppermute(own, "lat", [(i, i ^ 1) for i in range(2 * NB)])
    vectors = shape((NB * rows, wide), BF16)
    slopes = shape((NB * rows, wide), F32)
    by_pair = pltpu.VMEM((NB, rows, wide), F32)
    points0, hidden0, slope0 = call(
        own_kernel,
        (vectors, vectors, slopes),
        [by_pair],
        (*received, mat1, bias),
        (),
        2 * 10**9,
    )
    packed = shape((rows + rows // 2 + 4, LANES), BF16)
    scratch, sems = scratch_for(assignment)
    both = shape((2, NB * rows, wide), BF16)
    *chunks, points1, hidden1, grad_pre, grad_y = call(
        filter_kernel,
        (packed,) * NB + (vectors, vectors, both, both),
        scratch
        + [
            pltpu.VMEM((n_rows, rows, wide), F32),
            by_pair,
            pltpu.VMEM((NB * rows, wide), F32),
            sems,
        ],
        (*received, other, slope0, mat1, mat2, bias, lat, lat_t),
        (assignment,),
    )
    backs = swap(chunks)
    matrix = shape((2, BS // 2, BS), F32)
    gw1, gw2, gb1 = call(
        products_kernel,
        (matrix, matrix, shape((2, BS // 2), F32)),
        [],
        (points0, hidden0, points1, hidden1, grad_pre, grad_y),
        (),
        2 * 10**9,
    )
    total = call(
        compose_kernel,
        shape((length, width), BF16),
        [by_pair],
        (*backs, field, forward),
        (),
    )
    shifted = from_next(total[None, None], "section")
    return shifted, gw1.swapaxes(1, 2)[None], gw2.swapaxes(1, 2)[None], gb1[None]


def apply_mat(vec, mat):
    return jnp.einsum("kpi,ipj->kpj", vec, mat, preferred_element_type=F32)


def adjoint_mat(vec, mat):
    return jnp.einsum("kpj,ipj->kpi", vec, mat, preferred_element_type=F32)


def outer_sum(left, right):
    return jnp.einsum("kpi,kpj->ipj", left, right, preferred_element_type=F32)


def split_blocks(grad_out, spec_saved, w1, w2, b1, mode_counts, assignment):
    rows_dev = grad_out.shape[1]
    length = grad_out.shape[2]
    width = grad_out.shape[3]
    n_rows = assignment.shape[0]
    pairs_dev = spec_saved.shape[3] // BS
    forward, inverse = (jnp.asarray(t.astype(BF16)) for t in lon_tables(KM, length))
    cosine, sine = (jnp.asarray(t.astype(BF16))[:, assignment] for t in lat_waves(n_rows))
    table = jnp.stack(
        [jnp.stack([cosine, sine], axis=-1), jnp.stack([-sine, cosine], axis=-1)], axis=1
    )
    lat_pos = lax.axis_index("lat")
    lat_count = lax.axis_size("lat")
    own_lat = lax.dynamic_slice_in_dim(assignment, lat_pos * rows_dev, rows_dev)
    active = (jnp.arange(KM, dtype=jnp.int32)[None, :] < mode_counts[own_lat][:, None]).astype(F32)
    cotan = grad_out[0]
    spectral = jnp.einsum(
        "cml,rlni->rcmni",
        inverse,
        cotan.reshape(rows_dev, length, NB, BS),
        preferred_element_type=F32,
    )
    spectral = (spectral * active[:, None, :, None, None]).astype(BF16)
    spectral = spectral.reshape(rows_dev, 2, KM * NB * BS)
    pencil = lax.all_to_all(spectral, "lat", split_axis=2, concat_axis=0, tiled=True)
    pencil = pencil.reshape(n_rows, 2, pairs_dev, BS)
    grad_y = jnp.einsum("kerc,rcpi->kepi", table, pencil, preferred_element_type=F32).astype(BF16)
    saved = spec_saved[0].reshape(n_rows, 2, pairs_dev, BS)
    pair_ids = lat_pos * pairs_dev + jnp.arange(pairs_dev, dtype=jnp.int32)
    owner = (pair_ids % NB)[:, None] == jnp.arange(NB, dtype=jnp.int32)[None, :]
    owner = owner.astype(F32)
    first = jnp.take(w1[0].reshape(2, BS, NB, BS), pair_ids % NB, axis=2)
    second = jnp.take(w2[0].reshape(2, BS, NB, BS), pair_ids % NB, axis=2)
    shift_b = jnp.take(b1[0].reshape(2, NB, BS), pair_ids % NB, axis=1).astype(F32)
    v_r = saved[:, 0]
    v_i = saved[:, 1]
    pre_r = apply_mat(v_r, first[0]) - apply_mat(v_i, first[1]) + shift_b[0][None]
    pre_i = apply_mat(v_i, first[0]) + apply_mat(v_r, first[1]) + shift_b[1][None]
    hid_r = jax.nn.silu(pre_r).astype(BF16)
    hid_i = jax.nn.silu(pre_i).astype(BF16)
    dy_r = grad_y[:, 0]
    dy_i = grad_y[:, 1]
    dh_r = adjoint_mat(dy_r, second[0]) + adjoint_mat(dy_i, second[1])
    dh_i = adjoint_mat(dy_i, second[0]) - adjoint_mat(dy_r, second[1])
    dp_r = (dh_r * silu_slope(pre_r)).astype(BF16)
    dp_i = (dh_i * silu_slope(pre_i)).astype(BF16)
    gw2 = jnp.stack(
        [
            outer_sum(hid_r, dy_r) + outer_sum(hid_i, dy_i),
            outer_sum(hid_r, dy_i) - outer_sum(hid_i, dy_r),
        ]
    )
    gw1 = jnp.stack(
        [outer_sum(v_r, dp_r) + outer_sum(v_i, dp_i), outer_sum(v_r, dp_i) - outer_sum(v_i, dp_r)]
    )
    gb1 = jnp.stack([jnp.sum(dp_r.astype(F32), axis=0), jnp.sum(dp_i.astype(F32), axis=0)])
    dv_r = adjoint_mat(dp_r, first[0]) + adjoint_mat(dp_i, first[1])
    dv_i = adjoint_mat(dp_i, first[0]) - adjoint_mat(dp_r, first[1])
    grad_v = jnp.stack([dv_r, dv_i], axis=1).astype(BF16)
    grad_u = jnp.einsum("kerc,kepi->rcpi", table, grad_v, preferred_element_type=F32).astype(BF16)
    grad_u = grad_u.reshape(n_rows, 2, pairs_dev * BS)
    back = lax.all_to_all(grad_u, "lat", split_axis=0, concat_axis=2, tiled=True)
    back = back.reshape(rows_dev, 2, KM, NB, BS) * active[:, None, :, None, None].astype(BF16)
    mixed = jnp.einsum("cml,rcmni->rlni", forward, back, preferred_element_type=F32)
    mixed = mixed.reshape(rows_dev, length, width).astype(BF16)
    block_w1 = jnp.einsum("pn,cipj->cinj", owner, gw1).reshape(1, 2, BS, width)
    block_w2 = jnp.einsum("pn,cipj->cinj", owner, gw2).reshape(1, 2, BS, width)
    block_b1 = jnp.einsum("pn,cpj->cnj", owner, gb1).reshape(1, 2, width)
    columns = width // lat_count
    full_w1, full_w2, full_b1 = lax.psum((block_w1, block_w2, block_b1), "lat")
    sum_w1 = lax.dynamic_slice_in_dim(full_w1, lat_pos * columns, columns, 3)
    sum_w2 = lax.dynamic_slice_in_dim(full_w2, lat_pos * columns, columns, 3)
    sum_b1 = lax.dynamic_slice_in_dim(full_b1, lat_pos * columns, columns, 2)
    whole = (cotan.astype(F32) + mixed.astype(F32)).astype(BF16)
    received = from_behind(whole[None], "section", -1)
    return (received, sum_w1, sum_w2, sum_b1)


def per_device(grad_out, spec_saved, w1, w2, b1, mode_counts, assignment):
    n_dev = lax.axis_size("lat")
    pairs_dev = spec_saved.shape[3] // BS
    paired = n_dev == 2 * NB and grad_out.shape[1] == 1 and pairs_dev % NB == 0
    body = paired_blocks if paired else split_blocks
    return body(grad_out, spec_saved, w1, w2, b1, mode_counts, assignment)


def solution(mesh):
    return jax.shard_map(
        per_device,
        mesh=mesh,
        in_specs=(
            P("section", "lat", None, None),
            P("section", None, None, "lat"),
            P("section", None, None, None),
            P("section", None, None, None),
            P("section", None, None),
            P(),
            P(),
        ),
        out_specs=(
            P("section", "lat", None, None),
            P("section", None, None, "lat"),
            P("section", None, None, "lat"),
            P("section", None, "lat"),
        ),
        check_vma=False,
    )
```

```python
import functools
import math

import jax
import jax.numpy as jnp
import numpy as np
from jax import lax
from jax.experimental import pallas as pl
from jax.experimental.pallas import tpu as pltpu
from jax.sharding import PartitionSpec as P

NB = 4
BS = 96
KM = 72
LANES = 128
F32 = jnp.float32
BF16 = jnp.bfloat16


def from_behind(value, axis, by):
    length = lax.axis_size(axis)
    pairs = [(i, i + by) for i in range(length) if 0 <= i + by < length]
    return lax.ppermute(value, axis, pairs)


def from_next(value, axis):
    length = lax.axis_size(axis)
    turned = lax.ppermute(value, axis, [(i, (i - 1) % length) for i in range(length)])
    return jnp.where(lax.axis_index(axis) == length - 1, jnp.zeros_like(value), turned)


def lon_tables(n_modes, length):
    modes = np.arange(n_modes)
    phase = modes[:, None] * np.arange(length)[None, :] % length
    angle = phase * (2.0 * math.pi / length)
    forward = np.stack([np.cos(angle), -np.sin(angle)]) / math.sqrt(length)
    weight = np.where(modes == 0, 1.0, 2.0)[None, :, None]
    return forward, forward * weight


def lat_waves(n_rows):
    freqs = np.arange(n_rows)
    angle = (freqs[:, None] * freqs[None, :] % n_rows) * (2.0 * math.pi / n_rows)
    factor = 1.0 / math.sqrt(n_rows)
    return np.cos(angle) * factor, np.sin(angle) * factor


def silu_slope(pre):
    sig = jax.nn.sigmoid(pre)
    return sig * (1.0 + pre * (1.0 - sig))


def window(x, start):
    low = start // LANES * LANES
    shift = start - low
    if shift == 0:
        return x[:, low : low + LANES]
    if shift + BS <= LANES:
        return pltpu.roll(x[:, low : low + LANES], LANES - shift, 1)
    return pltpu.roll(x[:, low : low + 2 * LANES], 2 * LANES - shift, 1)[:, :LANES]


def dense(parts):
    lane = lax.broadcasted_iota(jnp.int32, parts[0].shape, 1)
    first = pltpu.roll(parts[1], 96, 1)
    second = pltpu.roll(parts[2], 64, 1)
    third = pltpu.roll(parts[3], 32, 1)
    return jnp.concatenate(
        [
            jnp.where(lane < 96, parts[0], first),
            jnp.where(lane < 64, first, second),
            jnp.where(lane < 32, second, third),
        ],
        axis=1,
    )


def dot(a, b, contract):
    return lax.dot_general(a, b, ((contract[:1], contract[1:]), ((), ())), preferred_element_type=F32)


def mode_numbers(shape, axis, q):
    number = lax.broadcasted_iota(jnp.int32, shape, axis)
    number = jnp.where(number >= NB * q, number - NB * q, number)
    mode = number
    for z in range(1, NB):
        mode = jnp.where(number >= z * q, number + z * q, mode)
    return mode


def fetch(sems, sources, targets):
    copies = [
        pltpu.make_async_copy(source, target, sems.at[i])
        for i, (source, target) in enumerate(zip(sources, targets))
    ]
    for copy in copies:
        copy.start()
    return copies


def wait(copies):
    for copy in copies:
        copy.wait()


def partner(d):
    return jnp.bitwise_xor(lax.axis_index("lat") // 2, d)


def analyse_kernel(q, *refs):
    hbm, outs, held, (by_block, sems) = refs[:5], refs[5:9], refs[9:14], refs[14:]
    counts, assign, field, table, saved = held
    copies = fetch(sems, hbm, held)
    wait(copies[4:])
    parts = [saved[:, c, :].astype(F32) for c in range(2)]
    points = [
        [
            jnp.concatenate([window(part, (mm * NB + n) * BS) for mm in range(q)], axis=0)
            for part in parts
        ]
        for n in range(NB)
    ]
    wait(copies[:4])
    rows = by_block.shape[1]
    spectral = jnp.dot(table[...], field[...], preferred_element_type=F32)
    active = counts[assign[lax.axis_index("lat")]]
    mode = mode_numbers((rows, spectral.shape[1]), 0, q)
    groups = [
        jnp.where(mode < active - g * q, spectral[g * rows : (g + 1) * rows], 0.0)
        for g in range(2)
    ]
    for n in range(NB):
        pieces = [window(group, n * BS) for group in groups]
        by_block[n] = dense(pieces + points[n]).astype(BF16)
    for d, out in enumerate(outs):
        out[...] = by_block[partner(d)]


def ready_kernel(q, *refs):
    hbm, (mat1, mat2, bias, lat, lat_t, own_field, own_table) = refs[:9], refs[9:16]
    counts, assign, w1, w2, b1, table, sems = refs[16:]
    copies = fetch(sems, hbm, (counts, assign, w1, w2, b1, table, lat, lat_t, own_field))
    wait(copies[:6])
    active = counts[assign[lax.axis_index("lat")]]
    rows = table.shape[1] // 2
    mode = mode_numbers((table.shape[0], rows), 1, q)
    for g in range(2):
        part = table[:, g * rows : (g + 1) * rows].astype(F32)
        part = jnp.where(mode < active - g * q, part, 0.0)
        own_table[:, g * rows : (g + 1) * rows] = part.astype(BF16)
    block = lax.axis_index("lat") // 2

    def pick(x):
        value = window(x, 0)
        for n in range(1, NB):
            value = jnp.where(block == n, window(x, n * BS), value)
        lane = lax.broadcasted_iota(jnp.int32, value.shape, 1)
        return jnp.where(lane < BS, value, 0.0)

    gap = jnp.zeros((LANES - BS, 2 * LANES), BF16)
    for source, mat in ((w1, mat1), (w2, mat2)):
        real, imag = (pick(source[c].astype(F32)) for c in range(2))
        mat[0:BS] = jnp.concatenate([real, imag], axis=1).astype(BF16)
        mat[BS:LANES] = gap
        mat[LANES : LANES + BS] = jnp.concatenate([-imag, real], axis=1).astype(BF16)
        mat[LANES + BS : 2 * LANES] = gap
    shift_b = pick(b1[...].astype(F32))
    bias[...] = jnp.concatenate([shift_b[0:1], shift_b[1:2]], axis=1)
    wait(copies[6:])


def join_kernel(*refs):
    chunks, out = refs[:-2], refs[-1]
    for d, ref in enumerate(chunks):
        out[d] = ref[...]


def pack(band):
    rows = band.shape[0]
    tail = rows // 2 + 4
    left, right = band[:, :LANES], pltpu.roll(band[:, LANES:], 96, 1)
    lane = lax.broadcasted_iota(jnp.int32, left.shape, 1)
    upper = jnp.where(lane < 96, left, right)
    lower = pltpu.roll(right[rows - tail :], 64, 1)
    lower = jnp.where(lane[:tail] < 64, right[:tail], lower)
    return jnp.concatenate([upper, lower], axis=0)


def unpack(packed, rows):
    tail = rows // 2 + 4
    upper, lower = packed[:rows], packed[rows:]
    rest = jnp.concatenate([lower, pltpu.roll(lower, 64, 1)[2 * tail - rows :]], axis=0)
    lane = lax.broadcasted_iota(jnp.int32, upper.shape, 1)
    right = jnp.where(lane < 32, pltpu.roll(upper, 32, 1), pltpu.roll(rest, 32, 1))
    return [upper, right]


def silu_points(chunks, mat, bias, by_pair, points, hidden, slope):
    for d, chunk in enumerate(chunks):
        parts = [window(chunk, j * BS) for j in (2, 3)]
        by_pair[partner(d)] = jnp.concatenate(parts, axis=1)
    v = by_pair[...].reshape(points.shape).astype(BF16)
    pre = dot(v, mat[...], (1, 0)) + bias[...]
    sig = jax.nn.sigmoid(pre)
    points[...] = v
    hidden[...] = (pre * sig).astype(BF16)
    slope[...] = sig * (1.0 + pre * (1.0 - sig))


def own_kernel(*refs):
    chunks, (mat1, bias), (points, hidden, slope), by_pair = refs[:4], refs[4:6], refs[6:9], refs[9]
    silu_points([chunk[...].astype(F32) for chunk in chunks], mat1, bias, by_pair, points, hidden, slope)


def filter_kernel(*refs):
    owns, (other, slope_own, mat1, mat2, bias, lat, lat_t, assign_hbm) = refs[:4], refs[4:12]
    outs, (points, hidden, grad_pre, grad_y) = refs[12:16], refs[16:20]
    assign, by_lat, by_pair, slope, sems = refs[20:]
    copies = fetch(sems, (assign_hbm,), (assign,))
    core = lax.rem(lax.axis_index("lat"), 2)
    sides = [[own[...].astype(F32) for own in owns], [other[d].astype(F32) for d in range(NB)]]
    silu_points(sides[1], mat1, bias, by_pair, points, hidden, slope)
    wait(copies)
    for side, chunks in zip((core, 1 - core), sides):
        for d, chunk in enumerate(chunks):
            groups = [window(chunk, j * BS) for j in range(2)]
            by_lat[assign[2 * partner(d) + side]] = jnp.concatenate(groups, axis=1)
    field = by_lat[...].reshape(lat.shape[1], 2 * LANES).astype(BF16)
    waves = dot(lat[...], field, (1, 0)).astype(BF16)
    rows = waves.shape[0] // 2
    inner = []
    for side, slopes in enumerate((slope_own, slope)):
        dy = []
        for c in range(2):
            part = waves[c * rows : (c + 1) * rows]
            flip = core == 0 if side == 0 else core == 1
            dy.append(jnp.where(flip, part[:, :LANES], part[:, LANES:]))
        dy = jnp.concatenate(dy, axis=1)
        dp = (dot(dy, mat2[...], (1, 1)) * slopes[...]).astype(BF16)
        dv = dot(dp, mat1[...], (1, 1))
        grad_y[side] = dy
        grad_pre[side] = dp
        inner.append(jnp.concatenate([dv[:, :LANES], dv[:, LANES:]], axis=0))
    left = jnp.where(core == 0, inner[0], inner[1])
    right = jnp.where(core == 0, inner[1], inner[0])
    inner = jnp.concatenate([left, right], axis=1).astype(BF16)
    for d, out in enumerate(outs):
        band = dot(lat_t[assign[2 * partner(d) + core]], inner, (1, 0))
        out[...] = pack(band).astype(BF16)


def products_kernel(points0, hidden0, points1, hidden1, grad_pre, grad_y, gw1, gw2, gb1):
    core = lax.rem(lax.axis_index("lat"), 2)
    half = BS // 2
    for ref, grads, values in ((gw1, grad_pre, (points0, points1)), (gw2, grad_y, (hidden0, hidden1))):
        both = dot(grads[0], values[0][...], (0, 0)) + dot(grads[1], values[1][...], (0, 0))
        real = both[:BS, :LANES] + both[LANES : LANES + BS, LANES:]
        imag = both[LANES : LANES + BS, :LANES] - both[:BS, LANES:]
        for c, full in enumerate((real, imag)):
            ref[c] = jnp.where(core == 0, full[:half], full[half:])[:, :BS]
    sums = sum(jnp.sum(grad_pre[side].astype(F32), axis=0, keepdims=True) for side in range(2))
    for c in range(2):
        line = sums[:, c * LANES : (c + 1) * LANES]
        gb1[c : c + 1] = jnp.where(core == 0, line[:, :half], line[:, half:BS])


def compose_kernel(*refs):
    backs, (field, table, out, by_block) = refs[:4], refs[4:]
    rows = by_block.shape[1]
    for d, back in enumerate(backs):
        by_block[partner(d)] = jnp.concatenate(unpack(back[...].astype(F32), rows), axis=1)
    groups = [
        dense([by_block[n, :, g * LANES : (g + 1) * LANES] for n in range(NB)]) for g in range(2)
    ]
    groups = jnp.concatenate(groups, axis=0).astype(BF16)
    mixed = jnp.dot(table[...], groups, preferred_element_type=F32).astype(BF16)
    out[...] = (field[...].astype(F32) + mixed.astype(F32)).astype(BF16)


VMEM = pl.BlockSpec(memory_space=pltpu.VMEM)
HBM = pl.BlockSpec(memory_space=pltpu.HBM)


def call(kernel, outs, scratch, near, far, flops=10**8):
    many = isinstance(outs, tuple)
    many = isinstance(outs, tuple)
    return pl.pallas_call(
        kernel,
        out_shape=outs,
        in_specs=[VMEM] * len(near) + [HBM] * len(far),
        out_specs=tuple([VMEM] * len(outs)) if many else VMEM,
        scratch_shapes=scratch,
        cost_estimate=pl.CostEstimate(flops=flops, bytes_accessed=10**6, transcendentals=0),
        compiler_params=pltpu.CompilerParams(vmem_limit_bytes=32 * 2**20),
    )(*near, *(pltpu.with_memory_space_constraint(x, pltpu.HBM) for x in far))


def scratch_for(*arrays):
    scratch = []
    for x in arrays:
        space = pltpu.SMEM if x.dtype == jnp.int32 else pltpu.VMEM
        scratch.append(space(x.shape, x.dtype))
    return scratch, pltpu.SemaphoreType.DMA((len(arrays),))


def paired_blocks(grad_out, spec_saved, w1, w2, b1, mode_counts, assignment):
    length, width = grad_out.shape[2:]
    n_rows = assignment.shape[0]
    q = spec_saved.shape[3] // (NB * BS)
    rows = 2 * NB * q
    forward, inverse = lon_tables(KM, length)

    def by_group(table):
        table = table.reshape(2, NB, 2, q, length).transpose(2, 0, 1, 3, 4)
        return table.reshape(2 * rows, length).astype(BF16)

    cosine, sine = lat_waves(n_rows)
    waves = np.array([[cosine, sine], [-sine, cosine]])
    lat = np.einsum("eckr,uv->eukrcv", waves, np.eye(NB * q))
    lat = lat.reshape(2 * NB * q * n_rows, n_rows * rows).astype(BF16)
    lat_t = np.ascontiguousarray(lat.T).reshape(n_rows, rows, -1)

    lat, lat_t = jnp.asarray(lat), jnp.asarray(lat_t)
    inverse = jnp.asarray(by_group(inverse))
    forward = jnp.asarray(by_group(forward).T)

    def swap(chunks):
        pairs = [[(i, i ^ (2 * d)) for i in range(2 * NB)] for d in range(NB)]
        return [chunks[0]] + [lax.ppermute(chunks[d], "lat", pairs[d]) for d in (3, 2, 1)][::-1]

    field = grad_out.reshape(length, width)
    shape = jax.ShapeDtypeStruct
    far = (mode_counts, assignment, field, inverse, spec_saved[0])
    scratch, sems = scratch_for(*far)
    sent = call(
        functools.partial(analyse_kernel, q),
        (shape((rows, width), BF16),) * NB,
        scratch + [pltpu.VMEM((NB, rows, width), BF16), sems],
        (),
        far,
    )
    received = swap(sent)
    far = (mode_counts, assignment, w1[0], w2[0], b1[0], forward)
    scratch, _ = scratch_for(*far)
    far = (*far, lat, lat_t, field)
    wide = 2 * LANES
    mat1, mat2, bias, lat, lat_t, field, forward = call(
        functools.partial(ready_kernel, q),
        (
            shape((wide, wide), BF16),
            shape((wide, wide), BF16),
            shape((1, wide), F32),
            shape(lat.shape, BF16),
            shape(lat_t.shape, BF16),
            shape(field.shape, BF16),
            shape(forward.shape, BF16),
        ),
        scratch + [pltpu.SemaphoreType.DMA((len(far),))],
        (),
        far,
        2 * 10**9,
    )
    own = call(join_kernel, shape((NB, rows, width), BF16), [], (*received, bias), ())
    other = lax.ppermute(own, "lat", [(i, i ^ 1) for i in range(2 * NB)])
    vectors = shape((NB * rows, wide), BF16)
    slopes = shape((NB * rows, wide), F32)
    by_pair = pltpu.VMEM((NB, rows, wide), F32)
    points0, hidden0, slope0 = call(
        own_kernel,
        (vectors, vectors, slopes),
        [by_pair],
        (*received, mat1, bias),
        (),
        2 * 10**9,
    )
    packed = shape((rows + rows // 2 + 4, LANES), BF16)
    scratch, sems = scratch_for(assignment)
    both = shape((2, NB * rows, wide), BF16)
    *chunks, points1, hidden1, grad_pre, grad_y = call(
        filter_kernel,
        (packed,) * NB + (vectors, vectors, both, both),
        scratch
        + [
            pltpu.VMEM((n_rows, rows, wide), F32),
            by_pair,
            pltpu.VMEM((NB * rows, wide), F32),
            sems,
        ],
        (*received, other, slope0, mat1, mat2, bias, lat, lat_t),
        (assignment,),
    )
    backs = swap(chunks)
    matrix = shape((2, BS // 2, BS), F32)
    gw1, gw2, gb1 = call(
        products_kernel,
        (matrix, matrix, shape((2, BS // 2), F32)),
        [],
        (points0, hidden0, points1, hidden1, grad_pre, grad_y),
        (),
        2 * 10**9,
    )
    total = call(
        compose_kernel,
        shape((length, width), BF16),
        [by_pair],
        (*backs, field, forward),
        (),
    )
    shifted = from_next(total[None, None], "section")
    return shifted, gw1.swapaxes(1, 2)[None], gw2.swapaxes(1, 2)[None], gb1[None]


def apply_mat(vec, mat):
    return jnp.einsum("kpi,ipj->kpj", vec, mat, preferred_element_type=F32)


def adjoint_mat(vec, mat):
    return jnp.einsum("kpj,ipj->kpi", vec, mat, preferred_element_type=F32)


def outer_sum(left, right):
    return jnp.einsum("kpi,kpj->ipj", left, right, preferred_element_type=F32)


def split_blocks(grad_out, spec_saved, w1, w2, b1, mode_counts, assignment):
    rows_dev = grad_out.shape[1]
    length = grad_out.shape[2]
    width = grad_out.shape[3]
    n_rows = assignment.shape[0]
    pairs_dev = spec_saved.shape[3] // BS
    forward, inverse = (jnp.asarray(t.astype(BF16)) for t in lon_tables(KM, length))
    cosine, sine = (jnp.asarray(t.astype(BF16))[:, assignment] for t in lat_waves(n_rows))
    table = jnp.stack(
        [jnp.stack([cosine, sine], axis=-1), jnp.stack([-sine, cosine], axis=-1)], axis=1
    )
    lat_pos = lax.axis_index("lat")
    lat_count = lax.axis_size("lat")
    own_lat = lax.dynamic_slice_in_dim(assignment, lat_pos * rows_dev, rows_dev)
    active = (jnp.arange(KM, dtype=jnp.int32)[None, :] < mode_counts[own_lat][:, None]).astype(F32)
    cotan = grad_out[0]
    spectral = jnp.einsum(
        "cml,rlni->rcmni",
        inverse,
        cotan.reshape(rows_dev, length, NB, BS),
        preferred_element_type=F32,
    )
    spectral = (spectral * active[:, None, :, None, None]).astype(BF16)
    spectral = spectral.reshape(rows_dev, 2, KM * NB * BS)
    pencil = lax.all_to_all(spectral, "lat", split_axis=2, concat_axis=0, tiled=True)
    pencil = pencil.reshape(n_rows, 2, pairs_dev, BS)
    grad_y = jnp.einsum("kerc,rcpi->kepi", table, pencil, preferred_element_type=F32).astype(BF16)
    saved = spec_saved[0].reshape(n_rows, 2, pairs_dev, BS)
    pair_ids = lat_pos * pairs_dev + jnp.arange(pairs_dev, dtype=jnp.int32)
    owner = (pair_ids % NB)[:, None] == jnp.arange(NB, dtype=jnp.int32)[None, :]
    owner = owner.astype(F32)
    first = jnp.take(w1[0].reshape(2, BS, NB, BS), pair_ids % NB, axis=2)
    second = jnp.take(w2[0].reshape(2, BS, NB, BS), pair_ids % NB, axis=2)
    shift_b = jnp.take(b1[0].reshape(2, NB, BS), pair_ids % NB, axis=1).astype(F32)
    v_r = saved[:, 0]
    v_i = saved[:, 1]
    pre_r = apply_mat(v_r, first[0]) - apply_mat(v_i, first[1]) + shift_b[0][None]
    pre_i = apply_mat(v_i, first[0]) + apply_mat(v_r, first[1]) + shift_b[1][None]
    hid_r = jax.nn.silu(pre_r).astype(BF16)
    hid_i = jax.nn.silu(pre_i).astype(BF16)
    dy_r = grad_y[:, 0]
    dy_i = grad_y[:, 1]
    dh_r = adjoint_mat(dy_r, second[0]) + adjoint_mat(dy_i, second[1])
    dh_i = adjoint_mat(dy_i, second[0]) - adjoint_mat(dy_r, second[1])
    dp_r = (dh_r * silu_slope(pre_r)).astype(BF16)
    dp_i = (dh_i * silu_slope(pre_i)).astype(BF16)
    gw2 = jnp.stack(
        [
            outer_sum(hid_r, dy_r) + outer_sum(hid_i, dy_i),
            outer_sum(hid_r, dy_i) - outer_sum(hid_i, dy_r),
        ]
    )
    gw1 = jnp.stack(
        [outer_sum(v_r, dp_r) + outer_sum(v_i, dp_i), outer_sum(v_r, dp_i) - outer_sum(v_i, dp_r)]
    )
    gb1 = jnp.stack([jnp.sum(dp_r.astype(F32), axis=0), jnp.sum(dp_i.astype(F32), axis=0)])
    dv_r = adjoint_mat(dp_r, first[0]) + adjoint_mat(dp_i, first[1])
    dv_i = adjoint_mat(dp_i, first[0]) - adjoint_mat(dp_r, first[1])
    grad_v = jnp.stack([dv_r, dv_i], axis=1).astype(BF16)
    grad_u = jnp.einsum("kerc,kepi->rcpi", table, grad_v, preferred_element_type=F32).astype(BF16)
    grad_u = grad_u.reshape(n_rows, 2, pairs_dev * BS)
    back = lax.all_to_all(grad_u, "lat", split_axis=0, concat_axis=2, tiled=True)
    back = back.reshape(rows_dev, 2, KM, NB, BS) * active[:, None, :, None, None].astype(BF16)
    mixed = jnp.einsum("cml,rcmni->rlni", forward, back, preferred_element_type=F32)
    mixed = mixed.reshape(rows_dev, length, width).astype(BF16)
    block_w1 = jnp.einsum("pn,cipj->cinj", owner, gw1).reshape(1, 2, BS, width)
    block_w2 = jnp.einsum("pn,cipj->cinj", owner, gw2).reshape(1, 2, BS, width)
    block_b1 = jnp.einsum("pn,cpj->cnj", owner, gb1).reshape(1, 2, width)
    columns = width // lat_count
    full_w1, full_w2, full_b1 = lax.psum((block_w1, block_w2, block_b1), "lat")
    sum_w1 = lax.dynamic_slice_in_dim(full_w1, lat_pos * columns, columns, 3)
    sum_w2 = lax.dynamic_slice_in_dim(full_w2, lat_pos * columns, columns, 3)
    sum_b1 = lax.dynamic_slice_in_dim(full_b1, lat_pos * columns, columns, 2)
    whole = (cotan.astype(F32) + mixed.astype(F32)).astype(BF16)
    received = from_behind(whole[None], "section", -1)
    return (received, sum_w1, sum_w2, sum_b1)


def per_device(grad_out, spec_saved, w1, w2, b1, mode_counts, assignment):
    n_dev = lax.axis_size("lat")
    pairs_dev = spec_saved.shape[3] // BS
    paired = n_dev == 2 * NB and grad_out.shape[1] == 1 and pairs_dev % NB == 0
    body = paired_blocks if paired else split_blocks
    return body(grad_out, spec_saved, w1, w2, b1, mode_counts, assignment)


def solution(mesh):
    return jax.shard_map(
        per_device,
        mesh=mesh,
        in_specs=(
            P("section", "lat", None, None),
            P("section", None, None, "lat"),
            P("section", None, None, None),
            P("section", None, None, None),
            P("section", None, None),
            P(),
            P(),
        ),
        out_specs=(
            P("section", "lat", None, None),
            P("section", None, None, "lat"),
            P("section", None, None, "lat"),
            P("section", None, "lat"),
        ),
        check_vma=False,
    )
```

```python
import functools
import math

import jax
import jax.numpy as jnp
import numpy as np
from jax import lax
from jax.experimental import pallas as pl
from jax.experimental.pallas import tpu as pltpu
from jax.sharding import PartitionSpec as P

NB = 4
BS = 96
KM = 72
LANES = 128
F32 = jnp.float32
BF16 = jnp.bfloat16


def from_behind(value, axis, by):
    length = lax.axis_size(axis)
    pairs = [(i, i + by) for i in range(length) if 0 <= i + by < length]
    return lax.ppermute(value, axis, pairs)


def turn(value, axis):
    length = lax.axis_size(axis)
    return lax.ppermute(value, axis, [(i, (i - 1) % length) for i in range(length)])


def lon_tables(n_modes, length):
    modes = np.arange(n_modes)
    phase = modes[:, None] * np.arange(length)[None, :] % length
    angle = phase * (2.0 * math.pi / length)
    forward = np.stack([np.cos(angle), -np.sin(angle)]) / math.sqrt(length)
    weight = np.where(modes == 0, 1.0, 2.0)[None, :, None]
    return forward, forward * weight


def lat_waves(n_rows):
    freqs = np.arange(n_rows)
    angle = (freqs[:, None] * freqs[None, :] % n_rows) * (2.0 * math.pi / n_rows)
    factor = 1.0 / math.sqrt(n_rows)
    return np.cos(angle) * factor, np.sin(angle) * factor


def silu_slope(pre):
    sig = jax.nn.sigmoid(pre)
    return sig * (1.0 + pre * (1.0 - sig))


def window(x, start):
    low = start // LANES * LANES
    shift = start - low
    if shift == 0:
        return x[:, low : low + LANES]
    if shift + BS <= LANES:
        return pltpu.roll(x[:, low : low + LANES], LANES - shift, 1)
    return pltpu.roll(x[:, low : low + 2 * LANES], 2 * LANES - shift, 1)[:, :LANES]


def dense(parts):
    lane = lax.broadcasted_iota(jnp.int32, parts[0].shape, 1)
    first = pltpu.roll(parts[1], 96, 1)
    second = pltpu.roll(parts[2], 64, 1)
    third = pltpu.roll(parts[3], 32, 1)
    return jnp.concatenate(
        [
            jnp.where(lane < 96, parts[0], first),
            jnp.where(lane < 64, first, second),
            jnp.where(lane < 32, second, third),
        ],
        axis=1,
    )


def dot(a, b, contract):
    return lax.dot_general(a, b, ((contract[:1], contract[1:]), ((), ())), preferred_element_type=F32)


def mode_numbers(shape, axis, q):
    number = lax.broadcasted_iota(jnp.int32, shape, axis)
    number = jnp.where(number >= NB * q, number - NB * q, number)
    mode = number
    for z in range(1, NB):
        mode = jnp.where(number >= z * q, number + z * q, mode)
    return mode


def fetch(sems, sources, targets):
    copies = [
        pltpu.make_async_copy(source, target, sems.at[i])
        for i, (source, target) in enumerate(zip(sources, targets))
    ]
    for copy in copies:
        copy.start()
    return copies


def wait(copies):
    for copy in copies:
        copy.wait()


def partner(d):
    return jnp.bitwise_xor(lax.axis_index("lat") // 2, d)


def analyse_kernel(q, *refs):
    hbm, outs, held, (by_block, sems) = refs[:5], refs[5:9], refs[9:14], refs[14:]
    counts, assign, field, table, saved = held
    copies = fetch(sems, hbm, held)
    wait(copies[4:])
    parts = [saved[:, c, :].astype(F32) for c in range(2)]
    points = [
        [
            jnp.concatenate([window(part, (mm * NB + n) * BS) for mm in range(q)], axis=0)
            for part in parts
        ]
        for n in range(NB)
    ]
    wait(copies[:4])
    rows = by_block.shape[1]
    spectral = jnp.dot(table[...], field[...], preferred_element_type=F32)
    active = counts[assign[lax.axis_index("lat")]]
    mode = mode_numbers((rows, spectral.shape[1]), 0, q)
    groups = [
        jnp.where(mode < active - g * q, spectral[g * rows : (g + 1) * rows], 0.0)
        for g in range(2)
    ]
    for n in range(NB):
        pieces = [window(group, n * BS) for group in groups]
        by_block[n] = dense(pieces + points[n]).astype(BF16)
    for d, out in enumerate(outs):
        out[...] = by_block[partner(d)]


def ready_kernel(q, *refs):
    hbm, (mat1, mat2, bias, lat, lat_t, own_field, own_table) = refs[:9], refs[9:16]
    counts, assign, w1, w2, b1, table, sems = refs[16:]
    copies = fetch(sems, hbm, (counts, assign, w1, w2, b1, table, lat, lat_t, own_field))
    wait(copies[:6])
    active = counts[assign[lax.axis_index("lat")]]
    rows = table.shape[1] // 2
    mode = mode_numbers((table.shape[0], rows), 1, q)
    for g in range(2):
        part = table[:, g * rows : (g + 1) * rows].astype(F32)
        part = jnp.where(mode < active - g * q, part, 0.0)
        own_table[:, g * rows : (g + 1) * rows] = part.astype(BF16)
    block = lax.axis_index("lat") // 2

    def pick(x):
        value = window(x, 0)
        for n in range(1, NB):
            value = jnp.where(block == n, window(x, n * BS), value)
        lane = lax.broadcasted_iota(jnp.int32, value.shape, 1)
        return jnp.where(lane < BS, value, 0.0)

    gap = jnp.zeros((LANES - BS, 2 * LANES), BF16)
    for source, mat in ((w1, mat1), (w2, mat2)):
        real, imag = (pick(source[c].astype(F32)) for c in range(2))
        mat[0:BS] = jnp.concatenate([real, imag], axis=1).astype(BF16)
        mat[BS:LANES] = gap
        mat[LANES : LANES + BS] = jnp.concatenate([-imag, real], axis=1).astype(BF16)
        mat[LANES + BS : 2 * LANES] = gap
    shift_b = pick(b1[...].astype(F32))
    bias[...] = jnp.concatenate([shift_b[0:1], shift_b[1:2]], axis=1)
    wait(copies[6:])


def join_kernel(count, *refs):
    out = refs[-1]
    for d, ref in enumerate(refs[:count]):
        out[d] = ref[...]


def pack(band):
    rows = band.shape[0]
    tail = rows // 2 + 4
    left, right = band[:, :LANES], pltpu.roll(band[:, LANES:], 96, 1)
    lane = lax.broadcasted_iota(jnp.int32, left.shape, 1)
    upper = jnp.where(lane < 96, left, right)
    lower = pltpu.roll(right[rows - tail :], 64, 1)
    lower = jnp.where(lane[:tail] < 64, right[:tail], lower)
    return jnp.concatenate([upper, lower], axis=0)


def unpack(packed, rows):
    tail = rows // 2 + 4
    upper, lower = packed[:rows], packed[rows:]
    rest = jnp.concatenate([lower, pltpu.roll(lower, 64, 1)[2 * tail - rows :]], axis=0)
    lane = lax.broadcasted_iota(jnp.int32, upper.shape, 1)
    right = jnp.where(lane < 32, pltpu.roll(upper, 32, 1), pltpu.roll(rest, 32, 1))
    return [upper, right]


def silu_points(chunks, mat, bias, by_pair, points, hidden, slope):
    for d, chunk in enumerate(chunks):
        parts = [window(chunk, j * BS) for j in (2, 3)]
        by_pair[partner(d)] = jnp.concatenate(parts, axis=1)
    v = by_pair[...].reshape(points.shape).astype(BF16)
    pre = dot(v, mat[...], (1, 0)) + bias[...]
    sig = jax.nn.sigmoid(pre)
    points[...] = v
    hidden[...] = (pre * sig).astype(BF16)
    slope[...] = sig * (1.0 + pre * (1.0 - sig))


def own_kernel(*refs):
    chunks, (mat1, bias), (points, hidden, slope), by_pair = refs[:4], refs[4:6], refs[6:9], refs[9]
    silu_points([chunk[...].astype(F32) for chunk in chunks], mat1, bias, by_pair, points, hidden, slope)


def filter_kernel(*refs):
    owns, (other, slope_own, mat1, mat2, bias, lat, lat_t, assign_hbm) = refs[:4], refs[4:12]
    outs, (points, hidden, grad_pre, grad_y) = refs[12:16], refs[16:20]
    assign, by_lat, by_pair, slope, sems = refs[20:]
    copies = fetch(sems, (assign_hbm,), (assign,))
    core = lax.rem(lax.axis_index("lat"), 2)
    sides = [[own[...].astype(F32) for own in owns], [other[d].astype(F32) for d in range(NB)]]
    silu_points(sides[1], mat1, bias, by_pair, points, hidden, slope)
    wait(copies)
    for side, chunks in zip((core, 1 - core), sides):
        for d, chunk in enumerate(chunks):
            groups = [window(chunk, j * BS) for j in range(2)]
            by_lat[assign[2 * partner(d) + side]] = jnp.concatenate(groups, axis=1)
    field = by_lat[...].reshape(lat.shape[1], 2 * LANES).astype(BF16)
    waves = dot(lat[...], field, (1, 0)).astype(BF16)
    rows = waves.shape[0] // 2
    inner = []
    for side, slopes in enumerate((slope_own, slope)):
        dy = []
        for c in range(2):
            part = waves[c * rows : (c + 1) * rows]
            flip = core == 0 if side == 0 else core == 1
            dy.append(jnp.where(flip, part[:, :LANES], part[:, LANES:]))
        dy = jnp.concatenate(dy, axis=1)
        dp = (dot(dy, mat2[...], (1, 1)) * slopes[...]).astype(BF16)
        dv = dot(dp, mat1[...], (1, 1))
        grad_y[side] = dy
        grad_pre[side] = dp
        inner.append(jnp.concatenate([dv[:, :LANES], dv[:, LANES:]], axis=0))
    left = jnp.where(core == 0, inner[0], inner[1])
    right = jnp.where(core == 0, inner[1], inner[0])
    inner = jnp.concatenate([left, right], axis=1).astype(BF16)
    for d, out in enumerate(outs):
        band = dot(lat_t[assign[2 * partner(d) + core]], inner, (1, 0))
        out[...] = pack(band).astype(BF16)


def products_kernel(points0, hidden0, points1, hidden1, grad_pre, grad_y, gw1, gw2, gb1):
    core = lax.rem(lax.axis_index("lat"), 2)
    half = BS // 2
    for ref, grads, values in ((gw1, grad_pre, (points0, points1)), (gw2, grad_y, (hidden0, hidden1))):
        both = dot(grads[0], values[0][...], (0, 0)) + dot(grads[1], values[1][...], (0, 0))
        real = both[:BS, :LANES] + both[LANES : LANES + BS, LANES:]
        imag = both[LANES : LANES + BS, :LANES] - both[:BS, LANES:]
        for c, full in enumerate((real, imag)):
            ref[c] = jnp.where(core == 0, full[:half], full[half:])[:, :BS]
    sums = sum(jnp.sum(grad_pre[side].astype(F32), axis=0, keepdims=True) for side in range(2))
    for c in range(2):
        line = sums[:, c * LANES : (c + 1) * LANES]
        gb1[c : c + 1] = jnp.where(core == 0, line[:, :half], line[:, half:BS])


def compose_kernel(last, three, one, field, table, out, by_block):
    rows = by_block.shape[1]
    for d, back in ((0, three[0]), (1, one[...]), (2, three[1]), (3, three[2])):
        by_block[partner(d)] = jnp.concatenate(unpack(back.astype(F32), rows), axis=1)
    groups = [
        dense([by_block[n, :, g * LANES : (g + 1) * LANES] for n in range(NB)]) for g in range(2)
    ]
    groups = jnp.concatenate(groups, axis=0).astype(BF16)
    mixed = jnp.dot(table[...], groups, preferred_element_type=F32).astype(BF16)
    whole = field[...].astype(F32) + mixed.astype(F32)
    out[...] = jnp.where(lax.axis_index("section") == last, 0.0, whole).astype(BF16)


VMEM = pl.BlockSpec(memory_space=pltpu.VMEM)
HBM = pl.BlockSpec(memory_space=pltpu.HBM)


def call(kernel, outs, scratch, near, far, flops=10**8):
    many = isinstance(outs, tuple)
    many = isinstance(outs, tuple)
    return pl.pallas_call(
        kernel,
        out_shape=outs,
        in_specs=[VMEM] * len(near) + [HBM] * len(far),
        out_specs=tuple([VMEM] * len(outs)) if many else VMEM,
        scratch_shapes=scratch,
        cost_estimate=pl.CostEstimate(flops=flops, bytes_accessed=10**6, transcendentals=0),
        compiler_params=pltpu.CompilerParams(vmem_limit_bytes=32 * 2**20),
    )(*near, *(pltpu.with_memory_space_constraint(x, pltpu.HBM) for x in far))


def scratch_for(*arrays):
    scratch = []
    for x in arrays:
        space = pltpu.SMEM if x.dtype == jnp.int32 else pltpu.VMEM
        scratch.append(space(x.shape, x.dtype))
    return scratch, pltpu.SemaphoreType.DMA((len(arrays),))


def paired_blocks(grad_out, spec_saved, w1, w2, b1, mode_counts, assignment):
    length, width = grad_out.shape[2:]
    n_rows = assignment.shape[0]
    q = spec_saved.shape[3] // (NB * BS)
    rows = 2 * NB * q
    forward, inverse = lon_tables(KM, length)

    def by_group(table):
        table = table.reshape(2, NB, 2, q, length).transpose(2, 0, 1, 3, 4)
        return table.reshape(2 * rows, length).astype(BF16)

    cosine, sine = lat_waves(n_rows)
    waves = np.array([[cosine, sine], [-sine, cosine]])
    lat = np.einsum("eckr,uv->eukrcv", waves, np.eye(NB * q))
    lat = lat.reshape(2 * NB * q * n_rows, n_rows * rows).astype(BF16)
    lat_t = np.ascontiguousarray(lat.T).reshape(n_rows, rows, -1)

    lat, lat_t = jnp.asarray(lat), jnp.asarray(lat_t)
    inverse = jnp.asarray(by_group(inverse))
    forward = jnp.asarray(by_group(forward).T)

    def swap(chunks):
        pairs = [[(i, i ^ (2 * d)) for i in range(2 * NB)] for d in range(NB)]
        return [chunks[0]] + [lax.ppermute(chunks[d], "lat", pairs[d]) for d in (3, 2, 1)][::-1]

    field = grad_out.reshape(length, width)
    shape = jax.ShapeDtypeStruct
    far = (mode_counts, assignment, field, inverse, spec_saved[0])
    scratch, sems = scratch_for(*far)
    sent = call(
        functools.partial(analyse_kernel, q),
        (shape((rows, width), BF16),) * NB,
        scratch + [pltpu.VMEM((NB, rows, width), BF16), sems],
        (),
        far,
    )
    received = swap(sent)
    far = (mode_counts, assignment, w1[0], w2[0], b1[0], forward)
    scratch, _ = scratch_for(*far)
    far = (*far, lat, lat_t, field)
    wide = 2 * LANES
    mat1, mat2, bias, lat, lat_t, field, forward = call(
        functools.partial(ready_kernel, q),
        (
            shape((wide, wide), BF16),
            shape((wide, wide), BF16),
            shape((1, wide), F32),
            shape(lat.shape, BF16),
            shape(lat_t.shape, BF16),
            shape(field.shape, BF16),
            shape(forward.shape, BF16),
        ),
        scratch + [pltpu.SemaphoreType.DMA((len(far),))],
        (),
        far,
        2 * 10**9,
    )
    next_field = turn(field, "section")
    own = call(
        functools.partial(join_kernel, NB),
        shape((NB, rows, width), BF16),
        [],
        (*received, bias),
        (),
    )
    other = lax.ppermute(own, "lat", [(i, i ^ 1) for i in range(2 * NB)])
    vectors = shape((NB * rows, wide), BF16)
    slopes = shape((NB * rows, wide), F32)
    by_pair = pltpu.VMEM((NB, rows, wide), F32)
    points0, hidden0, slope0 = call(
        own_kernel,
        (vectors, vectors, slopes),
        [by_pair],
        (*received, mat1, bias),
        (),
        2 * 10**9,
    )
    packed = shape((rows + rows // 2 + 4, LANES), BF16)
    scratch, sems = scratch_for(assignment)
    both = shape((2, NB * rows, wide), BF16)
    *chunks, points1, hidden1, grad_pre, grad_y = call(
        filter_kernel,
        (packed,) * NB + (vectors, vectors, both, both),
        scratch
        + [
            pltpu.VMEM((n_rows, rows, wide), F32),
            by_pair,
            pltpu.VMEM((NB * rows, wide), F32),
            sems,
        ],
        (*received, other, slope0, mat1, mat2, bias, lat, lat_t),
        (assignment,),
    )
    backs = swap(chunks)
    matrix = shape((2, BS // 2, BS), F32)
    gw1, gw2, gb1 = call(
        products_kernel,
        (matrix, matrix, shape((2, BS // 2), F32)),
        [],
        (points0, hidden0, points1, hidden1, grad_pre, grad_y),
        (),
        2 * 10**9,
    )
    three = call(
        functools.partial(join_kernel, 3),
        shape((3, *packed.shape), BF16),
        [],
        (backs[0], backs[2], backs[3]),
        (),
    )
    three = turn(three, "section")
    one = turn(backs[1], "section")
    shifted = call(
        functools.partial(compose_kernel, lax.axis_size("section") - 1),
        shape((length, width), BF16),
        [by_pair],
        (three, one, next_field, forward),
        (),
    )
    shifted = shifted[None, None]
    return shifted, gw1.swapaxes(1, 2)[None], gw2.swapaxes(1, 2)[None], gb1[None]


def apply_mat(vec, mat):
    return jnp.einsum("kpi,ipj->kpj", vec, mat, preferred_element_type=F32)


def adjoint_mat(vec, mat):
    return jnp.einsum("kpj,ipj->kpi", vec, mat, preferred_element_type=F32)


def outer_sum(left, right):
    return jnp.einsum("kpi,kpj->ipj", left, right, preferred_element_type=F32)


def split_blocks(grad_out, spec_saved, w1, w2, b1, mode_counts, assignment):
    rows_dev = grad_out.shape[1]
    length = grad_out.shape[2]
    width = grad_out.shape[3]
    n_rows = assignment.shape[0]
    pairs_dev = spec_saved.shape[3] // BS
    forward, inverse = (jnp.asarray(t.astype(BF16)) for t in lon_tables(KM, length))
    cosine, sine = (jnp.asarray(t.astype(BF16))[:, assignment] for t in lat_waves(n_rows))
    table = jnp.stack(
        [jnp.stack([cosine, sine], axis=-1), jnp.stack([-sine, cosine], axis=-1)], axis=1
    )
    lat_pos = lax.axis_index("lat")
    lat_count = lax.axis_size("lat")
    own_lat = lax.dynamic_slice_in_dim(assignment, lat_pos * rows_dev, rows_dev)
    active = (jnp.arange(KM, dtype=jnp.int32)[None, :] < mode_counts[own_lat][:, None]).astype(F32)
    cotan = grad_out[0]
    spectral = jnp.einsum(
        "cml,rlni->rcmni",
        inverse,
        cotan.reshape(rows_dev, length, NB, BS),
        preferred_element_type=F32,
    )
    spectral = (spectral * active[:, None, :, None, None]).astype(BF16)
    spectral = spectral.reshape(rows_dev, 2, KM * NB * BS)
    pencil = lax.all_to_all(spectral, "lat", split_axis=2, concat_axis=0, tiled=True)
    pencil = pencil.reshape(n_rows, 2, pairs_dev, BS)
    grad_y = jnp.einsum("kerc,rcpi->kepi", table, pencil, preferred_element_type=F32).astype(BF16)
    saved = spec_saved[0].reshape(n_rows, 2, pairs_dev, BS)
    pair_ids = lat_pos * pairs_dev + jnp.arange(pairs_dev, dtype=jnp.int32)
    owner = (pair_ids % NB)[:, None] == jnp.arange(NB, dtype=jnp.int32)[None, :]
    owner = owner.astype(F32)
    first = jnp.take(w1[0].reshape(2, BS, NB, BS), pair_ids % NB, axis=2)
    second = jnp.take(w2[0].reshape(2, BS, NB, BS), pair_ids % NB, axis=2)
    shift_b = jnp.take(b1[0].reshape(2, NB, BS), pair_ids % NB, axis=1).astype(F32)
    v_r = saved[:, 0]
    v_i = saved[:, 1]
    pre_r = apply_mat(v_r, first[0]) - apply_mat(v_i, first[1]) + shift_b[0][None]
    pre_i = apply_mat(v_i, first[0]) + apply_mat(v_r, first[1]) + shift_b[1][None]
    hid_r = jax.nn.silu(pre_r).astype(BF16)
    hid_i = jax.nn.silu(pre_i).astype(BF16)
    dy_r = grad_y[:, 0]
    dy_i = grad_y[:, 1]
    dh_r = adjoint_mat(dy_r, second[0]) + adjoint_mat(dy_i, second[1])
    dh_i = adjoint_mat(dy_i, second[0]) - adjoint_mat(dy_r, second[1])
    dp_r = (dh_r * silu_slope(pre_r)).astype(BF16)
    dp_i = (dh_i * silu_slope(pre_i)).astype(BF16)
    gw2 = jnp.stack(
        [
            outer_sum(hid_r, dy_r) + outer_sum(hid_i, dy_i),
            outer_sum(hid_r, dy_i) - outer_sum(hid_i, dy_r),
        ]
    )
    gw1 = jnp.stack(
        [outer_sum(v_r, dp_r) + outer_sum(v_i, dp_i), outer_sum(v_r, dp_i) - outer_sum(v_i, dp_r)]
    )
    gb1 = jnp.stack([jnp.sum(dp_r.astype(F32), axis=0), jnp.sum(dp_i.astype(F32), axis=0)])
    dv_r = adjoint_mat(dp_r, first[0]) + adjoint_mat(dp_i, first[1])
    dv_i = adjoint_mat(dp_i, first[0]) - adjoint_mat(dp_r, first[1])
    grad_v = jnp.stack([dv_r, dv_i], axis=1).astype(BF16)
    grad_u = jnp.einsum("kerc,kepi->rcpi", table, grad_v, preferred_element_type=F32).astype(BF16)
    grad_u = grad_u.reshape(n_rows, 2, pairs_dev * BS)
    back = lax.all_to_all(grad_u, "lat", split_axis=0, concat_axis=2, tiled=True)
    back = back.reshape(rows_dev, 2, KM, NB, BS) * active[:, None, :, None, None].astype(BF16)
    mixed = jnp.einsum("cml,rcmni->rlni", forward, back, preferred_element_type=F32)
    mixed = mixed.reshape(rows_dev, length, width).astype(BF16)
    block_w1 = jnp.einsum("pn,cipj->cinj", owner, gw1).reshape(1, 2, BS, width)
    block_w2 = jnp.einsum("pn,cipj->cinj", owner, gw2).reshape(1, 2, BS, width)
    block_b1 = jnp.einsum("pn,cpj->cnj", owner, gb1).reshape(1, 2, width)
    columns = width // lat_count
    full_w1, full_w2, full_b1 = lax.psum((block_w1, block_w2, block_b1), "lat")
    sum_w1 = lax.dynamic_slice_in_dim(full_w1, lat_pos * columns, columns, 3)
    sum_w2 = lax.dynamic_slice_in_dim(full_w2, lat_pos * columns, columns, 3)
    sum_b1 = lax.dynamic_slice_in_dim(full_b1, lat_pos * columns, columns, 2)
    whole = (cotan.astype(F32) + mixed.astype(F32)).astype(BF16)
    received = from_behind(whole[None], "section", -1)
    return (received, sum_w1, sum_w2, sum_b1)


def per_device(grad_out, spec_saved, w1, w2, b1, mode_counts, assignment):
    n_dev = lax.axis_size("lat")
    pairs_dev = spec_saved.shape[3] // BS
    paired = n_dev == 2 * NB and grad_out.shape[1] == 1 and pairs_dev % NB == 0
    body = paired_blocks if paired else split_blocks
    return body(grad_out, spec_saved, w1, w2, b1, mode_counts, assignment)


def solution(mesh):
    return jax.shard_map(
        per_device,
        mesh=mesh,
        in_specs=(
            P("section", "lat", None, None),
            P("section", None, None, "lat"),
            P("section", None, None, None),
            P("section", None, None, None),
            P("section", None, None),
            P(),
            P(),
        ),
        out_specs=(
            P("section", "lat", None, None),
            P("section", None, None, "lat"),
            P("section", None, None, "lat"),
            P("section", None, "lat"),
        ),
        check_vma=False,
    )
```

```python
import functools
import math

import jax
import jax.numpy as jnp
import numpy as np
from jax import lax
from jax.experimental import pallas as pl
from jax.experimental.pallas import tpu as pltpu
from jax.sharding import PartitionSpec as P

NB = 4
BS = 96
KM = 72
LANES = 128
F32 = jnp.float32
BF16 = jnp.bfloat16


def from_behind(value, axis, by):
    length = lax.axis_size(axis)
    pairs = [(i, i + by) for i in range(length) if 0 <= i + by < length]
    return lax.ppermute(value, axis, pairs)


def turn(value, axis):
    length = lax.axis_size(axis)
    return lax.ppermute(value, axis, [(i, (i - 1) % length) for i in range(length)])


def lon_tables(n_modes, length):
    modes = np.arange(n_modes)
    phase = modes[:, None] * np.arange(length)[None, :] % length
    angle = phase * (2.0 * math.pi / length)
    forward = np.stack([np.cos(angle), -np.sin(angle)]) / math.sqrt(length)
    weight = np.where(modes == 0, 1.0, 2.0)[None, :, None]
    return forward, forward * weight


def lat_waves(n_rows):
    freqs = np.arange(n_rows)
    angle = (freqs[:, None] * freqs[None, :] % n_rows) * (2.0 * math.pi / n_rows)
    factor = 1.0 / math.sqrt(n_rows)
    return np.cos(angle) * factor, np.sin(angle) * factor


def silu_slope(pre):
    sig = jax.nn.sigmoid(pre)
    return sig * (1.0 + pre * (1.0 - sig))


def window(x, start):
    low = start // LANES * LANES
    shift = start - low
    if shift == 0:
        return x[:, low : low + LANES]
    if shift + BS <= LANES:
        return pltpu.roll(x[:, low : low + LANES], LANES - shift, 1)
    return pltpu.roll(x[:, low : low + 2 * LANES], 2 * LANES - shift, 1)[:, :LANES]


def dense(parts):
    lane = lax.broadcasted_iota(jnp.int32, parts[0].shape, 1)
    first = pltpu.roll(parts[1], 96, 1)
    second = pltpu.roll(parts[2], 64, 1)
    third = pltpu.roll(parts[3], 32, 1)
    return jnp.concatenate(
        [
            jnp.where(lane < 96, parts[0], first),
            jnp.where(lane < 64, first, second),
            jnp.where(lane < 32, second, third),
        ],
        axis=1,
    )


def dot(a, b, contract):
    return lax.dot_general(a, b, ((contract[:1], contract[1:]), ((), ())), preferred_element_type=F32)


def mode_numbers(shape, axis, q):
    number = lax.broadcasted_iota(jnp.int32, shape, axis)
    number = jnp.where(number >= NB * q, number - NB * q, number)
    mode = number
    for z in range(1, NB):
        mode = jnp.where(number >= z * q, number + z * q, mode)
    return mode


def fetch(sems, sources, targets):
    copies = [
        pltpu.make_async_copy(source, target, sems.at[i])
        for i, (source, target) in enumerate(zip(sources, targets))
    ]
    for copy in copies:
        copy.start()
    return copies


def wait(copies):
    for copy in copies:
        copy.wait()


def partner(d):
    return jnp.bitwise_xor(lax.axis_index("lat") // 2, d)


def analyse_kernel(q, *refs):
    hbm, outs, held, (by_block, sems) = refs[:5], refs[5:9], refs[9:14], refs[14:]
    counts, assign, field, table, saved = held
    copies = fetch(sems, hbm, held)
    wait(copies[4:])
    parts = [saved[:, c, :].astype(F32) for c in range(2)]
    points = [
        [
            jnp.concatenate([window(part, (mm * NB + n) * BS) for mm in range(q)], axis=0)
            for part in parts
        ]
        for n in range(NB)
    ]
    wait(copies[:4])
    rows = by_block.shape[1]
    spectral = jnp.dot(table[...], field[...], preferred_element_type=F32)
    active = counts[assign[lax.axis_index("lat")]]
    mode = mode_numbers((rows, spectral.shape[1]), 0, q)
    groups = [
        jnp.where(mode < active - g * q, spectral[g * rows : (g + 1) * rows], 0.0)
        for g in range(2)
    ]
    for n in range(NB):
        pieces = [window(group, n * BS) for group in groups]
        by_block[n] = dense(pieces + points[n]).astype(BF16)
    for d, out in enumerate(outs):
        out[...] = by_block[partner(d)]


def ready_kernel(q, *refs):
    hbm, (mat1, mat2, bias, lat, lat_t, own_field, own_table) = refs[:9], refs[9:16]
    counts, assign, w1, w2, b1, table, sems = refs[16:]
    copies = fetch(sems, hbm, (counts, assign, w1, w2, b1, table, lat, lat_t, own_field))
    wait(copies[:6])
    active = counts[assign[lax.axis_index("lat")]]
    rows = table.shape[1] // 2
    mode = mode_numbers((table.shape[0], rows), 1, q)
    for g in range(2):
        part = table[:, g * rows : (g + 1) * rows].astype(F32)
        part = jnp.where(mode < active - g * q, part, 0.0)
        own_table[:, g * rows : (g + 1) * rows] = part.astype(BF16)
    block = lax.axis_index("lat") // 2

    def pick(x):
        value = window(x, 0)
        for n in range(1, NB):
            value = jnp.where(block == n, window(x, n * BS), value)
        lane = lax.broadcasted_iota(jnp.int32, value.shape, 1)
        return jnp.where(lane < BS, value, 0.0)

    gap = jnp.zeros((LANES - BS, 2 * LANES), BF16)
    for source, mat in ((w1, mat1), (w2, mat2)):
        real, imag = (pick(source[c].astype(F32)) for c in range(2))
        mat[0:BS] = jnp.concatenate([real, imag], axis=1).astype(BF16)
        mat[BS:LANES] = gap
        mat[LANES : LANES + BS] = jnp.concatenate([-imag, real], axis=1).astype(BF16)
        mat[LANES + BS : 2 * LANES] = gap
    shift_b = pick(b1[...].astype(F32))
    bias[...] = jnp.concatenate([shift_b[0:1], shift_b[1:2]], axis=1)
    wait(copies[6:])


def join_kernel(count, *refs):
    out = refs[-1]
    for d, ref in enumerate(refs[:count]):
        out[d] = ref[...]


def pack(band):
    rows = band.shape[0]
    tail = rows // 2 + 4
    left, right = band[:, :LANES], pltpu.roll(band[:, LANES:], 96, 1)
    lane = lax.broadcasted_iota(jnp.int32, left.shape, 1)
    upper = jnp.where(lane < 96, left, right)
    lower = pltpu.roll(right[rows - tail :], 64, 1)
    lower = jnp.where(lane[:tail] < 64, right[:tail], lower)
    return jnp.concatenate([upper, lower], axis=0)


def unpack(packed, rows):
    tail = rows // 2 + 4
    upper, lower = packed[:rows], packed[rows:]
    rest = jnp.concatenate([lower, pltpu.roll(lower, 64, 1)[2 * tail - rows :]], axis=0)
    lane = lax.broadcasted_iota(jnp.int32, upper.shape, 1)
    right = jnp.where(lane < 32, pltpu.roll(upper, 32, 1), pltpu.roll(rest, 32, 1))
    return [upper, right]


def silu_points(chunks, mat, bias, by_pair, points, hidden, slope):
    for d, chunk in enumerate(chunks):
        parts = [window(chunk, j * BS) for j in (2, 3)]
        by_pair[partner(d)] = jnp.concatenate(parts, axis=1)
    v = by_pair[...].reshape(points.shape).astype(BF16)
    pre = dot(v, mat[...], (1, 0)) + bias[...]
    sig = jax.nn.sigmoid(pre)
    points[...] = v
    hidden[...] = (pre * sig).astype(BF16)
    slope[...] = sig * (1.0 + pre * (1.0 - sig))


def own_kernel(*refs):
    chunks, (mat1, bias), (points, hidden, slope), by_pair = refs[:4], refs[4:6], refs[6:9], refs[9]
    silu_points([chunk[...].astype(F32) for chunk in chunks], mat1, bias, by_pair, points, hidden, slope)


def filter_kernel(*refs):
    owns, (other, slope_own, mat1, mat2, bias, lat, lat_t, assign_hbm) = refs[:4], refs[4:12]
    outs, (points, hidden, grad_pre, grad_y) = refs[12:16], refs[16:20]
    assign, by_lat, by_pair, slope, sems = refs[20:]
    copies = fetch(sems, (assign_hbm,), (assign,))
    core = lax.rem(lax.axis_index("lat"), 2)
    sides = [[own[...].astype(F32) for own in owns], [other[d].astype(F32) for d in range(NB)]]
    silu_points(sides[1], mat1, bias, by_pair, points, hidden, slope)
    wait(copies)
    for side, chunks in zip((core, 1 - core), sides):
        for d, chunk in enumerate(chunks):
            groups = [window(chunk, j * BS) for j in range(2)]
            by_lat[assign[2 * partner(d) + side]] = jnp.concatenate(groups, axis=1)
    field = by_lat[...].reshape(lat.shape[1], 2 * LANES).astype(BF16)
    waves = dot(lat[...], field, (1, 0)).astype(BF16)
    rows = waves.shape[0] // 2
    inner = []
    for side, slopes in enumerate((slope_own, slope)):
        dy = []
        for c in range(2):
            part = waves[c * rows : (c + 1) * rows]
            flip = core == 0 if side == 0 else core == 1
            dy.append(jnp.where(flip, part[:, :LANES], part[:, LANES:]))
        dy = jnp.concatenate(dy, axis=1)
        dp = (dot(dy, mat2[...], (1, 1)) * slopes[...]).astype(BF16)
        dv = dot(dp, mat1[...], (1, 1))
        grad_y[side] = dy
        grad_pre[side] = dp
        inner.append(jnp.concatenate([dv[:, :LANES], dv[:, LANES:]], axis=0))
    left = jnp.where(core == 0, inner[0], inner[1])
    right = jnp.where(core == 0, inner[1], inner[0])
    inner = jnp.concatenate([left, right], axis=1).astype(BF16)
    for d, out in enumerate(outs):
        band = dot(lat_t[assign[2 * partner(d) + core]], inner, (1, 0))
        out[...] = pack(band).astype(BF16)


def products_kernel(points0, hidden0, points1, hidden1, grad_pre, grad_y, _, gw1, gw2, gb1):
    core = lax.rem(lax.axis_index("lat"), 2)
    half = BS // 2
    for ref, grads, values in ((gw1, grad_pre, (points0, points1)), (gw2, grad_y, (hidden0, hidden1))):
        both = dot(grads[0], values[0][...], (0, 0)) + dot(grads[1], values[1][...], (0, 0))
        real = both[:BS, :LANES] + both[LANES : LANES + BS, LANES:]
        imag = both[LANES : LANES + BS, :LANES] - both[:BS, LANES:]
        for c, full in enumerate((real, imag)):
            ref[c] = jnp.where(core == 0, full[:half], full[half:])[:, :BS]
    sums = sum(jnp.sum(grad_pre[side].astype(F32), axis=0, keepdims=True) for side in range(2))
    for c in range(2):
        line = sums[:, c * LANES : (c + 1) * LANES]
        gb1[c : c + 1] = jnp.where(core == 0, line[:, :half], line[:, half:BS])


def compose_kernel(last, three, one, field, table, out, by_block):
    rows = by_block.shape[1]
    for d, back in ((0, three[0]), (1, one[...]), (2, three[1]), (3, three[2])):
        by_block[partner(d)] = jnp.concatenate(unpack(back.astype(F32), rows), axis=1)
    groups = [
        dense([by_block[n, :, g * LANES : (g + 1) * LANES] for n in range(NB)]) for g in range(2)
    ]
    groups = jnp.concatenate(groups, axis=0).astype(BF16)
    mixed = jnp.dot(table[...], groups, preferred_element_type=F32).astype(BF16)
    whole = field[...].astype(F32) + mixed.astype(F32)
    out[...] = jnp.where(lax.axis_index("section") == last, 0.0, whole).astype(BF16)


VMEM = pl.BlockSpec(memory_space=pltpu.VMEM)
HBM = pl.BlockSpec(memory_space=pltpu.HBM)


def call(kernel, outs, scratch, near, far, flops=10**8):
    many = isinstance(outs, tuple)
    many = isinstance(outs, tuple)
    return pl.pallas_call(
        kernel,
        out_shape=outs,
        in_specs=[VMEM] * len(near) + [HBM] * len(far),
        out_specs=tuple([VMEM] * len(outs)) if many else VMEM,
        scratch_shapes=scratch,
        cost_estimate=pl.CostEstimate(flops=flops, bytes_accessed=10**6, transcendentals=0),
        compiler_params=pltpu.CompilerParams(vmem_limit_bytes=32 * 2**20),
    )(*near, *(pltpu.with_memory_space_constraint(x, pltpu.HBM) for x in far))


def scratch_for(*arrays):
    scratch = []
    for x in arrays:
        space = pltpu.SMEM if x.dtype == jnp.int32 else pltpu.VMEM
        scratch.append(space(x.shape, x.dtype))
    return scratch, pltpu.SemaphoreType.DMA((len(arrays),))


def paired_blocks(grad_out, spec_saved, w1, w2, b1, mode_counts, assignment):
    length, width = grad_out.shape[2:]
    n_rows = assignment.shape[0]
    q = spec_saved.shape[3] // (NB * BS)
    rows = 2 * NB * q
    forward, inverse = lon_tables(KM, length)

    def by_group(table):
        table = table.reshape(2, NB, 2, q, length).transpose(2, 0, 1, 3, 4)
        return table.reshape(2 * rows, length).astype(BF16)

    cosine, sine = lat_waves(n_rows)
    waves = np.array([[cosine, sine], [-sine, cosine]])
    lat = np.einsum("eckr,uv->eukrcv", waves, np.eye(NB * q))
    lat = lat.reshape(2 * NB * q * n_rows, n_rows * rows).astype(BF16)
    lat_t = np.ascontiguousarray(lat.T).reshape(n_rows, rows, -1)

    lat, lat_t = jnp.asarray(lat), jnp.asarray(lat_t)
    inverse = jnp.asarray(by_group(inverse))
    forward = jnp.asarray(by_group(forward).T)

    def swap(chunks):
        pairs = [[(i, i ^ (2 * d)) for i in range(2 * NB)] for d in range(NB)]
        return [chunks[0]] + [lax.ppermute(chunks[d], "lat", pairs[d]) for d in (3, 2, 1)][::-1]

    field = grad_out.reshape(length, width)
    shape = jax.ShapeDtypeStruct
    far = (mode_counts, assignment, field, inverse, spec_saved[0])
    scratch, sems = scratch_for(*far)
    sent = call(
        functools.partial(analyse_kernel, q),
        (shape((rows, width), BF16),) * NB,
        scratch + [pltpu.VMEM((NB, rows, width), BF16), sems],
        (),
        far,
    )
    received = swap(sent)
    far = (mode_counts, assignment, w1[0], w2[0], b1[0], forward)
    scratch, _ = scratch_for(*far)
    far = (*far, lat, lat_t, field)
    wide = 2 * LANES
    mat1, mat2, bias, lat, lat_t, field, forward = call(
        functools.partial(ready_kernel, q),
        (
            shape((wide, wide), BF16),
            shape((wide, wide), BF16),
            shape((1, wide), F32),
            shape(lat.shape, BF16),
            shape(lat_t.shape, BF16),
            shape(field.shape, BF16),
            shape(forward.shape, BF16),
        ),
        scratch + [pltpu.SemaphoreType.DMA((len(far),))],
        (),
        far,
        2 * 10**9,
    )
    next_field = turn(field, "section")
    own = call(
        functools.partial(join_kernel, NB),
        shape((NB, rows, width), BF16),
        [],
        (*received, bias),
        (),
    )
    other = lax.ppermute(own, "lat", [(i, i ^ 1) for i in range(2 * NB)])
    vectors = shape((NB * rows, wide), BF16)
    slopes = shape((NB * rows, wide), F32)
    by_pair = pltpu.VMEM((NB, rows, wide), F32)
    points0, hidden0, slope0 = call(
        own_kernel,
        (vectors, vectors, slopes),
        [by_pair],
        (*received, mat1, bias),
        (),
        2 * 10**9,
    )
    packed = shape((rows + rows // 2 + 4, LANES), BF16)
    scratch, sems = scratch_for(assignment)
    both = shape((2, NB * rows, wide), BF16)
    *chunks, points1, hidden1, grad_pre, grad_y = call(
        filter_kernel,
        (packed,) * NB + (vectors, vectors, both, both),
        scratch
        + [
            pltpu.VMEM((n_rows, rows, wide), F32),
            by_pair,
            pltpu.VMEM((NB * rows, wide), F32),
            sems,
        ],
        (*received, other, slope0, mat1, mat2, bias, lat, lat_t),
        (assignment,),
    )
    backs = swap(chunks)
    matrix = shape((2, BS // 2, BS), F32)
    gw1, gw2, gb1 = call(
        products_kernel,
        (matrix, matrix, shape((2, BS // 2), F32)),
        [],
        (points0, hidden0, points1, hidden1, grad_pre, grad_y, next_field),
        (),
        2 * 10**9,
    )
    three = call(
        functools.partial(join_kernel, 3),
        shape((3, *packed.shape), BF16),
        [],
        (backs[0], backs[2], backs[3], gb1),
        (),
    )
    three = turn(three, "section")
    one = turn(backs[1], "section")
    shifted = call(
        functools.partial(compose_kernel, lax.axis_size("section") - 1),
        shape((length, width), BF16),
        [by_pair],
        (three, one, next_field, forward),
        (),
    )
    shifted = shifted[None, None]
    return shifted, gw1.swapaxes(1, 2)[None], gw2.swapaxes(1, 2)[None], gb1[None]


def apply_mat(vec, mat):
    return jnp.einsum("kpi,ipj->kpj", vec, mat, preferred_element_type=F32)


def adjoint_mat(vec, mat):
    return jnp.einsum("kpj,ipj->kpi", vec, mat, preferred_element_type=F32)


def outer_sum(left, right):
    return jnp.einsum("kpi,kpj->ipj", left, right, preferred_element_type=F32)


def split_blocks(grad_out, spec_saved, w1, w2, b1, mode_counts, assignment):
    rows_dev = grad_out.shape[1]
    length = grad_out.shape[2]
    width = grad_out.shape[3]
    n_rows = assignment.shape[0]
    pairs_dev = spec_saved.shape[3] // BS
    forward, inverse = (jnp.asarray(t.astype(BF16)) for t in lon_tables(KM, length))
    cosine, sine = (jnp.asarray(t.astype(BF16))[:, assignment] for t in lat_waves(n_rows))
    table = jnp.stack(
        [jnp.stack([cosine, sine], axis=-1), jnp.stack([-sine, cosine], axis=-1)], axis=1
    )
    lat_pos = lax.axis_index("lat")
    lat_count = lax.axis_size("lat")
    own_lat = lax.dynamic_slice_in_dim(assignment, lat_pos * rows_dev, rows_dev)
    active = (jnp.arange(KM, dtype=jnp.int32)[None, :] < mode_counts[own_lat][:, None]).astype(F32)
    cotan = grad_out[0]
    spectral = jnp.einsum(
        "cml,rlni->rcmni",
        inverse,
        cotan.reshape(rows_dev, length, NB, BS),
        preferred_element_type=F32,
    )
    spectral = (spectral * active[:, None, :, None, None]).astype(BF16)
    spectral = spectral.reshape(rows_dev, 2, KM * NB * BS)
    pencil = lax.all_to_all(spectral, "lat", split_axis=2, concat_axis=0, tiled=True)
    pencil = pencil.reshape(n_rows, 2, pairs_dev, BS)
    grad_y = jnp.einsum("kerc,rcpi->kepi", table, pencil, preferred_element_type=F32).astype(BF16)
    saved = spec_saved[0].reshape(n_rows, 2, pairs_dev, BS)
    pair_ids = lat_pos * pairs_dev + jnp.arange(pairs_dev, dtype=jnp.int32)
    owner = (pair_ids % NB)[:, None] == jnp.arange(NB, dtype=jnp.int32)[None, :]
    owner = owner.astype(F32)
    first = jnp.take(w1[0].reshape(2, BS, NB, BS), pair_ids % NB, axis=2)
    second = jnp.take(w2[0].reshape(2, BS, NB, BS), pair_ids % NB, axis=2)
    shift_b = jnp.take(b1[0].reshape(2, NB, BS), pair_ids % NB, axis=1).astype(F32)
    v_r = saved[:, 0]
    v_i = saved[:, 1]
    pre_r = apply_mat(v_r, first[0]) - apply_mat(v_i, first[1]) + shift_b[0][None]
    pre_i = apply_mat(v_i, first[0]) + apply_mat(v_r, first[1]) + shift_b[1][None]
    hid_r = jax.nn.silu(pre_r).astype(BF16)
    hid_i = jax.nn.silu(pre_i).astype(BF16)
    dy_r = grad_y[:, 0]
    dy_i = grad_y[:, 1]
    dh_r = adjoint_mat(dy_r, second[0]) + adjoint_mat(dy_i, second[1])
    dh_i = adjoint_mat(dy_i, second[0]) - adjoint_mat(dy_r, second[1])
    dp_r = (dh_r * silu_slope(pre_r)).astype(BF16)
    dp_i = (dh_i * silu_slope(pre_i)).astype(BF16)
    gw2 = jnp.stack(
        [
            outer_sum(hid_r, dy_r) + outer_sum(hid_i, dy_i),
            outer_sum(hid_r, dy_i) - outer_sum(hid_i, dy_r),
        ]
    )
    gw1 = jnp.stack(
        [outer_sum(v_r, dp_r) + outer_sum(v_i, dp_i), outer_sum(v_r, dp_i) - outer_sum(v_i, dp_r)]
    )
    gb1 = jnp.stack([jnp.sum(dp_r.astype(F32), axis=0), jnp.sum(dp_i.astype(F32), axis=0)])
    dv_r = adjoint_mat(dp_r, first[0]) + adjoint_mat(dp_i, first[1])
    dv_i = adjoint_mat(dp_i, first[0]) - adjoint_mat(dp_r, first[1])
    grad_v = jnp.stack([dv_r, dv_i], axis=1).astype(BF16)
    grad_u = jnp.einsum("kerc,kepi->rcpi", table, grad_v, preferred_element_type=F32).astype(BF16)
    grad_u = grad_u.reshape(n_rows, 2, pairs_dev * BS)
    back = lax.all_to_all(grad_u, "lat", split_axis=0, concat_axis=2, tiled=True)
    back = back.reshape(rows_dev, 2, KM, NB, BS) * active[:, None, :, None, None].astype(BF16)
    mixed = jnp.einsum("cml,rcmni->rlni", forward, back, preferred_element_type=F32)
    mixed = mixed.reshape(rows_dev, length, width).astype(BF16)
    block_w1 = jnp.einsum("pn,cipj->cinj", owner, gw1).reshape(1, 2, BS, width)
    block_w2 = jnp.einsum("pn,cipj->cinj", owner, gw2).reshape(1, 2, BS, width)
    block_b1 = jnp.einsum("pn,cpj->cnj", owner, gb1).reshape(1, 2, width)
    columns = width // lat_count
    full_w1, full_w2, full_b1 = lax.psum((block_w1, block_w2, block_b1), "lat")
    sum_w1 = lax.dynamic_slice_in_dim(full_w1, lat_pos * columns, columns, 3)
    sum_w2 = lax.dynamic_slice_in_dim(full_w2, lat_pos * columns, columns, 3)
    sum_b1 = lax.dynamic_slice_in_dim(full_b1, lat_pos * columns, columns, 2)
    whole = (cotan.astype(F32) + mixed.astype(F32)).astype(BF16)
    received = from_behind(whole[None], "section", -1)
    return (received, sum_w1, sum_w2, sum_b1)


def per_device(grad_out, spec_saved, w1, w2, b1, mode_counts, assignment):
    n_dev = lax.axis_size("lat")
    pairs_dev = spec_saved.shape[3] // BS
    paired = n_dev == 2 * NB and grad_out.shape[1] == 1 and pairs_dev % NB == 0
    body = paired_blocks if paired else split_blocks
    return body(grad_out, spec_saved, w1, w2, b1, mode_counts, assignment)


def solution(mesh):
    return jax.shard_map(
        per_device,
        mesh=mesh,
        in_specs=(
            P("section", "lat", None, None),
            P("section", None, None, "lat"),
            P("section", None, None, None),
            P("section", None, None, None),
            P("section", None, None),
            P(),
            P(),
        ),
        out_specs=(
            P("section", "lat", None, None),
            P("section", None, None, "lat"),
            P("section", None, None, "lat"),
            P("section", None, "lat"),
        ),
        check_vma=False,
    )
```

```python
import functools
import math

import jax
import jax.numpy as jnp
import numpy as np
from jax import lax
from jax.experimental import pallas as pl
from jax.experimental.pallas import tpu as pltpu
from jax.sharding import PartitionSpec as P

NB = 4
BS = 96
KM = 72
LANES = 128
F32 = jnp.float32
BF16 = jnp.bfloat16


def from_behind(value, axis, by):
    length = lax.axis_size(axis)
    pairs = [(i, i + by) for i in range(length) if 0 <= i + by < length]
    return lax.ppermute(value, axis, pairs)


def turn(value, axis):
    length = lax.axis_size(axis)
    return lax.ppermute(value, axis, [(i, (i - 1) % length) for i in range(length)])


def lon_tables(n_modes, length):
    modes = np.arange(n_modes)
    phase = modes[:, None] * np.arange(length)[None, :] % length
    angle = phase * (2.0 * math.pi / length)
    forward = np.stack([np.cos(angle), -np.sin(angle)]) / math.sqrt(length)
    weight = np.where(modes == 0, 1.0, 2.0)[None, :, None]
    return forward, forward * weight


def lat_waves(n_rows):
    freqs = np.arange(n_rows)
    angle = (freqs[:, None] * freqs[None, :] % n_rows) * (2.0 * math.pi / n_rows)
    factor = 1.0 / math.sqrt(n_rows)
    return np.cos(angle) * factor, np.sin(angle) * factor


def silu_slope(pre):
    sig = jax.nn.sigmoid(pre)
    return sig * (1.0 + pre * (1.0 - sig))


def window(x, start):
    low = start // LANES * LANES
    shift = start - low
    if shift == 0:
        return x[:, low : low + LANES]
    if shift + BS <= LANES:
        return pltpu.roll(x[:, low : low + LANES], LANES - shift, 1)
    return pltpu.roll(x[:, low : low + 2 * LANES], 2 * LANES - shift, 1)[:, :LANES]


def dense(parts):
    lane = lax.broadcasted_iota(jnp.int32, parts[0].shape, 1)
    first = pltpu.roll(parts[1], 96, 1)
    second = pltpu.roll(parts[2], 64, 1)
    third = pltpu.roll(parts[3], 32, 1)
    return jnp.concatenate(
        [
            jnp.where(lane < 96, parts[0], first),
            jnp.where(lane < 64, first, second),
            jnp.where(lane < 32, second, third),
        ],
        axis=1,
    )


def dot(a, b, contract):
    return lax.dot_general(a, b, ((contract[:1], contract[1:]), ((), ())), preferred_element_type=F32)


def mode_numbers(shape, axis, q):
    number = lax.broadcasted_iota(jnp.int32, shape, axis)
    number = jnp.where(number >= NB * q, number - NB * q, number)
    mode = number
    for z in range(1, NB):
        mode = jnp.where(number >= z * q, number + z * q, mode)
    return mode


def fetch(sems, sources, targets):
    copies = [
        pltpu.make_async_copy(source, target, sems.at[i])
        for i, (source, target) in enumerate(zip(sources, targets))
    ]
    for copy in copies:
        copy.start()
    return copies


def wait(copies):
    for copy in copies:
        copy.wait()


def partner(d):
    return jnp.bitwise_xor(lax.axis_index("lat") // 2, d)


def analyse_kernel(q, *refs):
    hbm, outs, held, (by_block, sems) = refs[:5], refs[5:9], refs[9:14], refs[14:]
    counts, assign, field, table, saved = held
    copies = fetch(sems, hbm, held)
    wait(copies[4:])
    parts = [saved[:, c, :].astype(F32) for c in range(2)]
    points = [
        [
            jnp.concatenate([window(part, (mm * NB + n) * BS) for mm in range(q)], axis=0)
            for part in parts
        ]
        for n in range(NB)
    ]
    wait(copies[:4])
    rows = by_block.shape[1]
    spectral = jnp.dot(table[...], field[...], preferred_element_type=F32)
    active = counts[assign[lax.axis_index("lat")]]
    mode = mode_numbers((rows, spectral.shape[1]), 0, q)
    groups = [
        jnp.where(mode < active - g * q, spectral[g * rows : (g + 1) * rows], 0.0)
        for g in range(2)
    ]
    for n in range(NB):
        pieces = [window(group, n * BS) for group in groups]
        by_block[n] = dense(pieces + points[n]).astype(BF16)
    for d, out in enumerate(outs):
        out[...] = by_block[partner(d)]


def ready_kernel(q, *refs):
    hbm, (mat1, mat2, bias, lat, lat_t, own_field, own_table) = refs[:9], refs[9:16]
    counts, assign, w1, w2, b1, table, sems = refs[16:]
    copies = fetch(sems, hbm, (counts, assign, w1, w2, b1, table, lat, lat_t, own_field))
    wait(copies[:6])
    active = counts[assign[lax.axis_index("lat")]]
    rows = table.shape[1] // 2
    mode = mode_numbers((table.shape[0], rows), 1, q)
    for g in range(2):
        part = table[:, g * rows : (g + 1) * rows].astype(F32)
        part = jnp.where(mode < active - g * q, part, 0.0)
        own_table[:, g * rows : (g + 1) * rows] = part.astype(BF16)
    block = lax.axis_index("lat") // 2

    def pick(x):
        value = window(x, 0)
        for n in range(1, NB):
            value = jnp.where(block == n, window(x, n * BS), value)
        lane = lax.broadcasted_iota(jnp.int32, value.shape, 1)
        return jnp.where(lane < BS, value, 0.0)

    gap = jnp.zeros((LANES - BS, 2 * LANES), BF16)
    for source, mat in ((w1, mat1), (w2, mat2)):
        real, imag = (pick(source[c].astype(F32)) for c in range(2))
        mat[0:BS] = jnp.concatenate([real, imag], axis=1).astype(BF16)
        mat[BS:LANES] = gap
        mat[LANES : LANES + BS] = jnp.concatenate([-imag, real], axis=1).astype(BF16)
        mat[LANES + BS : 2 * LANES] = gap
    shift_b = pick(b1[...].astype(F32))
    bias[...] = jnp.concatenate([shift_b[0:1], shift_b[1:2]], axis=1)
    wait(copies[6:])


ORDER = (0, 3, 2, 1)


def join_kernel(*refs):
    for d, ref in zip(ORDER, refs):
        refs[-1][d] = ref[...]


def pack(band):
    rows = band.shape[0]
    tail = rows // 2 + 4
    left, right = band[:, :LANES], pltpu.roll(band[:, LANES:], 96, 1)
    lane = lax.broadcasted_iota(jnp.int32, left.shape, 1)
    upper = jnp.where(lane < 96, left, right)
    lower = pltpu.roll(right[rows - tail :], 64, 1)
    lower = jnp.where(lane[:tail] < 64, right[:tail], lower)
    return jnp.concatenate([upper, lower], axis=0)


def unpack(packed, rows):
    tail = rows // 2 + 4
    upper, lower = packed[:rows], packed[rows:]
    rest = jnp.concatenate([lower, pltpu.roll(lower, 64, 1)[2 * tail - rows :]], axis=0)
    lane = lax.broadcasted_iota(jnp.int32, upper.shape, 1)
    right = jnp.where(lane < 32, pltpu.roll(upper, 32, 1), pltpu.roll(rest, 32, 1))
    return [upper, right]


def silu_points(chunks, mat, bias, by_pair, points, hidden, slope):
    for d, chunk in enumerate(chunks):
        parts = [window(chunk, j * BS) for j in (2, 3)]
        by_pair[partner(d)] = jnp.concatenate(parts, axis=1)
    v = by_pair[...].reshape(points.shape).astype(BF16)
    pre = dot(v, mat[...], (1, 0)) + bias[...]
    sig = jax.nn.sigmoid(pre)
    points[...] = v
    hidden[...] = (pre * sig).astype(BF16)
    slope[...] = sig * (1.0 + pre * (1.0 - sig))


def own_kernel(*refs):
    mat1, bias, points, hidden, slope, by_pair = refs[NB:]
    chunks = [refs[i][...].astype(F32) for i in ORDER]
    silu_points(chunks, mat1, bias, by_pair, points, hidden, slope)


def filter_kernel(*refs):
    owns, (other, slope_own, mat1, mat2, bias, lat, lat_t, assign_hbm) = refs[:4], refs[4:12]
    outs, (points, hidden, grad_pre, grad_y) = refs[12:16], refs[16:20]
    assign, by_lat, by_pair, slope, sems = refs[20:]
    copies = fetch(sems, (assign_hbm,), (assign,))
    core = lax.rem(lax.axis_index("lat"), 2)
    sides = [[owns[i][...].astype(F32) for i in ORDER], [other[d].astype(F32) for d in range(NB)]]
    silu_points(sides[1], mat1, bias, by_pair, points, hidden, slope)
    wait(copies)
    for side, chunks in zip((core, 1 - core), sides):
        for d, chunk in enumerate(chunks):
            groups = [window(chunk, j * BS) for j in range(2)]
            by_lat[assign[2 * partner(d) + side]] = jnp.concatenate(groups, axis=1)
    field = by_lat[...].reshape(lat.shape[1], 2 * LANES).astype(BF16)
    waves = dot(lat[...], field, (1, 0)).astype(BF16)
    rows = waves.shape[0] // 2
    inner = []
    for side, slopes in enumerate((slope_own, slope)):
        dy = []
        for c in range(2):
            part = waves[c * rows : (c + 1) * rows]
            flip = core == 0 if side == 0 else core == 1
            dy.append(jnp.where(flip, part[:, :LANES], part[:, LANES:]))
        dy = jnp.concatenate(dy, axis=1)
        dp = (dot(dy, mat2[...], (1, 1)) * slopes[...]).astype(BF16)
        dv = dot(dp, mat1[...], (1, 1))
        grad_y[side] = dy
        grad_pre[side] = dp
        inner.append(jnp.concatenate([dv[:, :LANES], dv[:, LANES:]], axis=0))
    left = jnp.where(core == 0, inner[0], inner[1])
    right = jnp.where(core == 0, inner[1], inner[0])
    inner = jnp.concatenate([left, right], axis=1).astype(BF16)
    for d, out in enumerate(outs):
        band = dot(lat_t[assign[2 * partner(d) + core]], inner, (1, 0))
        out[...] = pack(band).astype(BF16)


def products_kernel(points0, hidden0, points1, hidden1, grad_pre, grad_y, gw1, gw2, gb1):
    core = lax.rem(lax.axis_index("lat"), 2)
    half = BS // 2
    for ref, grads, values in ((gw1, grad_pre, (points0, points1)), (gw2, grad_y, (hidden0, hidden1))):
        both = dot(grads[0], values[0][...], (0, 0)) + dot(grads[1], values[1][...], (0, 0))
        real = both[:BS, :LANES] + both[LANES : LANES + BS, LANES:]
        imag = both[LANES : LANES + BS, :LANES] - both[:BS, LANES:]
        for c, full in enumerate((real, imag)):
            ref[c] = jnp.where(core == 0, full[:half], full[half:])[:, :BS]
    sums = sum(jnp.sum(grad_pre[side].astype(F32), axis=0, keepdims=True) for side in range(2))
    for c in range(2):
        line = sums[:, c * LANES : (c + 1) * LANES]
        gb1[c : c + 1] = jnp.where(core == 0, line[:, :half], line[:, half:BS])


def compose_kernel(last, four, field, table, out, by_block):
    rows = by_block.shape[1]
    for d in range(NB):
        by_block[partner(d)] = jnp.concatenate(unpack(four[d].astype(F32), rows), axis=1)
    groups = [
        dense([by_block[n, :, g * LANES : (g + 1) * LANES] for n in range(NB)]) for g in range(2)
    ]
    groups = jnp.concatenate(groups, axis=0).astype(BF16)
    mixed = jnp.dot(table[...], groups, preferred_element_type=F32).astype(BF16)
    whole = field[...].astype(F32) + mixed.astype(F32)
    out[...] = jnp.where(lax.axis_index("section") == last, 0.0, whole).astype(BF16)


VMEM = pl.BlockSpec(memory_space=pltpu.VMEM)
HBM = pl.BlockSpec(memory_space=pltpu.HBM)


def call(kernel, outs, scratch, near, far, flops=10**8):
    many = isinstance(outs, tuple)
    many = isinstance(outs, tuple)
    return pl.pallas_call(
        kernel,
        out_shape=outs,
        in_specs=[VMEM] * len(near) + [HBM] * len(far),
        out_specs=tuple([VMEM] * len(outs)) if many else VMEM,
        scratch_shapes=scratch,
        cost_estimate=pl.CostEstimate(flops=flops, bytes_accessed=10**6, transcendentals=0),
        compiler_params=pltpu.CompilerParams(vmem_limit_bytes=32 * 2**20),
    )(*near, *(pltpu.with_memory_space_constraint(x, pltpu.HBM) for x in far))


def scratch_for(*arrays):
    scratch = []
    for x in arrays:
        space = pltpu.SMEM if x.dtype == jnp.int32 else pltpu.VMEM
        scratch.append(space(x.shape, x.dtype))
    return scratch, pltpu.SemaphoreType.DMA((len(arrays),))


def paired_blocks(grad_out, spec_saved, w1, w2, b1, mode_counts, assignment):
    length, width = grad_out.shape[2:]
    n_rows = assignment.shape[0]
    q = spec_saved.shape[3] // (NB * BS)
    rows = 2 * NB * q
    forward, inverse = lon_tables(KM, length)

    def by_group(table):
        table = table.reshape(2, NB, 2, q, length).transpose(2, 0, 1, 3, 4)
        return table.reshape(2 * rows, length).astype(BF16)

    cosine, sine = lat_waves(n_rows)
    waves = np.array([[cosine, sine], [-sine, cosine]])
    lat = np.einsum("eckr,uv->eukrcv", waves, np.eye(NB * q))
    lat = lat.reshape(2 * NB * q * n_rows, n_rows * rows).astype(BF16)
    lat_t = np.ascontiguousarray(lat.T).reshape(n_rows, rows, -1)

    lat, lat_t = jnp.asarray(lat), jnp.asarray(lat_t)
    inverse = jnp.asarray(by_group(inverse))
    forward = jnp.asarray(by_group(forward).T)

    def swap(chunks):
        pairs = [[(i, i ^ (2 * d)) for i in range(2 * NB)] for d in range(NB)]
        return [lax.ppermute(chunks[d], "lat", pairs[d]) if d else chunks[0] for d in ORDER]

    field = grad_out.reshape(length, width)
    shape = jax.ShapeDtypeStruct
    far = (mode_counts, assignment, field, inverse, spec_saved[0])
    scratch, sems = scratch_for(*far)
    sent = call(
        functools.partial(analyse_kernel, q),
        (shape((rows, width), BF16),) * NB,
        scratch + [pltpu.VMEM((NB, rows, width), BF16), sems],
        (),
        far,
    )
    received = swap(sent)
    far = (mode_counts, assignment, w1[0], w2[0], b1[0], forward)
    scratch, _ = scratch_for(*far)
    far = (*far, lat, lat_t, field)
    wide = 2 * LANES
    mat1, mat2, bias, lat, lat_t, field, forward = call(
        functools.partial(ready_kernel, q),
        (
            shape((wide, wide), BF16),
            shape((wide, wide), BF16),
            shape((1, wide), F32),
            shape(lat.shape, BF16),
            shape(lat_t.shape, BF16),
            shape(field.shape, BF16),
            shape(forward.shape, BF16),
        ),
        scratch + [pltpu.SemaphoreType.DMA((len(far),))],
        (),
        far,
        2 * 10**9,
    )
    next_field = turn(field, "section")
    own = call(
        join_kernel,
        shape((NB, rows, width), BF16),
        [],
        (*received, bias),
        (),
    )
    other = lax.ppermute(own, "lat", [(i, i ^ 1) for i in range(2 * NB)])
    vectors = shape((NB * rows, wide), BF16)
    slopes = shape((NB * rows, wide), F32)
    by_pair = pltpu.VMEM((NB, rows, wide), F32)
    points0, hidden0, slope0 = call(
        own_kernel,
        (vectors, vectors, slopes),
        [by_pair],
        (*received, mat1, bias),
        (),
        2 * 10**9,
    )
    packed = shape((rows + rows // 2 + 4, LANES), BF16)
    scratch, sems = scratch_for(assignment)
    both = shape((2, NB * rows, wide), BF16)
    *chunks, points1, hidden1, grad_pre, grad_y = call(
        filter_kernel,
        (packed,) * NB + (vectors, vectors, both, both),
        scratch
        + [
            pltpu.VMEM((n_rows, rows, wide), F32),
            by_pair,
            pltpu.VMEM((NB * rows, wide), F32),
            sems,
        ],
        (*received, other, slope0, mat1, mat2, bias, lat, lat_t),
        (assignment,),
    )
    backs = swap(chunks)
    matrix = shape((2, BS // 2, BS), F32)
    gw1, gw2, gb1 = call(
        products_kernel,
        (matrix, matrix, shape((2, BS // 2), F32)),
        [],
        (points0, hidden0, points1, hidden1, grad_pre, grad_y),
        (),
        2 * 10**9,
    )
    four = turn(call(join_kernel, shape((NB, *packed.shape), BF16), [], backs, ()), "section")
    shifted = call(
        functools.partial(compose_kernel, lax.axis_size("section") - 1),
        shape((length, width), BF16),
        [by_pair],
        (four, next_field, forward),
        (),
    )
    shifted = shifted[None, None]
    return shifted, gw1.swapaxes(1, 2)[None], gw2.swapaxes(1, 2)[None], gb1[None]


def apply_mat(vec, mat):
    return jnp.einsum("kpi,ipj->kpj", vec, mat, preferred_element_type=F32)


def adjoint_mat(vec, mat):
    return jnp.einsum("kpj,ipj->kpi", vec, mat, preferred_element_type=F32)


def outer_sum(left, right):
    return jnp.einsum("kpi,kpj->ipj", left, right, preferred_element_type=F32)


def split_blocks(grad_out, spec_saved, w1, w2, b1, mode_counts, assignment):
    rows_dev = grad_out.shape[1]
    length = grad_out.shape[2]
    width = grad_out.shape[3]
    n_rows = assignment.shape[0]
    pairs_dev = spec_saved.shape[3] // BS
    forward, inverse = (jnp.asarray(t.astype(BF16)) for t in lon_tables(KM, length))
    cosine, sine = (jnp.asarray(t.astype(BF16))[:, assignment] for t in lat_waves(n_rows))
    table = jnp.stack(
        [jnp.stack([cosine, sine], axis=-1), jnp.stack([-sine, cosine], axis=-1)], axis=1
    )
    lat_pos = lax.axis_index("lat")
    lat_count = lax.axis_size("lat")
    own_lat = lax.dynamic_slice_in_dim(assignment, lat_pos * rows_dev, rows_dev)
    active = (jnp.arange(KM, dtype=jnp.int32)[None, :] < mode_counts[own_lat][:, None]).astype(F32)
    cotan = grad_out[0]
    spectral = jnp.einsum(
        "cml,rlni->rcmni",
        inverse,
        cotan.reshape(rows_dev, length, NB, BS),
        preferred_element_type=F32,
    )
    spectral = (spectral * active[:, None, :, None, None]).astype(BF16)
    spectral = spectral.reshape(rows_dev, 2, KM * NB * BS)
    pencil = lax.all_to_all(spectral, "lat", split_axis=2, concat_axis=0, tiled=True)
    pencil = pencil.reshape(n_rows, 2, pairs_dev, BS)
    grad_y = jnp.einsum("kerc,rcpi->kepi", table, pencil, preferred_element_type=F32).astype(BF16)
    saved = spec_saved[0].reshape(n_rows, 2, pairs_dev, BS)
    pair_ids = lat_pos * pairs_dev + jnp.arange(pairs_dev, dtype=jnp.int32)
    owner = (pair_ids % NB)[:, None] == jnp.arange(NB, dtype=jnp.int32)[None, :]
    owner = owner.astype(F32)
    first = jnp.take(w1[0].reshape(2, BS, NB, BS), pair_ids % NB, axis=2)
    second = jnp.take(w2[0].reshape(2, BS, NB, BS), pair_ids % NB, axis=2)
    shift_b = jnp.take(b1[0].reshape(2, NB, BS), pair_ids % NB, axis=1).astype(F32)
    v_r = saved[:, 0]
    v_i = saved[:, 1]
    pre_r = apply_mat(v_r, first[0]) - apply_mat(v_i, first[1]) + shift_b[0][None]
    pre_i = apply_mat(v_i, first[0]) + apply_mat(v_r, first[1]) + shift_b[1][None]
    hid_r = jax.nn.silu(pre_r).astype(BF16)
    hid_i = jax.nn.silu(pre_i).astype(BF16)
    dy_r = grad_y[:, 0]
    dy_i = grad_y[:, 1]
    dh_r = adjoint_mat(dy_r, second[0]) + adjoint_mat(dy_i, second[1])
    dh_i = adjoint_mat(dy_i, second[0]) - adjoint_mat(dy_r, second[1])
    dp_r = (dh_r * silu_slope(pre_r)).astype(BF16)
    dp_i = (dh_i * silu_slope(pre_i)).astype(BF16)
    gw2 = jnp.stack(
        [
            outer_sum(hid_r, dy_r) + outer_sum(hid_i, dy_i),
            outer_sum(hid_r, dy_i) - outer_sum(hid_i, dy_r),
        ]
    )
    gw1 = jnp.stack(
        [outer_sum(v_r, dp_r) + outer_sum(v_i, dp_i), outer_sum(v_r, dp_i) - outer_sum(v_i, dp_r)]
    )
    gb1 = jnp.stack([jnp.sum(dp_r.astype(F32), axis=0), jnp.sum(dp_i.astype(F32), axis=0)])
    dv_r = adjoint_mat(dp_r, first[0]) + adjoint_mat(dp_i, first[1])
    dv_i = adjoint_mat(dp_i, first[0]) - adjoint_mat(dp_r, first[1])
    grad_v = jnp.stack([dv_r, dv_i], axis=1).astype(BF16)
    grad_u = jnp.einsum("kerc,kepi->rcpi", table, grad_v, preferred_element_type=F32).astype(BF16)
    grad_u = grad_u.reshape(n_rows, 2, pairs_dev * BS)
    back = lax.all_to_all(grad_u, "lat", split_axis=0, concat_axis=2, tiled=True)
    back = back.reshape(rows_dev, 2, KM, NB, BS) * active[:, None, :, None, None].astype(BF16)
    mixed = jnp.einsum("cml,rcmni->rlni", forward, back, preferred_element_type=F32)
    mixed = mixed.reshape(rows_dev, length, width).astype(BF16)
    block_w1 = jnp.einsum("pn,cipj->cinj", owner, gw1).reshape(1, 2, BS, width)
    block_w2 = jnp.einsum("pn,cipj->cinj", owner, gw2).reshape(1, 2, BS, width)
    block_b1 = jnp.einsum("pn,cpj->cnj", owner, gb1).reshape(1, 2, width)
    columns = width // lat_count
    full_w1, full_w2, full_b1 = lax.psum((block_w1, block_w2, block_b1), "lat")
    sum_w1 = lax.dynamic_slice_in_dim(full_w1, lat_pos * columns, columns, 3)
    sum_w2 = lax.dynamic_slice_in_dim(full_w2, lat_pos * columns, columns, 3)
    sum_b1 = lax.dynamic_slice_in_dim(full_b1, lat_pos * columns, columns, 2)
    whole = (cotan.astype(F32) + mixed.astype(F32)).astype(BF16)
    received = from_behind(whole[None], "section", -1)
    return (received, sum_w1, sum_w2, sum_b1)


def per_device(grad_out, spec_saved, w1, w2, b1, mode_counts, assignment):
    n_dev = lax.axis_size("lat")
    pairs_dev = spec_saved.shape[3] // BS
    paired = n_dev == 2 * NB and grad_out.shape[1] == 1 and pairs_dev % NB == 0
    body = paired_blocks if paired else split_blocks
    return body(grad_out, spec_saved, w1, w2, b1, mode_counts, assignment)


def solution(mesh):
    return jax.shard_map(
        per_device,
        mesh=mesh,
        in_specs=(
            P("section", "lat", None, None),
            P("section", None, None, "lat"),
            P("section", None, None, None),
            P("section", None, None, None),
            P("section", None, None),
            P(),
            P(),
        ),
        out_specs=(
            P("section", "lat", None, None),
            P("section", None, None, "lat"),
            P("section", None, None, "lat"),
            P("section", None, "lat"),
        ),
        check_vma=False,
    )
```

```python
import functools
import math

import jax
import jax.numpy as jnp
import numpy as np
from jax import lax
from jax.experimental import pallas as pl
from jax.experimental.pallas import tpu as pltpu
from jax.sharding import PartitionSpec as P

NB = 4
BS = 96
KM = 72
LANES = 128
F32 = jnp.float32
BF16 = jnp.bfloat16


def from_behind(value, axis, by):
    length = lax.axis_size(axis)
    pairs = [(i, i + by) for i in range(length) if 0 <= i + by < length]
    return lax.ppermute(value, axis, pairs)


def turn(value, axis):
    length = lax.axis_size(axis)
    return lax.ppermute(value, axis, [(i, (i - 1) % length) for i in range(length)])


def lon_tables(n_modes, length):
    modes = np.arange(n_modes)
    phase = modes[:, None] * np.arange(length)[None, :] % length
    angle = phase * (2.0 * math.pi / length)
    forward = np.stack([np.cos(angle), -np.sin(angle)]) / math.sqrt(length)
    weight = np.where(modes == 0, 1.0, 2.0)[None, :, None]
    return forward, forward * weight


def lat_waves(n_rows):
    freqs = np.arange(n_rows)
    angle = (freqs[:, None] * freqs[None, :] % n_rows) * (2.0 * math.pi / n_rows)
    factor = 1.0 / math.sqrt(n_rows)
    return np.cos(angle) * factor, np.sin(angle) * factor


def silu_slope(pre):
    sig = jax.nn.sigmoid(pre)
    return sig * (1.0 + pre * (1.0 - sig))


def window(x, start):
    low = start // LANES * LANES
    shift = start - low
    if shift == 0:
        return x[:, low : low + LANES]
    if shift + BS <= LANES:
        return pltpu.roll(x[:, low : low + LANES], LANES - shift, 1)
    return pltpu.roll(x[:, low : low + 2 * LANES], 2 * LANES - shift, 1)[:, :LANES]


def dense(parts):
    lane = lax.broadcasted_iota(jnp.int32, parts[0].shape, 1)
    first = pltpu.roll(parts[1], 96, 1)
    second = pltpu.roll(parts[2], 64, 1)
    third = pltpu.roll(parts[3], 32, 1)
    return jnp.concatenate(
        [
            jnp.where(lane < 96, parts[0], first),
            jnp.where(lane < 64, first, second),
            jnp.where(lane < 32, second, third),
        ],
        axis=1,
    )


def dot(a, b, contract):
    return lax.dot_general(a, b, ((contract[:1], contract[1:]), ((), ())), preferred_element_type=F32)


def mode_numbers(shape, axis, q):
    number = lax.broadcasted_iota(jnp.int32, shape, axis)
    number = jnp.where(number >= NB * q, number - NB * q, number)
    mode = number
    for z in range(1, NB):
        mode = jnp.where(number >= z * q, number + z * q, mode)
    return mode


def fetch(sems, sources, targets):
    copies = [
        pltpu.make_async_copy(source, target, sems.at[i])
        for i, (source, target) in enumerate(zip(sources, targets))
    ]
    for copy in copies:
        copy.start()
    return copies


def wait(copies):
    for copy in copies:
        copy.wait()


def partner(d):
    return jnp.bitwise_xor(lax.axis_index("lat") // 2, d)


def analyse_kernel(q, *refs):
    hbm, outs, held, (by_block, sems) = refs[:5], refs[5:9], refs[9:14], refs[14:]
    counts, assign, field, table, saved = held
    copies = fetch(sems, hbm, held)
    wait(copies[4:])
    parts = [saved[:, c, :].astype(F32) for c in range(2)]
    points = [
        [
            jnp.concatenate([window(part, (mm * NB + n) * BS) for mm in range(q)], axis=0)
            for part in parts
        ]
        for n in range(NB)
    ]
    wait(copies[:4])
    rows = by_block.shape[1]
    spectral = jnp.dot(table[...], field[...], preferred_element_type=F32)
    active = counts[assign[lax.axis_index("lat")]]
    mode = mode_numbers((rows, spectral.shape[1]), 0, q)
    groups = [
        jnp.where(mode < active - g * q, spectral[g * rows : (g + 1) * rows], 0.0)
        for g in range(2)
    ]
    for n in range(NB):
        pieces = [window(group, n * BS) for group in groups]
        by_block[n] = dense(pieces + points[n]).astype(BF16)
    for d, out in enumerate(outs):
        out[...] = by_block[partner(d)]


def ready_kernel(q, *refs):
    hbm, (mat1, mat2, bias, lat, lat_t, own_field, own_table) = refs[:9], refs[9:16]
    counts, assign, w1, w2, b1, table, sems = refs[16:]
    copies = fetch(sems, hbm, (counts, assign, w1, w2, b1, table, lat, lat_t, own_field))
    wait(copies[:6])
    active = counts[assign[lax.axis_index("lat")]]
    rows = table.shape[1] // 2
    mode = mode_numbers((table.shape[0], rows), 1, q)
    for g in range(2):
        part = table[:, g * rows : (g + 1) * rows].astype(F32)
        part = jnp.where(mode < active - g * q, part, 0.0)
        own_table[:, g * rows : (g + 1) * rows] = part.astype(BF16)
    block = lax.axis_index("lat") // 2

    def pick(x):
        value = window(x, 0)
        for n in range(1, NB):
            value = jnp.where(block == n, window(x, n * BS), value)
        lane = lax.broadcasted_iota(jnp.int32, value.shape, 1)
        return jnp.where(lane < BS, value, 0.0)

    gap = jnp.zeros((LANES - BS, 2 * LANES), BF16)
    for source, mat in ((w1, mat1), (w2, mat2)):
        real, imag = (pick(source[c].astype(F32)) for c in range(2))
        mat[0:BS] = jnp.concatenate([real, imag], axis=1).astype(BF16)
        mat[BS:LANES] = gap
        mat[LANES : LANES + BS] = jnp.concatenate([-imag, real], axis=1).astype(BF16)
        mat[LANES + BS : 2 * LANES] = gap
    shift_b = pick(b1[...].astype(F32))
    bias[...] = jnp.concatenate([shift_b[0:1], shift_b[1:2]], axis=1)
    wait(copies[6:])


ORDER = (0, 3, 2, 1)


def join_kernel(*refs):
    for d, ref in zip(ORDER, refs):
        refs[-1][d] = ref[...]


def pack(band):
    rows = band.shape[0]
    tail = rows // 2 + 4
    left, right = band[:, :LANES], pltpu.roll(band[:, LANES:], 96, 1)
    lane = lax.broadcasted_iota(jnp.int32, left.shape, 1)
    upper = jnp.where(lane < 96, left, right)
    lower = pltpu.roll(right[rows - tail :], 64, 1)
    lower = jnp.where(lane[:tail] < 64, right[:tail], lower)
    return jnp.concatenate([upper, lower], axis=0)


def unpack(packed, rows):
    tail = rows // 2 + 4
    upper, lower = packed[:rows], packed[rows:]
    rest = jnp.concatenate([lower, pltpu.roll(lower, 64, 1)[2 * tail - rows :]], axis=0)
    lane = lax.broadcasted_iota(jnp.int32, upper.shape, 1)
    right = jnp.where(lane < 32, pltpu.roll(upper, 32, 1), pltpu.roll(rest, 32, 1))
    return [upper, right]


def silu_points(chunks, mat, bias, by_pair, points, hidden, slope):
    for d, chunk in enumerate(chunks):
        parts = [window(chunk, j * BS) for j in (2, 3)]
        by_pair[partner(d)] = jnp.concatenate(parts, axis=1)
    v = by_pair[...].reshape(points.shape).astype(BF16)
    pre = dot(v, mat[...], (1, 0)) + bias[...]
    sig = jax.nn.sigmoid(pre)
    points[...] = v
    hidden[...] = (pre * sig).astype(BF16)
    slope[...] = sig * (1.0 + pre * (1.0 - sig))


def own_kernel(*refs):
    mat1, bias, points, hidden, slope, by_pair = refs[NB:]
    chunks = [refs[i][...].astype(F32) for i in ORDER]
    silu_points(chunks, mat1, bias, by_pair, points, hidden, slope)


def filter_kernel(*refs):
    owns, (other, slope_own, mat1, mat2, bias, lat, lat_t, assign_hbm) = refs[:4], refs[4:12]
    outs, (points, hidden, grad_pre, grad_y) = refs[12:16], refs[16:20]
    assign, by_lat, by_pair, slope, sems = refs[20:]
    copies = fetch(sems, (assign_hbm,), (assign,))
    core = lax.rem(lax.axis_index("lat"), 2)
    sides = [[owns[i][...].astype(F32) for i in ORDER], [other[d].astype(F32) for d in range(NB)]]
    silu_points(sides[1], mat1, bias, by_pair, points, hidden, slope)
    wait(copies)
    for side, chunks in zip((core, 1 - core), sides):
        for d, chunk in enumerate(chunks):
            groups = [window(chunk, j * BS) for j in range(2)]
            by_lat[assign[2 * partner(d) + side]] = jnp.concatenate(groups, axis=1)
    field = by_lat[...].reshape(lat.shape[1], 2 * LANES).astype(BF16)
    waves = dot(lat[...], field, (1, 0)).astype(BF16)
    rows = waves.shape[0] // 2
    inner = []
    for side, slopes in enumerate((slope_own, slope)):
        dy = []
        for c in range(2):
            part = waves[c * rows : (c + 1) * rows]
            flip = core == 0 if side == 0 else core == 1
            dy.append(jnp.where(flip, part[:, :LANES], part[:, LANES:]))
        dy = jnp.concatenate(dy, axis=1)
        dp = (dot(dy, mat2[...], (1, 1)) * slopes[...]).astype(BF16)
        dv = dot(dp, mat1[...], (1, 1))
        grad_y[side] = dy
        grad_pre[side] = dp
        inner.append(jnp.concatenate([dv[:, :LANES], dv[:, LANES:]], axis=0))
    left = jnp.where(core == 0, inner[0], inner[1])
    right = jnp.where(core == 0, inner[1], inner[0])
    inner = jnp.concatenate([left, right], axis=1).astype(BF16)
    for d, out in enumerate(outs):
        band = dot(lat_t[assign[2 * partner(d) + core]], inner, (1, 0))
        out[...] = pack(band).astype(BF16)


def products_kernel(points0, hidden0, points1, hidden1, grad_pre, grad_y, _, gw1, gw2, gb1):
    core = lax.rem(lax.axis_index("lat"), 2)
    half = BS // 2
    for ref, grads, values in ((gw1, grad_pre, (points0, points1)), (gw2, grad_y, (hidden0, hidden1))):
        both = dot(grads[0], values[0][...], (0, 0)) + dot(grads[1], values[1][...], (0, 0))
        real = both[:BS, :LANES] + both[LANES : LANES + BS, LANES:]
        imag = both[LANES : LANES + BS, :LANES] - both[:BS, LANES:]
        for c, full in enumerate((real, imag)):
            ref[c] = jnp.where(core == 0, full[:half], full[half:])[:, :BS]
    sums = sum(jnp.sum(grad_pre[side].astype(F32), axis=0, keepdims=True) for side in range(2))
    for c in range(2):
        line = sums[:, c * LANES : (c + 1) * LANES]
        gb1[c : c + 1] = jnp.where(core == 0, line[:, :half], line[:, half:BS])


def compose_kernel(last, four, field, table, out, by_block):
    rows = by_block.shape[1]
    for d in range(NB):
        by_block[partner(d)] = jnp.concatenate(unpack(four[d].astype(F32), rows), axis=1)
    groups = [
        dense([by_block[n, :, g * LANES : (g + 1) * LANES] for n in range(NB)]) for g in range(2)
    ]
    groups = jnp.concatenate(groups, axis=0).astype(BF16)
    mixed = jnp.dot(table[...], groups, preferred_element_type=F32).astype(BF16)
    whole = field[...].astype(F32) + mixed.astype(F32)
    out[...] = jnp.where(lax.axis_index("section") == last, 0.0, whole).astype(BF16)


VMEM = pl.BlockSpec(memory_space=pltpu.VMEM)
HBM = pl.BlockSpec(memory_space=pltpu.HBM)


def call(kernel, outs, scratch, near, far, flops=10**8):
    many = isinstance(outs, tuple)
    many = isinstance(outs, tuple)
    return pl.pallas_call(
        kernel,
        out_shape=outs,
        in_specs=[VMEM] * len(near) + [HBM] * len(far),
        out_specs=tuple([VMEM] * len(outs)) if many else VMEM,
        scratch_shapes=scratch,
        cost_estimate=pl.CostEstimate(flops=flops, bytes_accessed=10**6, transcendentals=0),
        compiler_params=pltpu.CompilerParams(vmem_limit_bytes=32 * 2**20),
    )(*near, *(pltpu.with_memory_space_constraint(x, pltpu.HBM) for x in far))


def scratch_for(*arrays):
    scratch = []
    for x in arrays:
        space = pltpu.SMEM if x.dtype == jnp.int32 else pltpu.VMEM
        scratch.append(space(x.shape, x.dtype))
    return scratch, pltpu.SemaphoreType.DMA((len(arrays),))


def paired_blocks(grad_out, spec_saved, w1, w2, b1, mode_counts, assignment):
    length, width = grad_out.shape[2:]
    n_rows = assignment.shape[0]
    q = spec_saved.shape[3] // (NB * BS)
    rows = 2 * NB * q
    forward, inverse = lon_tables(KM, length)

    def by_group(table):
        table = table.reshape(2, NB, 2, q, length).transpose(2, 0, 1, 3, 4)
        return table.reshape(2 * rows, length).astype(BF16)

    cosine, sine = lat_waves(n_rows)
    waves = np.array([[cosine, sine], [-sine, cosine]])
    lat = np.einsum("eckr,uv->eukrcv", waves, np.eye(NB * q))
    lat = lat.reshape(2 * NB * q * n_rows, n_rows * rows).astype(BF16)
    lat_t = np.ascontiguousarray(lat.T).reshape(n_rows, rows, -1)

    lat, lat_t = jnp.asarray(lat), jnp.asarray(lat_t)
    inverse = jnp.asarray(by_group(inverse))
    forward = jnp.asarray(by_group(forward).T)

    def swap(chunks):
        pairs = [[(i, i ^ (2 * d)) for i in range(2 * NB)] for d in range(NB)]
        return [lax.ppermute(chunks[d], "lat", pairs[d]) if d else chunks[0] for d in ORDER]

    field = grad_out.reshape(length, width)
    shape = jax.ShapeDtypeStruct
    far = (mode_counts, assignment, field, inverse, spec_saved[0])
    scratch, sems = scratch_for(*far)
    sent = call(
        functools.partial(analyse_kernel, q),
        (shape((rows, width), BF16),) * NB,
        scratch + [pltpu.VMEM((NB, rows, width), BF16), sems],
        (),
        far,
    )
    received = swap(sent)
    far = (mode_counts, assignment, w1[0], w2[0], b1[0], forward)
    scratch, _ = scratch_for(*far)
    far = (*far, lat, lat_t, field)
    wide = 2 * LANES
    mat1, mat2, bias, lat, lat_t, field, forward = call(
        functools.partial(ready_kernel, q),
        (
            shape((wide, wide), BF16),
            shape((wide, wide), BF16),
            shape((1, wide), F32),
            shape(lat.shape, BF16),
            shape(lat_t.shape, BF16),
            shape(field.shape, BF16),
            shape(forward.shape, BF16),
        ),
        scratch + [pltpu.SemaphoreType.DMA((len(far),))],
        (),
        far,
        2 * 10**9,
    )
    next_field = turn(field, "section")
    own = call(
        join_kernel,
        shape((NB, rows, width), BF16),
        [],
        (*received, bias),
        (),
    )
    other = lax.ppermute(own, "lat", [(i, i ^ 1) for i in range(2 * NB)])
    vectors = shape((NB * rows, wide), BF16)
    slopes = shape((NB * rows, wide), F32)
    by_pair = pltpu.VMEM((NB, rows, wide), F32)
    points0, hidden0, slope0 = call(
        own_kernel,
        (vectors, vectors, slopes),
        [by_pair],
        (*received, mat1, bias),
        (),
        2 * 10**9,
    )
    packed = shape((rows + rows // 2 + 4, LANES), BF16)
    scratch, sems = scratch_for(assignment)
    both = shape((2, NB * rows, wide), BF16)
    *chunks, points1, hidden1, grad_pre, grad_y = call(
        filter_kernel,
        (packed,) * NB + (vectors, vectors, both, both),
        scratch
        + [
            pltpu.VMEM((n_rows, rows, wide), F32),
            by_pair,
            pltpu.VMEM((NB * rows, wide), F32),
            sems,
        ],
        (*received, other, slope0, mat1, mat2, bias, lat, lat_t),
        (assignment,),
    )
    backs = swap(chunks)
    matrix = shape((2, BS // 2, BS), F32)
    gw1, gw2, gb1 = call(
        products_kernel,
        (matrix, matrix, shape((2, BS // 2), F32)),
        [],
        (points0, hidden0, points1, hidden1, grad_pre, grad_y, next_field),
        (),
        2 * 10**9,
    )
    four = call(join_kernel, shape((NB, *packed.shape), BF16), [], (*backs, gb1), ())
    four = turn(four, "section")
    shifted = call(
        functools.partial(compose_kernel, lax.axis_size("section") - 1),
        shape((length, width), BF16),
        [by_pair],
        (four, next_field, forward),
        (),
    )
    shifted = shifted[None, None]
    return shifted, gw1.swapaxes(1, 2)[None], gw2.swapaxes(1, 2)[None], gb1[None]


def apply_mat(vec, mat):
    return jnp.einsum("kpi,ipj->kpj", vec, mat, preferred_element_type=F32)


def adjoint_mat(vec, mat):
    return jnp.einsum("kpj,ipj->kpi", vec, mat, preferred_element_type=F32)


def outer_sum(left, right):
    return jnp.einsum("kpi,kpj->ipj", left, right, preferred_element_type=F32)


def split_blocks(grad_out, spec_saved, w1, w2, b1, mode_counts, assignment):
    rows_dev = grad_out.shape[1]
    length = grad_out.shape[2]
    width = grad_out.shape[3]
    n_rows = assignment.shape[0]
    pairs_dev = spec_saved.shape[3] // BS
    forward, inverse = (jnp.asarray(t.astype(BF16)) for t in lon_tables(KM, length))
    cosine, sine = (jnp.asarray(t.astype(BF16))[:, assignment] for t in lat_waves(n_rows))
    table = jnp.stack(
        [jnp.stack([cosine, sine], axis=-1), jnp.stack([-sine, cosine], axis=-1)], axis=1
    )
    lat_pos = lax.axis_index("lat")
    lat_count = lax.axis_size("lat")
    own_lat = lax.dynamic_slice_in_dim(assignment, lat_pos * rows_dev, rows_dev)
    active = (jnp.arange(KM, dtype=jnp.int32)[None, :] < mode_counts[own_lat][:, None]).astype(F32)
    cotan = grad_out[0]
    spectral = jnp.einsum(
        "cml,rlni->rcmni",
        inverse,
        cotan.reshape(rows_dev, length, NB, BS),
        preferred_element_type=F32,
    )
    spectral = (spectral * active[:, None, :, None, None]).astype(BF16)
    spectral = spectral.reshape(rows_dev, 2, KM * NB * BS)
    pencil = lax.all_to_all(spectral, "lat", split_axis=2, concat_axis=0, tiled=True)
    pencil = pencil.reshape(n_rows, 2, pairs_dev, BS)
    grad_y = jnp.einsum("kerc,rcpi->kepi", table, pencil, preferred_element_type=F32).astype(BF16)
    saved = spec_saved[0].reshape(n_rows, 2, pairs_dev, BS)
    pair_ids = lat_pos * pairs_dev + jnp.arange(pairs_dev, dtype=jnp.int32)
    owner = (pair_ids % NB)[:, None] == jnp.arange(NB, dtype=jnp.int32)[None, :]
    owner = owner.astype(F32)
    first = jnp.take(w1[0].reshape(2, BS, NB, BS), pair_ids % NB, axis=2)
    second = jnp.take(w2[0].reshape(2, BS, NB, BS), pair_ids % NB, axis=2)
    shift_b = jnp.take(b1[0].reshape(2, NB, BS), pair_ids % NB, axis=1).astype(F32)
    v_r = saved[:, 0]
    v_i = saved[:, 1]
    pre_r = apply_mat(v_r, first[0]) - apply_mat(v_i, first[1]) + shift_b[0][None]
    pre_i = apply_mat(v_i, first[0]) + apply_mat(v_r, first[1]) + shift_b[1][None]
    hid_r = jax.nn.silu(pre_r).astype(BF16)
    hid_i = jax.nn.silu(pre_i).astype(BF16)
    dy_r = grad_y[:, 0]
    dy_i = grad_y[:, 1]
    dh_r = adjoint_mat(dy_r, second[0]) + adjoint_mat(dy_i, second[1])
    dh_i = adjoint_mat(dy_i, second[0]) - adjoint_mat(dy_r, second[1])
    dp_r = (dh_r * silu_slope(pre_r)).astype(BF16)
    dp_i = (dh_i * silu_slope(pre_i)).astype(BF16)
    gw2 = jnp.stack(
        [
            outer_sum(hid_r, dy_r) + outer_sum(hid_i, dy_i),
            outer_sum(hid_r, dy_i) - outer_sum(hid_i, dy_r),
        ]
    )
    gw1 = jnp.stack(
        [outer_sum(v_r, dp_r) + outer_sum(v_i, dp_i), outer_sum(v_r, dp_i) - outer_sum(v_i, dp_r)]
    )
    gb1 = jnp.stack([jnp.sum(dp_r.astype(F32), axis=0), jnp.sum(dp_i.astype(F32), axis=0)])
    dv_r = adjoint_mat(dp_r, first[0]) + adjoint_mat(dp_i, first[1])
    dv_i = adjoint_mat(dp_i, first[0]) - adjoint_mat(dp_r, first[1])
    grad_v = jnp.stack([dv_r, dv_i], axis=1).astype(BF16)
    grad_u = jnp.einsum("kerc,kepi->rcpi", table, grad_v, preferred_element_type=F32).astype(BF16)
    grad_u = grad_u.reshape(n_rows, 2, pairs_dev * BS)
    back = lax.all_to_all(grad_u, "lat", split_axis=0, concat_axis=2, tiled=True)
    back = back.reshape(rows_dev, 2, KM, NB, BS) * active[:, None, :, None, None].astype(BF16)
    mixed = jnp.einsum("cml,rcmni->rlni", forward, back, preferred_element_type=F32)
    mixed = mixed.reshape(rows_dev, length, width).astype(BF16)
    block_w1 = jnp.einsum("pn,cipj->cinj", owner, gw1).reshape(1, 2, BS, width)
    block_w2 = jnp.einsum("pn,cipj->cinj", owner, gw2).reshape(1, 2, BS, width)
    block_b1 = jnp.einsum("pn,cpj->cnj", owner, gb1).reshape(1, 2, width)
    columns = width // lat_count
    full_w1, full_w2, full_b1 = lax.psum((block_w1, block_w2, block_b1), "lat")
    sum_w1 = lax.dynamic_slice_in_dim(full_w1, lat_pos * columns, columns, 3)
    sum_w2 = lax.dynamic_slice_in_dim(full_w2, lat_pos * columns, columns, 3)
    sum_b1 = lax.dynamic_slice_in_dim(full_b1, lat_pos * columns, columns, 2)
    whole = (cotan.astype(F32) + mixed.astype(F32)).astype(BF16)
    received = from_behind(whole[None], "section", -1)
    return (received, sum_w1, sum_w2, sum_b1)


def per_device(grad_out, spec_saved, w1, w2, b1, mode_counts, assignment):
    n_dev = lax.axis_size("lat")
    pairs_dev = spec_saved.shape[3] // BS
    paired = n_dev == 2 * NB and grad_out.shape[1] == 1 and pairs_dev % NB == 0
    body = paired_blocks if paired else split_blocks
    return body(grad_out, spec_saved, w1, w2, b1, mode_counts, assignment)


def solution(mesh):
    return jax.shard_map(
        per_device,
        mesh=mesh,
        in_specs=(
            P("section", "lat", None, None),
            P("section", None, None, "lat"),
            P("section", None, None, None),
            P("section", None, None, None),
            P("section", None, None),
            P(),
            P(),
        ),
        out_specs=(
            P("section", "lat", None, None),
            P("section", None, None, "lat"),
            P("section", None, None, "lat"),
            P("section", None, "lat"),
        ),
        check_vma=False,
    )
```

```python
import functools
import math

import jax
import jax.numpy as jnp
import numpy as np
from jax import lax
from jax.experimental import pallas as pl
from jax.experimental.pallas import tpu as pltpu
from jax.sharding import PartitionSpec as P

NB = 4
BS = 96
KM = 72
LANES = 128
F32 = jnp.float32
BF16 = jnp.bfloat16


def from_behind(value, axis, by):
    length = lax.axis_size(axis)
    pairs = [(i, i + by) for i in range(length) if 0 <= i + by < length]
    return lax.ppermute(value, axis, pairs)


def turn(value, axis):
    length = lax.axis_size(axis)
    return lax.ppermute(value, axis, [(i, (i - 1) % length) for i in range(length)])


def lon_tables(n_modes, length):
    modes = np.arange(n_modes)
    phase = modes[:, None] * np.arange(length)[None, :] % length
    angle = phase * (2.0 * math.pi / length)
    forward = np.stack([np.cos(angle), -np.sin(angle)]) / math.sqrt(length)
    weight = np.where(modes == 0, 1.0, 2.0)[None, :, None]
    return forward, forward * weight


def lat_waves(n_rows):
    freqs = np.arange(n_rows)
    angle = (freqs[:, None] * freqs[None, :] % n_rows) * (2.0 * math.pi / n_rows)
    factor = 1.0 / math.sqrt(n_rows)
    return np.cos(angle) * factor, np.sin(angle) * factor


def silu_slope(pre):
    sig = jax.nn.sigmoid(pre)
    return sig * (1.0 + pre * (1.0 - sig))


def window(x, start):
    low = start // LANES * LANES
    shift = start - low
    if shift == 0:
        return x[:, low : low + LANES]
    if shift + BS <= LANES:
        return pltpu.roll(x[:, low : low + LANES], LANES - shift, 1)
    return pltpu.roll(x[:, low : low + 2 * LANES], 2 * LANES - shift, 1)[:, :LANES]


def dense(parts):
    lane = lax.broadcasted_iota(jnp.int32, parts[0].shape, 1)
    first = pltpu.roll(parts[1], 96, 1)
    second = pltpu.roll(parts[2], 64, 1)
    third = pltpu.roll(parts[3], 32, 1)
    return jnp.concatenate(
        [
            jnp.where(lane < 96, parts[0], first),
            jnp.where(lane < 64, first, second),
            jnp.where(lane < 32, second, third),
        ],
        axis=1,
    )


def dot(a, b, contract):
    return lax.dot_general(a, b, ((contract[:1], contract[1:]), ((), ())), preferred_element_type=F32)


def mode_numbers(shape, axis, q):
    number = lax.broadcasted_iota(jnp.int32, shape, axis)
    number = jnp.where(number >= NB * q, number - NB * q, number)
    mode = number
    for z in range(1, NB):
        mode = jnp.where(number >= z * q, number + z * q, mode)
    return mode


def fetch(sems, sources, targets):
    copies = [
        pltpu.make_async_copy(source, target, sems.at[i])
        for i, (source, target) in enumerate(zip(sources, targets))
    ]
    for copy in copies:
        copy.start()
    return copies


def wait(copies):
    for copy in copies:
        copy.wait()


def partner(d):
    return jnp.bitwise_xor(lax.axis_index("lat") // 2, d)


def analyse_kernel(q, *refs):
    hbm, outs, held, (by_block, sems) = refs[:5], refs[5:9], refs[9:14], refs[14:]
    counts, assign, field, table, saved = held
    copies = fetch(sems, hbm, held)
    wait(copies[4:])
    parts = [saved[:, c, :].astype(F32) for c in range(2)]
    points = [
        [
            jnp.concatenate([window(part, (mm * NB + n) * BS) for mm in range(q)], axis=0)
            for part in parts
        ]
        for n in range(NB)
    ]
    wait(copies[:4])
    rows = by_block.shape[1]
    spectral = jnp.dot(table[...], field[...], preferred_element_type=F32)
    active = counts[assign[lax.axis_index("lat")]]
    mode = mode_numbers((rows, spectral.shape[1]), 0, q)
    groups = [
        jnp.where(mode < active - g * q, spectral[g * rows : (g + 1) * rows], 0.0)
        for g in range(2)
    ]
    for n in range(NB):
        pieces = [window(group, n * BS) for group in groups]
        by_block[n] = dense(pieces + points[n]).astype(BF16)
    for d, out in enumerate(outs):
        out[...] = by_block[partner(d)]


def ready_kernel(q, *refs):
    hbm, (mat1, mat2, bias, lat, lat_t, own_field, own_table) = refs[:9], refs[9:16]
    counts, assign, w1, w2, b1, table, sems = refs[16:]
    copies = fetch(sems, hbm, (counts, assign, w1, w2, b1, table, lat, lat_t, own_field))
    wait(copies[:6])
    active = counts[assign[lax.axis_index("lat")]]
    rows = table.shape[1] // 2
    mode = mode_numbers((table.shape[0], rows), 1, q)
    for g in range(2):
        part = table[:, g * rows : (g + 1) * rows].astype(F32)
        part = jnp.where(mode < active - g * q, part, 0.0)
        own_table[:, g * rows : (g + 1) * rows] = part.astype(BF16)
    block = lax.axis_index("lat") // 2

    def pick(x):
        value = window(x, 0)
        for n in range(1, NB):
            value = jnp.where(block == n, window(x, n * BS), value)
        lane = lax.broadcasted_iota(jnp.int32, value.shape, 1)
        return jnp.where(lane < BS, value, 0.0)

    gap = jnp.zeros((LANES - BS, 2 * LANES), BF16)
    for source, mat in ((w1, mat1), (w2, mat2)):
        real, imag = (pick(source[c].astype(F32)) for c in range(2))
        mat[0:BS] = jnp.concatenate([real, imag], axis=1).astype(BF16)
        mat[BS:LANES] = gap
        mat[LANES : LANES + BS] = jnp.concatenate([-imag, real], axis=1).astype(BF16)
        mat[LANES + BS : 2 * LANES] = gap
    shift_b = pick(b1[...].astype(F32))
    bias[...] = jnp.concatenate([shift_b[0:1], shift_b[1:2]], axis=1)
    wait(copies[6:])


ORDER = (0, 3, 2, 1)
FIELD_ROWS = 192


def join_kernel(*refs):
    out = refs[-1]
    for i in range(out.shape[0]):
        out[i] = refs[i][...]


def pack(band):
    rows = band.shape[0]
    tail = rows // 2 + 4
    left, right = band[:, :LANES], pltpu.roll(band[:, LANES:], 96, 1)
    lane = lax.broadcasted_iota(jnp.int32, left.shape, 1)
    upper = jnp.where(lane < 96, left, right)
    lower = pltpu.roll(right[rows - tail :], 64, 1)
    lower = jnp.where(lane[:tail] < 64, right[:tail], lower)
    return jnp.concatenate([upper, lower], axis=0)


def unpack(packed, rows):
    tail = rows // 2 + 4
    upper, lower = packed[:rows], packed[rows:]
    rest = jnp.concatenate([lower, pltpu.roll(lower, 64, 1)[2 * tail - rows :]], axis=0)
    lane = lax.broadcasted_iota(jnp.int32, upper.shape, 1)
    right = jnp.where(lane < 32, pltpu.roll(upper, 32, 1), pltpu.roll(rest, 32, 1))
    return [upper, right]


def silu_points(chunks, mat, bias, by_pair, points, hidden, slope):
    for d, chunk in enumerate(chunks):
        parts = [window(chunk, j * BS) for j in (2, 3)]
        by_pair[partner(d)] = jnp.concatenate(parts, axis=1)
    v = by_pair[...].reshape(points.shape).astype(BF16)
    pre = dot(v, mat[...], (1, 0)) + bias[...]
    sig = jax.nn.sigmoid(pre)
    points[...] = v
    hidden[...] = (pre * sig).astype(BF16)
    slope[...] = sig * (1.0 + pre * (1.0 - sig))


def own_kernel(*refs):
    mat1, bias, points, hidden, slope, by_pair = refs[NB:]
    chunks = [refs[i][...].astype(F32) for i in ORDER]
    silu_points(chunks, mat1, bias, by_pair, points, hidden, slope)


def filter_kernel(*refs):
    owns, (other, slope_own, mat1, mat2, bias, lat, lat_t, own_field, assign_hbm) = refs[:4], refs[4:13]
    outs, (bundle, points, hidden, grad_pre, grad_y) = refs[13:16], refs[16:21]
    assign, by_lat, by_pair, slope, sems = refs[21:]
    copies = fetch(sems, (assign_hbm,), (assign,))
    core = lax.rem(lax.axis_index("lat"), 2)
    sides = [[owns[i][...].astype(F32) for i in ORDER], [other[i].astype(F32) for i in ORDER]]
    silu_points(sides[1], mat1, bias, by_pair, points, hidden, slope)
    wait(copies)
    for side, chunks in zip((core, 1 - core), sides):
        for d, chunk in enumerate(chunks):
            groups = [window(chunk, j * BS) for j in range(2)]
            by_lat[assign[2 * partner(d) + side]] = jnp.concatenate(groups, axis=1)
    field = by_lat[...].reshape(lat.shape[1], 2 * LANES).astype(BF16)
    waves = dot(lat[...], field, (1, 0)).astype(BF16)
    rows = waves.shape[0] // 2
    inner = []
    for side, slopes in enumerate((slope_own, slope)):
        dy = []
        for c in range(2):
            part = waves[c * rows : (c + 1) * rows]
            flip = core == 0 if side == 0 else core == 1
            dy.append(jnp.where(flip, part[:, :LANES], part[:, LANES:]))
        dy = jnp.concatenate(dy, axis=1)
        dp = (dot(dy, mat2[...], (1, 1)) * slopes[...]).astype(BF16)
        dv = dot(dp, mat1[...], (1, 1))
        grad_y[side] = dy
        grad_pre[side] = dp
        inner.append(jnp.concatenate([dv[:, :LANES], dv[:, LANES:]], axis=0))
    left = jnp.where(core == 0, inner[0], inner[1])
    right = jnp.where(core == 0, inner[1], inner[0])
    inner = jnp.concatenate([left, right], axis=1).astype(BF16)
    length = own_field.shape[0]
    bundle[0:length] = own_field[...]
    for i, d in enumerate(ORDER):
        band = pack(dot(lat_t[assign[2 * partner(d) + core]], inner, (1, 0)))
        if d:
            outs[i - 1][...] = band.astype(BF16)
        else:
            rows = bundle.shape[0] - FIELD_ROWS
            band = jnp.concatenate([band, jnp.zeros((3 * rows - band.shape[0], LANES), F32)], axis=0)
            band = [band[i * rows : (i + 1) * rows] for i in range(3)]
            bundle[FIELD_ROWS:] = jnp.concatenate(band, axis=1).astype(BF16)


def products_kernel(points0, hidden0, points1, hidden1, grad_pre, grad_y, gw1, gw2, gb1):
    core = lax.rem(lax.axis_index("lat"), 2)
    half = BS // 2
    for ref, grads, values in ((gw1, grad_pre, (points0, points1)), (gw2, grad_y, (hidden0, hidden1))):
        both = dot(grads[0], values[0][...], (0, 0)) + dot(grads[1], values[1][...], (0, 0))
        real = both[:BS, :LANES] + both[LANES : LANES + BS, LANES:]
        imag = both[LANES : LANES + BS, :LANES] - both[:BS, LANES:]
        for c, full in enumerate((real, imag)):
            ref[c] = jnp.where(core == 0, full[:half], full[half:])[:, :BS]
    sums = sum(jnp.sum(grad_pre[side].astype(F32), axis=0, keepdims=True) for side in range(2))
    for c in range(2):
        line = sums[:, c * LANES : (c + 1) * LANES]
        gb1[c : c + 1] = jnp.where(core == 0, line[:, :half], line[:, half:BS])


def compose_kernel(last, three, bundle, table, out, by_block):
    rows = by_block.shape[1]
    own = bundle[FIELD_ROWS:].astype(F32)
    own = jnp.concatenate([own[:, i * LANES : (i + 1) * LANES] for i in range(3)], axis=0)
    chunks = [own[: three.shape[1]]] + [three[i].astype(F32) for i in range(3)]
    for d, chunk in zip(ORDER, chunks):
        by_block[partner(d)] = jnp.concatenate(unpack(chunk, rows), axis=1)
    groups = [
        dense([by_block[n, :, g * LANES : (g + 1) * LANES] for n in range(NB)]) for g in range(2)
    ]
    groups = jnp.concatenate(groups, axis=0).astype(BF16)
    mixed = jnp.dot(table[...], groups, preferred_element_type=F32).astype(BF16)
    whole = bundle[0 : out.shape[0]].astype(F32) + mixed.astype(F32)
    out[...] = jnp.where(lax.axis_index("section") == last, 0.0, whole).astype(BF16)


VMEM = pl.BlockSpec(memory_space=pltpu.VMEM)
HBM = pl.BlockSpec(memory_space=pltpu.HBM)


def call(kernel, outs, scratch, near, far, flops=10**8):
    many = isinstance(outs, tuple)
    many = isinstance(outs, tuple)
    return pl.pallas_call(
        kernel,
        out_shape=outs,
        in_specs=[VMEM] * len(near) + [HBM] * len(far),
        out_specs=tuple([VMEM] * len(outs)) if many else VMEM,
        scratch_shapes=scratch,
        cost_estimate=pl.CostEstimate(flops=flops, bytes_accessed=10**6, transcendentals=0),
        compiler_params=pltpu.CompilerParams(vmem_limit_bytes=32 * 2**20),
    )(*near, *(pltpu.with_memory_space_constraint(x, pltpu.HBM) for x in far))


def scratch_for(*arrays):
    scratch = []
    for x in arrays:
        space = pltpu.SMEM if x.dtype == jnp.int32 else pltpu.VMEM
        scratch.append(space(x.shape, x.dtype))
    return scratch, pltpu.SemaphoreType.DMA((len(arrays),))


def paired_blocks(grad_out, spec_saved, w1, w2, b1, mode_counts, assignment):
    length, width = grad_out.shape[2:]
    n_rows = assignment.shape[0]
    q = spec_saved.shape[3] // (NB * BS)
    rows = 2 * NB * q
    forward, inverse = lon_tables(KM, length)

    def by_group(table):
        table = table.reshape(2, NB, 2, q, length).transpose(2, 0, 1, 3, 4)
        return table.reshape(2 * rows, length).astype(BF16)

    cosine, sine = lat_waves(n_rows)
    waves = np.array([[cosine, sine], [-sine, cosine]])
    lat = np.einsum("eckr,uv->eukrcv", waves, np.eye(NB * q))
    lat = lat.reshape(2 * NB * q * n_rows, n_rows * rows).astype(BF16)
    lat_t = np.ascontiguousarray(lat.T).reshape(n_rows, rows, -1)

    lat, lat_t = jnp.asarray(lat), jnp.asarray(lat_t)
    inverse = jnp.asarray(by_group(inverse))
    forward = jnp.asarray(by_group(forward).T)

    def swap(chunks):
        pairs = [[(i, i ^ (2 * d)) for i in range(2 * NB)] for d in ORDER[1:]]
        return [lax.ppermute(chunk, "lat", p) for chunk, p in zip(chunks, pairs)]

    field = grad_out.reshape(length, width)
    shape = jax.ShapeDtypeStruct
    far = (mode_counts, assignment, field, inverse, spec_saved[0])
    scratch, sems = scratch_for(*far)
    sent = call(
        functools.partial(analyse_kernel, q),
        (shape((rows, width), BF16),) * NB,
        scratch + [pltpu.VMEM((NB, rows, width), BF16), sems],
        (),
        far,
    )
    received = [sent[0], *swap([sent[d] for d in ORDER[1:]])]
    far = (mode_counts, assignment, w1[0], w2[0], b1[0], forward)
    scratch, _ = scratch_for(*far)
    far = (*far, lat, lat_t, field)
    wide = 2 * LANES
    mat1, mat2, bias, lat, lat_t, field, forward = call(
        functools.partial(ready_kernel, q),
        (
            shape((wide, wide), BF16),
            shape((wide, wide), BF16),
            shape((1, wide), F32),
            shape(lat.shape, BF16),
            shape(lat_t.shape, BF16),
            shape(field.shape, BF16),
            shape(forward.shape, BF16),
        ),
        scratch + [pltpu.SemaphoreType.DMA((len(far),))],
        (),
        far,
        2 * 10**9,
    )
    own = call(
        join_kernel,
        shape((NB, rows, width), BF16),
        [],
        (*received, bias),
        (),
    )
    other = lax.ppermute(own, "lat", [(i, i ^ 1) for i in range(2 * NB)])
    vectors = shape((NB * rows, wide), BF16)
    slopes = shape((NB * rows, wide), F32)
    by_pair = pltpu.VMEM((NB, rows, wide), F32)
    points0, hidden0, slope0 = call(
        own_kernel,
        (vectors, vectors, slopes),
        [by_pair],
        (*received, mat1, bias),
        (),
        2 * 10**9,
    )
    packed = shape((rows + rows // 2 + 4, LANES), BF16)
    scratch, sems = scratch_for(assignment)
    both = shape((2, NB * rows, wide), BF16)
    tail = -(-packed.shape[0] // 48) * 16
    bundle = shape((FIELD_ROWS + tail, width), BF16)
    *chunks, bundle, points1, hidden1, grad_pre, grad_y = call(
        filter_kernel,
        (packed,) * (NB - 1) + (bundle, vectors, vectors, both, both),
        scratch
        + [
            pltpu.VMEM((n_rows, rows, wide), F32),
            by_pair,
            pltpu.VMEM((NB * rows, wide), F32),
            sems,
        ],
        (*received, other, slope0, mat1, mat2, bias, lat, lat_t, field),
        (assignment,),
    )
    backs = swap(chunks)
    matrix = shape((2, BS // 2, BS), F32)
    gw1, gw2, gb1 = call(
        products_kernel,
        (matrix, matrix, shape((2, BS // 2), F32)),
        [],
        (points0, hidden0, points1, hidden1, grad_pre, grad_y),
        (),
        2 * 10**9,
    )
    three = call(join_kernel, shape((NB - 1, *packed.shape), BF16), [], backs, ())
    three = turn(three, "section")
    bundle = turn(bundle, "section")
    shifted = call(
        functools.partial(compose_kernel, lax.axis_size("section") - 1),
        shape((length, width), BF16),
        [by_pair],
        (three, bundle, forward),
        (),
    )
    shifted = shifted[None, None]
    return shifted, gw1.swapaxes(1, 2)[None], gw2.swapaxes(1, 2)[None], gb1[None]


def apply_mat(vec, mat):
    return jnp.einsum("kpi,ipj->kpj", vec, mat, preferred_element_type=F32)


def adjoint_mat(vec, mat):
    return jnp.einsum("kpj,ipj->kpi", vec, mat, preferred_element_type=F32)


def outer_sum(left, right):
    return jnp.einsum("kpi,kpj->ipj", left, right, preferred_element_type=F32)


def split_blocks(grad_out, spec_saved, w1, w2, b1, mode_counts, assignment):
    rows_dev = grad_out.shape[1]
    length = grad_out.shape[2]
    width = grad_out.shape[3]
    n_rows = assignment.shape[0]
    pairs_dev = spec_saved.shape[3] // BS
    forward, inverse = (jnp.asarray(t.astype(BF16)) for t in lon_tables(KM, length))
    cosine, sine = (jnp.asarray(t.astype(BF16))[:, assignment] for t in lat_waves(n_rows))
    table = jnp.stack(
        [jnp.stack([cosine, sine], axis=-1), jnp.stack([-sine, cosine], axis=-1)], axis=1
    )
    lat_pos = lax.axis_index("lat")
    lat_count = lax.axis_size("lat")
    own_lat = lax.dynamic_slice_in_dim(assignment, lat_pos * rows_dev, rows_dev)
    active = (jnp.arange(KM, dtype=jnp.int32)[None, :] < mode_counts[own_lat][:, None]).astype(F32)
    cotan = grad_out[0]
    spectral = jnp.einsum(
        "cml,rlni->rcmni",
        inverse,
        cotan.reshape(rows_dev, length, NB, BS),
        preferred_element_type=F32,
    )
    spectral = (spectral * active[:, None, :, None, None]).astype(BF16)
    spectral = spectral.reshape(rows_dev, 2, KM * NB * BS)
    pencil = lax.all_to_all(spectral, "lat", split_axis=2, concat_axis=0, tiled=True)
    pencil = pencil.reshape(n_rows, 2, pairs_dev, BS)
    grad_y = jnp.einsum("kerc,rcpi->kepi", table, pencil, preferred_element_type=F32).astype(BF16)
    saved = spec_saved[0].reshape(n_rows, 2, pairs_dev, BS)
    pair_ids = lat_pos * pairs_dev + jnp.arange(pairs_dev, dtype=jnp.int32)
    owner = (pair_ids % NB)[:, None] == jnp.arange(NB, dtype=jnp.int32)[None, :]
    owner = owner.astype(F32)
    first = jnp.take(w1[0].reshape(2, BS, NB, BS), pair_ids % NB, axis=2)
    second = jnp.take(w2[0].reshape(2, BS, NB, BS), pair_ids % NB, axis=2)
    shift_b = jnp.take(b1[0].reshape(2, NB, BS), pair_ids % NB, axis=1).astype(F32)
    v_r = saved[:, 0]
    v_i = saved[:, 1]
    pre_r = apply_mat(v_r, first[0]) - apply_mat(v_i, first[1]) + shift_b[0][None]
    pre_i = apply_mat(v_i, first[0]) + apply_mat(v_r, first[1]) + shift_b[1][None]
    hid_r = jax.nn.silu(pre_r).astype(BF16)
    hid_i = jax.nn.silu(pre_i).astype(BF16)
    dy_r = grad_y[:, 0]
    dy_i = grad_y[:, 1]
    dh_r = adjoint_mat(dy_r, second[0]) + adjoint_mat(dy_i, second[1])
    dh_i = adjoint_mat(dy_i, second[0]) - adjoint_mat(dy_r, second[1])
    dp_r = (dh_r * silu_slope(pre_r)).astype(BF16)
    dp_i = (dh_i * silu_slope(pre_i)).astype(BF16)
    gw2 = jnp.stack(
        [
            outer_sum(hid_r, dy_r) + outer_sum(hid_i, dy_i),
            outer_sum(hid_r, dy_i) - outer_sum(hid_i, dy_r),
        ]
    )
    gw1 = jnp.stack(
        [outer_sum(v_r, dp_r) + outer_sum(v_i, dp_i), outer_sum(v_r, dp_i) - outer_sum(v_i, dp_r)]
    )
    gb1 = jnp.stack([jnp.sum(dp_r.astype(F32), axis=0), jnp.sum(dp_i.astype(F32), axis=0)])
    dv_r = adjoint_mat(dp_r, first[0]) + adjoint_mat(dp_i, first[1])
    dv_i = adjoint_mat(dp_i, first[0]) - adjoint_mat(dp_r, first[1])
    grad_v = jnp.stack([dv_r, dv_i], axis=1).astype(BF16)
    grad_u = jnp.einsum("kerc,kepi->rcpi", table, grad_v, preferred_element_type=F32).astype(BF16)
    grad_u = grad_u.reshape(n_rows, 2, pairs_dev * BS)
    back = lax.all_to_all(grad_u, "lat", split_axis=0, concat_axis=2, tiled=True)
    back = back.reshape(rows_dev, 2, KM, NB, BS) * active[:, None, :, None, None].astype(BF16)
    mixed = jnp.einsum("cml,rcmni->rlni", forward, back, preferred_element_type=F32)
    mixed = mixed.reshape(rows_dev, length, width).astype(BF16)
    block_w1 = jnp.einsum("pn,cipj->cinj", owner, gw1).reshape(1, 2, BS, width)
    block_w2 = jnp.einsum("pn,cipj->cinj", owner, gw2).reshape(1, 2, BS, width)
    block_b1 = jnp.einsum("pn,cpj->cnj", owner, gb1).reshape(1, 2, width)
    columns = width // lat_count
    full_w1, full_w2, full_b1 = lax.psum((block_w1, block_w2, block_b1), "lat")
    sum_w1 = lax.dynamic_slice_in_dim(full_w1, lat_pos * columns, columns, 3)
    sum_w2 = lax.dynamic_slice_in_dim(full_w2, lat_pos * columns, columns, 3)
    sum_b1 = lax.dynamic_slice_in_dim(full_b1, lat_pos * columns, columns, 2)
    whole = (cotan.astype(F32) + mixed.astype(F32)).astype(BF16)
    received = from_behind(whole[None], "section", -1)
    return (received, sum_w1, sum_w2, sum_b1)


def per_device(grad_out, spec_saved, w1, w2, b1, mode_counts, assignment):
    n_dev = lax.axis_size("lat")
    pairs_dev = spec_saved.shape[3] // BS
    paired = n_dev == 2 * NB and grad_out.shape[1] == 1 and pairs_dev % NB == 0
    body = paired_blocks if paired else split_blocks
    return body(grad_out, spec_saved, w1, w2, b1, mode_counts, assignment)


def solution(mesh):
    return jax.shard_map(
        per_device,
        mesh=mesh,
        in_specs=(
            P("section", "lat", None, None),
            P("section", None, None, "lat"),
            P("section", None, None, None),
            P("section", None, None, None),
            P("section", None, None),
            P(),
            P(),
        ),
        out_specs=(
            P("section", "lat", None, None),
            P("section", None, None, "lat"),
            P("section", None, None, "lat"),
            P("section", None, "lat"),
        ),
        check_vma=False,
    )
```

```python
import functools
import math

import jax
import jax.numpy as jnp
import numpy as np
from jax import lax
from jax.experimental import pallas as pl
from jax.experimental.pallas import tpu as pltpu
from jax.sharding import PartitionSpec as P

NB = 4
BS = 96
KM = 72
LANES = 128
F32 = jnp.float32
BF16 = jnp.bfloat16


def from_behind(value, axis, by):
    length = lax.axis_size(axis)
    pairs = [(i, i + by) for i in range(length) if 0 <= i + by < length]
    return lax.ppermute(value, axis, pairs)


def turn(value, axis):
    length = lax.axis_size(axis)
    return lax.ppermute(value, axis, [(i, (i - 1) % length) for i in range(length)])


def lon_tables(n_modes, length):
    modes = np.arange(n_modes)
    phase = modes[:, None] * np.arange(length)[None, :] % length
    angle = phase * (2.0 * math.pi / length)
    forward = np.stack([np.cos(angle), -np.sin(angle)]) / math.sqrt(length)
    weight = np.where(modes == 0, 1.0, 2.0)[None, :, None]
    return forward, forward * weight


def lat_waves(n_rows):
    freqs = np.arange(n_rows)
    angle = (freqs[:, None] * freqs[None, :] % n_rows) * (2.0 * math.pi / n_rows)
    factor = 1.0 / math.sqrt(n_rows)
    return np.cos(angle) * factor, np.sin(angle) * factor


def silu_slope(pre):
    sig = jax.nn.sigmoid(pre)
    return sig * (1.0 + pre * (1.0 - sig))


def window(x, start):
    low = start // LANES * LANES
    shift = start - low
    if shift == 0:
        return x[:, low : low + LANES]
    if shift + BS <= LANES:
        return pltpu.roll(x[:, low : low + LANES], LANES - shift, 1)
    return pltpu.roll(x[:, low : low + 2 * LANES], 2 * LANES - shift, 1)[:, :LANES]


def dense(parts):
    lane = lax.broadcasted_iota(jnp.int32, parts[0].shape, 1)
    first = pltpu.roll(parts[1], 96, 1)
    second = pltpu.roll(parts[2], 64, 1)
    third = pltpu.roll(parts[3], 32, 1)
    return jnp.concatenate(
        [
            jnp.where(lane < 96, parts[0], first),
            jnp.where(lane < 64, first, second),
            jnp.where(lane < 32, second, third),
        ],
        axis=1,
    )


def dot(a, b, contract):
    return lax.dot_general(a, b, ((contract[:1], contract[1:]), ((), ())), preferred_element_type=F32)


def mode_numbers(shape, axis, q):
    number = lax.broadcasted_iota(jnp.int32, shape, axis)
    number = jnp.where(number >= NB * q, number - NB * q, number)
    mode = number
    for z in range(1, NB):
        mode = jnp.where(number >= z * q, number + z * q, mode)
    return mode


def fetch(sems, sources, targets):
    copies = [
        pltpu.make_async_copy(source, target, sems.at[i])
        for i, (source, target) in enumerate(zip(sources, targets))
    ]
    for copy in copies:
        copy.start()
    return copies


def wait(copies):
    for copy in copies:
        copy.wait()


def partner(d):
    return jnp.bitwise_xor(lax.axis_index("lat") // 2, d)


def analyse_kernel(q, *refs):
    hbm, outs, held, (by_block, sems) = refs[:5], refs[5:9], refs[9:14], refs[14:]
    counts, assign, field, table, saved = held
    copies = fetch(sems, hbm, held)
    wait(copies[4:])
    parts = [saved[:, c, :].astype(F32) for c in range(2)]
    points = [
        [
            jnp.concatenate([window(part, (mm * NB + n) * BS) for mm in range(q)], axis=0)
            for part in parts
        ]
        for n in range(NB)
    ]
    wait(copies[2:4])
    rows = by_block.shape[1]
    spectral = jnp.dot(table[...], field[...], preferred_element_type=F32)
    wait(copies[:2])
    active = counts[assign[lax.axis_index("lat")]]
    mode = mode_numbers((rows, spectral.shape[1]), 0, q)
    groups = [
        jnp.where(mode < active - g * q, spectral[g * rows : (g + 1) * rows], 0.0)
        for g in range(2)
    ]
    for n in range(NB):
        pieces = [window(group, n * BS) for group in groups]
        by_block[n] = dense(pieces + points[n]).astype(BF16)
    for d, out in enumerate(outs):
        out[...] = by_block[partner(d)]


def ready_kernel(q, *refs):
    hbm, (mat1, mat2, bias, lat, lat_t, own_field, own_table) = refs[:9], refs[9:16]
    counts, assign, w1, w2, b1, table, sems = refs[16:]
    copies = fetch(sems, hbm, (counts, assign, w1, w2, b1, table, lat, lat_t, own_field))
    wait(copies[:6])
    active = counts[assign[lax.axis_index("lat")]]
    rows = table.shape[1] // 2
    mode = mode_numbers((table.shape[0], rows), 1, q)
    for g in range(2):
        part = table[:, g * rows : (g + 1) * rows].astype(F32)
        part = jnp.where(mode < active - g * q, part, 0.0)
        own_table[:, g * rows : (g + 1) * rows] = part.astype(BF16)
    block = lax.axis_index("lat") // 2

    def pick(x):
        value = window(x, 0)
        for n in range(1, NB):
            value = jnp.where(block == n, window(x, n * BS), value)
        lane = lax.broadcasted_iota(jnp.int32, value.shape, 1)
        return jnp.where(lane < BS, value, 0.0)

    gap = jnp.zeros((LANES - BS, 2 * LANES), BF16)
    for source, mat in ((w1, mat1), (w2, mat2)):
        real, imag = (pick(source[c].astype(F32)) for c in range(2))
        mat[0:BS] = jnp.concatenate([real, imag], axis=1).astype(BF16)
        mat[BS:LANES] = gap
        mat[LANES : LANES + BS] = jnp.concatenate([-imag, real], axis=1).astype(BF16)
        mat[LANES + BS : 2 * LANES] = gap
    shift_b = pick(b1[...].astype(F32))
    bias[...] = jnp.concatenate([shift_b[0:1], shift_b[1:2]], axis=1)
    wait(copies[6:])


ORDER = (0, 3, 2, 1)
FIELD_ROWS = 192


def join_kernel(*refs):
    out = refs[-1]
    for i in range(out.shape[0]):
        out[i] = refs[i][...]


def pack(band):
    rows = band.shape[0]
    tail = rows // 2 + 4
    left, right = band[:, :LANES], pltpu.roll(band[:, LANES:], 96, 1)
    lane = lax.broadcasted_iota(jnp.int32, left.shape, 1)
    upper = jnp.where(lane < 96, left, right)
    lower = pltpu.roll(right[rows - tail :], 64, 1)
    lower = jnp.where(lane[:tail] < 64, right[:tail], lower)
    return jnp.concatenate([upper, lower], axis=0)


def unpack(packed, rows):
    tail = rows // 2 + 4
    upper, lower = packed[:rows], packed[rows:]
    rest = jnp.concatenate([lower, pltpu.roll(lower, 64, 1)[2 * tail - rows :]], axis=0)
    lane = lax.broadcasted_iota(jnp.int32, upper.shape, 1)
    right = jnp.where(lane < 32, pltpu.roll(upper, 32, 1), pltpu.roll(rest, 32, 1))
    return [upper, right]


def silu_points(chunks, mat, bias, by_pair, points, hidden, slope):
    for d, chunk in enumerate(chunks):
        parts = [window(chunk, j * BS) for j in (2, 3)]
        by_pair[partner(d)] = jnp.concatenate(parts, axis=1)
    v = by_pair[...].reshape(points.shape).astype(BF16)
    pre = dot(v, mat[...], (1, 0)) + bias[...]
    sig = jax.nn.sigmoid(pre)
    points[...] = v
    hidden[...] = (pre * sig).astype(BF16)
    slope[...] = sig * (1.0 + pre * (1.0 - sig))


def row_groups(chunk):
    return jnp.concatenate([window(chunk, j * BS) for j in range(2)], axis=1)


def own_kernel(*refs):
    early, mat1, bias, points, hidden, slope, fields, by_pair = refs[NB:]
    chunks = [refs[i][...].astype(F32) for i in ORDER]
    silu_points(chunks, mat1, bias, by_pair, points, hidden, slope)
    for i in range(NB):
        fields[i] = row_groups(refs[i][...].astype(F32))
    for i in range(2):
        fields[NB + i] = row_groups(early[i].astype(F32))


def filter_kernel(*refs):
    early, late, fields, slope_own, mat1, mat2, bias, lat, lat_t, own_field, assign_hbm = refs[:11]
    outs, (bundle, points, hidden, grad_pre, grad_y) = refs[11:14], refs[14:19]
    assign, by_lat, by_pair, slope, sems = refs[19:]
    copies = fetch(sems, (assign_hbm,), (assign,))
    core = lax.rem(lax.axis_index("lat"), 2)
    others = [half[i].astype(F32) for half in (early, late) for i in range(2)]
    silu_points([others[i] for i in ORDER], mat1, bias, by_pair, points, hidden, slope)
    wait(copies)
    for i, d in enumerate(ORDER):
        by_lat[assign[2 * partner(d) + core]] = fields[i]
        spectrum = fields[NB + i] if i < 2 else row_groups(others[i])
        by_lat[assign[2 * partner(d) + 1 - core]] = spectrum
    field = by_lat[...].reshape(lat.shape[1], 2 * LANES).astype(BF16)
    waves = dot(lat[...], field, (1, 0)).astype(BF16)
    rows = waves.shape[0] // 2
    inner = []
    for side, slopes in enumerate((slope_own, slope)):
        dy = []
        for c in range(2):
            part = waves[c * rows : (c + 1) * rows]
            flip = core == 0 if side == 0 else core == 1
            dy.append(jnp.where(flip, part[:, :LANES], part[:, LANES:]))
        dy = jnp.concatenate(dy, axis=1)
        dp = (dot(dy, mat2[...], (1, 1)) * slopes[...]).astype(BF16)
        dv = dot(dp, mat1[...], (1, 1))
        grad_y[side] = dy
        grad_pre[side] = dp
        inner.append(jnp.concatenate([dv[:, :LANES], dv[:, LANES:]], axis=0))
    left = jnp.where(core == 0, inner[0], inner[1])
    right = jnp.where(core == 0, inner[1], inner[0])
    inner = jnp.concatenate([left, right], axis=1).astype(BF16)
    length = own_field.shape[0]
    bundle[0:length] = own_field[...]
    for i, d in enumerate(ORDER):
        band = pack(dot(lat_t[assign[2 * partner(d) + core]], inner, (1, 0)))
        if d:
            outs[i - 1][...] = band.astype(BF16)
        else:
            rows = bundle.shape[0] - FIELD_ROWS
            band = jnp.concatenate([band, jnp.zeros((3 * rows - band.shape[0], LANES), F32)], axis=0)
            band = [band[i * rows : (i + 1) * rows] for i in range(3)]
            bundle[FIELD_ROWS:] = jnp.concatenate(band, axis=1).astype(BF16)


def products_kernel(points0, hidden0, points1, hidden1, grad_pre, grad_y, gw1, gw2, gb1):
    core = lax.rem(lax.axis_index("lat"), 2)
    half = BS // 2
    for ref, grads, values in ((gw1, grad_pre, (points0, points1)), (gw2, grad_y, (hidden0, hidden1))):
        both = dot(grads[0], values[0][...], (0, 0)) + dot(grads[1], values[1][...], (0, 0))
        real = both[:BS, :LANES] + both[LANES : LANES + BS, LANES:]
        imag = both[LANES : LANES + BS, :LANES] - both[:BS, LANES:]
        for c, full in enumerate((real, imag)):
            ref[c] = jnp.where(core == 0, full[:half], full[half:])[:, :BS]
    sums = sum(jnp.sum(grad_pre[side].astype(F32), axis=0, keepdims=True) for side in range(2))
    for c in range(2):
        line = sums[:, c * LANES : (c + 1) * LANES]
        gb1[c : c + 1] = jnp.where(core == 0, line[:, :half], line[:, half:BS])


def compose_kernel(last, three, bundle, table, out, by_block):
    rows = by_block.shape[1]
    own = bundle[FIELD_ROWS:].astype(F32)
    own = jnp.concatenate([own[:, i * LANES : (i + 1) * LANES] for i in range(3)], axis=0)
    chunks = [own[: three.shape[1]]] + [three[i].astype(F32) for i in range(3)]
    for d, chunk in zip(ORDER, chunks):
        by_block[partner(d)] = jnp.concatenate(unpack(chunk, rows), axis=1)
    groups = [
        dense([by_block[n, :, g * LANES : (g + 1) * LANES] for n in range(NB)]) for g in range(2)
    ]
    groups = jnp.concatenate(groups, axis=0).astype(BF16)
    mixed = jnp.dot(table[...], groups, preferred_element_type=F32).astype(BF16)
    whole = bundle[0 : out.shape[0]].astype(F32) + mixed.astype(F32)
    out[...] = jnp.where(lax.axis_index("section") == last, 0.0, whole).astype(BF16)


VMEM = pl.BlockSpec(memory_space=pltpu.VMEM)
HBM = pl.BlockSpec(memory_space=pltpu.HBM)


def call(kernel, outs, scratch, near, far, flops=10**8):
    many = isinstance(outs, tuple)
    many = isinstance(outs, tuple)
    return pl.pallas_call(
        kernel,
        out_shape=outs,
        in_specs=[VMEM] * len(near) + [HBM] * len(far),
        out_specs=tuple([VMEM] * len(outs)) if many else VMEM,
        scratch_shapes=scratch,
        cost_estimate=pl.CostEstimate(flops=flops, bytes_accessed=10**6, transcendentals=0),
        compiler_params=pltpu.CompilerParams(vmem_limit_bytes=32 * 2**20),
    )(*near, *(pltpu.with_memory_space_constraint(x, pltpu.HBM) for x in far))


def scratch_for(*arrays):
    scratch = []
    for x in arrays:
        space = pltpu.SMEM if x.dtype == jnp.int32 else pltpu.VMEM
        scratch.append(space(x.shape, x.dtype))
    return scratch, pltpu.SemaphoreType.DMA((len(arrays),))


def paired_blocks(grad_out, spec_saved, w1, w2, b1, mode_counts, assignment):
    length, width = grad_out.shape[2:]
    n_rows = assignment.shape[0]
    q = spec_saved.shape[3] // (NB * BS)
    rows = 2 * NB * q
    forward, inverse = lon_tables(KM, length)

    def by_group(table):
        table = table.reshape(2, NB, 2, q, length).transpose(2, 0, 1, 3, 4)
        return table.reshape(2 * rows, length).astype(BF16)

    cosine, sine = lat_waves(n_rows)
    waves = np.array([[cosine, sine], [-sine, cosine]])
    lat = np.einsum("eckr,uv->eukrcv", waves, np.eye(NB * q))
    lat = lat.reshape(2 * NB * q * n_rows, n_rows * rows).astype(BF16)
    lat_t = np.ascontiguousarray(lat.T).reshape(n_rows, rows, -1)

    lat, lat_t = jnp.asarray(lat), jnp.asarray(lat_t)
    inverse = jnp.asarray(by_group(inverse))
    forward = jnp.asarray(by_group(forward).T)

    def swap(chunks):
        pairs = [[(i, i ^ (2 * d)) for i in range(2 * NB)] for d in ORDER[1:]]
        return [lax.ppermute(chunk, "lat", p) for chunk, p in zip(chunks, pairs)]

    def twin(value):
        return lax.ppermute(value, "lat", [(i, i ^ 1) for i in range(2 * NB)])

    field = grad_out.reshape(length, width)
    shape = jax.ShapeDtypeStruct
    far = (mode_counts, assignment, field, inverse, spec_saved[0])
    scratch, sems = scratch_for(*far)
    sent = call(
        functools.partial(analyse_kernel, q),
        (shape((rows, width), BF16),) * NB,
        scratch + [pltpu.VMEM((NB, rows, width), BF16), sems],
        (),
        far,
    )
    received = [sent[0], *swap([sent[d] for d in ORDER[1:]])]
    far = (mode_counts, assignment, w1[0], w2[0], b1[0], forward)
    scratch, _ = scratch_for(*far)
    far = (*far, lat, lat_t, field)
    wide = 2 * LANES
    mat1, mat2, bias, lat, lat_t, field, forward = call(
        functools.partial(ready_kernel, q),
        (
            shape((wide, wide), BF16),
            shape((wide, wide), BF16),
            shape((1, wide), F32),
            shape(lat.shape, BF16),
            shape(lat_t.shape, BF16),
            shape(field.shape, BF16),
            shape(forward.shape, BF16),
        ),
        scratch + [pltpu.SemaphoreType.DMA((len(far),))],
        (),
        far,
        2 * 10**9,
    )
    pair = shape((2, rows, width), BF16)
    early = twin(call(join_kernel, pair, [], received[:2], ()))
    late = twin(call(join_kernel, pair, [], (*received[2:], bias), ()))
    vectors = shape((NB * rows, wide), BF16)
    slopes = shape((NB * rows, wide), F32)
    by_pair = pltpu.VMEM((NB, rows, wide), F32)
    points0, hidden0, slope0, fields = call(
        own_kernel,
        (vectors, vectors, slopes, shape((NB + 2, rows, wide), F32)),
        [by_pair],
        (*received, early, mat1, bias),
        (),
        2 * 10**9,
    )
    packed = shape((rows + rows // 2 + 4, LANES), BF16)
    scratch, sems = scratch_for(assignment)
    both = shape((2, NB * rows, wide), BF16)
    tail = -(-packed.shape[0] // 48) * 16
    bundle = shape((FIELD_ROWS + tail, width), BF16)
    *chunks, bundle, points1, hidden1, grad_pre, grad_y = call(
        filter_kernel,
        (packed,) * (NB - 1) + (bundle, vectors, vectors, both, both),
        scratch
        + [
            pltpu.VMEM((n_rows, rows, wide), F32),
            by_pair,
            pltpu.VMEM((NB * rows, wide), F32),
            sems,
        ],
        (early, late, fields, slope0, mat1, mat2, bias, lat, lat_t, field),
        (assignment,),
    )
    backs = swap(chunks)
    matrix = shape((2, BS // 2, BS), F32)
    gw1, gw2, gb1 = call(
        products_kernel,
        (matrix, matrix, shape((2, BS // 2), F32)),
        [],
        (points0, hidden0, points1, hidden1, grad_pre, grad_y),
        (),
        2 * 10**9,
    )
    three = call(join_kernel, shape((NB - 1, *packed.shape), BF16), [], backs, ())
    three = turn(three, "section")
    bundle = turn(bundle, "section")
    shifted = call(
        functools.partial(compose_kernel, lax.axis_size("section") - 1),
        shape((length, width), BF16),
        [by_pair],
        (three, bundle, forward),
        (),
    )
    shifted = shifted[None, None]
    return shifted, gw1.swapaxes(1, 2)[None], gw2.swapaxes(1, 2)[None], gb1[None]


def apply_mat(vec, mat):
    return jnp.einsum("kpi,ipj->kpj", vec, mat, preferred_element_type=F32)


def adjoint_mat(vec, mat):
    return jnp.einsum("kpj,ipj->kpi", vec, mat, preferred_element_type=F32)


def outer_sum(left, right):
    return jnp.einsum("kpi,kpj->ipj", left, right, preferred_element_type=F32)


def split_blocks(grad_out, spec_saved, w1, w2, b1, mode_counts, assignment):
    rows_dev = grad_out.shape[1]
    length = grad_out.shape[2]
    width = grad_out.shape[3]
    n_rows = assignment.shape[0]
    pairs_dev = spec_saved.shape[3] // BS
    forward, inverse = (jnp.asarray(t.astype(BF16)) for t in lon_tables(KM, length))
    cosine, sine = (jnp.asarray(t.astype(BF16))[:, assignment] for t in lat_waves(n_rows))
    table = jnp.stack(
        [jnp.stack([cosine, sine], axis=-1), jnp.stack([-sine, cosine], axis=-1)], axis=1
    )
    lat_pos = lax.axis_index("lat")
    lat_count = lax.axis_size("lat")
    own_lat = lax.dynamic_slice_in_dim(assignment, lat_pos * rows_dev, rows_dev)
    active = (jnp.arange(KM, dtype=jnp.int32)[None, :] < mode_counts[own_lat][:, None]).astype(F32)
    cotan = grad_out[0]
    spectral = jnp.einsum(
        "cml,rlni->rcmni",
        inverse,
        cotan.reshape(rows_dev, length, NB, BS),
        preferred_element_type=F32,
    )
    spectral = (spectral * active[:, None, :, None, None]).astype(BF16)
    spectral = spectral.reshape(rows_dev, 2, KM * NB * BS)
    pencil = lax.all_to_all(spectral, "lat", split_axis=2, concat_axis=0, tiled=True)
    pencil = pencil.reshape(n_rows, 2, pairs_dev, BS)
    grad_y = jnp.einsum("kerc,rcpi->kepi", table, pencil, preferred_element_type=F32).astype(BF16)
    saved = spec_saved[0].reshape(n_rows, 2, pairs_dev, BS)
    pair_ids = lat_pos * pairs_dev + jnp.arange(pairs_dev, dtype=jnp.int32)
    owner = (pair_ids % NB)[:, None] == jnp.arange(NB, dtype=jnp.int32)[None, :]
    owner = owner.astype(F32)
    first = jnp.take(w1[0].reshape(2, BS, NB, BS), pair_ids % NB, axis=2)
    second = jnp.take(w2[0].reshape(2, BS, NB, BS), pair_ids % NB, axis=2)
    shift_b = jnp.take(b1[0].reshape(2, NB, BS), pair_ids % NB, axis=1).astype(F32)
    v_r = saved[:, 0]
    v_i = saved[:, 1]
    pre_r = apply_mat(v_r, first[0]) - apply_mat(v_i, first[1]) + shift_b[0][None]
    pre_i = apply_mat(v_i, first[0]) + apply_mat(v_r, first[1]) + shift_b[1][None]
    hid_r = jax.nn.silu(pre_r).astype(BF16)
    hid_i = jax.nn.silu(pre_i).astype(BF16)
    dy_r = grad_y[:, 0]
    dy_i = grad_y[:, 1]
    dh_r = adjoint_mat(dy_r, second[0]) + adjoint_mat(dy_i, second[1])
    dh_i = adjoint_mat(dy_i, second[0]) - adjoint_mat(dy_r, second[1])
    dp_r = (dh_r * silu_slope(pre_r)).astype(BF16)
    dp_i = (dh_i * silu_slope(pre_i)).astype(BF16)
    gw2 = jnp.stack(
        [
            outer_sum(hid_r, dy_r) + outer_sum(hid_i, dy_i),
            outer_sum(hid_r, dy_i) - outer_sum(hid_i, dy_r),
        ]
    )
    gw1 = jnp.stack(
        [outer_sum(v_r, dp_r) + outer_sum(v_i, dp_i), outer_sum(v_r, dp_i) - outer_sum(v_i, dp_r)]
    )
    gb1 = jnp.stack([jnp.sum(dp_r.astype(F32), axis=0), jnp.sum(dp_i.astype(F32), axis=0)])
    dv_r = adjoint_mat(dp_r, first[0]) + adjoint_mat(dp_i, first[1])
    dv_i = adjoint_mat(dp_i, first[0]) - adjoint_mat(dp_r, first[1])
    grad_v = jnp.stack([dv_r, dv_i], axis=1).astype(BF16)
    grad_u = jnp.einsum("kerc,kepi->rcpi", table, grad_v, preferred_element_type=F32).astype(BF16)
    grad_u = grad_u.reshape(n_rows, 2, pairs_dev * BS)
    back = lax.all_to_all(grad_u, "lat", split_axis=0, concat_axis=2, tiled=True)
    back = back.reshape(rows_dev, 2, KM, NB, BS) * active[:, None, :, None, None].astype(BF16)
    mixed = jnp.einsum("cml,rcmni->rlni", forward, back, preferred_element_type=F32)
    mixed = mixed.reshape(rows_dev, length, width).astype(BF16)
    block_w1 = jnp.einsum("pn,cipj->cinj", owner, gw1).reshape(1, 2, BS, width)
    block_w2 = jnp.einsum("pn,cipj->cinj", owner, gw2).reshape(1, 2, BS, width)
    block_b1 = jnp.einsum("pn,cpj->cnj", owner, gb1).reshape(1, 2, width)
    columns = width // lat_count
    full_w1, full_w2, full_b1 = lax.psum((block_w1, block_w2, block_b1), "lat")
    sum_w1 = lax.dynamic_slice_in_dim(full_w1, lat_pos * columns, columns, 3)
    sum_w2 = lax.dynamic_slice_in_dim(full_w2, lat_pos * columns, columns, 3)
    sum_b1 = lax.dynamic_slice_in_dim(full_b1, lat_pos * columns, columns, 2)
    whole = (cotan.astype(F32) + mixed.astype(F32)).astype(BF16)
    received = from_behind(whole[None], "section", -1)
    return (received, sum_w1, sum_w2, sum_b1)


def per_device(grad_out, spec_saved, w1, w2, b1, mode_counts, assignment):
    n_dev = lax.axis_size("lat")
    pairs_dev = spec_saved.shape[3] // BS
    paired = n_dev == 2 * NB and grad_out.shape[1] == 1 and pairs_dev % NB == 0
    body = paired_blocks if paired else split_blocks
    return body(grad_out, spec_saved, w1, w2, b1, mode_counts, assignment)


def solution(mesh):
    return jax.shard_map(
        per_device,
        mesh=mesh,
        in_specs=(
            P("section", "lat", None, None),
            P("section", None, None, "lat"),
            P("section", None, None, None),
            P("section", None, None, None),
            P("section", None, None),
            P(),
            P(),
        ),
        out_specs=(
            P("section", "lat", None, None),
            P("section", None, None, "lat"),
            P("section", None, None, "lat"),
            P("section", None, "lat"),
        ),
        check_vma=False,
    )
```

```python
import functools
import math

import jax
import jax.numpy as jnp
import numpy as np
from jax import lax
from jax.experimental import pallas as pl
from jax.experimental.pallas import tpu as pltpu
from jax.sharding import PartitionSpec as P

NB = 4
BS = 96
KM = 72
LANES = 128
F32 = jnp.float32
BF16 = jnp.bfloat16


def from_behind(value, axis, by):
    length = lax.axis_size(axis)
    pairs = [(i, i + by) for i in range(length) if 0 <= i + by < length]
    return lax.ppermute(value, axis, pairs)


def turn(value, axis):
    length = lax.axis_size(axis)
    return lax.ppermute(value, axis, [(i, (i - 1) % length) for i in range(length)])


def lon_tables(n_modes, length):
    modes = np.arange(n_modes)
    phase = modes[:, None] * np.arange(length)[None, :] % length
    angle = phase * (2.0 * math.pi / length)
    forward = np.stack([np.cos(angle), -np.sin(angle)]) / math.sqrt(length)
    weight = np.where(modes == 0, 1.0, 2.0)[None, :, None]
    return forward, forward * weight


def lat_waves(n_rows):
    freqs = np.arange(n_rows)
    angle = (freqs[:, None] * freqs[None, :] % n_rows) * (2.0 * math.pi / n_rows)
    factor = 1.0 / math.sqrt(n_rows)
    return np.cos(angle) * factor, np.sin(angle) * factor


def silu_slope(pre):
    sig = jax.nn.sigmoid(pre)
    return sig * (1.0 + pre * (1.0 - sig))


def window(x, start):
    low = start // LANES * LANES
    shift = start - low
    if shift == 0:
        return x[:, low : low + LANES]
    if shift + BS <= LANES:
        return pltpu.roll(x[:, low : low + LANES], LANES - shift, 1)
    return pltpu.roll(x[:, low : low + 2 * LANES], 2 * LANES - shift, 1)[:, :LANES]


def dense(parts):
    lane = lax.broadcasted_iota(jnp.int32, parts[0].shape, 1)
    first = pltpu.roll(parts[1], 96, 1)
    second = pltpu.roll(parts[2], 64, 1)
    third = pltpu.roll(parts[3], 32, 1)
    return jnp.concatenate(
        [
            jnp.where(lane < 96, parts[0], first),
            jnp.where(lane < 64, first, second),
            jnp.where(lane < 32, second, third),
        ],
        axis=1,
    )


def dot(a, b, contract):
    return lax.dot_general(a, b, ((contract[:1], contract[1:]), ((), ())), preferred_element_type=F32)


def mode_numbers(shape, axis, q):
    number = lax.broadcasted_iota(jnp.int32, shape, axis)
    second = number >= NB * q
    number = jnp.where(second, number - NB * q, number)
    mode = number
    for z in range(1, NB):
        mode = jnp.where(number >= z * q, number + z * q, mode)
    return jnp.where(second, mode + q, mode)


def eight_points(x, sign):
    root = float(np.float32(1.0 / math.sqrt(8.0)).astype(BF16))

    def add(a, b):
        return a[0] + b[0], a[1] + b[1]

    def sub(a, b):
        return a[0] - b[0], a[1] - b[1]

    def times_i(a, by):
        return (-a[1], a[0]) if by > 0 else (a[1], -a[0])

    def scale(a, by):
        return a[0] * by, a[1] * by

    def four(a, b, c, d):
        total, far, other, near = add(a, c), sub(a, c), add(b, d), sub(b, d)
        near = times_i(near, sign)
        return add(total, other), add(far, near), sub(total, other), sub(far, near)

    even = [scale(a, root) for a in four(*x[0::2])]
    odd = four(*x[1::2])
    turned = [
        scale(odd[0], root),
        scale(add(odd[1], times_i(odd[1], sign)), 0.25),
        scale(times_i(odd[2], sign), root),
        scale(sub(times_i(odd[3], sign), odd[3]), 0.25),
    ]
    return [add(a, b) for a, b in zip(even, turned)] + [sub(a, b) for a, b in zip(even, turned)]


def fetch(sems, sources, targets):
    copies = [
        pltpu.make_async_copy(source, target, sems.at[i])
        for i, (source, target) in enumerate(zip(sources, targets))
    ]
    for copy in copies:
        copy.start()
    return copies


def wait(copies):
    for copy in copies:
        copy.wait()


def partner(d):
    return jnp.bitwise_xor(lax.axis_index("lat") // 2, d)


def analyse_kernel(q, *refs):
    hbm, outs, held, (by_block, sems) = refs[:5], refs[5:9], refs[9:14], refs[14:]
    counts, assign, field, table, saved = held
    copies = fetch(sems, hbm, held)
    wait(copies[4:])
    parts = [saved[:, c, :].astype(F32) for c in range(2)]
    points = [
        [
            jnp.concatenate([window(part, (mm * NB + n) * BS) for mm in range(q)], axis=0)
            for part in parts
        ]
        for n in range(NB)
    ]
    wait(copies[:4])
    rows = by_block.shape[1]
    spectral = jnp.dot(table[...], field[...], preferred_element_type=F32)
    active = counts[assign[lax.axis_index("lat")]]
    held_modes = mode_numbers((rows, spectral.shape[1]), 0, q) < active
    spectra = [jnp.where(held_modes, spectral[c * rows : (c + 1) * rows], 0.0) for c in range(2)]
    for n in range(NB):
        pieces = [window(spectrum, n * BS) for spectrum in spectra]
        by_block[n] = dense(pieces + points[n]).astype(BF16)
    for d, out in enumerate(outs):
        out[...] = by_block[partner(d)]


def ready_kernel(q, *refs):
    hbm, (mat1, mat2, bias, own_field, own_table) = refs[:7], refs[7:12]
    counts, assign, w1, w2, b1, table, sems = refs[12:]
    copies = fetch(sems, hbm, (counts, assign, w1, w2, b1, table, own_field))
    wait(copies[:6])
    active = counts[assign[lax.axis_index("lat")]]
    rows = table.shape[1] // 2
    held_modes = mode_numbers((table.shape[0], rows), 1, q) < active
    for c in range(2):
        part = table[:, c * rows : (c + 1) * rows].astype(F32)
        own_table[:, c * rows : (c + 1) * rows] = jnp.where(held_modes, part, 0.0).astype(BF16)
    block = lax.axis_index("lat") // 2

    def pick(x):
        value = window(x, 0)
        for n in range(1, NB):
            value = jnp.where(block == n, window(x, n * BS), value)
        lane = lax.broadcasted_iota(jnp.int32, value.shape, 1)
        return jnp.where(lane < BS, value, 0.0)

    gap = jnp.zeros((LANES - BS, 2 * LANES), BF16)
    for source, mat in ((w1, mat1), (w2, mat2)):
        real, imag = (pick(source[c].astype(F32)) for c in range(2))
        mat[0:BS] = jnp.concatenate([real, imag], axis=1).astype(BF16)
        mat[BS:LANES] = gap
        mat[LANES : LANES + BS] = jnp.concatenate([-imag, real], axis=1).astype(BF16)
        mat[LANES + BS : 2 * LANES] = gap
    shift_b = pick(b1[...].astype(F32))
    bias[...] = jnp.concatenate([shift_b[0:1], shift_b[1:2]], axis=1)
    wait(copies[6:])


ORDER = (0, 3, 2, 1)
FIELD_ROWS = 192


def join_kernel(*refs):
    out = refs[-1]
    for i in range(out.shape[0]):
        out[i] = refs[i][...]


def pack(band):
    rows = band.shape[0]
    tail = rows // 2 + 4
    left, right = band[:, :LANES], pltpu.roll(band[:, LANES:], 96, 1)
    lane = lax.broadcasted_iota(jnp.int32, left.shape, 1)
    upper = jnp.where(lane < 96, left, right)
    lower = pltpu.roll(right[rows - tail :], 64, 1)
    lower = jnp.where(lane[:tail] < 64, right[:tail], lower)
    return jnp.concatenate([upper, lower], axis=0)


def unpack(packed, rows):
    tail = rows // 2 + 4
    upper, lower = packed[:rows], packed[rows:]
    rest = jnp.concatenate([lower, pltpu.roll(lower, 64, 1)[2 * tail - rows :]], axis=0)
    lane = lax.broadcasted_iota(jnp.int32, upper.shape, 1)
    right = jnp.where(lane < 32, pltpu.roll(upper, 32, 1), pltpu.roll(rest, 32, 1))
    return [upper, right]


def silu_points(chunks, mat, bias, by_pair, points, hidden, slope):
    for d, chunk in enumerate(chunks):
        parts = [window(chunk, j * BS) for j in (2, 3)]
        by_pair[partner(d)] = jnp.concatenate(parts, axis=1)
    v = by_pair[...].reshape(points.shape).astype(BF16)
    pre = dot(v, mat[...], (1, 0)) + bias[...]
    sig = jax.nn.sigmoid(pre)
    points[...] = v
    hidden[...] = (pre * sig).astype(BF16)
    slope[...] = sig * (1.0 + pre * (1.0 - sig))


def own_kernel(*refs):
    mat1, bias, points, hidden, slope, by_pair = refs[NB:]
    chunks = [refs[i][...].astype(F32) for i in ORDER]
    silu_points(chunks, mat1, bias, by_pair, points, hidden, slope)


def filter_kernel(*refs):
    owns, (other, slope_own, mat1, mat2, bias, own_field, assign_hbm) = refs[:4], refs[4:11]
    outs, (bundle, points, hidden, grad_pre, grad_y) = refs[11:14], refs[14:19]
    assign, by_lat, by_pair, slope, real, imag, sems = refs[19:]
    copies = fetch(sems, (assign_hbm,), (assign,))
    core = lax.rem(lax.axis_index("lat"), 2)
    sides = [[owns[i][...].astype(F32) for i in ORDER], [other[i].astype(F32) for i in ORDER]]
    silu_points(sides[1], mat1, bias, by_pair, points, hidden, slope)
    wait(copies)
    for side, chunks in zip((core, 1 - core), sides):
        for d, chunk in enumerate(chunks):
            parts = [window(chunk, j * BS) for j in range(2)]
            by_lat[assign[2 * partner(d) + side]] = jnp.concatenate(parts, axis=1)
    n_rows, rows, _ = by_lat.shape
    half = rows * n_rows // 2
    waves = eight_points([(by_lat[r][:, :LANES], by_lat[r][:, LANES:]) for r in range(n_rows)], -1)
    for k, wave in enumerate(waves):
        real[k * rows : (k + 1) * rows] = wave[0]
        imag[k * rows : (k + 1) * rows] = wave[1]
    dy = [
        jnp.concatenate([ref[pl.ds(m, n_rows, stride=rows), :] for m in range(rows)], axis=0)
        for ref in (real, imag)
    ]
    dy = jnp.concatenate(dy, axis=1).astype(BF16)
    dy = [jnp.where(core == side, dy[:half], dy[half:]) for side in range(2)]
    dh = dot(jnp.concatenate(dy, axis=0), mat2[...], (1, 1))
    dp = [(dh[:half] * slope_own[...]).astype(BF16), (dh[half:] * slope[...]).astype(BF16)]
    dv = dot(jnp.concatenate(dp, axis=0), mat1[...], (1, 1)).astype(BF16).astype(F32)
    for side in range(2):
        grad_y[side] = dy[side]
        grad_pre[side] = dp[side]
        place = pl.ds(pl.multiple_of((core if side == 0 else 1 - core) * half, 8), half)
        real[place] = dv[side * half : (side + 1) * half, :LANES]
        imag[place] = dv[side * half : (side + 1) * half, LANES:]
    inner = [
        tuple(ref[pl.ds(k, rows, stride=n_rows), :] for ref in (real, imag)) for k in range(n_rows)
    ]
    for r, band in enumerate(eight_points(inner, 1)):
        by_lat[r] = jnp.concatenate(band, axis=1)
    length = own_field.shape[0]
    bundle[0:length] = own_field[...]
    for i, d in enumerate(ORDER):
        band = pack(by_lat[assign[2 * partner(d) + core]])
        if d:
            outs[i - 1][...] = band.astype(BF16)
        else:
            tail = bundle.shape[0] - FIELD_ROWS
            band = jnp.concatenate([band, jnp.zeros((3 * tail - band.shape[0], LANES), F32)], axis=0)
            band = [band[i * tail : (i + 1) * tail] for i in range(3)]
            bundle[FIELD_ROWS:] = jnp.concatenate(band, axis=1).astype(BF16)


def products_kernel(points0, hidden0, points1, hidden1, grad_pre, grad_y, gw1, gw2, gb1):
    core = lax.rem(lax.axis_index("lat"), 2)
    half = BS // 2
    for ref, grads, values in ((gw1, grad_pre, (points0, points1)), (gw2, grad_y, (hidden0, hidden1))):
        both = dot(grads[0], values[0][...], (0, 0)) + dot(grads[1], values[1][...], (0, 0))
        real = both[:BS, :LANES] + both[LANES : LANES + BS, LANES:]
        imag = both[LANES : LANES + BS, :LANES] - both[:BS, LANES:]
        for c, full in enumerate((real, imag)):
            ref[c] = jnp.where(core == 0, full[:half], full[half:])[:, :BS]
    sums = sum(jnp.sum(grad_pre[side].astype(F32), axis=0, keepdims=True) for side in range(2))
    for c in range(2):
        line = sums[:, c * LANES : (c + 1) * LANES]
        gb1[c : c + 1] = jnp.where(core == 0, line[:, :half], line[:, half:BS])


def compose_kernel(last, three, bundle, table, out, by_block):
    rows = by_block.shape[1]
    own = bundle[FIELD_ROWS:].astype(F32)
    own = jnp.concatenate([own[:, i * LANES : (i + 1) * LANES] for i in range(3)], axis=0)
    chunks = [own[: three.shape[1]]] + [three[i].astype(F32) for i in range(3)]
    for d, chunk in zip(ORDER, chunks):
        by_block[partner(d)] = jnp.concatenate(unpack(chunk, rows), axis=1)
    groups = [
        dense([by_block[n, :, g * LANES : (g + 1) * LANES] for n in range(NB)]) for g in range(2)
    ]
    groups = jnp.concatenate(groups, axis=0).astype(BF16)
    mixed = jnp.dot(table[...], groups, preferred_element_type=F32).astype(BF16)
    whole = bundle[0 : out.shape[0]].astype(F32) + mixed.astype(F32)
    out[...] = jnp.where(lax.axis_index("section") == last, 0.0, whole).astype(BF16)


VMEM = pl.BlockSpec(memory_space=pltpu.VMEM)
HBM = pl.BlockSpec(memory_space=pltpu.HBM)


def call(kernel, outs, scratch, near, far, flops=10**8):
    many = isinstance(outs, tuple)
    many = isinstance(outs, tuple)
    return pl.pallas_call(
        kernel,
        out_shape=outs,
        in_specs=[VMEM] * len(near) + [HBM] * len(far),
        out_specs=tuple([VMEM] * len(outs)) if many else VMEM,
        scratch_shapes=scratch,
        cost_estimate=pl.CostEstimate(flops=flops, bytes_accessed=10**6, transcendentals=0),
        compiler_params=pltpu.CompilerParams(vmem_limit_bytes=32 * 2**20),
    )(*near, *(pltpu.with_memory_space_constraint(x, pltpu.HBM) for x in far))


def scratch_for(*arrays):
    scratch = []
    for x in arrays:
        space = pltpu.SMEM if x.dtype == jnp.int32 else pltpu.VMEM
        scratch.append(space(x.shape, x.dtype))
    return scratch, pltpu.SemaphoreType.DMA((len(arrays),))


def paired_blocks(grad_out, spec_saved, w1, w2, b1, mode_counts, assignment):
    length, width = grad_out.shape[2:]
    n_rows = assignment.shape[0]
    q = spec_saved.shape[3] // (NB * BS)
    rows = 2 * NB * q
    forward, inverse = lon_tables(KM, length)

    def by_part(table):
        table = table.reshape(2, NB, 2, q, length).transpose(0, 2, 1, 3, 4)
        return table.reshape(2 * rows, length).astype(BF16)

    inverse = jnp.asarray(by_part(inverse))
    forward = jnp.asarray(by_part(forward).T)

    def swap(chunks):
        pairs = [[(i, i ^ (2 * d)) for i in range(2 * NB)] for d in ORDER[1:]]
        return [lax.ppermute(chunk, "lat", p) for chunk, p in zip(chunks, pairs)]

    field = grad_out.reshape(length, width)
    shape = jax.ShapeDtypeStruct
    far = (mode_counts, assignment, field, inverse, spec_saved[0])
    scratch, sems = scratch_for(*far)
    sent = call(
        functools.partial(analyse_kernel, q),
        (shape((rows, width), BF16),) * NB,
        scratch + [pltpu.VMEM((NB, rows, width), BF16), sems],
        (),
        far,
    )
    received = [sent[0], *swap([sent[d] for d in ORDER[1:]])]
    far = (mode_counts, assignment, w1[0], w2[0], b1[0], forward)
    scratch, _ = scratch_for(*far)
    far = (*far, field)
    wide = 2 * LANES
    mat1, mat2, bias, field, forward = call(
        functools.partial(ready_kernel, q),
        (
            shape((wide, wide), BF16),
            shape((wide, wide), BF16),
            shape((1, wide), F32),
            shape(field.shape, BF16),
            shape(forward.shape, BF16),
        ),
        scratch + [pltpu.SemaphoreType.DMA((len(far),))],
        (),
        far,
        2 * 10**9,
    )
    own = call(
        join_kernel,
        shape((NB, rows, width), BF16),
        [],
        (*received, bias),
        (),
    )
    other = lax.ppermute(own, "lat", [(i, i ^ 1) for i in range(2 * NB)])
    vectors = shape((NB * rows, wide), BF16)
    slopes = shape((NB * rows, wide), F32)
    by_pair = pltpu.VMEM((NB, rows, wide), F32)
    points0, hidden0, slope0 = call(
        own_kernel,
        (vectors, vectors, slopes),
        [by_pair],
        (*received, mat1, bias),
        (),
        2 * 10**9,
    )
    packed = shape((rows + rows // 2 + 4, LANES), BF16)
    scratch, sems = scratch_for(assignment)
    both = shape((2, NB * rows, wide), BF16)
    tail = -(-packed.shape[0] // 48) * 16
    bundle = shape((FIELD_ROWS + tail, width), BF16)
    *chunks, bundle, points1, hidden1, grad_pre, grad_y = call(
        filter_kernel,
        (packed,) * (NB - 1) + (bundle, vectors, vectors, both, both),
        scratch
        + [
            pltpu.VMEM((n_rows, rows, wide), F32),
            by_pair,
            pltpu.VMEM((NB * rows, wide), F32),
            pltpu.VMEM((n_rows * rows, LANES), F32),
            pltpu.VMEM((n_rows * rows, LANES), F32),
            sems,
        ],
        (*received, other, slope0, mat1, mat2, bias, field),
        (assignment,),
    )
    backs = swap(chunks)
    matrix = shape((2, BS // 2, BS), F32)
    gw1, gw2, gb1 = call(
        products_kernel,
        (matrix, matrix, shape((2, BS // 2), F32)),
        [],
        (points0, hidden0, points1, hidden1, grad_pre, grad_y),
        (),
        2 * 10**9,
    )
    three = call(join_kernel, shape((NB - 1, *packed.shape), BF16), [], backs, ())
    three = turn(three, "section")
    bundle = turn(bundle, "section")
    shifted = call(
        functools.partial(compose_kernel, lax.axis_size("section") - 1),
        shape((length, width), BF16),
        [by_pair],
        (three, bundle, forward),
        (),
    )
    shifted = shifted[None, None]
    return shifted, gw1.swapaxes(1, 2)[None], gw2.swapaxes(1, 2)[None], gb1[None]


def apply_mat(vec, mat):
    return jnp.einsum("kpi,ipj->kpj", vec, mat, preferred_element_type=F32)


def adjoint_mat(vec, mat):
    return jnp.einsum("kpj,ipj->kpi", vec, mat, preferred_element_type=F32)


def outer_sum(left, right):
    return jnp.einsum("kpi,kpj->ipj", left, right, preferred_element_type=F32)


def split_blocks(grad_out, spec_saved, w1, w2, b1, mode_counts, assignment):
    rows_dev = grad_out.shape[1]
    length = grad_out.shape[2]
    width = grad_out.shape[3]
    n_rows = assignment.shape[0]
    pairs_dev = spec_saved.shape[3] // BS
    forward, inverse = (jnp.asarray(t.astype(BF16)) for t in lon_tables(KM, length))
    cosine, sine = (jnp.asarray(t.astype(BF16))[:, assignment] for t in lat_waves(n_rows))
    table = jnp.stack(
        [jnp.stack([cosine, sine], axis=-1), jnp.stack([-sine, cosine], axis=-1)], axis=1
    )
    lat_pos = lax.axis_index("lat")
    lat_count = lax.axis_size("lat")
    own_lat = lax.dynamic_slice_in_dim(assignment, lat_pos * rows_dev, rows_dev)
    active = (jnp.arange(KM, dtype=jnp.int32)[None, :] < mode_counts[own_lat][:, None]).astype(F32)
    cotan = grad_out[0]
    spectral = jnp.einsum(
        "cml,rlni->rcmni",
        inverse,
        cotan.reshape(rows_dev, length, NB, BS),
        preferred_element_type=F32,
    )
    spectral = (spectral * active[:, None, :, None, None]).astype(BF16)
    spectral = spectral.reshape(rows_dev, 2, KM * NB * BS)
    pencil = lax.all_to_all(spectral, "lat", split_axis=2, concat_axis=0, tiled=True)
    pencil = pencil.reshape(n_rows, 2, pairs_dev, BS)
    grad_y = jnp.einsum("kerc,rcpi->kepi", table, pencil, preferred_element_type=F32).astype(BF16)
    saved = spec_saved[0].reshape(n_rows, 2, pairs_dev, BS)
    pair_ids = lat_pos * pairs_dev + jnp.arange(pairs_dev, dtype=jnp.int32)
    owner = (pair_ids % NB)[:, None] == jnp.arange(NB, dtype=jnp.int32)[None, :]
    owner = owner.astype(F32)
    first = jnp.take(w1[0].reshape(2, BS, NB, BS), pair_ids % NB, axis=2)
    second = jnp.take(w2[0].reshape(2, BS, NB, BS), pair_ids % NB, axis=2)
    shift_b = jnp.take(b1[0].reshape(2, NB, BS), pair_ids % NB, axis=1).astype(F32)
    v_r = saved[:, 0]
    v_i = saved[:, 1]
    pre_r = apply_mat(v_r, first[0]) - apply_mat(v_i, first[1]) + shift_b[0][None]
    pre_i = apply_mat(v_i, first[0]) + apply_mat(v_r, first[1]) + shift_b[1][None]
    hid_r = jax.nn.silu(pre_r).astype(BF16)
    hid_i = jax.nn.silu(pre_i).astype(BF16)
    dy_r = grad_y[:, 0]
    dy_i = grad_y[:, 1]
    dh_r = adjoint_mat(dy_r, second[0]) + adjoint_mat(dy_i, second[1])
    dh_i = adjoint_mat(dy_i, second[0]) - adjoint_mat(dy_r, second[1])
    dp_r = (dh_r * silu_slope(pre_r)).astype(BF16)
    dp_i = (dh_i * silu_slope(pre_i)).astype(BF16)
    gw2 = jnp.stack(
        [
            outer_sum(hid_r, dy_r) + outer_sum(hid_i, dy_i),
            outer_sum(hid_r, dy_i) - outer_sum(hid_i, dy_r),
        ]
    )
    gw1 = jnp.stack(
        [outer_sum(v_r, dp_r) + outer_sum(v_i, dp_i), outer_sum(v_r, dp_i) - outer_sum(v_i, dp_r)]
    )
    gb1 = jnp.stack([jnp.sum(dp_r.astype(F32), axis=0), jnp.sum(dp_i.astype(F32), axis=0)])
    dv_r = adjoint_mat(dp_r, first[0]) + adjoint_mat(dp_i, first[1])
    dv_i = adjoint_mat(dp_i, first[0]) - adjoint_mat(dp_r, first[1])
    grad_v = jnp.stack([dv_r, dv_i], axis=1).astype(BF16)
    grad_u = jnp.einsum("kerc,kepi->rcpi", table, grad_v, preferred_element_type=F32).astype(BF16)
    grad_u = grad_u.reshape(n_rows, 2, pairs_dev * BS)
    back = lax.all_to_all(grad_u, "lat", split_axis=0, concat_axis=2, tiled=True)
    back = back.reshape(rows_dev, 2, KM, NB, BS) * active[:, None, :, None, None].astype(BF16)
    mixed = jnp.einsum("cml,rcmni->rlni", forward, back, preferred_element_type=F32)
    mixed = mixed.reshape(rows_dev, length, width).astype(BF16)
    block_w1 = jnp.einsum("pn,cipj->cinj", owner, gw1).reshape(1, 2, BS, width)
    block_w2 = jnp.einsum("pn,cipj->cinj", owner, gw2).reshape(1, 2, BS, width)
    block_b1 = jnp.einsum("pn,cpj->cnj", owner, gb1).reshape(1, 2, width)
    columns = width // lat_count
    full_w1, full_w2, full_b1 = lax.psum((block_w1, block_w2, block_b1), "lat")
    sum_w1 = lax.dynamic_slice_in_dim(full_w1, lat_pos * columns, columns, 3)
    sum_w2 = lax.dynamic_slice_in_dim(full_w2, lat_pos * columns, columns, 3)
    sum_b1 = lax.dynamic_slice_in_dim(full_b1, lat_pos * columns, columns, 2)
    whole = (cotan.astype(F32) + mixed.astype(F32)).astype(BF16)
    received = from_behind(whole[None], "section", -1)
    return (received, sum_w1, sum_w2, sum_b1)


def per_device(grad_out, spec_saved, w1, w2, b1, mode_counts, assignment):
    n_dev = lax.axis_size("lat")
    pairs_dev = spec_saved.shape[3] // BS
    paired = n_dev == 2 * NB and grad_out.shape[1] == 1 and pairs_dev % NB == 0
    body = paired_blocks if paired else split_blocks
    return body(grad_out, spec_saved, w1, w2, b1, mode_counts, assignment)


def solution(mesh):
    return jax.shard_map(
        per_device,
        mesh=mesh,
        in_specs=(
            P("section", "lat", None, None),
            P("section", None, None, "lat"),
            P("section", None, None, None),
            P("section", None, None, None),
            P("section", None, None),
            P(),
            P(),
        ),
        out_specs=(
            P("section", "lat", None, None),
            P("section", None, None, "lat"),
            P("section", None, None, "lat"),
            P("section", None, "lat"),
        ),
        check_vma=False,
    )
```

```python
import functools
import math

import jax
import jax.numpy as jnp
import numpy as np
from jax import lax
from jax.experimental import pallas as pl
from jax.experimental.pallas import tpu as pltpu
from jax.sharding import PartitionSpec as P

NB = 4
BS = 96
KM = 72
LANES = 128
F32 = jnp.float32
BF16 = jnp.bfloat16


def from_behind(value, axis, by):
    length = lax.axis_size(axis)
    pairs = [(i, i + by) for i in range(length) if 0 <= i + by < length]
    return lax.ppermute(value, axis, pairs)


def turn(value, axis):
    length = lax.axis_size(axis)
    return lax.ppermute(value, axis, [(i, (i - 1) % length) for i in range(length)])


def lon_tables(n_modes, length):
    modes = np.arange(n_modes)
    phase = modes[:, None] * np.arange(length)[None, :] % length
    angle = phase * (2.0 * math.pi / length)
    forward = np.stack([np.cos(angle), -np.sin(angle)]) / math.sqrt(length)
    weight = np.where(modes == 0, 1.0, 2.0)[None, :, None]
    return forward, forward * weight


def lat_waves(n_rows):
    freqs = np.arange(n_rows)
    angle = (freqs[:, None] * freqs[None, :] % n_rows) * (2.0 * math.pi / n_rows)
    factor = 1.0 / math.sqrt(n_rows)
    return np.cos(angle) * factor, np.sin(angle) * factor


def silu_slope(pre):
    sig = jax.nn.sigmoid(pre)
    return sig * (1.0 + pre * (1.0 - sig))


def window(x, start):
    low = start // LANES * LANES
    shift = start - low
    if shift == 0:
        return x[:, low : low + LANES]
    if shift + BS <= LANES:
        return pltpu.roll(x[:, low : low + LANES], LANES - shift, 1)
    return pltpu.roll(x[:, low : low + 2 * LANES], 2 * LANES - shift, 1)[:, :LANES]


def dense(parts):
    lane = lax.broadcasted_iota(jnp.int32, parts[0].shape, 1)
    first = pltpu.roll(parts[1], 96, 1)
    second = pltpu.roll(parts[2], 64, 1)
    third = pltpu.roll(parts[3], 32, 1)
    return jnp.concatenate(
        [
            jnp.where(lane < 96, parts[0], first),
            jnp.where(lane < 64, first, second),
            jnp.where(lane < 32, second, third),
        ],
        axis=1,
    )


def dot(a, b, contract):
    return lax.dot_general(a, b, ((contract[:1], contract[1:]), ((), ())), preferred_element_type=F32)


def mode_numbers(shape, axis, q):
    number = lax.broadcasted_iota(jnp.int32, shape, axis)
    second = number >= NB * q
    number = jnp.where(second, number - NB * q, number)
    mode = number
    for z in range(1, NB):
        mode = jnp.where(number >= z * q, number + z * q, mode)
    return jnp.where(second, mode + q, mode)


def eight_points(x, sign):
    root = float(np.float32(1.0 / math.sqrt(8.0)).astype(BF16))

    def add(a, b):
        return a[0] + b[0], a[1] + b[1]

    def sub(a, b):
        return a[0] - b[0], a[1] - b[1]

    def times_i(a, by):
        return (-a[1], a[0]) if by > 0 else (a[1], -a[0])

    def scale(a, by):
        return a[0] * by, a[1] * by

    def four(a, b, c, d):
        total, far, other, near = add(a, c), sub(a, c), add(b, d), sub(b, d)
        near = times_i(near, sign)
        return add(total, other), add(far, near), sub(total, other), sub(far, near)

    even = [scale(a, root) for a in four(*x[0::2])]
    odd = four(*x[1::2])
    turned = [
        scale(odd[0], root),
        scale(add(odd[1], times_i(odd[1], sign)), 0.25),
        scale(times_i(odd[2], sign), root),
        scale(sub(times_i(odd[3], sign), odd[3]), 0.25),
    ]
    return [add(a, b) for a, b in zip(even, turned)] + [sub(a, b) for a, b in zip(even, turned)]


def fetch(sems, sources, targets):
    copies = [
        pltpu.make_async_copy(source, target, sems.at[i])
        for i, (source, target) in enumerate(zip(sources, targets))
    ]
    for copy in copies:
        copy.start()
    return copies


def wait(copies):
    for copy in copies:
        copy.wait()


def partner(d):
    return jnp.bitwise_xor(lax.axis_index("lat") // 2, d)


def analyse_kernel(q, *refs):
    hbm, outs, held, (lines, by_block, sems) = refs[:5], refs[5:9], refs[9:14], refs[14:]
    counts, assign, field, table, saved = held
    copies = fetch(sems, hbm, held)
    wait(copies[4:])
    n_rows, _, columns = saved.shape
    both = saved[...].reshape(2 * n_rows, columns).astype(F32)
    tiles = range(columns // LANES)
    for i in tiles:
        lines[i] = both[:, i * LANES : (i + 1) * LANES]
    parts = [
        jnp.concatenate([lines[i, pl.ds(c, n_rows, stride=2), :] for i in tiles], axis=1)
        for c in range(2)
    ]
    points = [
        [
            jnp.concatenate([window(part, (mm * NB + n) * BS) for mm in range(q)], axis=0)
            for part in parts
        ]
        for n in range(NB)
    ]
    wait(copies[:4])
    rows = by_block.shape[1]
    spectral = jnp.dot(table[...], field[...], preferred_element_type=F32)
    active = counts[assign[lax.axis_index("lat")]]
    held_modes = mode_numbers((rows, spectral.shape[1]), 0, q) < active
    spectra = [jnp.where(held_modes, spectral[c * rows : (c + 1) * rows], 0.0) for c in range(2)]
    for n in range(NB):
        pieces = [window(spectrum, n * BS) for spectrum in spectra]
        by_block[n] = dense(pieces + points[n]).astype(BF16)
    for d, out in enumerate(outs):
        out[...] = by_block[partner(d)]


def ready_kernel(q, *refs):
    hbm, (mat1, mat2, bias, own_field, own_table) = refs[:7], refs[7:12]
    counts, assign, w1, w2, b1, table, sems = refs[12:]
    copies = fetch(sems, hbm, (counts, assign, w1, w2, b1, table, own_field))
    wait(copies[:6])
    active = counts[assign[lax.axis_index("lat")]]
    rows = table.shape[1] // 2
    held_modes = mode_numbers((table.shape[0], rows), 1, q) < active
    for c in range(2):
        part = table[:, c * rows : (c + 1) * rows].astype(F32)
        own_table[:, c * rows : (c + 1) * rows] = jnp.where(held_modes, part, 0.0).astype(BF16)
    block = lax.axis_index("lat") // 2

    def pick(x):
        value = window(x, 0)
        for n in range(1, NB):
            value = jnp.where(block == n, window(x, n * BS), value)
        lane = lax.broadcasted_iota(jnp.int32, value.shape, 1)
        return jnp.where(lane < BS, value, 0.0)

    gap = jnp.zeros((LANES - BS, 2 * LANES), BF16)
    for source, mat in ((w1, mat1), (w2, mat2)):
        real, imag = (pick(source[c].astype(F32)) for c in range(2))
        mat[0:BS] = jnp.concatenate([real, imag], axis=1).astype(BF16)
        mat[BS:LANES] = gap
        mat[LANES : LANES + BS] = jnp.concatenate([-imag, real], axis=1).astype(BF16)
        mat[LANES + BS : 2 * LANES] = gap
    shift_b = pick(b1[...].astype(F32))
    bias[...] = jnp.concatenate([shift_b[0:1], shift_b[1:2]], axis=1)
    wait(copies[6:])


ORDER = (0, 3, 2, 1)
FIELD_ROWS = 192


def join_kernel(*refs):
    out = refs[-1]
    for i in range(out.shape[0]):
        out[i] = refs[i][...]


def pack(band):
    rows = band.shape[0]
    tail = rows // 2 + 4
    left, right = band[:, :LANES], pltpu.roll(band[:, LANES:], 96, 1)
    lane = lax.broadcasted_iota(jnp.int32, left.shape, 1)
    upper = jnp.where(lane < 96, left, right)
    lower = pltpu.roll(right[rows - tail :], 64, 1)
    lower = jnp.where(lane[:tail] < 64, right[:tail], lower)
    return jnp.concatenate([upper, lower], axis=0)


def unpack(packed, rows):
    tail = rows // 2 + 4
    upper, lower = packed[:rows], packed[rows:]
    rest = jnp.concatenate([lower, pltpu.roll(lower, 64, 1)[2 * tail - rows :]], axis=0)
    lane = lax.broadcasted_iota(jnp.int32, upper.shape, 1)
    right = jnp.where(lane < 32, pltpu.roll(upper, 32, 1), pltpu.roll(rest, 32, 1))
    return [upper, right]


def silu_points(chunks, mat, bias, by_pair, points, hidden, slope):
    for d, chunk in enumerate(chunks):
        parts = [window(chunk, j * BS) for j in (2, 3)]
        by_pair[partner(d)] = jnp.concatenate(parts, axis=1)
    v = by_pair[...].reshape(points.shape).astype(BF16)
    pre = dot(v, mat[...], (1, 0)) + bias[...]
    sig = jax.nn.sigmoid(pre)
    points[...] = v
    hidden[...] = (pre * sig).astype(BF16)
    slope[...] = sig * (1.0 + pre * (1.0 - sig))


def row_spectrum(chunk):
    return jnp.concatenate([window(chunk, j * BS) for j in range(2)], axis=1)


def own_kernel(*refs):
    mat1, bias, points, hidden, slope, spectra, by_pair = refs[NB:]
    chunks = [refs[i][...].astype(F32) for i in ORDER]
    silu_points(chunks, mat1, bias, by_pair, points, hidden, slope)
    for d, chunk in enumerate(chunks):
        spectra[d] = row_spectrum(chunk)


def filter_kernel(*refs):
    spectra, other, slope_own, mat1, mat2, bias, own_field, assign_hbm = refs[:8]
    outs, (bundle, points, hidden, grad_pre, grad_y) = refs[8:11], refs[11:16]
    assign, by_lat, by_pair, slope, real, imag, sems = refs[16:]
    copies = fetch(sems, (assign_hbm,), (assign,))
    core = lax.rem(lax.axis_index("lat"), 2)
    chunks = [other[i].astype(F32) for i in ORDER]
    silu_points(chunks, mat1, bias, by_pair, points, hidden, slope)
    wait(copies)
    for d, chunk in enumerate(chunks):
        by_lat[assign[2 * partner(d) + core]] = spectra[d]
        by_lat[assign[2 * partner(d) + 1 - core]] = row_spectrum(chunk)
    n_rows, rows, _ = by_lat.shape
    half = rows * n_rows // 2
    waves = eight_points([(by_lat[r][:, :LANES], by_lat[r][:, LANES:]) for r in range(n_rows)], -1)
    for k, wave in enumerate(waves):
        real[k * rows : (k + 1) * rows] = wave[0]
        imag[k * rows : (k + 1) * rows] = wave[1]
    dy = [
        jnp.concatenate([ref[pl.ds(m, n_rows, stride=rows), :] for m in range(rows)], axis=0)
        for ref in (real, imag)
    ]
    dy = jnp.concatenate(dy, axis=1).astype(BF16)
    dy = [jnp.where(core == side, dy[:half], dy[half:]) for side in range(2)]
    dh = dot(jnp.concatenate(dy, axis=0), mat2[...], (1, 1))
    dp = [(dh[:half] * slope_own[...]).astype(BF16), (dh[half:] * slope[...]).astype(BF16)]
    dv = dot(jnp.concatenate(dp, axis=0), mat1[...], (1, 1)).astype(BF16).astype(F32)
    for side in range(2):
        grad_y[side] = dy[side]
        grad_pre[side] = dp[side]
        place = pl.ds(pl.multiple_of((core if side == 0 else 1 - core) * half, 8), half)
        real[place] = dv[side * half : (side + 1) * half, :LANES]
        imag[place] = dv[side * half : (side + 1) * half, LANES:]
    inner = [
        tuple(ref[pl.ds(k, rows, stride=n_rows), :] for ref in (real, imag)) for k in range(n_rows)
    ]
    for r, band in enumerate(eight_points(inner, 1)):
        by_lat[r] = jnp.concatenate(band, axis=1)
    length = own_field.shape[0]
    bundle[0:length] = own_field[...]
    for i, d in enumerate(ORDER):
        band = pack(by_lat[assign[2 * partner(d) + core]])
        if d:
            outs[i - 1][...] = band.astype(BF16)
        else:
            tail = bundle.shape[0] - FIELD_ROWS
            band = jnp.concatenate([band, jnp.zeros((3 * tail - band.shape[0], LANES), F32)], axis=0)
            band = [band[i * tail : (i + 1) * tail] for i in range(3)]
            bundle[FIELD_ROWS:] = jnp.concatenate(band, axis=1).astype(BF16)


def products_kernel(points0, hidden0, points1, hidden1, grad_pre, grad_y, gw1, gw2, gb1):
    core = lax.rem(lax.axis_index("lat"), 2)
    half = BS // 2
    for ref, grads, values in ((gw1, grad_pre, (points0, points1)), (gw2, grad_y, (hidden0, hidden1))):
        both = dot(grads[0], values[0][...], (0, 0)) + dot(grads[1], values[1][...], (0, 0))
        real = both[:BS, :LANES] + both[LANES : LANES + BS, LANES:]
        imag = both[LANES : LANES + BS, :LANES] - both[:BS, LANES:]
        for c, full in enumerate((real, imag)):
            ref[c] = jnp.where(core == 0, full[:half], full[half:])[:, :BS]
    sums = sum(jnp.sum(grad_pre[side].astype(F32), axis=0, keepdims=True) for side in range(2))
    for c in range(2):
        line = sums[:, c * LANES : (c + 1) * LANES]
        gb1[c : c + 1] = jnp.where(core == 0, line[:, :half], line[:, half:BS])


def compose_kernel(last, three, bundle, table, out, by_block):
    rows = by_block.shape[1]
    own = bundle[FIELD_ROWS:].astype(F32)
    own = jnp.concatenate([own[:, i * LANES : (i + 1) * LANES] for i in range(3)], axis=0)
    chunks = [own[: three.shape[1]]] + [three[i].astype(F32) for i in range(3)]
    for d, chunk in zip(ORDER, chunks):
        by_block[partner(d)] = jnp.concatenate(unpack(chunk, rows), axis=1)
    groups = [
        dense([by_block[n, :, g * LANES : (g + 1) * LANES] for n in range(NB)]) for g in range(2)
    ]
    groups = jnp.concatenate(groups, axis=0).astype(BF16)
    mixed = jnp.dot(table[...], groups, preferred_element_type=F32).astype(BF16)
    whole = bundle[0 : out.shape[0]].astype(F32) + mixed.astype(F32)
    out[...] = jnp.where(lax.axis_index("section") == last, 0.0, whole).astype(BF16)


VMEM = pl.BlockSpec(memory_space=pltpu.VMEM)
HBM = pl.BlockSpec(memory_space=pltpu.HBM)


def call(kernel, outs, scratch, near, far, flops=10**8):
    many = isinstance(outs, tuple)
    many = isinstance(outs, tuple)
    return pl.pallas_call(
        kernel,
        out_shape=outs,
        in_specs=[VMEM] * len(near) + [HBM] * len(far),
        out_specs=tuple([VMEM] * len(outs)) if many else VMEM,
        scratch_shapes=scratch,
        cost_estimate=pl.CostEstimate(flops=flops, bytes_accessed=10**6, transcendentals=0),
        compiler_params=pltpu.CompilerParams(vmem_limit_bytes=32 * 2**20),
    )(*near, *(pltpu.with_memory_space_constraint(x, pltpu.HBM) for x in far))


def scratch_for(*arrays):
    scratch = []
    for x in arrays:
        space = pltpu.SMEM if x.dtype == jnp.int32 else pltpu.VMEM
        scratch.append(space(x.shape, x.dtype))
    return scratch, pltpu.SemaphoreType.DMA((len(arrays),))


def paired_blocks(grad_out, spec_saved, w1, w2, b1, mode_counts, assignment):
    length, width = grad_out.shape[2:]
    n_rows = assignment.shape[0]
    q = spec_saved.shape[3] // (NB * BS)
    rows = 2 * NB * q
    forward, inverse = lon_tables(KM, length)

    def by_part(table):
        table = table.reshape(2, NB, 2, q, length).transpose(0, 2, 1, 3, 4)
        return table.reshape(2 * rows, length).astype(BF16)

    inverse = jnp.asarray(by_part(inverse))
    forward = jnp.asarray(by_part(forward).T)

    def swap(chunks):
        pairs = [[(i, i ^ (2 * d)) for i in range(2 * NB)] for d in ORDER[1:]]
        return [lax.ppermute(chunk, "lat", p) for chunk, p in zip(chunks, pairs)]

    field = grad_out.reshape(length, width)
    shape = jax.ShapeDtypeStruct
    far = (mode_counts, assignment, field, inverse, spec_saved[0])
    scratch, sems = scratch_for(*far)
    scratch.append(pltpu.VMEM((spec_saved.shape[3] // LANES, 2 * n_rows, LANES), F32))
    sent = call(
        functools.partial(analyse_kernel, q),
        (shape((rows, width), BF16),) * NB,
        scratch + [pltpu.VMEM((NB, rows, width), BF16), sems],
        (),
        far,
    )
    received = [sent[0], *swap([sent[d] for d in ORDER[1:]])]
    far = (mode_counts, assignment, w1[0], w2[0], b1[0], forward)
    scratch, _ = scratch_for(*far)
    far = (*far, field)
    wide = 2 * LANES
    mat1, mat2, bias, field, forward = call(
        functools.partial(ready_kernel, q),
        (
            shape((wide, wide), BF16),
            shape((wide, wide), BF16),
            shape((1, wide), F32),
            shape(field.shape, BF16),
            shape(forward.shape, BF16),
        ),
        scratch + [pltpu.SemaphoreType.DMA((len(far),))],
        (),
        far,
        2 * 10**9,
    )
    own = call(
        join_kernel,
        shape((NB, rows, width), BF16),
        [],
        (*received, bias),
        (),
    )
    other = lax.ppermute(own, "lat", [(i, i ^ 1) for i in range(2 * NB)])
    vectors = shape((NB * rows, wide), BF16)
    slopes = shape((NB * rows, wide), F32)
    by_pair = pltpu.VMEM((NB, rows, wide), F32)
    points0, hidden0, slope0, spectra = call(
        own_kernel,
        (vectors, vectors, slopes, shape((NB, rows, wide), F32)),
        [by_pair],
        (*received, mat1, bias),
        (),
        2 * 10**9,
    )
    packed = shape((rows + rows // 2 + 4, LANES), BF16)
    scratch, sems = scratch_for(assignment)
    both = shape((2, NB * rows, wide), BF16)
    tail = -(-packed.shape[0] // 48) * 16
    bundle = shape((FIELD_ROWS + tail, width), BF16)
    *chunks, bundle, points1, hidden1, grad_pre, grad_y = call(
        filter_kernel,
        (packed,) * (NB - 1) + (bundle, vectors, vectors, both, both),
        scratch
        + [
            pltpu.VMEM((n_rows, rows, wide), F32),
            by_pair,
            pltpu.VMEM((NB * rows, wide), F32),
            pltpu.VMEM((n_rows * rows, LANES), F32),
            pltpu.VMEM((n_rows * rows, LANES), F32),
            sems,
        ],
        (spectra, other, slope0, mat1, mat2, bias, field),
        (assignment,),
    )
    backs = swap(chunks)
    matrix = shape((2, BS // 2, BS), F32)
    gw1, gw2, gb1 = call(
        products_kernel,
        (matrix, matrix, shape((2, BS // 2), F32)),
        [],
        (points0, hidden0, points1, hidden1, grad_pre, grad_y),
        (),
        2 * 10**9,
    )
    three = call(join_kernel, shape((NB - 1, *packed.shape), BF16), [], backs, ())
    three = turn(three, "section")
    bundle = turn(bundle, "section")
    shifted = call(
        functools.partial(compose_kernel, lax.axis_size("section") - 1),
        shape((length, width), BF16),
        [by_pair],
        (three, bundle, forward),
        (),
    )
    shifted = shifted[None, None]
    return shifted, gw1.swapaxes(1, 2)[None], gw2.swapaxes(1, 2)[None], gb1[None]


def apply_mat(vec, mat):
    return jnp.einsum("kpi,ipj->kpj", vec, mat, preferred_element_type=F32)


def adjoint_mat(vec, mat):
    return jnp.einsum("kpj,ipj->kpi", vec, mat, preferred_element_type=F32)


def outer_sum(left, right):
    return jnp.einsum("kpi,kpj->ipj", left, right, preferred_element_type=F32)


def split_blocks(grad_out, spec_saved, w1, w2, b1, mode_counts, assignment):
    rows_dev = grad_out.shape[1]
    length = grad_out.shape[2]
    width = grad_out.shape[3]
    n_rows = assignment.shape[0]
    pairs_dev = spec_saved.shape[3] // BS
    forward, inverse = (jnp.asarray(t.astype(BF16)) for t in lon_tables(KM, length))
    cosine, sine = (jnp.asarray(t.astype(BF16))[:, assignment] for t in lat_waves(n_rows))
    table = jnp.stack(
        [jnp.stack([cosine, sine], axis=-1), jnp.stack([-sine, cosine], axis=-1)], axis=1
    )
    lat_pos = lax.axis_index("lat")
    lat_count = lax.axis_size("lat")
    own_lat = lax.dynamic_slice_in_dim(assignment, lat_pos * rows_dev, rows_dev)
    active = (jnp.arange(KM, dtype=jnp.int32)[None, :] < mode_counts[own_lat][:, None]).astype(F32)
    cotan = grad_out[0]
    spectral = jnp.einsum(
        "cml,rlni->rcmni",
        inverse,
        cotan.reshape(rows_dev, length, NB, BS),
        preferred_element_type=F32,
    )
    spectral = (spectral * active[:, None, :, None, None]).astype(BF16)
    spectral = spectral.reshape(rows_dev, 2, KM * NB * BS)
    pencil = lax.all_to_all(spectral, "lat", split_axis=2, concat_axis=0, tiled=True)
    pencil = pencil.reshape(n_rows, 2, pairs_dev, BS)
    grad_y = jnp.einsum("kerc,rcpi->kepi", table, pencil, preferred_element_type=F32).astype(BF16)
    saved = spec_saved[0].reshape(n_rows, 2, pairs_dev, BS)
    pair_ids = lat_pos * pairs_dev + jnp.arange(pairs_dev, dtype=jnp.int32)
    owner = (pair_ids % NB)[:, None] == jnp.arange(NB, dtype=jnp.int32)[None, :]
    owner = owner.astype(F32)
    first = jnp.take(w1[0].reshape(2, BS, NB, BS), pair_ids % NB, axis=2)
    second = jnp.take(w2[0].reshape(2, BS, NB, BS), pair_ids % NB, axis=2)
    shift_b = jnp.take(b1[0].reshape(2, NB, BS), pair_ids % NB, axis=1).astype(F32)
    v_r = saved[:, 0]
    v_i = saved[:, 1]
    pre_r = apply_mat(v_r, first[0]) - apply_mat(v_i, first[1]) + shift_b[0][None]
    pre_i = apply_mat(v_i, first[0]) + apply_mat(v_r, first[1]) + shift_b[1][None]
    hid_r = jax.nn.silu(pre_r).astype(BF16)
    hid_i = jax.nn.silu(pre_i).astype(BF16)
    dy_r = grad_y[:, 0]
    dy_i = grad_y[:, 1]
    dh_r = adjoint_mat(dy_r, second[0]) + adjoint_mat(dy_i, second[1])
    dh_i = adjoint_mat(dy_i, second[0]) - adjoint_mat(dy_r, second[1])
    dp_r = (dh_r * silu_slope(pre_r)).astype(BF16)
    dp_i = (dh_i * silu_slope(pre_i)).astype(BF16)
    gw2 = jnp.stack(
        [
            outer_sum(hid_r, dy_r) + outer_sum(hid_i, dy_i),
            outer_sum(hid_r, dy_i) - outer_sum(hid_i, dy_r),
        ]
    )
    gw1 = jnp.stack(
        [outer_sum(v_r, dp_r) + outer_sum(v_i, dp_i), outer_sum(v_r, dp_i) - outer_sum(v_i, dp_r)]
    )
    gb1 = jnp.stack([jnp.sum(dp_r.astype(F32), axis=0), jnp.sum(dp_i.astype(F32), axis=0)])
    dv_r = adjoint_mat(dp_r, first[0]) + adjoint_mat(dp_i, first[1])
    dv_i = adjoint_mat(dp_i, first[0]) - adjoint_mat(dp_r, first[1])
    grad_v = jnp.stack([dv_r, dv_i], axis=1).astype(BF16)
    grad_u = jnp.einsum("kerc,kepi->rcpi", table, grad_v, preferred_element_type=F32).astype(BF16)
    grad_u = grad_u.reshape(n_rows, 2, pairs_dev * BS)
    back = lax.all_to_all(grad_u, "lat", split_axis=0, concat_axis=2, tiled=True)
    back = back.reshape(rows_dev, 2, KM, NB, BS) * active[:, None, :, None, None].astype(BF16)
    mixed = jnp.einsum("cml,rcmni->rlni", forward, back, preferred_element_type=F32)
    mixed = mixed.reshape(rows_dev, length, width).astype(BF16)
    block_w1 = jnp.einsum("pn,cipj->cinj", owner, gw1).reshape(1, 2, BS, width)
    block_w2 = jnp.einsum("pn,cipj->cinj", owner, gw2).reshape(1, 2, BS, width)
    block_b1 = jnp.einsum("pn,cpj->cnj", owner, gb1).reshape(1, 2, width)
    columns = width // lat_count
    full_w1, full_w2, full_b1 = lax.psum((block_w1, block_w2, block_b1), "lat")
    sum_w1 = lax.dynamic_slice_in_dim(full_w1, lat_pos * columns, columns, 3)
    sum_w2 = lax.dynamic_slice_in_dim(full_w2, lat_pos * columns, columns, 3)
    sum_b1 = lax.dynamic_slice_in_dim(full_b1, lat_pos * columns, columns, 2)
    whole = (cotan.astype(F32) + mixed.astype(F32)).astype(BF16)
    received = from_behind(whole[None], "section", -1)
    return (received, sum_w1, sum_w2, sum_b1)


def per_device(grad_out, spec_saved, w1, w2, b1, mode_counts, assignment):
    n_dev = lax.axis_size("lat")
    pairs_dev = spec_saved.shape[3] // BS
    paired = n_dev == 2 * NB and grad_out.shape[1] == 1 and pairs_dev % NB == 0
    body = paired_blocks if paired else split_blocks
    return body(grad_out, spec_saved, w1, w2, b1, mode_counts, assignment)


def solution(mesh):
    return jax.shard_map(
        per_device,
        mesh=mesh,
        in_specs=(
            P("section", "lat", None, None),
            P("section", None, None, "lat"),
            P("section", None, None, None),
            P("section", None, None, None),
            P("section", None, None),
            P(),
            P(),
        ),
        out_specs=(
            P("section", "lat", None, None),
            P("section", None, None, "lat"),
            P("section", None, None, "lat"),
            P("section", None, "lat"),
        ),
        check_vma=False,
    )
```

```python
import functools
import math

import jax
import jax.numpy as jnp
import numpy as np
from jax import lax
from jax.experimental import pallas as pl
from jax.experimental.pallas import tpu as pltpu
from jax.sharding import PartitionSpec as P

NB = 4
BS = 96
KM = 72
LANES = 128
F32 = jnp.float32
BF16 = jnp.bfloat16


def from_behind(value, axis, by):
    length = lax.axis_size(axis)
    pairs = [(i, i + by) for i in range(length) if 0 <= i + by < length]
    return lax.ppermute(value, axis, pairs)


def turn(value, axis):
    length = lax.axis_size(axis)
    return lax.ppermute(value, axis, [(i, (i - 1) % length) for i in range(length)])


def lon_tables(n_modes, length):
    modes = np.arange(n_modes)
    phase = modes[:, None] * np.arange(length)[None, :] % length
    angle = phase * (2.0 * math.pi / length)
    forward = np.stack([np.cos(angle), -np.sin(angle)]) / math.sqrt(length)
    weight = np.where(modes == 0, 1.0, 2.0)[None, :, None]
    return forward, forward * weight


def lat_waves(n_rows):
    freqs = np.arange(n_rows)
    angle = (freqs[:, None] * freqs[None, :] % n_rows) * (2.0 * math.pi / n_rows)
    factor = 1.0 / math.sqrt(n_rows)
    return np.cos(angle) * factor, np.sin(angle) * factor


def silu_slope(pre):
    sig = jax.nn.sigmoid(pre)
    return sig * (1.0 + pre * (1.0 - sig))


def window(x, start):
    low = start // LANES * LANES
    shift = start - low
    if shift == 0:
        return x[:, low : low + LANES]
    if shift + BS <= LANES:
        return pltpu.roll(x[:, low : low + LANES], LANES - shift, 1)
    return pltpu.roll(x[:, low : low + 2 * LANES], 2 * LANES - shift, 1)[:, :LANES]


def dense(parts):
    lane = lax.broadcasted_iota(jnp.int32, parts[0].shape, 1)
    first = pltpu.roll(parts[1], 96, 1)
    second = pltpu.roll(parts[2], 64, 1)
    third = pltpu.roll(parts[3], 32, 1)
    return jnp.concatenate(
        [
            jnp.where(lane < 96, parts[0], first),
            jnp.where(lane < 64, first, second),
            jnp.where(lane < 32, second, third),
        ],
        axis=1,
    )


def dot(a, b, contract):
    return lax.dot_general(a, b, ((contract[:1], contract[1:]), ((), ())), preferred_element_type=F32)


def mode_numbers(shape, axis, q):
    number = lax.broadcasted_iota(jnp.int32, shape, axis)
    second = number >= NB * q
    number = jnp.where(second, number - NB * q, number)
    mode = number
    for z in range(1, NB):
        mode = jnp.where(number >= z * q, number + z * q, mode)
    return jnp.where(second, mode + q, mode)


def eight_points(x, sign):
    root = float(np.float32(1.0 / math.sqrt(8.0)).astype(BF16))

    def add(a, b):
        return a[0] + b[0], a[1] + b[1]

    def sub(a, b):
        return a[0] - b[0], a[1] - b[1]

    def times_i(a, by):
        return (-a[1], a[0]) if by > 0 else (a[1], -a[0])

    def scale(a, by):
        return a[0] * by, a[1] * by

    def four(a, b, c, d):
        total, far, other, near = add(a, c), sub(a, c), add(b, d), sub(b, d)
        near = times_i(near, sign)
        return add(total, other), add(far, near), sub(total, other), sub(far, near)

    even = [scale(a, root) for a in four(*x[0::2])]
    odd = four(*x[1::2])
    turned = [
        scale(odd[0], root),
        scale(add(odd[1], times_i(odd[1], sign)), 0.25),
        scale(times_i(odd[2], sign), root),
        scale(sub(times_i(odd[3], sign), odd[3]), 0.25),
    ]
    return [add(a, b) for a, b in zip(even, turned)] + [sub(a, b) for a, b in zip(even, turned)]


def fetch(sems, sources, targets):
    copies = [
        pltpu.make_async_copy(source, target, sems.at[i])
        for i, (source, target) in enumerate(zip(sources, targets))
    ]
    for copy in copies:
        copy.start()
    return copies


def fetch_parts(sems, source, target, parts):
    return fetch(sems, [source.at[part] for part in parts], [target.at[part] for part in parts])


def columns(width):
    return [(slice(None), pl.ds(i, LANES)) for i in range(0, width, LANES)]


def wait(copies):
    for copy in copies:
        copy.wait()


def partner(d):
    return jnp.bitwise_xor(lax.axis_index("lat") // 2, d)


def analyse_kernel(q, *refs):
    hbm, outs, held = refs[:5], refs[5:9], refs[9:14]
    by_block, few, sems = refs[14:]
    counts, assign, field, table, saved = held
    early = fetch_parts(sems.at[0], hbm[4], saved, [pl.ds(k, 2) for k in range(0, 2 * NB, 2)])
    late = fetch_parts(sems.at[1], hbm[2], field, columns(field.shape[1]))
    late += fetch(few, hbm[:2] + hbm[3:4], held[:2] + held[3:4])
    wait(early)
    parts = [saved[:, c, :].astype(F32) for c in range(2)]
    points = [
        [
            jnp.concatenate([window(part, (mm * NB + n) * BS) for mm in range(q)], axis=0)
            for part in parts
        ]
        for n in range(NB)
    ]
    wait(late)
    rows = by_block.shape[1]
    spectral = jnp.dot(table[...], field[...], preferred_element_type=F32)
    active = counts[assign[lax.axis_index("lat")]]
    held_modes = mode_numbers((rows, spectral.shape[1]), 0, q) < active
    spectra = [jnp.where(held_modes, spectral[c * rows : (c + 1) * rows], 0.0) for c in range(2)]
    for n in range(NB):
        pieces = [window(spectrum, n * BS) for spectrum in spectra]
        by_block[n] = dense(pieces + points[n]).astype(BF16)
    for d, out in enumerate(outs):
        out[...] = by_block[partner(d)]


def ready_kernel(q, *refs):
    hbm, (mat1, turned1, turned2, bias, own_field, own_table) = refs[:7], refs[7:13]
    counts, assign, w1, w2, b1, table, sems = refs[13:]
    copies = fetch(sems, hbm, (counts, assign, w1, w2, b1, table, own_field))
    wait(copies[:6])
    active = counts[assign[lax.axis_index("lat")]]
    rows = table.shape[1] // 2
    held_modes = mode_numbers((table.shape[0], rows), 1, q) < active
    for c in range(2):
        part = table[:, c * rows : (c + 1) * rows].astype(F32)
        own_table[:, c * rows : (c + 1) * rows] = jnp.where(held_modes, part, 0.0).astype(BF16)
    block = lax.axis_index("lat") // 2

    def pick(x):
        value = window(x, 0)
        for n in range(1, NB):
            value = jnp.where(block == n, window(x, n * BS), value)
        lane = lax.broadcasted_iota(jnp.int32, value.shape, 1)
        return jnp.where(lane < BS, value, 0.0)

    gap = jnp.zeros((LANES - BS, 2 * LANES), F32)
    for source, mat, turned in ((w1, mat1, turned1), (w2, None, turned2)):
        real, imag = (pick(source[c].astype(F32)) for c in range(2))
        whole = [
            jnp.concatenate([real, imag], axis=1),
            gap,
            jnp.concatenate([-imag, real], axis=1),
            gap,
        ]
        whole = jnp.concatenate(whole, axis=0)
        turned[...] = whole.T.astype(BF16)
        if mat is not None:
            mat[...] = whole.astype(BF16)
    shift_b = pick(b1[...].astype(F32))
    bias[...] = jnp.concatenate([shift_b[0:1], shift_b[1:2]], axis=1)
    wait(copies[6:])


ORDER = (0, 3, 2, 1)
FIELD_ROWS = 192


def join_kernel(*refs):
    out = refs[-1]
    for i in range(out.shape[0]):
        out[i] = refs[i][...]


def pack(band):
    rows = band.shape[0]
    tail = rows // 2 + 4
    left, right = band[:, :LANES], pltpu.roll(band[:, LANES:], 96, 1)
    lane = lax.broadcasted_iota(jnp.int32, left.shape, 1)
    upper = jnp.where(lane < 96, left, right)
    lower = pltpu.roll(right[rows - tail :], 64, 1)
    lower = jnp.where(lane[:tail] < 64, right[:tail], lower)
    return jnp.concatenate([upper, lower], axis=0)


def unpack(packed, rows):
    tail = rows // 2 + 4
    upper, lower = packed[:rows], packed[rows:]
    rest = jnp.concatenate([lower, pltpu.roll(lower, 64, 1)[2 * tail - rows :]], axis=0)
    lane = lax.broadcasted_iota(jnp.int32, upper.shape, 1)
    right = jnp.where(lane < 32, pltpu.roll(upper, 32, 1), pltpu.roll(rest, 32, 1))
    return [upper, right]


def silu_points(chunks, mat, bias, by_pair, points, hidden, slope):
    for d, chunk in enumerate(chunks):
        parts = [window(chunk, j * BS) for j in (2, 3)]
        by_pair[partner(d)] = jnp.concatenate(parts, axis=1)
    v = by_pair[...].reshape(points.shape).astype(BF16)
    pre = dot(v, mat[...], (1, 0)) + bias[...]
    sig = jax.nn.sigmoid(pre)
    points[...] = v
    hidden[...] = (pre * sig).astype(BF16)
    slope[...] = sig * (1.0 + pre * (1.0 - sig))


def own_kernel(*refs):
    mat1, bias, points, hidden, slope, by_pair = refs[NB:]
    chunks = [refs[i][...].astype(F32) for i in ORDER]
    silu_points(chunks, mat1, bias, by_pair, points, hidden, slope)


def filter_kernel(*refs):
    owns, (other, slope_own, mat1, turned1, turned2, bias, own_field) = refs[:4], refs[4:11]
    assign_hbm, outs, (bundle, points, hidden, grad_pre, grad_y) = refs[11], refs[12:15], refs[15:20]
    assign, by_lat, by_pair, slope, real, imag, sems = refs[20:]
    copies = fetch(sems, (assign_hbm,), (assign,))
    core = lax.rem(lax.axis_index("lat"), 2)
    sides = [[owns[i][...].astype(F32) for i in ORDER], [other[i].astype(F32) for i in ORDER]]
    silu_points(sides[1], mat1, bias, by_pair, points, hidden, slope)
    wait(copies)
    for side, chunks in zip((core, 1 - core), sides):
        for d, chunk in enumerate(chunks):
            parts = [window(chunk, j * BS) for j in range(2)]
            by_lat[assign[2 * partner(d) + side]] = jnp.concatenate(parts, axis=1)
    n_rows, rows, _ = by_lat.shape
    half = rows * n_rows // 2
    waves = eight_points([(by_lat[r][:, :LANES], by_lat[r][:, LANES:]) for r in range(n_rows)], -1)
    for k, wave in enumerate(waves):
        real[k * rows : (k + 1) * rows] = wave[0]
        imag[k * rows : (k + 1) * rows] = wave[1]
    dy = [
        jnp.concatenate([ref[pl.ds(m, n_rows, stride=rows), :] for m in range(rows)], axis=0)
        for ref in (real, imag)
    ]
    dy = jnp.concatenate(dy, axis=1).astype(BF16)
    dy = [jnp.where(core == side, dy[:half], dy[half:]) for side in range(2)]
    dh = dot(jnp.concatenate(dy, axis=0), turned2[...], (1, 0))
    dp = [(dh[:half] * slope_own[...]).astype(BF16), (dh[half:] * slope[...]).astype(BF16)]
    dv = dot(jnp.concatenate(dp, axis=0), turned1[...], (1, 0)).astype(BF16).astype(F32)
    for side in range(2):
        grad_y[side] = dy[side]
        grad_pre[side] = dp[side]
        place = pl.ds(pl.multiple_of((core if side == 0 else 1 - core) * half, 8), half)
        real[place] = dv[side * half : (side + 1) * half, :LANES]
        imag[place] = dv[side * half : (side + 1) * half, LANES:]
    inner = [
        tuple(ref[pl.ds(k, rows, stride=n_rows), :] for ref in (real, imag)) for k in range(n_rows)
    ]
    for r, band in enumerate(eight_points(inner, 1)):
        by_lat[r] = jnp.concatenate(band, axis=1)
    length = own_field.shape[0]
    bundle[0:length] = own_field[...]
    for i, d in enumerate(ORDER):
        band = pack(by_lat[assign[2 * partner(d) + core]])
        if d:
            outs[i - 1][...] = band.astype(BF16)
        else:
            tail = bundle.shape[0] - FIELD_ROWS
            band = jnp.concatenate([band, jnp.zeros((3 * tail - band.shape[0], LANES), F32)], axis=0)
            band = [band[i * tail : (i + 1) * tail] for i in range(3)]
            bundle[FIELD_ROWS:] = jnp.concatenate(band, axis=1).astype(BF16)


def products_kernel(points0, hidden0, points1, hidden1, grad_pre, grad_y, gw1, gw2, gb1):
    core = lax.rem(lax.axis_index("lat"), 2)
    half = BS // 2
    for ref, grads, values in ((gw1, grad_pre, (points0, points1)), (gw2, grad_y, (hidden0, hidden1))):
        both = dot(grads[0], values[0][...], (0, 0)) + dot(grads[1], values[1][...], (0, 0))
        real = both[:BS, :LANES] + both[LANES : LANES + BS, LANES:]
        imag = both[LANES : LANES + BS, :LANES] - both[:BS, LANES:]
        for c, full in enumerate((real, imag)):
            ref[c] = jnp.where(core == 0, full[:half], full[half:])[:, :BS]
    sums = sum(jnp.sum(grad_pre[side].astype(F32), axis=0, keepdims=True) for side in range(2))
    for c in range(2):
        line = sums[:, c * LANES : (c + 1) * LANES]
        gb1[c : c + 1] = jnp.where(core == 0, line[:, :half], line[:, half:BS])


def compose_kernel(last, three, bundle, table, out, by_block, result, sems):
    rows = by_block.shape[1]
    own = bundle[FIELD_ROWS:].astype(F32)
    own = jnp.concatenate([own[:, i * LANES : (i + 1) * LANES] for i in range(3)], axis=0)
    chunks = [own[: three.shape[1]]] + [three[i].astype(F32) for i in range(3)]
    for d, chunk in zip(ORDER, chunks):
        by_block[partner(d)] = jnp.concatenate(unpack(chunk, rows), axis=1)
    parts = [
        dense([by_block[n, :, c * LANES : (c + 1) * LANES] for n in range(NB)]) for c in range(2)
    ]
    parts = jnp.concatenate(parts, axis=0).astype(BF16)
    none = lax.axis_index("section") == last
    copies = []
    for i, (_, tile) in enumerate(columns(out.shape[1])):
        mixed = jnp.dot(table[...], parts[:, i * LANES : (i + 1) * LANES], preferred_element_type=F32)
        whole = bundle[0 : out.shape[0], tile].astype(F32) + mixed.astype(BF16).astype(F32)
        result[:, tile] = jnp.where(none, 0.0, whole).astype(BF16)
        copies.append(pltpu.make_async_copy(result.at[:, tile], out.at[:, tile], sems.at[i]))
        copies[-1].start()
    wait(copies)


VMEM = pl.BlockSpec(memory_space=pltpu.VMEM)
HBM = pl.BlockSpec(memory_space=pltpu.HBM)


def call(kernel, outs, scratch, near, far, flops=10**8, out_specs=None):
    out_specs = out_specs or (tuple([VMEM] * len(outs)) if isinstance(outs, tuple) else VMEM)
    many = isinstance(outs, tuple)
    return pl.pallas_call(
        kernel,
        out_shape=outs,
        in_specs=[VMEM] * len(near) + [HBM] * len(far),
        out_specs=out_specs,
        scratch_shapes=scratch,
        cost_estimate=pl.CostEstimate(flops=flops, bytes_accessed=10**6, transcendentals=0),
        compiler_params=pltpu.CompilerParams(vmem_limit_bytes=32 * 2**20),
    )(*near, *(pltpu.with_memory_space_constraint(x, pltpu.HBM) for x in far))


def scratch_for(*arrays):
    scratch = []
    for x in arrays:
        space = pltpu.SMEM if x.dtype == jnp.int32 else pltpu.VMEM
        scratch.append(space(x.shape, x.dtype))
    return scratch, pltpu.SemaphoreType.DMA((len(arrays),))


def paired_blocks(grad_out, spec_saved, w1, w2, b1, mode_counts, assignment):
    length, width = grad_out.shape[2:]
    n_rows = assignment.shape[0]
    q = spec_saved.shape[3] // (NB * BS)
    rows = 2 * NB * q
    forward, inverse = lon_tables(KM, length)

    def by_part(table):
        table = table.reshape(2, NB, 2, q, length).transpose(0, 2, 1, 3, 4)
        return table.reshape(2 * rows, length).astype(BF16)

    inverse = jnp.asarray(by_part(inverse))
    forward = jnp.asarray(by_part(forward).T)

    def swap(chunks):
        pairs = [[(i, i ^ (2 * d)) for i in range(2 * NB)] for d in ORDER[1:]]
        return [lax.ppermute(chunk, "lat", p) for chunk, p in zip(chunks, pairs)]

    field = grad_out.reshape(length, width)
    shape = jax.ShapeDtypeStruct
    far = (mode_counts, assignment, field, inverse, spec_saved[0])
    scratch, sems = scratch_for(*far)
    sent = call(
        functools.partial(analyse_kernel, q),
        (shape((rows, width), BF16),) * NB,
        scratch + [pltpu.VMEM((NB, rows, width), BF16), sems, pltpu.SemaphoreType.DMA((2, 4))],
        (),
        far,
    )
    received = [sent[0], *swap([sent[d] for d in ORDER[1:]])]
    far = (mode_counts, assignment, w1[0], w2[0], b1[0], forward)
    scratch, _ = scratch_for(*far)
    far = (*far, field)
    wide = 2 * LANES
    mat1, turned1, turned2, bias, field, forward = call(
        functools.partial(ready_kernel, q),
        (
            shape((wide, wide), BF16),
            shape((wide, wide), BF16),
            shape((wide, wide), BF16),
            shape((1, wide), F32),
            shape(field.shape, BF16),
            shape(forward.shape, BF16),
        ),
        scratch + [pltpu.SemaphoreType.DMA((len(far),))],
        (),
        far,
        2 * 10**9,
    )
    own = call(
        join_kernel,
        shape((NB, rows, width), BF16),
        [],
        (*received, bias),
        (),
    )
    other = lax.ppermute(own, "lat", [(i, i ^ 1) for i in range(2 * NB)])
    vectors = shape((NB * rows, wide), BF16)
    slopes = shape((NB * rows, wide), F32)
    by_pair = pltpu.VMEM((NB, rows, wide), F32)
    points0, hidden0, slope0 = call(
        own_kernel,
        (vectors, vectors, slopes),
        [by_pair],
        (*received, mat1, bias),
        (),
        2 * 10**9,
    )
    packed = shape((rows + rows // 2 + 4, LANES), BF16)
    scratch, sems = scratch_for(assignment)
    both = shape((2, NB * rows, wide), BF16)
    tail = -(-packed.shape[0] // 48) * 16
    bundle = shape((FIELD_ROWS + tail, width), BF16)
    *chunks, bundle, points1, hidden1, grad_pre, grad_y = call(
        filter_kernel,
        (packed,) * (NB - 1) + (bundle, vectors, vectors, both, both),
        scratch
        + [
            pltpu.VMEM((n_rows, rows, wide), F32),
            by_pair,
            pltpu.VMEM((NB * rows, wide), F32),
            pltpu.VMEM((n_rows * rows, LANES), F32),
            pltpu.VMEM((n_rows * rows, LANES), F32),
            sems,
        ],
        (*received, other, slope0, mat1, turned1, turned2, bias, field),
        (assignment,),
    )
    backs = swap(chunks)
    matrix = shape((2, BS // 2, BS), F32)
    gw1, gw2, gb1 = call(
        products_kernel,
        (matrix, matrix, shape((2, BS // 2), F32)),
        [],
        (points0, hidden0, points1, hidden1, grad_pre, grad_y),
        (),
        2 * 10**9,
    )
    three = call(join_kernel, shape((NB - 1, *packed.shape), BF16), [], backs, ())
    three = turn(three, "section")
    bundle = turn(bundle, "section")
    shifted = call(
        functools.partial(compose_kernel, lax.axis_size("section") - 1),
        shape((length, width), BF16),
        [
            by_pair,
            pltpu.VMEM((length, width), BF16),
            pltpu.SemaphoreType.DMA((width // LANES,)),
        ],
        (three, bundle, forward),
        (),
        out_specs=HBM,
    )
    shifted = shifted[None, None]
    return shifted, gw1.swapaxes(1, 2)[None], gw2.swapaxes(1, 2)[None], gb1[None]


def apply_mat(vec, mat):
    return jnp.einsum("kpi,ipj->kpj", vec, mat, preferred_element_type=F32)


def adjoint_mat(vec, mat):
    return jnp.einsum("kpj,ipj->kpi", vec, mat, preferred_element_type=F32)


def outer_sum(left, right):
    return jnp.einsum("kpi,kpj->ipj", left, right, preferred_element_type=F32)


def split_blocks(grad_out, spec_saved, w1, w2, b1, mode_counts, assignment):
    rows_dev = grad_out.shape[1]
    length = grad_out.shape[2]
    width = grad_out.shape[3]
    n_rows = assignment.shape[0]
    pairs_dev = spec_saved.shape[3] // BS
    forward, inverse = (jnp.asarray(t.astype(BF16)) for t in lon_tables(KM, length))
    cosine, sine = (jnp.asarray(t.astype(BF16))[:, assignment] for t in lat_waves(n_rows))
    table = jnp.stack(
        [jnp.stack([cosine, sine], axis=-1), jnp.stack([-sine, cosine], axis=-1)], axis=1
    )
    lat_pos = lax.axis_index("lat")
    lat_count = lax.axis_size("lat")
    own_lat = lax.dynamic_slice_in_dim(assignment, lat_pos * rows_dev, rows_dev)
    active = (jnp.arange(KM, dtype=jnp.int32)[None, :] < mode_counts[own_lat][:, None]).astype(F32)
    cotan = grad_out[0]
    spectral = jnp.einsum(
        "cml,rlni->rcmni",
        inverse,
        cotan.reshape(rows_dev, length, NB, BS),
        preferred_element_type=F32,
    )
    spectral = (spectral * active[:, None, :, None, None]).astype(BF16)
    spectral = spectral.reshape(rows_dev, 2, KM * NB * BS)
    pencil = lax.all_to_all(spectral, "lat", split_axis=2, concat_axis=0, tiled=True)
    pencil = pencil.reshape(n_rows, 2, pairs_dev, BS)
    grad_y = jnp.einsum("kerc,rcpi->kepi", table, pencil, preferred_element_type=F32).astype(BF16)
    saved = spec_saved[0].reshape(n_rows, 2, pairs_dev, BS)
    pair_ids = lat_pos * pairs_dev + jnp.arange(pairs_dev, dtype=jnp.int32)
    owner = (pair_ids % NB)[:, None] == jnp.arange(NB, dtype=jnp.int32)[None, :]
    owner = owner.astype(F32)
    first = jnp.take(w1[0].reshape(2, BS, NB, BS), pair_ids % NB, axis=2)
    second = jnp.take(w2[0].reshape(2, BS, NB, BS), pair_ids % NB, axis=2)
    shift_b = jnp.take(b1[0].reshape(2, NB, BS), pair_ids % NB, axis=1).astype(F32)
    v_r = saved[:, 0]
    v_i = saved[:, 1]
    pre_r = apply_mat(v_r, first[0]) - apply_mat(v_i, first[1]) + shift_b[0][None]
    pre_i = apply_mat(v_i, first[0]) + apply_mat(v_r, first[1]) + shift_b[1][None]
    hid_r = jax.nn.silu(pre_r).astype(BF16)
    hid_i = jax.nn.silu(pre_i).astype(BF16)
    dy_r = grad_y[:, 0]
    dy_i = grad_y[:, 1]
    dh_r = adjoint_mat(dy_r, second[0]) + adjoint_mat(dy_i, second[1])
    dh_i = adjoint_mat(dy_i, second[0]) - adjoint_mat(dy_r, second[1])
    dp_r = (dh_r * silu_slope(pre_r)).astype(BF16)
    dp_i = (dh_i * silu_slope(pre_i)).astype(BF16)
    gw2 = jnp.stack(
        [
            outer_sum(hid_r, dy_r) + outer_sum(hid_i, dy_i),
            outer_sum(hid_r, dy_i) - outer_sum(hid_i, dy_r),
        ]
    )
    gw1 = jnp.stack(
        [outer_sum(v_r, dp_r) + outer_sum(v_i, dp_i), outer_sum(v_r, dp_i) - outer_sum(v_i, dp_r)]
    )
    gb1 = jnp.stack([jnp.sum(dp_r.astype(F32), axis=0), jnp.sum(dp_i.astype(F32), axis=0)])
    dv_r = adjoint_mat(dp_r, first[0]) + adjoint_mat(dp_i, first[1])
    dv_i = adjoint_mat(dp_i, first[0]) - adjoint_mat(dp_r, first[1])
    grad_v = jnp.stack([dv_r, dv_i], axis=1).astype(BF16)
    grad_u = jnp.einsum("kerc,kepi->rcpi", table, grad_v, preferred_element_type=F32).astype(BF16)
    grad_u = grad_u.reshape(n_rows, 2, pairs_dev * BS)
    back = lax.all_to_all(grad_u, "lat", split_axis=0, concat_axis=2, tiled=True)
    back = back.reshape(rows_dev, 2, KM, NB, BS) * active[:, None, :, None, None].astype(BF16)
    mixed = jnp.einsum("cml,rcmni->rlni", forward, back, preferred_element_type=F32)
    mixed = mixed.reshape(rows_dev, length, width).astype(BF16)
    block_w1 = jnp.einsum("pn,cipj->cinj", owner, gw1).reshape(1, 2, BS, width)
    block_w2 = jnp.einsum("pn,cipj->cinj", owner, gw2).reshape(1, 2, BS, width)
    block_b1 = jnp.einsum("pn,cpj->cnj", owner, gb1).reshape(1, 2, width)
    columns = width // lat_count
    full_w1, full_w2, full_b1 = lax.psum((block_w1, block_w2, block_b1), "lat")
    sum_w1 = lax.dynamic_slice_in_dim(full_w1, lat_pos * columns, columns, 3)
    sum_w2 = lax.dynamic_slice_in_dim(full_w2, lat_pos * columns, columns, 3)
    sum_b1 = lax.dynamic_slice_in_dim(full_b1, lat_pos * columns, columns, 2)
    whole = (cotan.astype(F32) + mixed.astype(F32)).astype(BF16)
    received = from_behind(whole[None], "section", -1)
    return (received, sum_w1, sum_w2, sum_b1)


def per_device(grad_out, spec_saved, w1, w2, b1, mode_counts, assignment):
    n_dev = lax.axis_size("lat")
    pairs_dev = spec_saved.shape[3] // BS
    paired = n_dev == 2 * NB and grad_out.shape[1] == 1 and pairs_dev % NB == 0
    body = paired_blocks if paired else split_blocks
    return body(grad_out, spec_saved, w1, w2, b1, mode_counts, assignment)


def solution(mesh):
    return jax.shard_map(
        per_device,
        mesh=mesh,
        in_specs=(
            P("section", "lat", None, None),
            P("section", None, None, "lat"),
            P("section", None, None, None),
            P("section", None, None, None),
            P("section", None, None),
            P(),
            P(),
        ),
        out_specs=(
            P("section", "lat", None, None),
            P("section", None, None, "lat"),
            P("section", None, None, "lat"),
            P("section", None, "lat"),
        ),
        check_vma=False,
    )
```

```python
import functools
import math

import jax
import jax.numpy as jnp
import numpy as np
from jax import lax
from jax.experimental import pallas as pl
from jax.experimental.pallas import tpu as pltpu
from jax.sharding import PartitionSpec as P

NB = 4
BS = 96
KM = 72
LANES = 128
F32 = jnp.float32
BF16 = jnp.bfloat16


def from_behind(value, axis, by):
    length = lax.axis_size(axis)
    pairs = [(i, i + by) for i in range(length) if 0 <= i + by < length]
    return lax.ppermute(value, axis, pairs)


def turn(value, axis):
    length = lax.axis_size(axis)
    return lax.ppermute(value, axis, [(i, (i - 1) % length) for i in range(length)])


def lon_tables(n_modes, length):
    modes = np.arange(n_modes)
    phase = modes[:, None] * np.arange(length)[None, :] % length
    angle = phase * (2.0 * math.pi / length)
    forward = np.stack([np.cos(angle), -np.sin(angle)]) / math.sqrt(length)
    weight = np.where(modes == 0, 1.0, 2.0)[None, :, None]
    return forward, forward * weight


def lat_waves(n_rows):
    freqs = np.arange(n_rows)
    angle = (freqs[:, None] * freqs[None, :] % n_rows) * (2.0 * math.pi / n_rows)
    factor = 1.0 / math.sqrt(n_rows)
    return np.cos(angle) * factor, np.sin(angle) * factor


def silu_slope(pre):
    sig = jax.nn.sigmoid(pre)
    return sig * (1.0 + pre * (1.0 - sig))


def window(x, start):
    low = start // LANES * LANES
    shift = start - low
    if shift == 0:
        return x[:, low : low + LANES]
    if shift + BS <= LANES:
        return pltpu.roll(x[:, low : low + LANES], LANES - shift, 1)
    return pltpu.roll(x[:, low : low + 2 * LANES], 2 * LANES - shift, 1)[:, :LANES]


def dense(parts):
    lane = lax.broadcasted_iota(jnp.int32, parts[0].shape, 1)
    first = pltpu.roll(parts[1], 96, 1)
    second = pltpu.roll(parts[2], 64, 1)
    third = pltpu.roll(parts[3], 32, 1)
    return jnp.concatenate(
        [
            jnp.where(lane < 96, parts[0], first),
            jnp.where(lane < 64, first, second),
            jnp.where(lane < 32, second, third),
        ],
        axis=1,
    )


def dot(a, b, contract):
    return lax.dot_general(a, b, ((contract[:1], contract[1:]), ((), ())), preferred_element_type=F32)


def mode_numbers(shape, axis, q):
    number = lax.broadcasted_iota(jnp.int32, shape, axis)
    second = number >= NB * q
    number = jnp.where(second, number - NB * q, number)
    mode = number
    for z in range(1, NB):
        mode = jnp.where(number >= z * q, number + z * q, mode)
    return jnp.where(second, mode + q, mode)


def eight_points(x, sign):
    root = float(np.float32(1.0 / math.sqrt(8.0)).astype(BF16))

    def add(a, b):
        return a[0] + b[0], a[1] + b[1]

    def sub(a, b):
        return a[0] - b[0], a[1] - b[1]

    def times_i(a, by):
        return (-a[1], a[0]) if by > 0 else (a[1], -a[0])

    def scale(a, by):
        return a[0] * by, a[1] * by

    def four(a, b, c, d):
        total, far, other, near = add(a, c), sub(a, c), add(b, d), sub(b, d)
        near = times_i(near, sign)
        return add(total, other), add(far, near), sub(total, other), sub(far, near)

    even = [scale(a, root) for a in four(*x[0::2])]
    odd = four(*x[1::2])
    turned = [
        scale(odd[0], root),
        scale(add(odd[1], times_i(odd[1], sign)), 0.25),
        scale(times_i(odd[2], sign), root),
        scale(sub(times_i(odd[3], sign), odd[3]), 0.25),
    ]
    return [add(a, b) for a, b in zip(even, turned)] + [sub(a, b) for a, b in zip(even, turned)]


def fetch(sems, sources, targets):
    copies = [
        pltpu.make_async_copy(source, target, sems.at[i])
        for i, (source, target) in enumerate(zip(sources, targets))
    ]
    for copy in copies:
        copy.start()
    return copies


def fetch_parts(sems, source, target, parts):
    return fetch(sems, [source.at[part] for part in parts], [target.at[part] for part in parts])


def columns(width):
    return [(slice(None), pl.ds(i, LANES)) for i in range(0, width, LANES)]


def wait(copies):
    for copy in copies:
        copy.wait()


def partner(d):
    return jnp.bitwise_xor(lax.axis_index("lat") // 2, d)


def analyse_kernel(q, *refs):
    hbm, outs, held = refs[:5], refs[5:9], refs[9:14]
    by_block, few, sems = refs[14:]
    counts, assign, field, table, saved = held
    early = fetch_parts(sems.at[0], hbm[4], saved, [pl.ds(k, 2) for k in range(0, 2 * NB, 2)])
    late = fetch_parts(sems.at[1], hbm[2], field, columns(field.shape[1]))
    late += fetch(few, hbm[:2] + hbm[3:4], held[:2] + held[3:4])
    wait(early)
    parts = [saved[:, c, :].astype(F32) for c in range(2)]
    points = [
        [
            jnp.concatenate([window(part, (mm * NB + n) * BS) for mm in range(q)], axis=0)
            for part in parts
        ]
        for n in range(NB)
    ]
    wait(late)
    rows = by_block.shape[1]
    spectral = jnp.dot(table[...], field[...], preferred_element_type=F32)
    active = counts[assign[lax.axis_index("lat")]]
    held_modes = mode_numbers((rows, spectral.shape[1]), 0, q) < active
    spectra = [jnp.where(held_modes, spectral[c * rows : (c + 1) * rows], 0.0) for c in range(2)]
    for n in range(NB):
        pieces = [window(spectrum, n * BS) for spectrum in spectra]
        by_block[n] = dense(pieces + points[n]).astype(BF16)
    for d, out in enumerate(outs):
        out[...] = by_block[partner(d)]


def ready_kernel(q, *refs):
    hbm, (mat1, turned1, turned2, bias, own_field, own_table) = refs[:7], refs[7:13]
    counts, assign, w1, w2, b1, table, sems = refs[13:]
    copies = fetch(sems, hbm, (counts, assign, w1, w2, b1, table, own_field))
    wait(copies[:6])
    active = counts[assign[lax.axis_index("lat")]]
    rows = table.shape[1] // 2
    held_modes = mode_numbers((table.shape[0], rows), 1, q) < active
    for c in range(2):
        part = table[:, c * rows : (c + 1) * rows].astype(F32)
        own_table[:, c * rows : (c + 1) * rows] = jnp.where(held_modes, part, 0.0).astype(BF16)
    block = lax.axis_index("lat") // 2

    def pick(x):
        value = window(x, 0)
        for n in range(1, NB):
            value = jnp.where(block == n, window(x, n * BS), value)
        lane = lax.broadcasted_iota(jnp.int32, value.shape, 1)
        return jnp.where(lane < BS, value, 0.0)

    gap = jnp.zeros((LANES - BS, 2 * LANES), F32)
    for source, mat, turned in ((w1, mat1, turned1), (w2, None, turned2)):
        real, imag = (pick(source[c].astype(F32)) for c in range(2))
        whole = [
            jnp.concatenate([real, imag], axis=1),
            gap,
            jnp.concatenate([-imag, real], axis=1),
            gap,
        ]
        whole = jnp.concatenate(whole, axis=0)
        turned[...] = whole.T.astype(BF16)
        if mat is not None:
            mat[...] = whole.astype(BF16)
    shift_b = pick(b1[...].astype(F32))
    bias[...] = jnp.concatenate([shift_b[0:1], shift_b[1:2]], axis=1)
    wait(copies[6:])


ORDER = (0, 3, 2, 1)
FIELD_ROWS = 192


def join_kernel(*refs):
    out = refs[-1]
    for i in range(out.shape[0]):
        out[i] = refs[i][...]


def others_kernel(backs, out):
    for i, d in enumerate(ORDER[1:]):
        out[i] = backs[partner(d)]


def pack(band):
    rows = band.shape[0]
    tail = rows // 2 + 4
    left, right = band[:, :LANES], pltpu.roll(band[:, LANES:], 96, 1)
    lane = lax.broadcasted_iota(jnp.int32, left.shape, 1)
    upper = jnp.where(lane < 96, left, right)
    lower = pltpu.roll(right[rows - tail :], 64, 1)
    lower = jnp.where(lane[:tail] < 64, right[:tail], lower)
    return jnp.concatenate([upper, lower], axis=0)


def unpack(packed, rows):
    tail = rows // 2 + 4
    upper, lower = packed[:rows], packed[rows:]
    rest = jnp.concatenate([lower, pltpu.roll(lower, 64, 1)[2 * tail - rows :]], axis=0)
    lane = lax.broadcasted_iota(jnp.int32, upper.shape, 1)
    right = jnp.where(lane < 32, pltpu.roll(upper, 32, 1), pltpu.roll(rest, 32, 1))
    return [upper, right]


def silu_points(chunks, mat, bias, by_pair, points, hidden, slope):
    for d, chunk in enumerate(chunks):
        parts = [window(chunk, j * BS) for j in (2, 3)]
        by_pair[partner(d)] = jnp.concatenate(parts, axis=1)
    v = by_pair[...].reshape(points.shape).astype(BF16)
    pre = dot(v, mat[...], (1, 0)) + bias[...]
    sig = jax.nn.sigmoid(pre)
    points[...] = v
    hidden[...] = (pre * sig).astype(BF16)
    slope[...] = sig * (1.0 + pre * (1.0 - sig))


def own_kernel(*refs):
    mat1, bias, points, hidden, slope, by_pair = refs[NB:]
    chunks = [refs[i][...].astype(F32) for i in ORDER]
    silu_points(chunks, mat1, bias, by_pair, points, hidden, slope)


def filter_kernel(*refs):
    owns, (other, slope_own, mat1, turned1, turned2, bias, own_field) = refs[:4], refs[4:11]
    assign_hbm, outs, bundle, points, hidden, grad_pre, grad_y = refs[11:18]
    assign, by_lat, by_pair, slope, real, imag, sems = refs[18:]
    copies = fetch(sems, (assign_hbm,), (assign,))
    core = lax.rem(lax.axis_index("lat"), 2)
    sides = [[owns[i][...].astype(F32) for i in ORDER], [other[i].astype(F32) for i in ORDER]]
    silu_points(sides[1], mat1, bias, by_pair, points, hidden, slope)
    wait(copies)
    for side, chunks in zip((core, 1 - core), sides):
        for d, chunk in enumerate(chunks):
            parts = [window(chunk, j * BS) for j in range(2)]
            by_lat[assign[2 * partner(d) + side]] = jnp.concatenate(parts, axis=1)
    n_rows, rows, _ = by_lat.shape
    half = rows * n_rows // 2
    waves = eight_points([(by_lat[r][:, :LANES], by_lat[r][:, LANES:]) for r in range(n_rows)], -1)
    for k, wave in enumerate(waves):
        real[k * rows : (k + 1) * rows] = wave[0]
        imag[k * rows : (k + 1) * rows] = wave[1]
    dy = [
        jnp.concatenate([ref[pl.ds(m, n_rows, stride=rows), :] for m in range(rows)], axis=0)
        for ref in (real, imag)
    ]
    dy = jnp.concatenate(dy, axis=1).astype(BF16)
    dy = [jnp.where(core == side, dy[:half], dy[half:]) for side in range(2)]
    dh = dot(jnp.concatenate(dy, axis=0), turned2[...], (1, 0))
    dp = [(dh[:half] * slope_own[...]).astype(BF16), (dh[half:] * slope[...]).astype(BF16)]
    dv = dot(jnp.concatenate(dp, axis=0), turned1[...], (1, 0)).astype(BF16).astype(F32)
    for side in range(2):
        grad_y[side] = dy[side]
        grad_pre[side] = dp[side]
        place = pl.ds(pl.multiple_of((core if side == 0 else 1 - core) * half, 8), half)
        real[place] = dv[side * half : (side + 1) * half, :LANES]
        imag[place] = dv[side * half : (side + 1) * half, LANES:]
    inner = [
        tuple(ref[pl.ds(k, rows, stride=n_rows), :] for ref in (real, imag)) for k in range(n_rows)
    ]
    for r, band in enumerate(eight_points(inner, 1)):
        by_lat[r] = jnp.concatenate(band, axis=1)
    length = own_field.shape[0]
    bundle[0:length] = own_field[...]
    for d in ORDER:
        band = pack(by_lat[assign[2 * partner(d) + core]])
        outs[partner(d)] = band.astype(BF16)
        if not d:
            tail = bundle.shape[0] - FIELD_ROWS
            band = jnp.concatenate([band, jnp.zeros((3 * tail - band.shape[0], LANES), F32)], axis=0)
            band = [band[i * tail : (i + 1) * tail] for i in range(3)]
            bundle[FIELD_ROWS:] = jnp.concatenate(band, axis=1).astype(BF16)


def products_kernel(points0, hidden0, points1, hidden1, grad_pre, grad_y, gw1, gw2, gb1):
    core = lax.rem(lax.axis_index("lat"), 2)
    half = BS // 2
    for ref, grads, values in ((gw1, grad_pre, (points0, points1)), (gw2, grad_y, (hidden0, hidden1))):
        both = dot(grads[0], values[0][...], (0, 0)) + dot(grads[1], values[1][...], (0, 0))
        real = both[:BS, :LANES] + both[LANES : LANES + BS, LANES:]
        imag = both[LANES : LANES + BS, :LANES] - both[:BS, LANES:]
        for c, full in enumerate((real, imag)):
            ref[c] = jnp.where(core == 0, full[:half], full[half:])[:, :BS]
    sums = sum(jnp.sum(grad_pre[side].astype(F32), axis=0, keepdims=True) for side in range(2))
    for c in range(2):
        line = sums[:, c * LANES : (c + 1) * LANES]
        gb1[c : c + 1] = jnp.where(core == 0, line[:, :half], line[:, half:BS])


def compose_kernel(last, three, bundle, table, out, by_block, result, sems):
    rows = by_block.shape[1]
    own = bundle[FIELD_ROWS:].astype(F32)
    own = jnp.concatenate([own[:, i * LANES : (i + 1) * LANES] for i in range(3)], axis=0)
    chunks = [own[: three.shape[1]]] + [three[i].astype(F32) for i in range(3)]
    for d, chunk in zip(ORDER, chunks):
        by_block[partner(d)] = jnp.concatenate(unpack(chunk, rows), axis=1)
    parts = [
        dense([by_block[n, :, c * LANES : (c + 1) * LANES] for n in range(NB)]) for c in range(2)
    ]
    parts = jnp.concatenate(parts, axis=0).astype(BF16)
    none = lax.axis_index("section") == last
    copies = []
    for i, (_, tile) in enumerate(columns(out.shape[1])):
        mixed = jnp.dot(table[...], parts[:, i * LANES : (i + 1) * LANES], preferred_element_type=F32)
        whole = bundle[0 : out.shape[0], tile].astype(F32) + mixed.astype(BF16).astype(F32)
        result[:, tile] = jnp.where(none, 0.0, whole).astype(BF16)
        copies.append(pltpu.make_async_copy(result.at[:, tile], out.at[:, tile], sems.at[i]))
        copies[-1].start()
    wait(copies)


VMEM = pl.BlockSpec(memory_space=pltpu.VMEM)
HBM = pl.BlockSpec(memory_space=pltpu.HBM)


def call(kernel, outs, scratch, near, far, flops=10**8, out_specs=None):
    out_specs = out_specs or (tuple([VMEM] * len(outs)) if isinstance(outs, tuple) else VMEM)
    many = isinstance(outs, tuple)
    return pl.pallas_call(
        kernel,
        out_shape=outs,
        in_specs=[VMEM] * len(near) + [HBM] * len(far),
        out_specs=out_specs,
        scratch_shapes=scratch,
        cost_estimate=pl.CostEstimate(flops=flops, bytes_accessed=10**6, transcendentals=0),
        compiler_params=pltpu.CompilerParams(vmem_limit_bytes=32 * 2**20),
    )(*near, *(pltpu.with_memory_space_constraint(x, pltpu.HBM) for x in far))


def scratch_for(*arrays):
    scratch = []
    for x in arrays:
        space = pltpu.SMEM if x.dtype == jnp.int32 else pltpu.VMEM
        scratch.append(space(x.shape, x.dtype))
    return scratch, pltpu.SemaphoreType.DMA((len(arrays),))


def paired_blocks(grad_out, spec_saved, w1, w2, b1, mode_counts, assignment):
    length, width = grad_out.shape[2:]
    n_rows = assignment.shape[0]
    q = spec_saved.shape[3] // (NB * BS)
    rows = 2 * NB * q
    forward, inverse = lon_tables(KM, length)

    def by_part(table):
        table = table.reshape(2, NB, 2, q, length).transpose(0, 2, 1, 3, 4)
        return table.reshape(2 * rows, length).astype(BF16)

    inverse = jnp.asarray(by_part(inverse))
    forward = jnp.asarray(by_part(forward).T)

    def swap(chunks):
        pairs = [[(i, i ^ (2 * d)) for i in range(2 * NB)] for d in ORDER[1:]]
        return [lax.ppermute(chunk, "lat", p) for chunk, p in zip(chunks, pairs)]

    field = grad_out.reshape(length, width)
    shape = jax.ShapeDtypeStruct
    far = (mode_counts, assignment, field, inverse, spec_saved[0])
    scratch, sems = scratch_for(*far)
    sent = call(
        functools.partial(analyse_kernel, q),
        (shape((rows, width), BF16),) * NB,
        scratch + [pltpu.VMEM((NB, rows, width), BF16), sems, pltpu.SemaphoreType.DMA((2, 4))],
        (),
        far,
    )
    received = [sent[0], *swap([sent[d] for d in ORDER[1:]])]
    far = (mode_counts, assignment, w1[0], w2[0], b1[0], forward)
    scratch, _ = scratch_for(*far)
    far = (*far, field)
    wide = 2 * LANES
    mat1, turned1, turned2, bias, field, forward = call(
        functools.partial(ready_kernel, q),
        (
            shape((wide, wide), BF16),
            shape((wide, wide), BF16),
            shape((wide, wide), BF16),
            shape((1, wide), F32),
            shape(field.shape, BF16),
            shape(forward.shape, BF16),
        ),
        scratch + [pltpu.SemaphoreType.DMA((len(far),))],
        (),
        far,
        2 * 10**9,
    )
    own = call(
        join_kernel,
        shape((NB, rows, width), BF16),
        [],
        (*received, bias),
        (),
    )
    other = lax.ppermute(own, "lat", [(i, i ^ 1) for i in range(2 * NB)])
    vectors = shape((NB * rows, wide), BF16)
    slopes = shape((NB * rows, wide), F32)
    by_pair = pltpu.VMEM((NB, rows, wide), F32)
    points0, hidden0, slope0 = call(
        own_kernel,
        (vectors, vectors, slopes),
        [by_pair],
        (*received, mat1, bias),
        (),
        2 * 10**9,
    )
    packed = shape((rows + rows // 2 + 4, LANES), BF16)
    scratch, sems = scratch_for(assignment)
    both = shape((2, NB * rows, wide), BF16)
    tail = -(-packed.shape[0] // 48) * 16
    bundle = shape((FIELD_ROWS + tail, width), BF16)
    chunks, bundle, points1, hidden1, grad_pre, grad_y = call(
        filter_kernel,
        (shape((NB, *packed.shape), BF16), bundle, vectors, vectors, both, both),
        scratch
        + [
            pltpu.VMEM((n_rows, rows, wide), F32),
            by_pair,
            pltpu.VMEM((NB * rows, wide), F32),
            pltpu.VMEM((n_rows * rows, LANES), F32),
            pltpu.VMEM((n_rows * rows, LANES), F32),
            sems,
        ],
        (*received, other, slope0, mat1, turned1, turned2, bias, field),
        (assignment,),
    )
    backs = lax.all_to_all(
        chunks,
        "lat",
        split_axis=0,
        concat_axis=0,
        axis_index_groups=[[2 * z + c for z in range(NB)] for c in range(2)],
        tiled=True,
    )
    matrix = shape((2, BS // 2, BS), F32)
    gw1, gw2, gb1 = call(
        products_kernel,
        (matrix, matrix, shape((2, BS // 2), F32)),
        [],
        (points0, hidden0, points1, hidden1, grad_pre, grad_y),
        (),
        2 * 10**9,
    )
    three = call(others_kernel, shape((NB - 1, *packed.shape), BF16), [], (backs,), ())
    three = turn(three, "section")
    bundle = turn(bundle, "section")
    shifted = call(
        functools.partial(compose_kernel, lax.axis_size("section") - 1),
        shape((length, width), BF16),
        [
            by_pair,
            pltpu.VMEM((length, width), BF16),
            pltpu.SemaphoreType.DMA((width // LANES,)),
        ],
        (three, bundle, forward),
        (),
        out_specs=HBM,
    )
    shifted = shifted[None, None]
    return shifted, gw1.swapaxes(1, 2)[None], gw2.swapaxes(1, 2)[None], gb1[None]


def apply_mat(vec, mat):
    return jnp.einsum("kpi,ipj->kpj", vec, mat, preferred_element_type=F32)


def adjoint_mat(vec, mat):
    return jnp.einsum("kpj,ipj->kpi", vec, mat, preferred_element_type=F32)


def outer_sum(left, right):
    return jnp.einsum("kpi,kpj->ipj", left, right, preferred_element_type=F32)


def split_blocks(grad_out, spec_saved, w1, w2, b1, mode_counts, assignment):
    rows_dev = grad_out.shape[1]
    length = grad_out.shape[2]
    width = grad_out.shape[3]
    n_rows = assignment.shape[0]
    pairs_dev = spec_saved.shape[3] // BS
    forward, inverse = (jnp.asarray(t.astype(BF16)) for t in lon_tables(KM, length))
    cosine, sine = (jnp.asarray(t.astype(BF16))[:, assignment] for t in lat_waves(n_rows))
    table = jnp.stack(
        [jnp.stack([cosine, sine], axis=-1), jnp.stack([-sine, cosine], axis=-1)], axis=1
    )
    lat_pos = lax.axis_index("lat")
    lat_count = lax.axis_size("lat")
    own_lat = lax.dynamic_slice_in_dim(assignment, lat_pos * rows_dev, rows_dev)
    active = (jnp.arange(KM, dtype=jnp.int32)[None, :] < mode_counts[own_lat][:, None]).astype(F32)
    cotan = grad_out[0]
    spectral = jnp.einsum(
        "cml,rlni->rcmni",
        inverse,
        cotan.reshape(rows_dev, length, NB, BS),
        preferred_element_type=F32,
    )
    spectral = (spectral * active[:, None, :, None, None]).astype(BF16)
    spectral = spectral.reshape(rows_dev, 2, KM * NB * BS)
    pencil = lax.all_to_all(spectral, "lat", split_axis=2, concat_axis=0, tiled=True)
    pencil = pencil.reshape(n_rows, 2, pairs_dev, BS)
    grad_y = jnp.einsum("kerc,rcpi->kepi", table, pencil, preferred_element_type=F32).astype(BF16)
    saved = spec_saved[0].reshape(n_rows, 2, pairs_dev, BS)
    pair_ids = lat_pos * pairs_dev + jnp.arange(pairs_dev, dtype=jnp.int32)
    owner = (pair_ids % NB)[:, None] == jnp.arange(NB, dtype=jnp.int32)[None, :]
    owner = owner.astype(F32)
    first = jnp.take(w1[0].reshape(2, BS, NB, BS), pair_ids % NB, axis=2)
    second = jnp.take(w2[0].reshape(2, BS, NB, BS), pair_ids % NB, axis=2)
    shift_b = jnp.take(b1[0].reshape(2, NB, BS), pair_ids % NB, axis=1).astype(F32)
    v_r = saved[:, 0]
    v_i = saved[:, 1]
    pre_r = apply_mat(v_r, first[0]) - apply_mat(v_i, first[1]) + shift_b[0][None]
    pre_i = apply_mat(v_i, first[0]) + apply_mat(v_r, first[1]) + shift_b[1][None]
    hid_r = jax.nn.silu(pre_r).astype(BF16)
    hid_i = jax.nn.silu(pre_i).astype(BF16)
    dy_r = grad_y[:, 0]
    dy_i = grad_y[:, 1]
    dh_r = adjoint_mat(dy_r, second[0]) + adjoint_mat(dy_i, second[1])
    dh_i = adjoint_mat(dy_i, second[0]) - adjoint_mat(dy_r, second[1])
    dp_r = (dh_r * silu_slope(pre_r)).astype(BF16)
    dp_i = (dh_i * silu_slope(pre_i)).astype(BF16)
    gw2 = jnp.stack(
        [
            outer_sum(hid_r, dy_r) + outer_sum(hid_i, dy_i),
            outer_sum(hid_r, dy_i) - outer_sum(hid_i, dy_r),
        ]
    )
    gw1 = jnp.stack(
        [outer_sum(v_r, dp_r) + outer_sum(v_i, dp_i), outer_sum(v_r, dp_i) - outer_sum(v_i, dp_r)]
    )
    gb1 = jnp.stack([jnp.sum(dp_r.astype(F32), axis=0), jnp.sum(dp_i.astype(F32), axis=0)])
    dv_r = adjoint_mat(dp_r, first[0]) + adjoint_mat(dp_i, first[1])
    dv_i = adjoint_mat(dp_i, first[0]) - adjoint_mat(dp_r, first[1])
    grad_v = jnp.stack([dv_r, dv_i], axis=1).astype(BF16)
    grad_u = jnp.einsum("kerc,kepi->rcpi", table, grad_v, preferred_element_type=F32).astype(BF16)
    grad_u = grad_u.reshape(n_rows, 2, pairs_dev * BS)
    back = lax.all_to_all(grad_u, "lat", split_axis=0, concat_axis=2, tiled=True)
    back = back.reshape(rows_dev, 2, KM, NB, BS) * active[:, None, :, None, None].astype(BF16)
    mixed = jnp.einsum("cml,rcmni->rlni", forward, back, preferred_element_type=F32)
    mixed = mixed.reshape(rows_dev, length, width).astype(BF16)
    block_w1 = jnp.einsum("pn,cipj->cinj", owner, gw1).reshape(1, 2, BS, width)
    block_w2 = jnp.einsum("pn,cipj->cinj", owner, gw2).reshape(1, 2, BS, width)
    block_b1 = jnp.einsum("pn,cpj->cnj", owner, gb1).reshape(1, 2, width)
    columns = width // lat_count
    full_w1, full_w2, full_b1 = lax.psum((block_w1, block_w2, block_b1), "lat")
    sum_w1 = lax.dynamic_slice_in_dim(full_w1, lat_pos * columns, columns, 3)
    sum_w2 = lax.dynamic_slice_in_dim(full_w2, lat_pos * columns, columns, 3)
    sum_b1 = lax.dynamic_slice_in_dim(full_b1, lat_pos * columns, columns, 2)
    whole = (cotan.astype(F32) + mixed.astype(F32)).astype(BF16)
    received = from_behind(whole[None], "section", -1)
    return (received, sum_w1, sum_w2, sum_b1)


def per_device(grad_out, spec_saved, w1, w2, b1, mode_counts, assignment):
    n_dev = lax.axis_size("lat")
    pairs_dev = spec_saved.shape[3] // BS
    paired = n_dev == 2 * NB and grad_out.shape[1] == 1 and pairs_dev % NB == 0
    body = paired_blocks if paired else split_blocks
    return body(grad_out, spec_saved, w1, w2, b1, mode_counts, assignment)


def solution(mesh):
    return jax.shard_map(
        per_device,
        mesh=mesh,
        in_specs=(
            P("section", "lat", None, None),
            P("section", None, None, "lat"),
            P("section", None, None, None),
            P("section", None, None, None),
            P("section", None, None),
            P(),
            P(),
        ),
        out_specs=(
            P("section", "lat", None, None),
            P("section", None, None, "lat"),
            P("section", None, None, "lat"),
            P("section", None, "lat"),
        ),
        check_vma=False,
    )
```

```python
import functools
import math

import jax
import jax.numpy as jnp
import numpy as np
from jax import lax
from jax.experimental import pallas as pl
from jax.experimental.pallas import tpu as pltpu
from jax.sharding import PartitionSpec as P

NB = 4
BS = 96
KM = 72
LANES = 128
F32 = jnp.float32
BF16 = jnp.bfloat16


def from_behind(value, axis, by):
    length = lax.axis_size(axis)
    pairs = [(i, i + by) for i in range(length) if 0 <= i + by < length]
    return lax.ppermute(value, axis, pairs)


def turn(value, axis):
    length = lax.axis_size(axis)
    return lax.ppermute(value, axis, [(i, (i - 1) % length) for i in range(length)])


def lon_tables(n_modes, length):
    modes = np.arange(n_modes)
    phase = modes[:, None] * np.arange(length)[None, :] % length
    angle = phase * (2.0 * math.pi / length)
    forward = np.stack([np.cos(angle), -np.sin(angle)]) / math.sqrt(length)
    weight = np.where(modes == 0, 1.0, 2.0)[None, :, None]
    return forward, forward * weight


def lat_waves(n_rows):
    freqs = np.arange(n_rows)
    angle = (freqs[:, None] * freqs[None, :] % n_rows) * (2.0 * math.pi / n_rows)
    factor = 1.0 / math.sqrt(n_rows)
    return np.cos(angle) * factor, np.sin(angle) * factor


def silu_slope(pre):
    sig = jax.nn.sigmoid(pre)
    return sig * (1.0 + pre * (1.0 - sig))


def window(x, start):
    low = start // LANES * LANES
    shift = start - low
    if shift == 0:
        return x[:, low : low + LANES]
    if shift + BS <= LANES:
        return pltpu.roll(x[:, low : low + LANES], LANES - shift, 1)
    return pltpu.roll(x[:, low : low + 2 * LANES], 2 * LANES - shift, 1)[:, :LANES]


def dense(parts):
    lane = lax.broadcasted_iota(jnp.int32, parts[0].shape, 1)
    first = pltpu.roll(parts[1], 96, 1)
    second = pltpu.roll(parts[2], 64, 1)
    third = pltpu.roll(parts[3], 32, 1)
    return jnp.concatenate(
        [
            jnp.where(lane < 96, parts[0], first),
            jnp.where(lane < 64, first, second),
            jnp.where(lane < 32, second, third),
        ],
        axis=1,
    )


def dot(a, b, contract):
    return lax.dot_general(a, b, ((contract[:1], contract[1:]), ((), ())), preferred_element_type=F32)


def mode_numbers(shape, axis, q):
    number = lax.broadcasted_iota(jnp.int32, shape, axis)
    second = number >= NB * q
    number = jnp.where(second, number - NB * q, number)
    mode = number
    for z in range(1, NB):
        mode = jnp.where(number >= z * q, number + z * q, mode)
    return jnp.where(second, mode + q, mode)


def eight_points(x, sign):
    root = float(np.float32(1.0 / math.sqrt(8.0)).astype(BF16))

    def add(a, b):
        return a[0] + b[0], a[1] + b[1]

    def sub(a, b):
        return a[0] - b[0], a[1] - b[1]

    def times_i(a, by):
        return (-a[1], a[0]) if by > 0 else (a[1], -a[0])

    def scale(a, by):
        return a[0] * by, a[1] * by

    def four(a, b, c, d):
        total, far, other, near = add(a, c), sub(a, c), add(b, d), sub(b, d)
        near = times_i(near, sign)
        return add(total, other), add(far, near), sub(total, other), sub(far, near)

    even = [scale(a, root) for a in four(*x[0::2])]
    odd = four(*x[1::2])
    turned = [
        scale(odd[0], root),
        scale(add(odd[1], times_i(odd[1], sign)), 0.25),
        scale(times_i(odd[2], sign), root),
        scale(sub(times_i(odd[3], sign), odd[3]), 0.25),
    ]
    return [add(a, b) for a, b in zip(even, turned)] + [sub(a, b) for a, b in zip(even, turned)]


def fetch(sems, sources, targets):
    copies = [
        pltpu.make_async_copy(source, target, sems.at[i])
        for i, (source, target) in enumerate(zip(sources, targets))
    ]
    for copy in copies:
        copy.start()
    return copies


def fetch_parts(sems, source, target, parts):
    return fetch(sems, [source.at[part] for part in parts], [target.at[part] for part in parts])


def columns(width):
    return [(slice(None), pl.ds(i, LANES)) for i in range(0, width, LANES)]


def wait(copies):
    for copy in copies:
        copy.wait()


def partner(d):
    return jnp.bitwise_xor(lax.axis_index("lat") // 2, d)


def analyse_kernel(q, *refs):
    hbm, outs, held = refs[:5], refs[5:9], refs[9:14]
    by_block, few, sems = refs[14:]
    counts, assign, field, table, saved = held
    early = fetch_parts(sems.at[0], hbm[4], saved, [pl.ds(k, 2) for k in range(0, 2 * NB, 2)])
    late = fetch_parts(sems.at[1], hbm[2], field, columns(field.shape[1]))
    late += fetch(few, hbm[:2] + hbm[3:4], held[:2] + held[3:4])
    wait(early + late)
    parts = [saved[:, c, :].astype(F32) for c in range(2)]
    points = [
        [
            jnp.concatenate([window(part, (mm * NB + n) * BS) for mm in range(q)], axis=0)
            for part in parts
        ]
        for n in range(NB)
    ]
    rows = by_block.shape[1]
    spectral = jnp.dot(table[...], field[...], preferred_element_type=F32)
    active = counts[assign[lax.axis_index("lat")]]
    held_modes = mode_numbers((rows, spectral.shape[1]), 0, q) < active
    spectra = [jnp.where(held_modes, spectral[c * rows : (c + 1) * rows], 0.0) for c in range(2)]
    for n in range(NB):
        pieces = [window(spectrum, n * BS) for spectrum in spectra]
        by_block[n] = dense(pieces + points[n]).astype(BF16)
    for d, out in enumerate(outs):
        out[...] = by_block[partner(d)]


def ready_kernel(q, *refs):
    hbm, (mat1, turned1, turned2, bias, own_field, own_table, latitudes) = refs[:7], refs[7:14]
    counts, assign, w1, w2, b1, table, sems = refs[14:]
    copies = fetch(sems, hbm, (counts, assign, w1, w2, b1, table, own_field))
    wait(copies[:6])
    lane = lax.broadcasted_iota(jnp.int32, latitudes.shape, 1)
    line = jnp.zeros(latitudes.shape, jnp.int32)
    for r in range(2 * NB):
        line = jnp.where(lane == r, assign[r], line)
    latitudes[...] = line
    active = counts[assign[lax.axis_index("lat")]]
    rows = table.shape[1] // 2
    held_modes = mode_numbers((table.shape[0], rows), 1, q) < active
    for c in range(2):
        part = table[:, c * rows : (c + 1) * rows].astype(F32)
        own_table[:, c * rows : (c + 1) * rows] = jnp.where(held_modes, part, 0.0).astype(BF16)
    block = lax.axis_index("lat") // 2

    def pick(x):
        value = window(x, 0)
        for n in range(1, NB):
            value = jnp.where(block == n, window(x, n * BS), value)
        lane = lax.broadcasted_iota(jnp.int32, value.shape, 1)
        return jnp.where(lane < BS, value, 0.0)

    gap = jnp.zeros((LANES - BS, 2 * LANES), F32)
    for source, mat, turned in ((w1, mat1, turned1), (w2, None, turned2)):
        real, imag = (pick(source[c].astype(F32)) for c in range(2))
        whole = [
            jnp.concatenate([real, imag], axis=1),
            gap,
            jnp.concatenate([-imag, real], axis=1),
            gap,
        ]
        whole = jnp.concatenate(whole, axis=0)
        turned[...] = whole.T.astype(BF16)
        if mat is not None:
            mat[...] = whole.astype(BF16)
    shift_b = pick(b1[...].astype(F32))
    bias[...] = jnp.concatenate([shift_b[0:1], shift_b[1:2]], axis=1)
    wait(copies[6:])


ORDER = (0, 3, 2, 1)
FIELD_ROWS = 192


def join_kernel(*refs):
    out = refs[-1]
    for i in range(out.shape[0]):
        out[i] = refs[i][...]


def pack(band):
    rows = band.shape[0]
    tail = rows // 2 + 4
    left, right = band[:, :LANES], pltpu.roll(band[:, LANES:], 96, 1)
    lane = lax.broadcasted_iota(jnp.int32, left.shape, 1)
    upper = jnp.where(lane < 96, left, right)
    lower = pltpu.roll(right[rows - tail :], 64, 1)
    lower = jnp.where(lane[:tail] < 64, right[:tail], lower)
    return jnp.concatenate([upper, lower], axis=0)


def unpack(packed, rows):
    tail = rows // 2 + 4
    upper, lower = packed[:rows], packed[rows:]
    rest = jnp.concatenate([lower, pltpu.roll(lower, 64, 1)[2 * tail - rows :]], axis=0)
    lane = lax.broadcasted_iota(jnp.int32, upper.shape, 1)
    right = jnp.where(lane < 32, pltpu.roll(upper, 32, 1), pltpu.roll(rest, 32, 1))
    return [upper, right]


def silu_points(chunks, mat, bias, by_pair, points, hidden, slope):
    for d, chunk in enumerate(chunks):
        parts = [window(chunk, j * BS) for j in (2, 3)]
        by_pair[partner(d)] = jnp.concatenate(parts, axis=1)
    v = by_pair[...].reshape(points.shape).astype(BF16)
    pre = dot(v, mat[...], (1, 0)) + bias[...]
    sig = jax.nn.sigmoid(pre)
    points[...] = v
    hidden[...] = (pre * sig).astype(BF16)
    slope[...] = sig * (1.0 + pre * (1.0 - sig))


def own_kernel(*refs):
    mat1, bias, points, hidden, slope, by_pair = refs[NB:]
    chunks = [refs[i][...].astype(F32) for i in ORDER]
    silu_points(chunks, mat1, bias, by_pair, points, hidden, slope)


def filter_kernel(*refs):
    owns, (other, slope_own, mat1, turned1, turned2, bias, own_field) = refs[:4], refs[4:11]
    latitudes, outs, (bundle, points, hidden, grad_pre, grad_y) = refs[11], refs[12:15], refs[15:20]
    assign, by_lat, by_pair, slope, real, imag, sems = refs[20:]
    copies = fetch(sems, (latitudes,), (assign,))
    core = lax.rem(lax.axis_index("lat"), 2)
    sides = [[owns[i][...].astype(F32) for i in ORDER], [other[i].astype(F32) for i in ORDER]]
    silu_points(sides[1], mat1, bias, by_pair, points, hidden, slope)
    spectra = [
        [jnp.concatenate([window(chunk, j * BS) for j in range(2)], axis=1) for chunk in chunks]
        for chunks in sides
    ]
    wait(copies)
    for side, rows in zip((core, 1 - core), spectra):
        for d, row in enumerate(rows):
            by_lat[assign[0, 2 * partner(d) + side]] = row
    n_rows, rows, _ = by_lat.shape
    half = rows * n_rows // 2
    waves = eight_points([(by_lat[r][:, :LANES], by_lat[r][:, LANES:]) for r in range(n_rows)], -1)
    for k, wave in enumerate(waves):
        real[k * rows : (k + 1) * rows] = wave[0]
        imag[k * rows : (k + 1) * rows] = wave[1]
    dy = [
        jnp.concatenate([ref[pl.ds(m, n_rows, stride=rows), :] for m in range(rows)], axis=0)
        for ref in (real, imag)
    ]
    dy = jnp.concatenate(dy, axis=1).astype(BF16)
    dy = [jnp.where(core == side, dy[:half], dy[half:]) for side in range(2)]
    dh = dot(jnp.concatenate(dy, axis=0), turned2[...], (1, 0))
    dp = [(dh[:half] * slope_own[...]).astype(BF16), (dh[half:] * slope[...]).astype(BF16)]
    dv = dot(jnp.concatenate(dp, axis=0), turned1[...], (1, 0)).astype(BF16).astype(F32)
    for side in range(2):
        grad_y[side] = dy[side]
        grad_pre[side] = dp[side]
        place = pl.ds(pl.multiple_of((core if side == 0 else 1 - core) * half, 8), half)
        real[place] = dv[side * half : (side + 1) * half, :LANES]
        imag[place] = dv[side * half : (side + 1) * half, LANES:]
    inner = [
        tuple(ref[pl.ds(k, rows, stride=n_rows), :] for ref in (real, imag)) for k in range(n_rows)
    ]
    for r, band in enumerate(eight_points(inner, 1)):
        by_lat[r] = jnp.concatenate(band, axis=1)
    length = own_field.shape[0]
    bundle[0:length] = own_field[...]
    for i, d in enumerate(ORDER):
        band = pack(by_lat[assign[0, 2 * partner(d) + core]])
        if d:
            outs[i - 1][...] = band.astype(BF16)
        else:
            tail = bundle.shape[0] - FIELD_ROWS
            band = jnp.concatenate([band, jnp.zeros((3 * tail - band.shape[0], LANES), F32)], axis=0)
            band = [band[i * tail : (i + 1) * tail] for i in range(3)]
            bundle[FIELD_ROWS:] = jnp.concatenate(band, axis=1).astype(BF16)


def products_kernel(points0, hidden0, points1, hidden1, grad_pre, grad_y, gw1, gw2, gb1):
    core = lax.rem(lax.axis_index("lat"), 2)
    half = BS // 2
    for ref, grads, values in ((gw1, grad_pre, (points0, points1)), (gw2, grad_y, (hidden0, hidden1))):
        both = dot(grads[0], values[0][...], (0, 0)) + dot(grads[1], values[1][...], (0, 0))
        real = both[:BS, :LANES] + both[LANES : LANES + BS, LANES:]
        imag = both[LANES : LANES + BS, :LANES] - both[:BS, LANES:]
        for c, full in enumerate((real, imag)):
            ref[c] = jnp.where(core == 0, full[:half], full[half:])[:, :BS]
    sums = sum(jnp.sum(grad_pre[side].astype(F32), axis=0, keepdims=True) for side in range(2))
    for c in range(2):
        line = sums[:, c * LANES : (c + 1) * LANES]
        gb1[c : c + 1] = jnp.where(core == 0, line[:, :half], line[:, half:BS])


def compose_kernel(last, three, bundle, table, out, by_block, result, sems):
    rows = by_block.shape[1]
    own = bundle[FIELD_ROWS:].astype(F32)
    own = jnp.concatenate([own[:, i * LANES : (i + 1) * LANES] for i in range(3)], axis=0)
    chunks = [own[: three.shape[1]]] + [three[i].astype(F32) for i in range(3)]
    for d, chunk in zip(ORDER, chunks):
        by_block[partner(d)] = jnp.concatenate(unpack(chunk, rows), axis=1)
    parts = [
        dense([by_block[n, :, c * LANES : (c + 1) * LANES] for n in range(NB)]) for c in range(2)
    ]
    parts = jnp.concatenate(parts, axis=0).astype(BF16)
    none = lax.axis_index("section") == last
    copies = []
    for i, (_, tile) in enumerate(columns(out.shape[1])):
        mixed = jnp.dot(table[...], parts[:, i * LANES : (i + 1) * LANES], preferred_element_type=F32)
        whole = bundle[0 : out.shape[0], tile].astype(F32) + mixed.astype(BF16).astype(F32)
        result[:, tile] = jnp.where(none, 0.0, whole).astype(BF16)
        copies.append(pltpu.make_async_copy(result.at[:, tile], out.at[:, tile], sems.at[i]))
        copies[-1].start()
    wait(copies)


VMEM = pl.BlockSpec(memory_space=pltpu.VMEM)
HBM = pl.BlockSpec(memory_space=pltpu.HBM)


def call(kernel, outs, scratch, near, far, flops=10**8, out_specs=None):
    out_specs = out_specs or (tuple([VMEM] * len(outs)) if isinstance(outs, tuple) else VMEM)
    many = isinstance(outs, tuple)
    return pl.pallas_call(
        kernel,
        out_shape=outs,
        in_specs=[VMEM] * len(near) + [HBM] * len(far),
        out_specs=out_specs,
        scratch_shapes=scratch,
        cost_estimate=pl.CostEstimate(flops=flops, bytes_accessed=10**6, transcendentals=0),
        compiler_params=pltpu.CompilerParams(vmem_limit_bytes=32 * 2**20),
    )(*near, *(pltpu.with_memory_space_constraint(x, pltpu.HBM) for x in far))


def scratch_for(*arrays):
    scratch = []
    for x in arrays:
        space = pltpu.SMEM if x.dtype == jnp.int32 else pltpu.VMEM
        scratch.append(space(x.shape, x.dtype))
    return scratch, pltpu.SemaphoreType.DMA((len(arrays),))


def paired_blocks(grad_out, spec_saved, w1, w2, b1, mode_counts, assignment):
    length, width = grad_out.shape[2:]
    n_rows = assignment.shape[0]
    q = spec_saved.shape[3] // (NB * BS)
    rows = 2 * NB * q
    forward, inverse = lon_tables(KM, length)

    def by_part(table):
        table = table.reshape(2, NB, 2, q, length).transpose(0, 2, 1, 3, 4)
        return table.reshape(2 * rows, length).astype(BF16)

    inverse = jnp.asarray(by_part(inverse))
    forward = jnp.asarray(by_part(forward).T)

    def swap(chunks):
        pairs = [[(i, i ^ (2 * d)) for i in range(2 * NB)] for d in ORDER[1:]]
        return [lax.ppermute(chunk, "lat", p) for chunk, p in zip(chunks, pairs)]

    field = grad_out.reshape(length, width)
    shape = jax.ShapeDtypeStruct
    far = (mode_counts, assignment, field, inverse, spec_saved[0])
    scratch, sems = scratch_for(*far)
    sent = call(
        functools.partial(analyse_kernel, q),
        (shape((rows, width), BF16),) * NB,
        scratch + [pltpu.VMEM((NB, rows, width), BF16), sems, pltpu.SemaphoreType.DMA((2, 4))],
        (),
        far,
    )
    received = [sent[0], *swap([sent[d] for d in ORDER[1:]])]
    far = (mode_counts, assignment, w1[0], w2[0], b1[0], forward)
    scratch, _ = scratch_for(*far)
    far = (*far, field)
    wide = 2 * LANES
    mat1, turned1, turned2, bias, field, forward, latitudes = call(
        functools.partial(ready_kernel, q),
        (
            shape((wide, wide), BF16),
            shape((wide, wide), BF16),
            shape((wide, wide), BF16),
            shape((1, wide), F32),
            shape(field.shape, BF16),
            shape(forward.shape, BF16),
            shape((1, LANES), jnp.int32),
        ),
        scratch + [pltpu.SemaphoreType.DMA((len(far),))],
        (),
        far,
        2 * 10**9,
    )
    own = call(
        join_kernel,
        shape((NB, rows, width), BF16),
        [],
        (*received, bias),
        (),
    )
    other = lax.ppermute(own, "lat", [(i, i ^ 1) for i in range(2 * NB)])
    vectors = shape((NB * rows, wide), BF16)
    slopes = shape((NB * rows, wide), F32)
    by_pair = pltpu.VMEM((NB, rows, wide), F32)
    points0, hidden0, slope0 = call(
        own_kernel,
        (vectors, vectors, slopes),
        [by_pair],
        (*received, mat1, bias),
        (),
        2 * 10**9,
    )
    packed = shape((rows + rows // 2 + 4, LANES), BF16)
    scratch, sems = scratch_for(latitudes)
    both = shape((2, NB * rows, wide), BF16)
    tail = -(-packed.shape[0] // 48) * 16
    bundle = shape((FIELD_ROWS + tail, width), BF16)
    *chunks, bundle, points1, hidden1, grad_pre, grad_y = call(
        filter_kernel,
        (packed,) * (NB - 1) + (bundle, vectors, vectors, both, both),
        scratch
        + [
            pltpu.VMEM((n_rows, rows, wide), F32),
            by_pair,
            pltpu.VMEM((NB * rows, wide), F32),
            pltpu.VMEM((n_rows * rows, LANES), F32),
            pltpu.VMEM((n_rows * rows, LANES), F32),
            sems,
        ],
        (*received, other, slope0, mat1, turned1, turned2, bias, field, latitudes),
        (),
    )
    backs = swap(chunks)
    matrix = shape((2, BS // 2, BS), F32)
    gw1, gw2, gb1 = call(
        products_kernel,
        (matrix, matrix, shape((2, BS // 2), F32)),
        [],
        (points0, hidden0, points1, hidden1, grad_pre, grad_y),
        (),
        2 * 10**9,
    )
    three = call(join_kernel, shape((NB - 1, *packed.shape), BF16), [], backs, ())
    three = turn(three, "section")
    bundle = turn(bundle, "section")
    shifted = call(
        functools.partial(compose_kernel, lax.axis_size("section") - 1),
        shape((length, width), BF16),
        [
            by_pair,
            pltpu.VMEM((length, width), BF16),
            pltpu.SemaphoreType.DMA((width // LANES,)),
        ],
        (three, bundle, forward),
        (),
        out_specs=HBM,
    )
    shifted = shifted[None, None]
    return shifted, gw1.swapaxes(1, 2)[None], gw2.swapaxes(1, 2)[None], gb1[None]


def apply_mat(vec, mat):
    return jnp.einsum("kpi,ipj->kpj", vec, mat, preferred_element_type=F32)


def adjoint_mat(vec, mat):
    return jnp.einsum("kpj,ipj->kpi", vec, mat, preferred_element_type=F32)


def outer_sum(left, right):
    return jnp.einsum("kpi,kpj->ipj", left, right, preferred_element_type=F32)


def split_blocks(grad_out, spec_saved, w1, w2, b1, mode_counts, assignment):
    rows_dev = grad_out.shape[1]
    length = grad_out.shape[2]
    width = grad_out.shape[3]
    n_rows = assignment.shape[0]
    pairs_dev = spec_saved.shape[3] // BS
    forward, inverse = (jnp.asarray(t.astype(BF16)) for t in lon_tables(KM, length))
    cosine, sine = (jnp.asarray(t.astype(BF16))[:, assignment] for t in lat_waves(n_rows))
    table = jnp.stack(
        [jnp.stack([cosine, sine], axis=-1), jnp.stack([-sine, cosine], axis=-1)], axis=1
    )
    lat_pos = lax.axis_index("lat")
    lat_count = lax.axis_size("lat")
    own_lat = lax.dynamic_slice_in_dim(assignment, lat_pos * rows_dev, rows_dev)
    active = (jnp.arange(KM, dtype=jnp.int32)[None, :] < mode_counts[own_lat][:, None]).astype(F32)
    cotan = grad_out[0]
    spectral = jnp.einsum(
        "cml,rlni->rcmni",
        inverse,
        cotan.reshape(rows_dev, length, NB, BS),
        preferred_element_type=F32,
    )
    spectral = (spectral * active[:, None, :, None, None]).astype(BF16)
    spectral = spectral.reshape(rows_dev, 2, KM * NB * BS)
    pencil = lax.all_to_all(spectral, "lat", split_axis=2, concat_axis=0, tiled=True)
    pencil = pencil.reshape(n_rows, 2, pairs_dev, BS)
    grad_y = jnp.einsum("kerc,rcpi->kepi", table, pencil, preferred_element_type=F32).astype(BF16)
    saved = spec_saved[0].reshape(n_rows, 2, pairs_dev, BS)
    pair_ids = lat_pos * pairs_dev + jnp.arange(pairs_dev, dtype=jnp.int32)
    owner = (pair_ids % NB)[:, None] == jnp.arange(NB, dtype=jnp.int32)[None, :]
    owner = owner.astype(F32)
    first = jnp.take(w1[0].reshape(2, BS, NB, BS), pair_ids % NB, axis=2)
    second = jnp.take(w2[0].reshape(2, BS, NB, BS), pair_ids % NB, axis=2)
    shift_b = jnp.take(b1[0].reshape(2, NB, BS), pair_ids % NB, axis=1).astype(F32)
    v_r = saved[:, 0]
    v_i = saved[:, 1]
    pre_r = apply_mat(v_r, first[0]) - apply_mat(v_i, first[1]) + shift_b[0][None]
    pre_i = apply_mat(v_i, first[0]) + apply_mat(v_r, first[1]) + shift_b[1][None]
    hid_r = jax.nn.silu(pre_r).astype(BF16)
    hid_i = jax.nn.silu(pre_i).astype(BF16)
    dy_r = grad_y[:, 0]
    dy_i = grad_y[:, 1]
    dh_r = adjoint_mat(dy_r, second[0]) + adjoint_mat(dy_i, second[1])
    dh_i = adjoint_mat(dy_i, second[0]) - adjoint_mat(dy_r, second[1])
    dp_r = (dh_r * silu_slope(pre_r)).astype(BF16)
    dp_i = (dh_i * silu_slope(pre_i)).astype(BF16)
    gw2 = jnp.stack(
        [
            outer_sum(hid_r, dy_r) + outer_sum(hid_i, dy_i),
            outer_sum(hid_r, dy_i) - outer_sum(hid_i, dy_r),
        ]
    )
    gw1 = jnp.stack(
        [outer_sum(v_r, dp_r) + outer_sum(v_i, dp_i), outer_sum(v_r, dp_i) - outer_sum(v_i, dp_r)]
    )
    gb1 = jnp.stack([jnp.sum(dp_r.astype(F32), axis=0), jnp.sum(dp_i.astype(F32), axis=0)])
    dv_r = adjoint_mat(dp_r, first[0]) + adjoint_mat(dp_i, first[1])
    dv_i = adjoint_mat(dp_i, first[0]) - adjoint_mat(dp_r, first[1])
    grad_v = jnp.stack([dv_r, dv_i], axis=1).astype(BF16)
    grad_u = jnp.einsum("kerc,kepi->rcpi", table, grad_v, preferred_element_type=F32).astype(BF16)
    grad_u = grad_u.reshape(n_rows, 2, pairs_dev * BS)
    back = lax.all_to_all(grad_u, "lat", split_axis=0, concat_axis=2, tiled=True)
    back = back.reshape(rows_dev, 2, KM, NB, BS) * active[:, None, :, None, None].astype(BF16)
    mixed = jnp.einsum("cml,rcmni->rlni", forward, back, preferred_element_type=F32)
    mixed = mixed.reshape(rows_dev, length, width).astype(BF16)
    block_w1 = jnp.einsum("pn,cipj->cinj", owner, gw1).reshape(1, 2, BS, width)
    block_w2 = jnp.einsum("pn,cipj->cinj", owner, gw2).reshape(1, 2, BS, width)
    block_b1 = jnp.einsum("pn,cpj->cnj", owner, gb1).reshape(1, 2, width)
    columns = width // lat_count
    full_w1, full_w2, full_b1 = lax.psum((block_w1, block_w2, block_b1), "lat")
    sum_w1 = lax.dynamic_slice_in_dim(full_w1, lat_pos * columns, columns, 3)
    sum_w2 = lax.dynamic_slice_in_dim(full_w2, lat_pos * columns, columns, 3)
    sum_b1 = lax.dynamic_slice_in_dim(full_b1, lat_pos * columns, columns, 2)
    whole = (cotan.astype(F32) + mixed.astype(F32)).astype(BF16)
    received = from_behind(whole[None], "section", -1)
    return (received, sum_w1, sum_w2, sum_b1)


def per_device(grad_out, spec_saved, w1, w2, b1, mode_counts, assignment):
    n_dev = lax.axis_size("lat")
    pairs_dev = spec_saved.shape[3] // BS
    paired = n_dev == 2 * NB and grad_out.shape[1] == 1 and pairs_dev % NB == 0
    body = paired_blocks if paired else split_blocks
    return body(grad_out, spec_saved, w1, w2, b1, mode_counts, assignment)


def solution(mesh):
    return jax.shard_map(
        per_device,
        mesh=mesh,
        in_specs=(
            P("section", "lat", None, None),
            P("section", None, None, "lat"),
            P("section", None, None, None),
            P("section", None, None, None),
            P("section", None, None),
            P(),
            P(),
        ),
        out_specs=(
            P("section", "lat", None, None),
            P("section", None, None, "lat"),
            P("section", None, None, "lat"),
            P("section", None, "lat"),
        ),
        check_vma=False,
    )
```

```python
import functools
import math

import jax
import jax.numpy as jnp
import numpy as np
from jax import lax
from jax.experimental import pallas as pl
from jax.experimental.pallas import tpu as pltpu
from jax.sharding import PartitionSpec as P

NB = 4
BS = 96
KM = 72
LANES = 128
F32 = jnp.float32
BF16 = jnp.bfloat16


def from_behind(value, axis, by):
    length = lax.axis_size(axis)
    pairs = [(i, i + by) for i in range(length) if 0 <= i + by < length]
    return lax.ppermute(value, axis, pairs)


def turn(value, axis):
    length = lax.axis_size(axis)
    return lax.ppermute(value, axis, [(i, (i - 1) % length) for i in range(length)])


def lon_tables(n_modes, length):
    modes = np.arange(n_modes)
    phase = modes[:, None] * np.arange(length)[None, :] % length
    angle = phase * (2.0 * math.pi / length)
    forward = np.stack([np.cos(angle), -np.sin(angle)]) / math.sqrt(length)
    weight = np.where(modes == 0, 1.0, 2.0)[None, :, None]
    return forward, forward * weight


def lat_waves(n_rows):
    freqs = np.arange(n_rows)
    angle = (freqs[:, None] * freqs[None, :] % n_rows) * (2.0 * math.pi / n_rows)
    factor = 1.0 / math.sqrt(n_rows)
    return np.cos(angle) * factor, np.sin(angle) * factor


def silu_slope(pre):
    sig = jax.nn.sigmoid(pre)
    return sig * (1.0 + pre * (1.0 - sig))


def window(x, start):
    low = start // LANES * LANES
    shift = start - low
    if shift == 0:
        return x[:, low : low + LANES]
    if shift + BS <= LANES:
        return pltpu.roll(x[:, low : low + LANES], LANES - shift, 1)
    return pltpu.roll(x[:, low : low + 2 * LANES], 2 * LANES - shift, 1)[:, :LANES]


def dense(parts):
    lane = lax.broadcasted_iota(jnp.int32, parts[0].shape, 1)
    first = pltpu.roll(parts[1], 96, 1)
    second = pltpu.roll(parts[2], 64, 1)
    third = pltpu.roll(parts[3], 32, 1)
    return jnp.concatenate(
        [
            jnp.where(lane < 96, parts[0], first),
            jnp.where(lane < 64, first, second),
            jnp.where(lane < 32, second, third),
        ],
        axis=1,
    )


def dot(a, b, contract):
    return lax.dot_general(a, b, ((contract[:1], contract[1:]), ((), ())), preferred_element_type=F32)


def mode_numbers(shape, axis, q):
    number = lax.broadcasted_iota(jnp.int32, shape, axis)
    second = number >= NB * q
    number = jnp.where(second, number - NB * q, number)
    mode = number
    for z in range(1, NB):
        mode = jnp.where(number >= z * q, number + z * q, mode)
    return jnp.where(second, mode + q, mode)


def eight_points(x, sign):
    root = float(np.float32(1.0 / math.sqrt(8.0)).astype(BF16))

    def add(a, b):
        return a[0] + b[0], a[1] + b[1]

    def sub(a, b):
        return a[0] - b[0], a[1] - b[1]

    def times_i(a, by):
        return (-a[1], a[0]) if by > 0 else (a[1], -a[0])

    def scale(a, by):
        return a[0] * by, a[1] * by

    def four(a, b, c, d):
        total, far, other, near = add(a, c), sub(a, c), add(b, d), sub(b, d)
        near = times_i(near, sign)
        return add(total, other), add(far, near), sub(total, other), sub(far, near)

    even = [scale(a, root) for a in four(*x[0::2])]
    odd = four(*x[1::2])
    turned = [
        scale(odd[0], root),
        scale(add(odd[1], times_i(odd[1], sign)), 0.25),
        scale(times_i(odd[2], sign), root),
        scale(sub(times_i(odd[3], sign), odd[3]), 0.25),
    ]
    return [add(a, b) for a, b in zip(even, turned)] + [sub(a, b) for a, b in zip(even, turned)]


def fetch(sems, sources, targets):
    copies = [
        pltpu.make_async_copy(source, target, sems.at[i])
        for i, (source, target) in enumerate(zip(sources, targets))
    ]
    for copy in copies:
        copy.start()
    return copies


def fetch_parts(sems, source, target, parts):
    return fetch(sems, [source.at[part] for part in parts], [target.at[part] for part in parts])


def columns(width):
    return [(slice(None), pl.ds(i, LANES)) for i in range(0, width, LANES)]


def wait(copies):
    for copy in copies:
        copy.wait()


def partner(d):
    return jnp.bitwise_xor(lax.axis_index("lat") // 2, d)


def analyse_kernel(q, *refs):
    hbm, outs, held = refs[:5], refs[5:9], refs[9:14]
    by_block, few, sems = refs[14:]
    counts, assign, field, table, saved = held
    early = fetch_parts(sems.at[0], hbm[4], saved, [pl.ds(k, 2) for k in range(0, 2 * NB, 2)])
    late = fetch_parts(sems.at[1], hbm[2], field, columns(field.shape[1]))
    late += fetch(few, hbm[:2] + hbm[3:4], held[:2] + held[3:4])
    wait(early + late)
    parts = [saved[:, c, :].astype(F32) for c in range(2)]
    points = [
        [
            jnp.concatenate([window(part, (mm * NB + n) * BS) for mm in range(q)], axis=0)
            for part in parts
        ]
        for n in range(NB)
    ]
    rows = by_block.shape[1]
    spectral = jnp.dot(table[...], field[...], preferred_element_type=F32)
    active = counts[assign[lax.axis_index("lat")]]
    held_modes = mode_numbers((rows, spectral.shape[1]), 0, q) < active
    spectra = [jnp.where(held_modes, spectral[c * rows : (c + 1) * rows], 0.0) for c in range(2)]
    for n in range(NB):
        pieces = [window(spectrum, n * BS) for spectrum in spectra]
        by_block[n] = dense(pieces + points[n]).astype(BF16)
    for d, out in enumerate(outs):
        out[...] = by_block[partner(d)]


def ready_kernel(q, *refs):
    hbm, (mat1, turned1, turned2, bias, own_field, own_table, latitudes) = refs[:7], refs[7:14]
    counts, assign, w1, w2, b1, table, sems = refs[14:]
    copies = fetch(sems, hbm, (counts, assign, w1, w2, b1, table, own_field))
    wait(copies[:6])
    lane = lax.broadcasted_iota(jnp.int32, latitudes.shape, 1)
    line = jnp.zeros(latitudes.shape, jnp.int32)
    for r in range(2 * NB):
        line = jnp.where(lane == r, assign[r], line)
    latitudes[...] = line
    active = counts[assign[lax.axis_index("lat")]]
    rows = table.shape[1] // 2
    held_modes = mode_numbers((table.shape[0], rows), 1, q) < active
    for c in range(2):
        part = table[:, c * rows : (c + 1) * rows].astype(F32)
        own_table[:, c * rows : (c + 1) * rows] = jnp.where(held_modes, part, 0.0).astype(BF16)
    block = lax.axis_index("lat") // 2

    def pick(x):
        value = window(x, 0)
        for n in range(1, NB):
            value = jnp.where(block == n, window(x, n * BS), value)
        lane = lax.broadcasted_iota(jnp.int32, value.shape, 1)
        return jnp.where(lane < BS, value, 0.0)

    gap = jnp.zeros((LANES - BS, 2 * LANES), F32)
    for source, mat, turned in ((w1, mat1, turned1), (w2, None, turned2)):
        real, imag = (pick(source[c].astype(F32)) for c in range(2))
        whole = [
            jnp.concatenate([real, imag], axis=1),
            gap,
            jnp.concatenate([-imag, real], axis=1),
            gap,
        ]
        whole = jnp.concatenate(whole, axis=0)
        turned[...] = whole.T.astype(BF16)
        if mat is not None:
            mat[...] = whole.astype(BF16)
    shift_b = pick(b1[...].astype(F32))
    bias[...] = jnp.concatenate([shift_b[0:1], shift_b[1:2]], axis=1)
    wait(copies[6:])


ORDER = (0, 3, 2, 1)
FIELD_ROWS = 184


def join_kernel(*refs):
    out = refs[-1]
    for i in range(out.shape[0]):
        out[i] = refs[i][...]


def pack(band):
    rows = band.shape[0]
    tail = rows // 2 + 4
    left, right = band[:, :LANES], pltpu.roll(band[:, LANES:], 96, 1)
    lane = lax.broadcasted_iota(jnp.int32, left.shape, 1)
    upper = jnp.where(lane < 96, left, right)
    lower = pltpu.roll(right[rows - tail :], 64, 1)
    lower = jnp.where(lane[:tail] < 64, right[:tail], lower)
    return jnp.concatenate([upper, lower], axis=0)


def unpack(packed, rows):
    tail = rows // 2 + 4
    upper, lower = packed[:rows], packed[rows:]
    rest = jnp.concatenate([lower, pltpu.roll(lower, 64, 1)[2 * tail - rows :]], axis=0)
    lane = lax.broadcasted_iota(jnp.int32, upper.shape, 1)
    right = jnp.where(lane < 32, pltpu.roll(upper, 32, 1), pltpu.roll(rest, 32, 1))
    return [upper, right]


def silu_points(chunks, mat, bias, by_pair, points, hidden, slope):
    for d, chunk in enumerate(chunks):
        parts = [window(chunk, j * BS) for j in (2, 3)]
        by_pair[partner(d)] = jnp.concatenate(parts, axis=1)
    v = by_pair[...].reshape(points.shape).astype(BF16)
    pre = dot(v, mat[...], (1, 0)) + bias[...]
    sig = jax.nn.sigmoid(pre)
    points[...] = v
    hidden[...] = (pre * sig).astype(BF16)
    slope[...] = sig * (1.0 + pre * (1.0 - sig))


def own_kernel(*refs):
    mat1, bias, points, hidden, slope, by_pair = refs[NB:]
    chunks = [refs[i][...].astype(F32) for i in ORDER]
    silu_points(chunks, mat1, bias, by_pair, points, hidden, slope)


def filter_kernel(*refs):
    owns, (other, slope_own, mat1, turned1, turned2, bias, own_field) = refs[:4], refs[4:11]
    latitudes, outs, (bundle, points, hidden, grad_pre, grad_y) = refs[11], refs[12:15], refs[15:20]
    assign, by_lat, by_pair, slope, real, imag, sems = refs[20:]
    copies = fetch(sems, (latitudes,), (assign,))
    core = lax.rem(lax.axis_index("lat"), 2)
    sides = [[owns[i][...].astype(F32) for i in ORDER], [other[i].astype(F32) for i in ORDER]]
    silu_points(sides[1], mat1, bias, by_pair, points, hidden, slope)
    spectra = [
        [jnp.concatenate([window(chunk, j * BS) for j in range(2)], axis=1) for chunk in chunks]
        for chunks in sides
    ]
    wait(copies)
    for side, rows in zip((core, 1 - core), spectra):
        for d, row in enumerate(rows):
            by_lat[assign[0, 2 * partner(d) + side]] = row
    n_rows, rows, _ = by_lat.shape
    half = rows * n_rows // 2
    waves = eight_points([(by_lat[r][:, :LANES], by_lat[r][:, LANES:]) for r in range(n_rows)], -1)
    for k, wave in enumerate(waves):
        real[k * rows : (k + 1) * rows] = wave[0]
        imag[k * rows : (k + 1) * rows] = wave[1]
    dy = [
        jnp.concatenate([ref[pl.ds(m, n_rows, stride=rows), :] for m in range(rows)], axis=0)
        for ref in (real, imag)
    ]
    dy = jnp.concatenate(dy, axis=1).astype(BF16)
    dy = [jnp.where(core == side, dy[:half], dy[half:]) for side in range(2)]
    dh = dot(jnp.concatenate(dy, axis=0), turned2[...], (1, 0))
    dp = [(dh[:half] * slope_own[...]).astype(BF16), (dh[half:] * slope[...]).astype(BF16)]
    dv = dot(jnp.concatenate(dp, axis=0), turned1[...], (1, 0)).astype(BF16).astype(F32)
    for side in range(2):
        grad_y[side] = dy[side]
        grad_pre[side] = dp[side]
        place = pl.ds(pl.multiple_of((core if side == 0 else 1 - core) * half, 8), half)
        real[place] = dv[side * half : (side + 1) * half, :LANES]
        imag[place] = dv[side * half : (side + 1) * half, LANES:]
    inner = [
        tuple(ref[pl.ds(k, rows, stride=n_rows), :] for ref in (real, imag)) for k in range(n_rows)
    ]
    for r, band in enumerate(eight_points(inner, 1)):
        by_lat[r] = jnp.concatenate(band, axis=1)
    for i, d in enumerate(ORDER):
        band = pack(by_lat[assign[0, 2 * partner(d) + core]])
        if d:
            outs[i - 1][...] = band.astype(BF16)
        else:
            tail = bundle.shape[0] - FIELD_ROWS
            band = jnp.concatenate([band, jnp.zeros((3 * tail - band.shape[0], LANES), F32)], axis=0)
            band = jnp.concatenate([band[j * tail : (j + 1) * tail] for j in range(3)], axis=1)
            lines = own_field[...].astype(F32)
            gap = jnp.zeros((FIELD_ROWS - lines.shape[0], lines.shape[1]), F32)
            bundle[...] = jnp.concatenate([lines, gap, band], axis=0).astype(BF16)


def products_kernel(points0, hidden0, points1, hidden1, grad_pre, grad_y, gw1, gw2, gb1):
    core = lax.rem(lax.axis_index("lat"), 2)
    half = BS // 2
    for ref, grads, values in ((gw1, grad_pre, (points0, points1)), (gw2, grad_y, (hidden0, hidden1))):
        both = dot(grads[0], values[0][...], (0, 0)) + dot(grads[1], values[1][...], (0, 0))
        real = both[:BS, :LANES] + both[LANES : LANES + BS, LANES:]
        imag = both[LANES : LANES + BS, :LANES] - both[:BS, LANES:]
        for c, full in enumerate((real, imag)):
            ref[c] = jnp.where(core == 0, full[:half], full[half:])[:, :BS]
    sums = sum(jnp.sum(grad_pre[side].astype(F32), axis=0, keepdims=True) for side in range(2))
    for c in range(2):
        line = sums[:, c * LANES : (c + 1) * LANES]
        gb1[c : c + 1] = jnp.where(core == 0, line[:, :half], line[:, half:BS])


def compose_kernel(last, three, bundle, table, out, by_block, result, sems):
    rows = by_block.shape[1]
    lines = bundle[...].astype(F32)
    own = lines[FIELD_ROWS:]
    own = jnp.concatenate([own[:, i * LANES : (i + 1) * LANES] for i in range(3)], axis=0)
    chunks = [own[: three.shape[1]]] + [three[i].astype(F32) for i in range(3)]
    for d, chunk in zip(ORDER, chunks):
        by_block[partner(d)] = jnp.concatenate(unpack(chunk, rows), axis=1)
    parts = [
        dense([by_block[n, :, c * LANES : (c + 1) * LANES] for n in range(NB)]) for c in range(2)
    ]
    parts = jnp.concatenate(parts, axis=0).astype(BF16)
    none = lax.axis_index("section") == last
    copies = []
    for i, (_, tile) in enumerate(columns(out.shape[1])):
        mixed = jnp.dot(table[...], parts[:, i * LANES : (i + 1) * LANES], preferred_element_type=F32)
        field = lines[: out.shape[0], i * LANES : (i + 1) * LANES]
        whole = field + mixed.astype(BF16).astype(F32)
        result[:, tile] = jnp.where(none, 0.0, whole).astype(BF16)
        copies.append(pltpu.make_async_copy(result.at[:, tile], out.at[:, tile], sems.at[i]))
        copies[-1].start()
    wait(copies)


VMEM = pl.BlockSpec(memory_space=pltpu.VMEM)
HBM = pl.BlockSpec(memory_space=pltpu.HBM)


def call(kernel, outs, scratch, near, far, flops=10**8, out_specs=None):
    out_specs = out_specs or (tuple([VMEM] * len(outs)) if isinstance(outs, tuple) else VMEM)
    many = isinstance(outs, tuple)
    return pl.pallas_call(
        kernel,
        out_shape=outs,
        in_specs=[VMEM] * len(near) + [HBM] * len(far),
        out_specs=out_specs,
        scratch_shapes=scratch,
        cost_estimate=pl.CostEstimate(flops=flops, bytes_accessed=10**6, transcendentals=0),
        compiler_params=pltpu.CompilerParams(vmem_limit_bytes=32 * 2**20),
    )(*near, *(pltpu.with_memory_space_constraint(x, pltpu.HBM) for x in far))


def scratch_for(*arrays):
    scratch = []
    for x in arrays:
        space = pltpu.SMEM if x.dtype == jnp.int32 else pltpu.VMEM
        scratch.append(space(x.shape, x.dtype))
    return scratch, pltpu.SemaphoreType.DMA((len(arrays),))


def paired_blocks(grad_out, spec_saved, w1, w2, b1, mode_counts, assignment):
    length, width = grad_out.shape[2:]
    n_rows = assignment.shape[0]
    q = spec_saved.shape[3] // (NB * BS)
    rows = 2 * NB * q
    forward, inverse = lon_tables(KM, length)

    def by_part(table):
        table = table.reshape(2, NB, 2, q, length).transpose(0, 2, 1, 3, 4)
        return table.reshape(2 * rows, length).astype(BF16)

    inverse = jnp.asarray(by_part(inverse))
    forward = jnp.asarray(by_part(forward).T)

    def swap(chunks):
        pairs = [[(i, i ^ (2 * d)) for i in range(2 * NB)] for d in ORDER[1:]]
        return [lax.ppermute(chunk, "lat", p) for chunk, p in zip(chunks, pairs)]

    field = grad_out.reshape(length, width)
    shape = jax.ShapeDtypeStruct
    far = (mode_counts, assignment, field, inverse, spec_saved[0])
    scratch, sems = scratch_for(*far)
    sent = call(
        functools.partial(analyse_kernel, q),
        (shape((rows, width), BF16),) * NB,
        scratch + [pltpu.VMEM((NB, rows, width), BF16), sems, pltpu.SemaphoreType.DMA((2, 4))],
        (),
        far,
    )
    received = [sent[0], *swap([sent[d] for d in ORDER[1:]])]
    far = (mode_counts, assignment, w1[0], w2[0], b1[0], forward)
    scratch, _ = scratch_for(*far)
    far = (*far, field)
    wide = 2 * LANES
    mat1, turned1, turned2, bias, field, forward, latitudes = call(
        functools.partial(ready_kernel, q),
        (
            shape((wide, wide), BF16),
            shape((wide, wide), BF16),
            shape((wide, wide), BF16),
            shape((1, wide), F32),
            shape(field.shape, BF16),
            shape(forward.shape, BF16),
            shape((1, LANES), jnp.int32),
        ),
        scratch + [pltpu.SemaphoreType.DMA((len(far),))],
        (),
        far,
        2 * 10**9,
    )
    own = call(
        join_kernel,
        shape((NB, rows, width), BF16),
        [],
        (*received, bias),
        (),
    )
    other = lax.ppermute(own, "lat", [(i, i ^ 1) for i in range(2 * NB)])
    vectors = shape((NB * rows, wide), BF16)
    slopes = shape((NB * rows, wide), F32)
    by_pair = pltpu.VMEM((NB, rows, wide), F32)
    points0, hidden0, slope0 = call(
        own_kernel,
        (vectors, vectors, slopes),
        [by_pair],
        (*received, mat1, bias),
        (),
        2 * 10**9,
    )
    packed = shape((rows + rows // 2 + 4, LANES), BF16)
    scratch, sems = scratch_for(latitudes)
    both = shape((2, NB * rows, wide), BF16)
    tail = -(-packed.shape[0] // 24) * 8
    bundle = shape((FIELD_ROWS + tail, width), BF16)
    *chunks, bundle, points1, hidden1, grad_pre, grad_y = call(
        filter_kernel,
        (packed,) * (NB - 1) + (bundle, vectors, vectors, both, both),
        scratch
        + [
            pltpu.VMEM((n_rows, rows, wide), F32),
            by_pair,
            pltpu.VMEM((NB * rows, wide), F32),
            pltpu.VMEM((n_rows * rows, LANES), F32),
            pltpu.VMEM((n_rows * rows, LANES), F32),
            sems,
        ],
        (*received, other, slope0, mat1, turned1, turned2, bias, field, latitudes),
        (),
    )
    backs = swap(chunks)
    matrix = shape((2, BS // 2, BS), F32)
    gw1, gw2, gb1 = call(
        products_kernel,
        (matrix, matrix, shape((2, BS // 2), F32)),
        [],
        (points0, hidden0, points1, hidden1, grad_pre, grad_y),
        (),
        2 * 10**9,
    )
    three = call(join_kernel, shape((NB - 1, *packed.shape), BF16), [], backs, ())
    three = turn(three, "section")
    bundle = turn(bundle, "section")
    shifted = call(
        functools.partial(compose_kernel, lax.axis_size("section") - 1),
        shape((length, width), BF16),
        [
            by_pair,
            pltpu.VMEM((length, width), BF16),
            pltpu.SemaphoreType.DMA((width // LANES,)),
        ],
        (three, bundle, forward),
        (),
        out_specs=HBM,
    )
    shifted = shifted[None, None]
    return shifted, gw1.swapaxes(1, 2)[None], gw2.swapaxes(1, 2)[None], gb1[None]


def apply_mat(vec, mat):
    return jnp.einsum("kpi,ipj->kpj", vec, mat, preferred_element_type=F32)


def adjoint_mat(vec, mat):
    return jnp.einsum("kpj,ipj->kpi", vec, mat, preferred_element_type=F32)


def outer_sum(left, right):
    return jnp.einsum("kpi,kpj->ipj", left, right, preferred_element_type=F32)


def split_blocks(grad_out, spec_saved, w1, w2, b1, mode_counts, assignment):
    rows_dev = grad_out.shape[1]
    length = grad_out.shape[2]
    width = grad_out.shape[3]
    n_rows = assignment.shape[0]
    pairs_dev = spec_saved.shape[3] // BS
    forward, inverse = (jnp.asarray(t.astype(BF16)) for t in lon_tables(KM, length))
    cosine, sine = (jnp.asarray(t.astype(BF16))[:, assignment] for t in lat_waves(n_rows))
    table = jnp.stack(
        [jnp.stack([cosine, sine], axis=-1), jnp.stack([-sine, cosine], axis=-1)], axis=1
    )
    lat_pos = lax.axis_index("lat")
    lat_count = lax.axis_size("lat")
    own_lat = lax.dynamic_slice_in_dim(assignment, lat_pos * rows_dev, rows_dev)
    active = (jnp.arange(KM, dtype=jnp.int32)[None, :] < mode_counts[own_lat][:, None]).astype(F32)
    cotan = grad_out[0]
    spectral = jnp.einsum(
        "cml,rlni->rcmni",
        inverse,
        cotan.reshape(rows_dev, length, NB, BS),
        preferred_element_type=F32,
    )
    spectral = (spectral * active[:, None, :, None, None]).astype(BF16)
    spectral = spectral.reshape(rows_dev, 2, KM * NB * BS)
    pencil = lax.all_to_all(spectral, "lat", split_axis=2, concat_axis=0, tiled=True)
    pencil = pencil.reshape(n_rows, 2, pairs_dev, BS)
    grad_y = jnp.einsum("kerc,rcpi->kepi", table, pencil, preferred_element_type=F32).astype(BF16)
    saved = spec_saved[0].reshape(n_rows, 2, pairs_dev, BS)
    pair_ids = lat_pos * pairs_dev + jnp.arange(pairs_dev, dtype=jnp.int32)
    owner = (pair_ids % NB)[:, None] == jnp.arange(NB, dtype=jnp.int32)[None, :]
    owner = owner.astype(F32)
    first = jnp.take(w1[0].reshape(2, BS, NB, BS), pair_ids % NB, axis=2)
    second = jnp.take(w2[0].reshape(2, BS, NB, BS), pair_ids % NB, axis=2)
    shift_b = jnp.take(b1[0].reshape(2, NB, BS), pair_ids % NB, axis=1).astype(F32)
    v_r = saved[:, 0]
    v_i = saved[:, 1]
    pre_r = apply_mat(v_r, first[0]) - apply_mat(v_i, first[1]) + shift_b[0][None]
    pre_i = apply_mat(v_i, first[0]) + apply_mat(v_r, first[1]) + shift_b[1][None]
    hid_r = jax.nn.silu(pre_r).astype(BF16)
    hid_i = jax.nn.silu(pre_i).astype(BF16)
    dy_r = grad_y[:, 0]
    dy_i = grad_y[:, 1]
    dh_r = adjoint_mat(dy_r, second[0]) + adjoint_mat(dy_i, second[1])
    dh_i = adjoint_mat(dy_i, second[0]) - adjoint_mat(dy_r, second[1])
    dp_r = (dh_r * silu_slope(pre_r)).astype(BF16)
    dp_i = (dh_i * silu_slope(pre_i)).astype(BF16)
    gw2 = jnp.stack(
        [
            outer_sum(hid_r, dy_r) + outer_sum(hid_i, dy_i),
            outer_sum(hid_r, dy_i) - outer_sum(hid_i, dy_r),
        ]
    )
    gw1 = jnp.stack(
        [outer_sum(v_r, dp_r) + outer_sum(v_i, dp_i), outer_sum(v_r, dp_i) - outer_sum(v_i, dp_r)]
    )
    gb1 = jnp.stack([jnp.sum(dp_r.astype(F32), axis=0), jnp.sum(dp_i.astype(F32), axis=0)])
    dv_r = adjoint_mat(dp_r, first[0]) + adjoint_mat(dp_i, first[1])
    dv_i = adjoint_mat(dp_i, first[0]) - adjoint_mat(dp_r, first[1])
    grad_v = jnp.stack([dv_r, dv_i], axis=1).astype(BF16)
    grad_u = jnp.einsum("kerc,kepi->rcpi", table, grad_v, preferred_element_type=F32).astype(BF16)
    grad_u = grad_u.reshape(n_rows, 2, pairs_dev * BS)
    back = lax.all_to_all(grad_u, "lat", split_axis=0, concat_axis=2, tiled=True)
    back = back.reshape(rows_dev, 2, KM, NB, BS) * active[:, None, :, None, None].astype(BF16)
    mixed = jnp.einsum("cml,rcmni->rlni", forward, back, preferred_element_type=F32)
    mixed = mixed.reshape(rows_dev, length, width).astype(BF16)
    block_w1 = jnp.einsum("pn,cipj->cinj", owner, gw1).reshape(1, 2, BS, width)
    block_w2 = jnp.einsum("pn,cipj->cinj", owner, gw2).reshape(1, 2, BS, width)
    block_b1 = jnp.einsum("pn,cpj->cnj", owner, gb1).reshape(1, 2, width)
    columns = width // lat_count
    full_w1, full_w2, full_b1 = lax.psum((block_w1, block_w2, block_b1), "lat")
    sum_w1 = lax.dynamic_slice_in_dim(full_w1, lat_pos * columns, columns, 3)
    sum_w2 = lax.dynamic_slice_in_dim(full_w2, lat_pos * columns, columns, 3)
    sum_b1 = lax.dynamic_slice_in_dim(full_b1, lat_pos * columns, columns, 2)
    whole = (cotan.astype(F32) + mixed.astype(F32)).astype(BF16)
    received = from_behind(whole[None], "section", -1)
    return (received, sum_w1, sum_w2, sum_b1)


def per_device(grad_out, spec_saved, w1, w2, b1, mode_counts, assignment):
    n_dev = lax.axis_size("lat")
    pairs_dev = spec_saved.shape[3] // BS
    paired = n_dev == 2 * NB and grad_out.shape[1] == 1 and pairs_dev % NB == 0
    body = paired_blocks if paired else split_blocks
    return body(grad_out, spec_saved, w1, w2, b1, mode_counts, assignment)


def solution(mesh):
    return jax.shard_map(
        per_device,
        mesh=mesh,
        in_specs=(
            P("section", "lat", None, None),
            P("section", None, None, "lat"),
            P("section", None, None, None),
            P("section", None, None, None),
            P("section", None, None),
            P(),
            P(),
        ),
        out_specs=(
            P("section", "lat", None, None),
            P("section", None, None, "lat"),
            P("section", None, None, "lat"),
            P("section", None, "lat"),
        ),
        check_vma=False,
    )
```

```python
import functools
import math

import jax
import jax.numpy as jnp
import numpy as np
from jax import lax
from jax.experimental import pallas as pl
from jax.experimental.pallas import tpu as pltpu
from jax.sharding import PartitionSpec as P

NB = 4
BS = 96
KM = 72
LANES = 128
F32 = jnp.float32
BF16 = jnp.bfloat16


def from_behind(value, axis, by):
    length = lax.axis_size(axis)
    pairs = [(i, i + by) for i in range(length) if 0 <= i + by < length]
    return lax.ppermute(value, axis, pairs)


def turn(value, axis):
    length = lax.axis_size(axis)
    return lax.ppermute(value, axis, [(i, (i - 1) % length) for i in range(length)])


def lon_tables(n_modes, length):
    modes = np.arange(n_modes)
    phase = modes[:, None] * np.arange(length)[None, :] % length
    angle = phase * (2.0 * math.pi / length)
    forward = np.stack([np.cos(angle), -np.sin(angle)]) / math.sqrt(length)
    weight = np.where(modes == 0, 1.0, 2.0)[None, :, None]
    return forward, forward * weight


def lat_waves(n_rows):
    freqs = np.arange(n_rows)
    angle = (freqs[:, None] * freqs[None, :] % n_rows) * (2.0 * math.pi / n_rows)
    factor = 1.0 / math.sqrt(n_rows)
    return np.cos(angle) * factor, np.sin(angle) * factor


def silu_slope(pre):
    sig = jax.nn.sigmoid(pre)
    return sig * (1.0 + pre * (1.0 - sig))


def window(x, start):
    low = start // LANES * LANES
    shift = start - low
    if shift == 0:
        return x[:, low : low + LANES]
    if shift + BS <= LANES:
        return pltpu.roll(x[:, low : low + LANES], LANES - shift, 1)
    return pltpu.roll(x[:, low : low + 2 * LANES], 2 * LANES - shift, 1)[:, :LANES]


def dense(parts):
    lane = lax.broadcasted_iota(jnp.int32, parts[0].shape, 1)
    first = pltpu.roll(parts[1], 96, 1)
    second = pltpu.roll(parts[2], 64, 1)
    third = pltpu.roll(parts[3], 32, 1)
    return jnp.concatenate(
        [
            jnp.where(lane < 96, parts[0], first),
            jnp.where(lane < 64, first, second),
            jnp.where(lane < 32, second, third),
        ],
        axis=1,
    )


def dot(a, b, contract):
    return lax.dot_general(a, b, ((contract[:1], contract[1:]), ((), ())), preferred_element_type=F32)


def mode_numbers(shape, axis, q):
    number = lax.broadcasted_iota(jnp.int32, shape, axis)
    second = number >= NB * q
    number = jnp.where(second, number - NB * q, number)
    mode = number
    for z in range(1, NB):
        mode = jnp.where(number >= z * q, number + z * q, mode)
    return jnp.where(second, mode + q, mode)


def eight_points(x, sign):
    root = float(np.float32(1.0 / math.sqrt(8.0)).astype(BF16))

    def add(a, b):
        return a[0] + b[0], a[1] + b[1]

    def sub(a, b):
        return a[0] - b[0], a[1] - b[1]

    def times_i(a, by):
        return (-a[1], a[0]) if by > 0 else (a[1], -a[0])

    def scale(a, by):
        return a[0] * by, a[1] * by

    def four(a, b, c, d):
        total, far, other, near = add(a, c), sub(a, c), add(b, d), sub(b, d)
        near = times_i(near, sign)
        return add(total, other), add(far, near), sub(total, other), sub(far, near)

    even = [scale(a, root) for a in four(*x[0::2])]
    odd = four(*x[1::2])
    turned = [
        scale(odd[0], root),
        scale(add(odd[1], times_i(odd[1], sign)), 0.25),
        scale(times_i(odd[2], sign), root),
        scale(sub(times_i(odd[3], sign), odd[3]), 0.25),
    ]
    return [add(a, b) for a, b in zip(even, turned)] + [sub(a, b) for a, b in zip(even, turned)]


def fetch(sems, sources, targets):
    copies = [
        pltpu.make_async_copy(source, target, sems.at[i])
        for i, (source, target) in enumerate(zip(sources, targets))
    ]
    for copy in copies:
        copy.start()
    return copies


def fetch_parts(sems, source, target, parts):
    return fetch(sems, [source.at[part] for part in parts], [target.at[part] for part in parts])


def columns(width):
    return [(slice(None), pl.ds(i, LANES)) for i in range(0, width, LANES)]


def wait(copies):
    for copy in copies:
        copy.wait()


def partner(d):
    return jnp.bitwise_xor(lax.axis_index("lat") // 2, d)


def analyse_kernel(q, *refs):
    hbm, outs, held = refs[:5], refs[5:9], refs[9:14]
    by_block, few, sems = refs[14:]
    counts, assign, field, table, saved = held
    early = fetch_parts(sems.at[0], hbm[4], saved, [pl.ds(k, 2) for k in range(0, 2 * NB, 2)])
    late = fetch_parts(sems.at[1], hbm[2], field, columns(field.shape[1]))
    late += fetch(few, hbm[:2] + hbm[3:4], held[:2] + held[3:4])
    wait(early + late)
    parts = [saved[:, c, :].astype(F32) for c in range(2)]
    points = [
        [
            jnp.concatenate([window(part, (mm * NB + n) * BS) for mm in range(q)], axis=0)
            for part in parts
        ]
        for n in range(NB)
    ]
    rows = by_block.shape[1]
    spectral = jnp.dot(table[...], field[...], preferred_element_type=F32)
    active = counts[assign[lax.axis_index("lat")]]
    held_modes = mode_numbers((rows, spectral.shape[1]), 0, q) < active
    spectra = [jnp.where(held_modes, spectral[c * rows : (c + 1) * rows], 0.0) for c in range(2)]
    for n in range(NB):
        pieces = [window(spectrum, n * BS) for spectrum in spectra]
        by_block[n] = dense(pieces + points[n]).astype(BF16)
    for d, out in enumerate(outs):
        out[...] = by_block[partner(d)]


def ready_kernel(q, *refs):
    hbm, (mat1, turned1, turned2, bias, own_field, own_table, latitudes) = refs[:7], refs[7:14]
    counts, assign, w1, w2, b1, table, sems = refs[14:]
    copies = fetch(sems, hbm, (counts, assign, w1, w2, b1, table, own_field))
    wait(copies[:6])
    lane = lax.broadcasted_iota(jnp.int32, latitudes.shape, 1)
    line = jnp.zeros(latitudes.shape, jnp.int32)
    for r in range(2 * NB):
        line = jnp.where(lane == r, assign[r], line)
    latitudes[...] = line
    active = counts[assign[lax.axis_index("lat")]]
    rows = table.shape[1] // 2
    held_modes = mode_numbers((table.shape[0], rows), 1, q) < active
    for c in range(2):
        part = table[:, c * rows : (c + 1) * rows].astype(F32)
        own_table[:, c * rows : (c + 1) * rows] = jnp.where(held_modes, part, 0.0).astype(BF16)
    block = lax.axis_index("lat") // 2

    def pick(x):
        value = window(x, 0)
        for n in range(1, NB):
            value = jnp.where(block == n, window(x, n * BS), value)
        lane = lax.broadcasted_iota(jnp.int32, value.shape, 1)
        return jnp.where(lane < BS, value, 0.0)

    gap = jnp.zeros((LANES - BS, 2 * LANES), F32)
    for source, mat, turned in ((w1, mat1, turned1), (w2, None, turned2)):
        real, imag = (pick(source[c].astype(F32)) for c in range(2))
        whole = [
            jnp.concatenate([real, imag], axis=1),
            gap,
            jnp.concatenate([-imag, real], axis=1),
            gap,
        ]
        whole = jnp.concatenate(whole, axis=0)
        turned[...] = whole.T.astype(BF16)
        if mat is not None:
            mat[...] = whole.astype(BF16)
    shift_b = pick(b1[...].astype(F32))
    bias[...] = jnp.concatenate([shift_b[0:1], shift_b[1:2]], axis=1)
    wait(copies[6:])


ORDER = (0, 3, 2, 1)
FIELD_ROWS = 184


def join_kernel(*refs):
    out = refs[-1]
    for i in range(out.shape[0]):
        out[i] = refs[i][...]


def pack(band):
    rows = band.shape[0]
    tail = rows // 2 + 4
    left, right = band[:, :LANES], pltpu.roll(band[:, LANES:], 96, 1)
    lane = lax.broadcasted_iota(jnp.int32, left.shape, 1)
    upper = jnp.where(lane < 96, left, right)
    lower = pltpu.roll(right[rows - tail :], 64, 1)
    lower = jnp.where(lane[:tail] < 64, right[:tail], lower)
    return jnp.concatenate([upper, lower], axis=0)


def unpack(packed, rows):
    tail = rows // 2 + 4
    upper, lower = packed[:rows], packed[rows:]
    rest = jnp.concatenate([lower, pltpu.roll(lower, 64, 1)[2 * tail - rows :]], axis=0)
    lane = lax.broadcasted_iota(jnp.int32, upper.shape, 1)
    right = jnp.where(lane < 32, pltpu.roll(upper, 32, 1), pltpu.roll(rest, 32, 1))
    return [upper, right]


def silu_points(chunks, mat, bias, by_pair, points, hidden, slope):
    for d, chunk in enumerate(chunks):
        parts = [window(chunk, j * BS) for j in (2, 3)]
        by_pair[partner(d)] = jnp.concatenate(parts, axis=1)
    v = by_pair[...].reshape(points.shape).astype(BF16)
    pre = dot(v, mat[...], (1, 0)) + bias[...]
    sig = jax.nn.sigmoid(pre)
    points[...] = v
    hidden[...] = (pre * sig).astype(BF16)
    slope[...] = sig * (1.0 + pre * (1.0 - sig))


def own_kernel(*refs):
    mat1, bias, points, hidden, slope, by_pair = refs[NB:]
    chunks = [refs[i][...].astype(F32) for i in ORDER]
    silu_points(chunks, mat1, bias, by_pair, points, hidden, slope)


def filter_kernel(*refs):
    owns, (other, slope_own, mat1, turned1, turned2, bias, own_field) = refs[:4], refs[4:11]
    latitudes, outs, (bundle, points, hidden, grad_pre, grad_y) = refs[11], refs[12:15], refs[15:20]
    assign, by_lat, by_pair, slope, real, imag, sems = refs[20:]
    copies = fetch(sems, (latitudes,), (assign,))
    core = lax.rem(lax.axis_index("lat"), 2)
    sides = [[owns[i][...].astype(F32) for i in ORDER], [other[i].astype(F32) for i in ORDER]]
    silu_points(sides[1], mat1, bias, by_pair, points, hidden, slope)
    spectra = [
        [jnp.concatenate([window(chunk, j * BS) for j in range(2)], axis=1) for chunk in chunks]
        for chunks in sides
    ]
    wait(copies)
    for side, rows in zip((core, 1 - core), spectra):
        for d, row in enumerate(rows):
            by_lat[assign[0, 2 * partner(d) + side]] = row
    n_rows, rows, _ = by_lat.shape
    half = rows * n_rows // 2
    waves = eight_points([(by_lat[r][:, :LANES], by_lat[r][:, LANES:]) for r in range(n_rows)], -1)
    step = rows + 1
    for k, wave in enumerate(waves):
        real[k * step : k * step + rows] = wave[0]
        imag[k * step : k * step + rows] = wave[1]
    dy = [
        jnp.concatenate([ref[pl.ds(m, n_rows, stride=step), :] for m in range(rows)], axis=0)
        for ref in (real, imag)
    ]
    dy = jnp.concatenate(dy, axis=1).astype(BF16)
    dy = [jnp.where(core == side, dy[:half], dy[half:]) for side in range(2)]
    dh = dot(jnp.concatenate(dy, axis=0), turned2[...], (1, 0))
    dp = [(dh[:half] * slope_own[...]).astype(BF16), (dh[half:] * slope[...]).astype(BF16)]
    dv = dot(jnp.concatenate(dp, axis=0), turned1[...], (1, 0)).astype(BF16).astype(F32)
    for side in range(2):
        grad_y[side] = dy[side]
        grad_pre[side] = dp[side]
    step = n_rows + 1
    dv = [jnp.where(core == g, dv[:half], dv[half:]) for g in range(2)]
    for g in range(2):
        for i in range(rows // 2):
            m = g * rows // 2 + i
            real[m * step : m * step + n_rows] = dv[g][i * n_rows : (i + 1) * n_rows, :LANES]
            imag[m * step : m * step + n_rows] = dv[g][i * n_rows : (i + 1) * n_rows, LANES:]
    inner = [tuple(ref[pl.ds(k, rows, stride=step), :] for ref in (real, imag)) for k in range(n_rows)]
    for r, band in enumerate(eight_points(inner, 1)):
        by_lat[r] = jnp.concatenate(band, axis=1)
    for i, d in enumerate(ORDER):
        band = pack(by_lat[assign[0, 2 * partner(d) + core]])
        if d:
            outs[i - 1][...] = band.astype(BF16)
        else:
            tail = bundle.shape[0] - FIELD_ROWS
            band = jnp.concatenate([band, jnp.zeros((3 * tail - band.shape[0], LANES), F32)], axis=0)
            band = jnp.concatenate([band[j * tail : (j + 1) * tail] for j in range(3)], axis=1)
            lines = own_field[...].astype(F32)
            gap = jnp.zeros((FIELD_ROWS - lines.shape[0], lines.shape[1]), F32)
            bundle[...] = jnp.concatenate([lines, gap, band], axis=0).astype(BF16)


def products_kernel(points0, hidden0, points1, hidden1, grad_pre, grad_y, gw1, gw2, gb1):
    core = lax.rem(lax.axis_index("lat"), 2)
    half = BS // 2
    for ref, grads, values in ((gw1, grad_pre, (points0, points1)), (gw2, grad_y, (hidden0, hidden1))):
        both = dot(grads[0], values[0][...], (0, 0)) + dot(grads[1], values[1][...], (0, 0))
        real = both[:BS, :LANES] + both[LANES : LANES + BS, LANES:]
        imag = both[LANES : LANES + BS, :LANES] - both[:BS, LANES:]
        for c, full in enumerate((real, imag)):
            ref[c] = jnp.where(core == 0, full[:half], full[half:])[:, :BS]
    sums = sum(jnp.sum(grad_pre[side].astype(F32), axis=0, keepdims=True) for side in range(2))
    for c in range(2):
        line = sums[:, c * LANES : (c + 1) * LANES]
        gb1[c : c + 1] = jnp.where(core == 0, line[:, :half], line[:, half:BS])


def compose_kernel(last, three, bundle, table, out, by_block, result, sems):
    rows = by_block.shape[1]
    lines = bundle[...].astype(F32)
    own = lines[FIELD_ROWS:]
    own = jnp.concatenate([own[:, i * LANES : (i + 1) * LANES] for i in range(3)], axis=0)
    chunks = [own[: three.shape[1]]] + [three[i].astype(F32) for i in range(3)]
    for d, chunk in zip(ORDER, chunks):
        by_block[partner(d)] = jnp.concatenate(unpack(chunk, rows), axis=1)
    parts = [
        dense([by_block[n, :, c * LANES : (c + 1) * LANES] for n in range(NB)]) for c in range(2)
    ]
    parts = jnp.concatenate(parts, axis=0).astype(BF16)
    none = lax.axis_index("section") == last
    copies = []
    for i, (_, tile) in enumerate(columns(out.shape[1])):
        mixed = jnp.dot(table[...], parts[:, i * LANES : (i + 1) * LANES], preferred_element_type=F32)
        field = lines[: out.shape[0], i * LANES : (i + 1) * LANES]
        whole = field + mixed.astype(BF16).astype(F32)
        result[:, tile] = jnp.where(none, 0.0, whole).astype(BF16)
        copies.append(pltpu.make_async_copy(result.at[:, tile], out.at[:, tile], sems.at[i]))
        copies[-1].start()
    wait(copies)


VMEM = pl.BlockSpec(memory_space=pltpu.VMEM)
HBM = pl.BlockSpec(memory_space=pltpu.HBM)


def call(kernel, outs, scratch, near, far, flops=10**8, out_specs=None):
    out_specs = out_specs or (tuple([VMEM] * len(outs)) if isinstance(outs, tuple) else VMEM)
    many = isinstance(outs, tuple)
    return pl.pallas_call(
        kernel,
        out_shape=outs,
        in_specs=[VMEM] * len(near) + [HBM] * len(far),
        out_specs=out_specs,
        scratch_shapes=scratch,
        cost_estimate=pl.CostEstimate(flops=flops, bytes_accessed=10**6, transcendentals=0),
        compiler_params=pltpu.CompilerParams(vmem_limit_bytes=32 * 2**20),
    )(*near, *(pltpu.with_memory_space_constraint(x, pltpu.HBM) for x in far))


def scratch_for(*arrays):
    scratch = []
    for x in arrays:
        space = pltpu.SMEM if x.dtype == jnp.int32 else pltpu.VMEM
        scratch.append(space(x.shape, x.dtype))
    return scratch, pltpu.SemaphoreType.DMA((len(arrays),))


def paired_blocks(grad_out, spec_saved, w1, w2, b1, mode_counts, assignment):
    length, width = grad_out.shape[2:]
    n_rows = assignment.shape[0]
    q = spec_saved.shape[3] // (NB * BS)
    rows = 2 * NB * q
    forward, inverse = lon_tables(KM, length)

    def by_part(table):
        table = table.reshape(2, NB, 2, q, length).transpose(0, 2, 1, 3, 4)
        return table.reshape(2 * rows, length).astype(BF16)

    inverse = jnp.asarray(by_part(inverse))
    forward = jnp.asarray(by_part(forward).T)

    def swap(chunks):
        pairs = [[(i, i ^ (2 * d)) for i in range(2 * NB)] for d in ORDER[1:]]
        return [lax.ppermute(chunk, "lat", p) for chunk, p in zip(chunks, pairs)]

    field = grad_out.reshape(length, width)
    shape = jax.ShapeDtypeStruct
    far = (mode_counts, assignment, field, inverse, spec_saved[0])
    scratch, sems = scratch_for(*far)
    sent = call(
        functools.partial(analyse_kernel, q),
        (shape((rows, width), BF16),) * NB,
        scratch + [pltpu.VMEM((NB, rows, width), BF16), sems, pltpu.SemaphoreType.DMA((2, 4))],
        (),
        far,
    )
    received = [sent[0], *swap([sent[d] for d in ORDER[1:]])]
    far = (mode_counts, assignment, w1[0], w2[0], b1[0], forward)
    scratch, _ = scratch_for(*far)
    far = (*far, field)
    wide = 2 * LANES
    mat1, turned1, turned2, bias, field, forward, latitudes = call(
        functools.partial(ready_kernel, q),
        (
            shape((wide, wide), BF16),
            shape((wide, wide), BF16),
            shape((wide, wide), BF16),
            shape((1, wide), F32),
            shape(field.shape, BF16),
            shape(forward.shape, BF16),
            shape((1, LANES), jnp.int32),
        ),
        scratch + [pltpu.SemaphoreType.DMA((len(far),))],
        (),
        far,
        2 * 10**9,
    )
    own = call(
        join_kernel,
        shape((NB, rows, width), BF16),
        [],
        (*received, bias),
        (),
    )
    other = lax.ppermute(own, "lat", [(i, i ^ 1) for i in range(2 * NB)])
    vectors = shape((NB * rows, wide), BF16)
    slopes = shape((NB * rows, wide), F32)
    by_pair = pltpu.VMEM((NB, rows, wide), F32)
    points0, hidden0, slope0 = call(
        own_kernel,
        (vectors, vectors, slopes),
        [by_pair],
        (*received, mat1, bias),
        (),
        2 * 10**9,
    )
    packed = shape((rows + rows // 2 + 4, LANES), BF16)
    scratch, sems = scratch_for(latitudes)
    both = shape((2, NB * rows, wide), BF16)
    tail = -(-packed.shape[0] // 24) * 8
    bundle = shape((FIELD_ROWS + tail, width), BF16)
    *chunks, bundle, points1, hidden1, grad_pre, grad_y = call(
        filter_kernel,
        (packed,) * (NB - 1) + (bundle, vectors, vectors, both, both),
        scratch
        + [
            pltpu.VMEM((n_rows, rows, wide), F32),
            by_pair,
            pltpu.VMEM((NB * rows, wide), F32),
            pltpu.VMEM(((n_rows + 1) * rows, LANES), F32),
            pltpu.VMEM(((n_rows + 1) * rows, LANES), F32),
            sems,
        ],
        (*received, other, slope0, mat1, turned1, turned2, bias, field, latitudes),
        (),
    )
    backs = swap(chunks)
    matrix = shape((2, BS // 2, BS), F32)
    gw1, gw2, gb1 = call(
        products_kernel,
        (matrix, matrix, shape((2, BS // 2), F32)),
        [],
        (points0, hidden0, points1, hidden1, grad_pre, grad_y),
        (),
        2 * 10**9,
    )
    three = call(join_kernel, shape((NB - 1, *packed.shape), BF16), [], backs, ())
    three = turn(three, "section")
    bundle = turn(bundle, "section")
    shifted = call(
        functools.partial(compose_kernel, lax.axis_size("section") - 1),
        shape((length, width), BF16),
        [
            by_pair,
            pltpu.VMEM((length, width), BF16),
            pltpu.SemaphoreType.DMA((width // LANES,)),
        ],
        (three, bundle, forward),
        (),
        out_specs=HBM,
    )
    shifted = shifted[None, None]
    return shifted, gw1.swapaxes(1, 2)[None], gw2.swapaxes(1, 2)[None], gb1[None]


def apply_mat(vec, mat):
    return jnp.einsum("kpi,ipj->kpj", vec, mat, preferred_element_type=F32)


def adjoint_mat(vec, mat):
    return jnp.einsum("kpj,ipj->kpi", vec, mat, preferred_element_type=F32)


def outer_sum(left, right):
    return jnp.einsum("kpi,kpj->ipj", left, right, preferred_element_type=F32)


def split_blocks(grad_out, spec_saved, w1, w2, b1, mode_counts, assignment):
    rows_dev = grad_out.shape[1]
    length = grad_out.shape[2]
    width = grad_out.shape[3]
    n_rows = assignment.shape[0]
    pairs_dev = spec_saved.shape[3] // BS
    forward, inverse = (jnp.asarray(t.astype(BF16)) for t in lon_tables(KM, length))
    cosine, sine = (jnp.asarray(t.astype(BF16))[:, assignment] for t in lat_waves(n_rows))
    table = jnp.stack(
        [jnp.stack([cosine, sine], axis=-1), jnp.stack([-sine, cosine], axis=-1)], axis=1
    )
    lat_pos = lax.axis_index("lat")
    lat_count = lax.axis_size("lat")
    own_lat = lax.dynamic_slice_in_dim(assignment, lat_pos * rows_dev, rows_dev)
    active = (jnp.arange(KM, dtype=jnp.int32)[None, :] < mode_counts[own_lat][:, None]).astype(F32)
    cotan = grad_out[0]
    spectral = jnp.einsum(
        "cml,rlni->rcmni",
        inverse,
        cotan.reshape(rows_dev, length, NB, BS),
        preferred_element_type=F32,
    )
    spectral = (spectral * active[:, None, :, None, None]).astype(BF16)
    spectral = spectral.reshape(rows_dev, 2, KM * NB * BS)
    pencil = lax.all_to_all(spectral, "lat", split_axis=2, concat_axis=0, tiled=True)
    pencil = pencil.reshape(n_rows, 2, pairs_dev, BS)
    grad_y = jnp.einsum("kerc,rcpi->kepi", table, pencil, preferred_element_type=F32).astype(BF16)
    saved = spec_saved[0].reshape(n_rows, 2, pairs_dev, BS)
    pair_ids = lat_pos * pairs_dev + jnp.arange(pairs_dev, dtype=jnp.int32)
    owner = (pair_ids % NB)[:, None] == jnp.arange(NB, dtype=jnp.int32)[None, :]
    owner = owner.astype(F32)
    first = jnp.take(w1[0].reshape(2, BS, NB, BS), pair_ids % NB, axis=2)
    second = jnp.take(w2[0].reshape(2, BS, NB, BS), pair_ids % NB, axis=2)
    shift_b = jnp.take(b1[0].reshape(2, NB, BS), pair_ids % NB, axis=1).astype(F32)
    v_r = saved[:, 0]
    v_i = saved[:, 1]
    pre_r = apply_mat(v_r, first[0]) - apply_mat(v_i, first[1]) + shift_b[0][None]
    pre_i = apply_mat(v_i, first[0]) + apply_mat(v_r, first[1]) + shift_b[1][None]
    hid_r = jax.nn.silu(pre_r).astype(BF16)
    hid_i = jax.nn.silu(pre_i).astype(BF16)
    dy_r = grad_y[:, 0]
    dy_i = grad_y[:, 1]
    dh_r = adjoint_mat(dy_r, second[0]) + adjoint_mat(dy_i, second[1])
    dh_i = adjoint_mat(dy_i, second[0]) - adjoint_mat(dy_r, second[1])
    dp_r = (dh_r * silu_slope(pre_r)).astype(BF16)
    dp_i = (dh_i * silu_slope(pre_i)).astype(BF16)
    gw2 = jnp.stack(
        [
            outer_sum(hid_r, dy_r) + outer_sum(hid_i, dy_i),
            outer_sum(hid_r, dy_i) - outer_sum(hid_i, dy_r),
        ]
    )
    gw1 = jnp.stack(
        [outer_sum(v_r, dp_r) + outer_sum(v_i, dp_i), outer_sum(v_r, dp_i) - outer_sum(v_i, dp_r)]
    )
    gb1 = jnp.stack([jnp.sum(dp_r.astype(F32), axis=0), jnp.sum(dp_i.astype(F32), axis=0)])
    dv_r = adjoint_mat(dp_r, first[0]) + adjoint_mat(dp_i, first[1])
    dv_i = adjoint_mat(dp_i, first[0]) - adjoint_mat(dp_r, first[1])
    grad_v = jnp.stack([dv_r, dv_i], axis=1).astype(BF16)
    grad_u = jnp.einsum("kerc,kepi->rcpi", table, grad_v, preferred_element_type=F32).astype(BF16)
    grad_u = grad_u.reshape(n_rows, 2, pairs_dev * BS)
    back = lax.all_to_all(grad_u, "lat", split_axis=0, concat_axis=2, tiled=True)
    back = back.reshape(rows_dev, 2, KM, NB, BS) * active[:, None, :, None, None].astype(BF16)
    mixed = jnp.einsum("cml,rcmni->rlni", forward, back, preferred_element_type=F32)
    mixed = mixed.reshape(rows_dev, length, width).astype(BF16)
    block_w1 = jnp.einsum("pn,cipj->cinj", owner, gw1).reshape(1, 2, BS, width)
    block_w2 = jnp.einsum("pn,cipj->cinj", owner, gw2).reshape(1, 2, BS, width)
    block_b1 = jnp.einsum("pn,cpj->cnj", owner, gb1).reshape(1, 2, width)
    columns = width // lat_count
    full_w1, full_w2, full_b1 = lax.psum((block_w1, block_w2, block_b1), "lat")
    sum_w1 = lax.dynamic_slice_in_dim(full_w1, lat_pos * columns, columns, 3)
    sum_w2 = lax.dynamic_slice_in_dim(full_w2, lat_pos * columns, columns, 3)
    sum_b1 = lax.dynamic_slice_in_dim(full_b1, lat_pos * columns, columns, 2)
    whole = (cotan.astype(F32) + mixed.astype(F32)).astype(BF16)
    received = from_behind(whole[None], "section", -1)
    return (received, sum_w1, sum_w2, sum_b1)


def per_device(grad_out, spec_saved, w1, w2, b1, mode_counts, assignment):
    n_dev = lax.axis_size("lat")
    pairs_dev = spec_saved.shape[3] // BS
    paired = n_dev == 2 * NB and grad_out.shape[1] == 1 and pairs_dev % NB == 0
    body = paired_blocks if paired else split_blocks
    return body(grad_out, spec_saved, w1, w2, b1, mode_counts, assignment)


def solution(mesh):
    return jax.shard_map(
        per_device,
        mesh=mesh,
        in_specs=(
            P("section", "lat", None, None),
            P("section", None, None, "lat"),
            P("section", None, None, None),
            P("section", None, None, None),
            P("section", None, None),
            P(),
            P(),
        ),
        out_specs=(
            P("section", "lat", None, None),
            P("section", None, None, "lat"),
            P("section", None, None, "lat"),
            P("section", None, "lat"),
        ),
        check_vma=False,
    )
```

```python
import functools
import math

import jax
import jax.numpy as jnp
import numpy as np
from jax import lax
from jax.experimental import pallas as pl
from jax.experimental.pallas import tpu as pltpu
from jax.sharding import PartitionSpec as P

NB = 4
BS = 96
KM = 72
LANES = 128
F32 = jnp.float32
BF16 = jnp.bfloat16


def from_behind(value, axis, by):
    length = lax.axis_size(axis)
    pairs = [(i, i + by) for i in range(length) if 0 <= i + by < length]
    return lax.ppermute(value, axis, pairs)


def turn(value, axis):
    length = lax.axis_size(axis)
    return lax.ppermute(value, axis, [(i, (i - 1) % length) for i in range(length)])


def lon_tables(n_modes, length):
    modes = np.arange(n_modes)
    phase = modes[:, None] * np.arange(length)[None, :] % length
    angle = phase * (2.0 * math.pi / length)
    forward = np.stack([np.cos(angle), -np.sin(angle)]) / math.sqrt(length)
    weight = np.where(modes == 0, 1.0, 2.0)[None, :, None]
    return forward, forward * weight


def lat_waves(n_rows):
    freqs = np.arange(n_rows)
    angle = (freqs[:, None] * freqs[None, :] % n_rows) * (2.0 * math.pi / n_rows)
    factor = 1.0 / math.sqrt(n_rows)
    return np.cos(angle) * factor, np.sin(angle) * factor


def silu_slope(pre):
    sig = jax.nn.sigmoid(pre)
    return sig * (1.0 + pre * (1.0 - sig))


def window(x, start):
    low = start // LANES * LANES
    shift = start - low
    if shift == 0:
        return x[:, low : low + LANES]
    if shift + BS <= LANES:
        return pltpu.roll(x[:, low : low + LANES], LANES - shift, 1)
    return pltpu.roll(x[:, low : low + 2 * LANES], 2 * LANES - shift, 1)[:, :LANES]


def dense(parts):
    lane = lax.broadcasted_iota(jnp.int32, parts[0].shape, 1)
    first = pltpu.roll(parts[1], 96, 1)
    second = pltpu.roll(parts[2], 64, 1)
    third = pltpu.roll(parts[3], 32, 1)
    return jnp.concatenate(
        [
            jnp.where(lane < 96, parts[0], first),
            jnp.where(lane < 64, first, second),
            jnp.where(lane < 32, second, third),
        ],
        axis=1,
    )


def dot(a, b, contract):
    return lax.dot_general(a, b, ((contract[:1], contract[1:]), ((), ())), preferred_element_type=F32)


def mode_numbers(shape, axis, q):
    number = lax.broadcasted_iota(jnp.int32, shape, axis)
    second = number >= NB * q
    number = jnp.where(second, number - NB * q, number)
    mode = number
    for z in range(1, NB):
        mode = jnp.where(number >= z * q, number + z * q, mode)
    return jnp.where(second, mode + q, mode)


def eight_points(x, sign):
    root = float(np.float32(1.0 / math.sqrt(8.0)).astype(BF16))

    def add(a, b):
        return a[0] + b[0], a[1] + b[1]

    def sub(a, b):
        return a[0] - b[0], a[1] - b[1]

    def times_i(a, by):
        return (-a[1], a[0]) if by > 0 else (a[1], -a[0])

    def scale(a, by):
        return a[0] * by, a[1] * by

    def four(a, b, c, d):
        total, far, other, near = add(a, c), sub(a, c), add(b, d), sub(b, d)
        near = times_i(near, sign)
        return add(total, other), add(far, near), sub(total, other), sub(far, near)

    even = [scale(a, root) for a in four(*x[0::2])]
    odd = four(*x[1::2])
    turned = [
        scale(odd[0], root),
        scale(add(odd[1], times_i(odd[1], sign)), 0.25),
        scale(times_i(odd[2], sign), root),
        scale(sub(times_i(odd[3], sign), odd[3]), 0.25),
    ]
    return [add(a, b) for a, b in zip(even, turned)] + [sub(a, b) for a, b in zip(even, turned)]


def fetch(sems, sources, targets):
    copies = [
        pltpu.make_async_copy(source, target, sems.at[i])
        for i, (source, target) in enumerate(zip(sources, targets))
    ]
    for copy in copies:
        copy.start()
    return copies


def fetch_parts(sems, source, target, parts):
    return fetch(sems, [source.at[part] for part in parts], [target.at[part] for part in parts])


def columns(width):
    return [(slice(None), pl.ds(i, LANES)) for i in range(0, width, LANES)]


def wait(copies):
    for copy in copies:
        copy.wait()


def partner(d):
    return jnp.bitwise_xor(lax.axis_index("lat") // 2, d)


def analyse_kernel(q, *refs):
    hbm, outs, held = refs[:5], refs[5:9], refs[9:14]
    by_block, few, sems = refs[14:]
    counts, assign, field, table, saved = held
    early = fetch_parts(sems.at[0], hbm[4], saved, [pl.ds(k, 2) for k in range(0, 2 * NB, 2)])
    late = fetch_parts(sems.at[1], hbm[2], field, columns(field.shape[1]))
    late += fetch(few, hbm[:2] + hbm[3:4], held[:2] + held[3:4])
    wait(early + late)
    parts = [saved[:, c, :].astype(F32) for c in range(2)]
    points = [
        [
            jnp.concatenate([window(part, (mm * NB + n) * BS) for mm in range(q)], axis=0)
            for part in parts
        ]
        for n in range(NB)
    ]
    rows = by_block.shape[1]
    spectral = jnp.dot(table[...], field[...], preferred_element_type=F32)
    active = counts[assign[lax.axis_index("lat")]]
    held_modes = mode_numbers((rows, spectral.shape[1]), 0, q) < active
    spectra = [jnp.where(held_modes, spectral[c * rows : (c + 1) * rows], 0.0) for c in range(2)]
    for n in range(NB):
        pieces = [window(spectrum, n * BS) for spectrum in spectra]
        by_block[n] = dense(pieces + points[n]).astype(BF16)
    core = lax.rem(lax.axis_index("lat"), 2)
    for step, out in enumerate(outs):
        out[...] = by_block[partner(swap_at(step, core))]


def ready_kernel(q, *refs):
    hbm, (mat1, turned1, turned2, bias, own_field, own_table, latitudes) = refs[:7], refs[7:14]
    counts, assign, w1, w2, b1, table, sems = refs[14:]
    copies = fetch(sems, hbm, (counts, assign, w1, w2, b1, table, own_field))
    wait(copies[:6])
    lane = lax.broadcasted_iota(jnp.int32, latitudes.shape, 1)
    line = jnp.zeros(latitudes.shape, jnp.int32)
    for r in range(2 * NB):
        line = jnp.where(lane == r, assign[r], line)
    latitudes[...] = line
    active = counts[assign[lax.axis_index("lat")]]
    rows = table.shape[1] // 2
    held_modes = mode_numbers((table.shape[0], rows), 1, q) < active
    for c in range(2):
        part = table[:, c * rows : (c + 1) * rows].astype(F32)
        own_table[:, c * rows : (c + 1) * rows] = jnp.where(held_modes, part, 0.0).astype(BF16)
    block = lax.axis_index("lat") // 2

    def pick(x):
        value = window(x, 0)
        for n in range(1, NB):
            value = jnp.where(block == n, window(x, n * BS), value)
        lane = lax.broadcasted_iota(jnp.int32, value.shape, 1)
        return jnp.where(lane < BS, value, 0.0)

    gap = jnp.zeros((LANES - BS, 2 * LANES), F32)
    for source, mat, turned in ((w1, mat1, turned1), (w2, None, turned2)):
        real, imag = (pick(source[c].astype(F32)) for c in range(2))
        whole = [
            jnp.concatenate([real, imag], axis=1),
            gap,
            jnp.concatenate([-imag, real], axis=1),
            gap,
        ]
        whole = jnp.concatenate(whole, axis=0)
        turned[...] = whole.T.astype(BF16)
        if mat is not None:
            mat[...] = whole.astype(BF16)
    shift_b = pick(b1[...].astype(F32))
    bias[...] = jnp.concatenate([shift_b[0:1], shift_b[1:2]], axis=1)
    wait(copies[6:])


def swap_at(step, core):
    return (0, 3, 2 - core, 1 + core)[step]


FIELD_ROWS = 184


def join_kernel(*refs):
    out = refs[-1]
    for i in range(out.shape[0]):
        out[i] = refs[i][...]


def pack(band):
    rows = band.shape[0]
    tail = rows // 2 + 4
    left, right = band[:, :LANES], pltpu.roll(band[:, LANES:], 96, 1)
    lane = lax.broadcasted_iota(jnp.int32, left.shape, 1)
    upper = jnp.where(lane < 96, left, right)
    lower = pltpu.roll(right[rows - tail :], 64, 1)
    lower = jnp.where(lane[:tail] < 64, right[:tail], lower)
    return jnp.concatenate([upper, lower], axis=0)


def unpack(packed, rows):
    tail = rows // 2 + 4
    upper, lower = packed[:rows], packed[rows:]
    rest = jnp.concatenate([lower, pltpu.roll(lower, 64, 1)[2 * tail - rows :]], axis=0)
    lane = lax.broadcasted_iota(jnp.int32, upper.shape, 1)
    right = jnp.where(lane < 32, pltpu.roll(upper, 32, 1), pltpu.roll(rest, 32, 1))
    return [upper, right]


def silu_points(core, chunks, mat, bias, by_pair, points, hidden, slope):
    for step, chunk in enumerate(chunks):
        parts = [window(chunk, j * BS) for j in (2, 3)]
        by_pair[partner(swap_at(step, core))] = jnp.concatenate(parts, axis=1)
    v = by_pair[...].reshape(points.shape).astype(BF16)
    pre = dot(v, mat[...], (1, 0)) + bias[...]
    sig = jax.nn.sigmoid(pre)
    points[...] = v
    hidden[...] = (pre * sig).astype(BF16)
    slope[...] = sig * (1.0 + pre * (1.0 - sig))


def own_kernel(*refs):
    chunks, rest = refs[:NB], refs[NB:]
    mat1, bias, points, hidden, slope, by_pair = rest
    core = lax.rem(lax.axis_index("lat"), 2)
    chunks = [chunk[...].astype(F32) for chunk in chunks]
    silu_points(core, chunks, mat1, bias, by_pair, points, hidden, slope)


def filter_kernel(*refs):
    owns, (other, slope_own, mat1, turned1, turned2, bias, own_field) = refs[:4], refs[4:11]
    latitudes, outs, (bundle, points, hidden, grad_pre, grad_y) = refs[11], refs[12:15], refs[15:20]
    assign, by_lat, by_pair, slope, real, imag, sems = refs[20:]
    copies = fetch(sems, (latitudes,), (assign,))
    core = lax.rem(lax.axis_index("lat"), 2)
    steps = range(NB)
    sides = [[owns[i][...].astype(F32) for i in steps], [other[i].astype(F32) for i in steps]]
    silu_points(1 - core, sides[1], mat1, bias, by_pair, points, hidden, slope)
    spectra = [
        [jnp.concatenate([window(chunk, j * BS) for j in range(2)], axis=1) for chunk in chunks]
        for chunks in sides
    ]
    wait(copies)
    for side, rows in zip((core, 1 - core), spectra):
        for i, row in enumerate(rows):
            by_lat[assign[0, 2 * partner(swap_at(i, side)) + side]] = row
    n_rows, rows, _ = by_lat.shape
    half = rows * n_rows // 2
    waves = eight_points([(by_lat[r][:, :LANES], by_lat[r][:, LANES:]) for r in range(n_rows)], -1)
    step = rows + 1
    for k, wave in enumerate(waves):
        real[k * step : k * step + rows] = wave[0]
        imag[k * step : k * step + rows] = wave[1]
    dy = [
        jnp.concatenate([ref[pl.ds(m, n_rows, stride=step), :] for m in range(rows)], axis=0)
        for ref in (real, imag)
    ]
    dy = jnp.concatenate(dy, axis=1).astype(BF16)
    dy = [jnp.where(core == side, dy[:half], dy[half:]) for side in range(2)]
    dh = dot(jnp.concatenate(dy, axis=0), turned2[...], (1, 0))
    dp = [(dh[:half] * slope_own[...]).astype(BF16), (dh[half:] * slope[...]).astype(BF16)]
    dv = dot(jnp.concatenate(dp, axis=0), turned1[...], (1, 0)).astype(BF16).astype(F32)
    for side in range(2):
        grad_y[side] = dy[side]
        grad_pre[side] = dp[side]
    step = n_rows + 1
    dv = [jnp.where(core == g, dv[:half], dv[half:]) for g in range(2)]
    for g in range(2):
        for i in range(rows // 2):
            m = g * rows // 2 + i
            real[m * step : m * step + n_rows] = dv[g][i * n_rows : (i + 1) * n_rows, :LANES]
            imag[m * step : m * step + n_rows] = dv[g][i * n_rows : (i + 1) * n_rows, LANES:]
    inner = [tuple(ref[pl.ds(k, rows, stride=step), :] for ref in (real, imag)) for k in range(n_rows)]
    for r, band in enumerate(eight_points(inner, 1)):
        by_lat[r] = jnp.concatenate(band, axis=1)
    for i in steps:
        band = pack(by_lat[assign[0, 2 * partner(swap_at(i, core)) + core]])
        if i:
            outs[i - 1][...] = band.astype(BF16)
        else:
            tail = bundle.shape[0] - FIELD_ROWS
            band = jnp.concatenate([band, jnp.zeros((3 * tail - band.shape[0], LANES), F32)], axis=0)
            band = jnp.concatenate([band[j * tail : (j + 1) * tail] for j in range(3)], axis=1)
            lines = own_field[...].astype(F32)
            gap = jnp.zeros((FIELD_ROWS - lines.shape[0], lines.shape[1]), F32)
            bundle[...] = jnp.concatenate([lines, gap, band], axis=0).astype(BF16)


def products_kernel(points0, hidden0, points1, hidden1, grad_pre, grad_y, gw1, gw2, gb1):
    core = lax.rem(lax.axis_index("lat"), 2)
    half = BS // 2
    for ref, grads, values in ((gw1, grad_pre, (points0, points1)), (gw2, grad_y, (hidden0, hidden1))):
        both = dot(grads[0], values[0][...], (0, 0)) + dot(grads[1], values[1][...], (0, 0))
        real = both[:BS, :LANES] + both[LANES : LANES + BS, LANES:]
        imag = both[LANES : LANES + BS, :LANES] - both[:BS, LANES:]
        for c, full in enumerate((real, imag)):
            ref[c] = jnp.where(core == 0, full[:half], full[half:])[:, :BS]
    sums = sum(jnp.sum(grad_pre[side].astype(F32), axis=0, keepdims=True) for side in range(2))
    for c in range(2):
        line = sums[:, c * LANES : (c + 1) * LANES]
        gb1[c : c + 1] = jnp.where(core == 0, line[:, :half], line[:, half:BS])


def compose_kernel(last, three, bundle, table, out, by_block, result, sems):
    rows = by_block.shape[1]
    lines = bundle[...].astype(F32)
    own = lines[FIELD_ROWS:]
    own = jnp.concatenate([own[:, i * LANES : (i + 1) * LANES] for i in range(3)], axis=0)
    chunks = [own[: three.shape[1]]] + [three[i].astype(F32) for i in range(3)]
    core = lax.rem(lax.axis_index("lat"), 2)
    for i, chunk in enumerate(chunks):
        by_block[partner(swap_at(i, core))] = jnp.concatenate(unpack(chunk, rows), axis=1)
    parts = [
        dense([by_block[n, :, c * LANES : (c + 1) * LANES] for n in range(NB)]) for c in range(2)
    ]
    parts = jnp.concatenate(parts, axis=0).astype(BF16)
    none = lax.axis_index("section") == last
    copies = []
    for i, (_, tile) in enumerate(columns(out.shape[1])):
        mixed = jnp.dot(table[...], parts[:, i * LANES : (i + 1) * LANES], preferred_element_type=F32)
        field = lines[: out.shape[0], i * LANES : (i + 1) * LANES]
        whole = field + mixed.astype(BF16).astype(F32)
        result[:, tile] = jnp.where(none, 0.0, whole).astype(BF16)
        copies.append(pltpu.make_async_copy(result.at[:, tile], out.at[:, tile], sems.at[i]))
        copies[-1].start()
    wait(copies)


VMEM = pl.BlockSpec(memory_space=pltpu.VMEM)
HBM = pl.BlockSpec(memory_space=pltpu.HBM)


def call(kernel, outs, scratch, near, far, flops=10**8, out_specs=None):
    out_specs = out_specs or (tuple([VMEM] * len(outs)) if isinstance(outs, tuple) else VMEM)
    many = isinstance(outs, tuple)
    return pl.pallas_call(
        kernel,
        out_shape=outs,
        in_specs=[VMEM] * len(near) + [HBM] * len(far),
        out_specs=out_specs,
        scratch_shapes=scratch,
        cost_estimate=pl.CostEstimate(flops=flops, bytes_accessed=10**6, transcendentals=0),
        compiler_params=pltpu.CompilerParams(vmem_limit_bytes=32 * 2**20),
    )(*near, *(pltpu.with_memory_space_constraint(x, pltpu.HBM) for x in far))


def scratch_for(*arrays):
    scratch = []
    for x in arrays:
        space = pltpu.SMEM if x.dtype == jnp.int32 else pltpu.VMEM
        scratch.append(space(x.shape, x.dtype))
    return scratch, pltpu.SemaphoreType.DMA((len(arrays),))


def paired_blocks(grad_out, spec_saved, w1, w2, b1, mode_counts, assignment):
    length, width = grad_out.shape[2:]
    n_rows = assignment.shape[0]
    q = spec_saved.shape[3] // (NB * BS)
    rows = 2 * NB * q
    forward, inverse = lon_tables(KM, length)

    def by_part(table):
        table = table.reshape(2, NB, 2, q, length).transpose(0, 2, 1, 3, 4)
        return table.reshape(2 * rows, length).astype(BF16)

    inverse = jnp.asarray(by_part(inverse))
    forward = jnp.asarray(by_part(forward).T)

    def swap(chunks):
        pairs = [[(i, i ^ (2 * swap_at(j, i % 2))) for i in range(2 * NB)] for j in range(1, NB)]
        return [lax.ppermute(chunk, "lat", p) for chunk, p in zip(chunks, pairs)]

    field = grad_out.reshape(length, width)
    shape = jax.ShapeDtypeStruct
    far = (mode_counts, assignment, field, inverse, spec_saved[0])
    scratch, sems = scratch_for(*far)
    sent = call(
        functools.partial(analyse_kernel, q),
        (shape((rows, width), BF16),) * NB,
        scratch + [pltpu.VMEM((NB, rows, width), BF16), sems, pltpu.SemaphoreType.DMA((2, 4))],
        (),
        far,
    )
    received = [sent[0], *swap(sent[1:])]
    far = (mode_counts, assignment, w1[0], w2[0], b1[0], forward)
    scratch, _ = scratch_for(*far)
    far = (*far, field)
    wide = 2 * LANES
    mat1, turned1, turned2, bias, field, forward, latitudes = call(
        functools.partial(ready_kernel, q),
        (
            shape((wide, wide), BF16),
            shape((wide, wide), BF16),
            shape((wide, wide), BF16),
            shape((1, wide), F32),
            shape(field.shape, BF16),
            shape(forward.shape, BF16),
            shape((1, LANES), jnp.int32),
        ),
        scratch + [pltpu.SemaphoreType.DMA((len(far),))],
        (),
        far,
        2 * 10**9,
    )
    own = call(
        join_kernel,
        shape((NB, rows, width), BF16),
        [],
        (*received, bias),
        (),
    )
    other = lax.ppermute(own, "lat", [(i, i ^ 1) for i in range(2 * NB)])
    vectors = shape((NB * rows, wide), BF16)
    slopes = shape((NB * rows, wide), F32)
    by_pair = pltpu.VMEM((NB, rows, wide), F32)
    points0, hidden0, slope0 = call(
        own_kernel,
        (vectors, vectors, slopes),
        [by_pair],
        (*received, mat1, bias),
        (),
        2 * 10**9,
    )
    packed = shape((rows + rows // 2 + 4, LANES), BF16)
    scratch, sems = scratch_for(latitudes)
    both = shape((2, NB * rows, wide), BF16)
    tail = -(-packed.shape[0] // 24) * 8
    bundle = shape((FIELD_ROWS + tail, width), BF16)
    *chunks, bundle, points1, hidden1, grad_pre, grad_y = call(
        filter_kernel,
        (packed,) * (NB - 1) + (bundle, vectors, vectors, both, both),
        scratch
        + [
            pltpu.VMEM((n_rows, rows, wide), F32),
            by_pair,
            pltpu.VMEM((NB * rows, wide), F32),
            pltpu.VMEM(((n_rows + 1) * rows, LANES), F32),
            pltpu.VMEM(((n_rows + 1) * rows, LANES), F32),
            sems,
        ],
        (*received, other, slope0, mat1, turned1, turned2, bias, field, latitudes),
        (),
    )
    backs = swap(chunks)
    matrix = shape((2, BS // 2, BS), F32)
    gw1, gw2, gb1 = call(
        products_kernel,
        (matrix, matrix, shape((2, BS // 2), F32)),
        [],
        (points0, hidden0, points1, hidden1, grad_pre, grad_y),
        (),
        2 * 10**9,
    )
    three = call(join_kernel, shape((NB - 1, *packed.shape), BF16), [], backs, ())
    three = turn(three, "section")
    bundle = turn(bundle, "section")
    shifted = call(
        functools.partial(compose_kernel, lax.axis_size("section") - 1),
        shape((length, width), BF16),
        [
            by_pair,
            pltpu.VMEM((length, width), BF16),
            pltpu.SemaphoreType.DMA((width // LANES,)),
        ],
        (three, bundle, forward),
        (),
        out_specs=HBM,
    )
    shifted = shifted[None, None]
    return shifted, gw1.swapaxes(1, 2)[None], gw2.swapaxes(1, 2)[None], gb1[None]


def apply_mat(vec, mat):
    return jnp.einsum("kpi,ipj->kpj", vec, mat, preferred_element_type=F32)


def adjoint_mat(vec, mat):
    return jnp.einsum("kpj,ipj->kpi", vec, mat, preferred_element_type=F32)


def outer_sum(left, right):
    return jnp.einsum("kpi,kpj->ipj", left, right, preferred_element_type=F32)


def split_blocks(grad_out, spec_saved, w1, w2, b1, mode_counts, assignment):
    rows_dev = grad_out.shape[1]
    length = grad_out.shape[2]
    width = grad_out.shape[3]
    n_rows = assignment.shape[0]
    pairs_dev = spec_saved.shape[3] // BS
    forward, inverse = (jnp.asarray(t.astype(BF16)) for t in lon_tables(KM, length))
    cosine, sine = (jnp.asarray(t.astype(BF16))[:, assignment] for t in lat_waves(n_rows))
    table = jnp.stack(
        [jnp.stack([cosine, sine], axis=-1), jnp.stack([-sine, cosine], axis=-1)], axis=1
    )
    lat_pos = lax.axis_index("lat")
    lat_count = lax.axis_size("lat")
    own_lat = lax.dynamic_slice_in_dim(assignment, lat_pos * rows_dev, rows_dev)
    active = (jnp.arange(KM, dtype=jnp.int32)[None, :] < mode_counts[own_lat][:, None]).astype(F32)
    cotan = grad_out[0]
    spectral = jnp.einsum(
        "cml,rlni->rcmni",
        inverse,
        cotan.reshape(rows_dev, length, NB, BS),
        preferred_element_type=F32,
    )
    spectral = (spectral * active[:, None, :, None, None]).astype(BF16)
    spectral = spectral.reshape(rows_dev, 2, KM * NB * BS)
    pencil = lax.all_to_all(spectral, "lat", split_axis=2, concat_axis=0, tiled=True)
    pencil = pencil.reshape(n_rows, 2, pairs_dev, BS)
    grad_y = jnp.einsum("kerc,rcpi->kepi", table, pencil, preferred_element_type=F32).astype(BF16)
    saved = spec_saved[0].reshape(n_rows, 2, pairs_dev, BS)
    pair_ids = lat_pos * pairs_dev + jnp.arange(pairs_dev, dtype=jnp.int32)
    owner = (pair_ids % NB)[:, None] == jnp.arange(NB, dtype=jnp.int32)[None, :]
    owner = owner.astype(F32)
    first = jnp.take(w1[0].reshape(2, BS, NB, BS), pair_ids % NB, axis=2)
    second = jnp.take(w2[0].reshape(2, BS, NB, BS), pair_ids % NB, axis=2)
    shift_b = jnp.take(b1[0].reshape(2, NB, BS), pair_ids % NB, axis=1).astype(F32)
    v_r = saved[:, 0]
    v_i = saved[:, 1]
    pre_r = apply_mat(v_r, first[0]) - apply_mat(v_i, first[1]) + shift_b[0][None]
    pre_i = apply_mat(v_i, first[0]) + apply_mat(v_r, first[1]) + shift_b[1][None]
    hid_r = jax.nn.silu(pre_r).astype(BF16)
    hid_i = jax.nn.silu(pre_i).astype(BF16)
    dy_r = grad_y[:, 0]
    dy_i = grad_y[:, 1]
    dh_r = adjoint_mat(dy_r, second[0]) + adjoint_mat(dy_i, second[1])
    dh_i = adjoint_mat(dy_i, second[0]) - adjoint_mat(dy_r, second[1])
    dp_r = (dh_r * silu_slope(pre_r)).astype(BF16)
    dp_i = (dh_i * silu_slope(pre_i)).astype(BF16)
    gw2 = jnp.stack(
        [
            outer_sum(hid_r, dy_r) + outer_sum(hid_i, dy_i),
            outer_sum(hid_r, dy_i) - outer_sum(hid_i, dy_r),
        ]
    )
    gw1 = jnp.stack(
        [outer_sum(v_r, dp_r) + outer_sum(v_i, dp_i), outer_sum(v_r, dp_i) - outer_sum(v_i, dp_r)]
    )
    gb1 = jnp.stack([jnp.sum(dp_r.astype(F32), axis=0), jnp.sum(dp_i.astype(F32), axis=0)])
    dv_r = adjoint_mat(dp_r, first[0]) + adjoint_mat(dp_i, first[1])
    dv_i = adjoint_mat(dp_i, first[0]) - adjoint_mat(dp_r, first[1])
    grad_v = jnp.stack([dv_r, dv_i], axis=1).astype(BF16)
    grad_u = jnp.einsum("kerc,kepi->rcpi", table, grad_v, preferred_element_type=F32).astype(BF16)
    grad_u = grad_u.reshape(n_rows, 2, pairs_dev * BS)
    back = lax.all_to_all(grad_u, "lat", split_axis=0, concat_axis=2, tiled=True)
    back = back.reshape(rows_dev, 2, KM, NB, BS) * active[:, None, :, None, None].astype(BF16)
    mixed = jnp.einsum("cml,rcmni->rlni", forward, back, preferred_element_type=F32)
    mixed = mixed.reshape(rows_dev, length, width).astype(BF16)
    block_w1 = jnp.einsum("pn,cipj->cinj", owner, gw1).reshape(1, 2, BS, width)
    block_w2 = jnp.einsum("pn,cipj->cinj", owner, gw2).reshape(1, 2, BS, width)
    block_b1 = jnp.einsum("pn,cpj->cnj", owner, gb1).reshape(1, 2, width)
    columns = width // lat_count
    full_w1, full_w2, full_b1 = lax.psum((block_w1, block_w2, block_b1), "lat")
    sum_w1 = lax.dynamic_slice_in_dim(full_w1, lat_pos * columns, columns, 3)
    sum_w2 = lax.dynamic_slice_in_dim(full_w2, lat_pos * columns, columns, 3)
    sum_b1 = lax.dynamic_slice_in_dim(full_b1, lat_pos * columns, columns, 2)
    whole = (cotan.astype(F32) + mixed.astype(F32)).astype(BF16)
    received = from_behind(whole[None], "section", -1)
    return (received, sum_w1, sum_w2, sum_b1)


def per_device(grad_out, spec_saved, w1, w2, b1, mode_counts, assignment):
    n_dev = lax.axis_size("lat")
    pairs_dev = spec_saved.shape[3] // BS
    paired = n_dev == 2 * NB and grad_out.shape[1] == 1 and pairs_dev % NB == 0
    body = paired_blocks if paired else split_blocks
    return body(grad_out, spec_saved, w1, w2, b1, mode_counts, assignment)


def solution(mesh):
    return jax.shard_map(
        per_device,
        mesh=mesh,
        in_specs=(
            P("section", "lat", None, None),
            P("section", None, None, "lat"),
            P("section", None, None, None),
            P("section", None, None, None),
            P("section", None, None),
            P(),
            P(),
        ),
        out_specs=(
            P("section", "lat", None, None),
            P("section", None, None, "lat"),
            P("section", None, None, "lat"),
            P("section", None, "lat"),
        ),
        check_vma=False,
    )
```

```python
import functools
import math

import jax
import jax.numpy as jnp
import numpy as np
from jax import lax
from jax.experimental import pallas as pl
from jax.experimental.pallas import tpu as pltpu
from jax.sharding import PartitionSpec as P

NB = 4
BS = 96
KM = 72
LANES = 128
F32 = jnp.float32
BF16 = jnp.bfloat16


def from_behind(value, axis, by):
    length = lax.axis_size(axis)
    pairs = [(i, i + by) for i in range(length) if 0 <= i + by < length]
    return lax.ppermute(value, axis, pairs)


def turn(value, axis):
    length = lax.axis_size(axis)
    return lax.ppermute(value, axis, [(i, (i - 1) % length) for i in range(length)])


def lon_tables(n_modes, length):
    modes = np.arange(n_modes)
    phase = modes[:, None] * np.arange(length)[None, :] % length
    angle = phase * (2.0 * math.pi / length)
    forward = np.stack([np.cos(angle), -np.sin(angle)]) / math.sqrt(length)
    weight = np.where(modes == 0, 1.0, 2.0)[None, :, None]
    return forward, forward * weight


def lat_waves(n_rows):
    freqs = np.arange(n_rows)
    angle = (freqs[:, None] * freqs[None, :] % n_rows) * (2.0 * math.pi / n_rows)
    factor = 1.0 / math.sqrt(n_rows)
    return np.cos(angle) * factor, np.sin(angle) * factor


def silu_slope(pre):
    sig = jax.nn.sigmoid(pre)
    return sig * (1.0 + pre * (1.0 - sig))


def window(x, start):
    low = start // LANES * LANES
    shift = start - low
    if shift == 0:
        return x[:, low : low + LANES]
    if shift + BS <= LANES:
        return pltpu.roll(x[:, low : low + LANES], LANES - shift, 1)
    return pltpu.roll(x[:, low : low + 2 * LANES], 2 * LANES - shift, 1)[:, :LANES]


def dense(parts):
    lane = lax.broadcasted_iota(jnp.int32, parts[0].shape, 1)
    first = pltpu.roll(parts[1], 96, 1)
    second = pltpu.roll(parts[2], 64, 1)
    third = pltpu.roll(parts[3], 32, 1)
    return jnp.concatenate(
        [
            jnp.where(lane < 96, parts[0], first),
            jnp.where(lane < 64, first, second),
            jnp.where(lane < 32, second, third),
        ],
        axis=1,
    )


def dot(a, b, contract):
    return lax.dot_general(a, b, ((contract[:1], contract[1:]), ((), ())), preferred_element_type=F32)


def mode_numbers(shape, axis, q):
    number = lax.broadcasted_iota(jnp.int32, shape, axis)
    second = number >= NB * q
    number = jnp.where(second, number - NB * q, number)
    mode = number
    for z in range(1, NB):
        mode = jnp.where(number >= z * q, number + z * q, mode)
    return jnp.where(second, mode + q, mode)


def eight_points(x, sign):
    root = float(np.float32(1.0 / math.sqrt(8.0)).astype(BF16))

    def add(a, b):
        return a[0] + b[0], a[1] + b[1]

    def sub(a, b):
        return a[0] - b[0], a[1] - b[1]

    def times_i(a, by):
        return (-a[1], a[0]) if by > 0 else (a[1], -a[0])

    def scale(a, by):
        return a[0] * by, a[1] * by

    def four(a, b, c, d):
        total, far, other, near = add(a, c), sub(a, c), add(b, d), sub(b, d)
        near = times_i(near, sign)
        return add(total, other), add(far, near), sub(total, other), sub(far, near)

    even = [scale(a, root) for a in four(*x[0::2])]
    odd = four(*x[1::2])
    turned = [
        scale(odd[0], root),
        scale(add(odd[1], times_i(odd[1], sign)), 0.25),
        scale(times_i(odd[2], sign), root),
        scale(sub(times_i(odd[3], sign), odd[3]), 0.25),
    ]
    return [add(a, b) for a, b in zip(even, turned)] + [sub(a, b) for a, b in zip(even, turned)]


def fetch(sems, sources, targets):
    copies = [
        pltpu.make_async_copy(source, target, sems.at[i])
        for i, (source, target) in enumerate(zip(sources, targets))
    ]
    for copy in copies:
        copy.start()
    return copies


def fetch_parts(sems, source, target, parts):
    return fetch(sems, [source.at[part] for part in parts], [target.at[part] for part in parts])


def columns(width):
    return [(slice(None), pl.ds(i, LANES)) for i in range(0, width, LANES)]


def wait(copies):
    for copy in copies:
        copy.wait()


def partner(d):
    return jnp.bitwise_xor(lax.axis_index("lat") // 2, d)


def analyse_kernel(q, *refs):
    hbm, outs, held = refs[:5], refs[5:9], refs[9:14]
    by_block, few, sems = refs[14:]
    counts, assign, field, table, saved = held
    early = fetch_parts(sems.at[0], hbm[4], saved, [pl.ds(k, 2) for k in range(0, 2 * NB, 2)])
    late = fetch_parts(sems.at[1], hbm[2], field, columns(field.shape[1]))
    late += fetch(few, hbm[:2] + hbm[3:4], held[:2] + held[3:4])
    wait(early + late)
    parts = [saved[:, c, :].astype(F32) for c in range(2)]
    points = [
        [
            jnp.concatenate([window(part, (mm * NB + n) * BS) for mm in range(q)], axis=0)
            for part in parts
        ]
        for n in range(NB)
    ]
    rows = by_block.shape[1]
    spectral = jnp.dot(table[...], field[...], preferred_element_type=F32)
    active = counts[assign[lax.axis_index("lat")]]
    held_modes = mode_numbers((rows, spectral.shape[1]), 0, q) < active
    spectra = [jnp.where(held_modes, spectral[c * rows : (c + 1) * rows], 0.0) for c in range(2)]
    for n in range(NB):
        pieces = [window(spectrum, n * BS) for spectrum in spectra]
        by_block[n] = dense(pieces + points[n]).astype(BF16)
    core = lax.rem(lax.axis_index("lat"), 2)
    for step, out in enumerate(outs):
        out[...] = by_block[partner(swap_at(step, core))]


def ready_kernel(q, *refs):
    hbm, (mat1, turned1, turned2, bias, own_field, own_table, latitudes) = refs[:7], refs[7:14]
    counts, assign, w1, w2, b1, table, sems = refs[14:]
    copies = fetch(sems, hbm, (counts, assign, w1, w2, b1, table, own_field))
    wait(copies[:6])
    lane = lax.broadcasted_iota(jnp.int32, latitudes.shape, 1)
    line = jnp.zeros(latitudes.shape, jnp.int32)
    for r in range(2 * NB):
        line = jnp.where(lane == r, assign[r], line)
    latitudes[...] = line
    active = counts[assign[lax.axis_index("lat")]]
    rows = table.shape[1] // 2
    held_modes = mode_numbers((table.shape[0], rows), 1, q) < active
    for c in range(2):
        part = table[:, c * rows : (c + 1) * rows].astype(F32)
        own_table[:, c * rows : (c + 1) * rows] = jnp.where(held_modes, part, 0.0).astype(BF16)
    block = lax.axis_index("lat") // 2

    def pick(x):
        value = window(x, 0)
        for n in range(1, NB):
            value = jnp.where(block == n, window(x, n * BS), value)
        lane = lax.broadcasted_iota(jnp.int32, value.shape, 1)
        return jnp.where(lane < BS, value, 0.0)

    gap = jnp.zeros((LANES - BS, 2 * LANES), F32)
    for source, mat, turned in ((w1, mat1, turned1), (w2, None, turned2)):
        real, imag = (pick(source[c].astype(F32)) for c in range(2))
        whole = [
            jnp.concatenate([real, imag], axis=1),
            gap,
            jnp.concatenate([-imag, real], axis=1),
            gap,
        ]
        whole = jnp.concatenate(whole, axis=0)
        turned[...] = whole.T.astype(BF16)
        if mat is not None:
            mat[...] = whole.astype(BF16)
    shift_b = pick(b1[...].astype(F32))
    bias[...] = jnp.concatenate([shift_b[0:1], shift_b[1:2]], axis=1)
    wait(copies[6:])


def swap_at(step, core):
    return (0, 3 - core, 2 + core, 1)[step]


FIELD_ROWS = 184


def join_kernel(*refs):
    out = refs[-1]
    for i in range(out.shape[0]):
        out[i] = refs[i][...]


def pack(band):
    rows = band.shape[0]
    tail = rows // 2 + 4
    left, right = band[:, :LANES], pltpu.roll(band[:, LANES:], 96, 1)
    lane = lax.broadcasted_iota(jnp.int32, left.shape, 1)
    upper = jnp.where(lane < 96, left, right)
    lower = pltpu.roll(right[rows - tail :], 64, 1)
    lower = jnp.where(lane[:tail] < 64, right[:tail], lower)
    return jnp.concatenate([upper, lower], axis=0)


def unpack(packed, rows):
    tail = rows // 2 + 4
    upper, lower = packed[:rows], packed[rows:]
    rest = jnp.concatenate([lower, pltpu.roll(lower, 64, 1)[2 * tail - rows :]], axis=0)
    lane = lax.broadcasted_iota(jnp.int32, upper.shape, 1)
    right = jnp.where(lane < 32, pltpu.roll(upper, 32, 1), pltpu.roll(rest, 32, 1))
    return [upper, right]


def silu_points(core, chunks, mat, bias, by_pair, points, hidden, slope):
    for step, chunk in enumerate(chunks):
        parts = [window(chunk, j * BS) for j in (2, 3)]
        by_pair[partner(swap_at(step, core))] = jnp.concatenate(parts, axis=1)
    v = by_pair[...].reshape(points.shape).astype(BF16)
    pre = dot(v, mat[...], (1, 0)) + bias[...]
    sig = jax.nn.sigmoid(pre)
    points[...] = v
    hidden[...] = (pre * sig).astype(BF16)
    slope[...] = sig * (1.0 + pre * (1.0 - sig))


def own_kernel(*refs):
    chunks, rest = refs[:NB], refs[NB:]
    mat1, bias, points, hidden, slope, by_pair = rest
    core = lax.rem(lax.axis_index("lat"), 2)
    chunks = [chunk[...].astype(F32) for chunk in chunks]
    silu_points(core, chunks, mat1, bias, by_pair, points, hidden, slope)


def filter_kernel(*refs):
    owns, (other, slope_own, mat1, turned1, turned2, bias, own_field) = refs[:4], refs[4:11]
    latitudes, outs, (bundle, points, hidden, grad_pre, grad_y) = refs[11], refs[12:15], refs[15:20]
    assign, by_lat, by_pair, slope, real, imag, sems = refs[20:]
    copies = fetch(sems, (latitudes,), (assign,))
    core = lax.rem(lax.axis_index("lat"), 2)
    steps = range(NB)
    sides = [[owns[i][...].astype(F32) for i in steps], [other[i].astype(F32) for i in steps]]
    silu_points(1 - core, sides[1], mat1, bias, by_pair, points, hidden, slope)
    spectra = [
        [jnp.concatenate([window(chunk, j * BS) for j in range(2)], axis=1) for chunk in chunks]
        for chunks in sides
    ]
    wait(copies)
    for side, rows in zip((core, 1 - core), spectra):
        for i, row in enumerate(rows):
            by_lat[assign[0, 2 * partner(swap_at(i, side)) + side]] = row
    n_rows, rows, _ = by_lat.shape
    half = rows * n_rows // 2
    waves = eight_points([(by_lat[r][:, :LANES], by_lat[r][:, LANES:]) for r in range(n_rows)], -1)
    step = rows + 1
    for k, wave in enumerate(waves):
        real[k * step : k * step + rows] = wave[0]
        imag[k * step : k * step + rows] = wave[1]
    dy = [
        jnp.concatenate([ref[pl.ds(m, n_rows, stride=step), :] for m in range(rows)], axis=0)
        for ref in (real, imag)
    ]
    dy = jnp.concatenate(dy, axis=1).astype(BF16)
    dy = [jnp.where(core == side, dy[:half], dy[half:]) for side in range(2)]
    dh = dot(jnp.concatenate(dy, axis=0), turned2[...], (1, 0))
    dp = [(dh[:half] * slope_own[...]).astype(BF16), (dh[half:] * slope[...]).astype(BF16)]
    dv = dot(jnp.concatenate(dp, axis=0), turned1[...], (1, 0)).astype(BF16).astype(F32)
    for side in range(2):
        grad_y[side] = dy[side]
        grad_pre[side] = dp[side]
    step = n_rows + 1
    dv = [jnp.where(core == g, dv[:half], dv[half:]) for g in range(2)]
    for g in range(2):
        for i in range(rows // 2):
            m = g * rows // 2 + i
            real[m * step : m * step + n_rows] = dv[g][i * n_rows : (i + 1) * n_rows, :LANES]
            imag[m * step : m * step + n_rows] = dv[g][i * n_rows : (i + 1) * n_rows, LANES:]
    inner = [tuple(ref[pl.ds(k, rows, stride=step), :] for ref in (real, imag)) for k in range(n_rows)]
    for r, band in enumerate(eight_points(inner, 1)):
        by_lat[r] = jnp.concatenate(band, axis=1)
    for i in steps:
        band = pack(by_lat[assign[0, 2 * partner(swap_at(i, core)) + core]])
        if i:
            outs[i - 1][...] = band.astype(BF16)
        else:
            tail = bundle.shape[0] - FIELD_ROWS
            band = jnp.concatenate([band, jnp.zeros((3 * tail - band.shape[0], LANES), F32)], axis=0)
            band = jnp.concatenate([band[j * tail : (j + 1) * tail] for j in range(3)], axis=1)
            lines = own_field[...].astype(F32)
            gap = jnp.zeros((FIELD_ROWS - lines.shape[0], lines.shape[1]), F32)
            bundle[...] = jnp.concatenate([lines, gap, band], axis=0).astype(BF16)


def products_kernel(points0, hidden0, points1, hidden1, grad_pre, grad_y, gw1, gw2, gb1):
    core = lax.rem(lax.axis_index("lat"), 2)
    half = BS // 2
    for ref, grads, values in ((gw1, grad_pre, (points0, points1)), (gw2, grad_y, (hidden0, hidden1))):
        both = dot(grads[0], values[0][...], (0, 0)) + dot(grads[1], values[1][...], (0, 0))
        real = both[:BS, :LANES] + both[LANES : LANES + BS, LANES:]
        imag = both[LANES : LANES + BS, :LANES] - both[:BS, LANES:]
        for c, full in enumerate((real, imag)):
            ref[c] = jnp.where(core == 0, full[:half], full[half:])[:, :BS]
    sums = sum(jnp.sum(grad_pre[side].astype(F32), axis=0, keepdims=True) for side in range(2))
    for c in range(2):
        line = sums[:, c * LANES : (c + 1) * LANES]
        gb1[c : c + 1] = jnp.where(core == 0, line[:, :half], line[:, half:BS])


def compose_kernel(last, three, bundle, table, out, by_block, result, sems):
    rows = by_block.shape[1]
    lines = bundle[...].astype(F32)
    own = lines[FIELD_ROWS:]
    own = jnp.concatenate([own[:, i * LANES : (i + 1) * LANES] for i in range(3)], axis=0)
    chunks = [own[: three.shape[1]]] + [three[i].astype(F32) for i in range(3)]
    core = lax.rem(lax.axis_index("lat"), 2)
    for i, chunk in enumerate(chunks):
        by_block[partner(swap_at(i, core))] = jnp.concatenate(unpack(chunk, rows), axis=1)
    parts = [
        dense([by_block[n, :, c * LANES : (c + 1) * LANES] for n in range(NB)]) for c in range(2)
    ]
    parts = jnp.concatenate(parts, axis=0).astype(BF16)
    none = lax.axis_index("section") == last
    copies = []
    for i, (_, tile) in enumerate(columns(out.shape[1])):
        mixed = jnp.dot(table[...], parts[:, i * LANES : (i + 1) * LANES], preferred_element_type=F32)
        field = lines[: out.shape[0], i * LANES : (i + 1) * LANES]
        whole = field + mixed.astype(BF16).astype(F32)
        result[:, tile] = jnp.where(none, 0.0, whole).astype(BF16)
        copies.append(pltpu.make_async_copy(result.at[:, tile], out.at[:, tile], sems.at[i]))
        copies[-1].start()
    wait(copies)


VMEM = pl.BlockSpec(memory_space=pltpu.VMEM)
HBM = pl.BlockSpec(memory_space=pltpu.HBM)


def call(kernel, outs, scratch, near, far, flops=10**8, out_specs=None):
    out_specs = out_specs or (tuple([VMEM] * len(outs)) if isinstance(outs, tuple) else VMEM)
    many = isinstance(outs, tuple)
    return pl.pallas_call(
        kernel,
        out_shape=outs,
        in_specs=[VMEM] * len(near) + [HBM] * len(far),
        out_specs=out_specs,
        scratch_shapes=scratch,
        cost_estimate=pl.CostEstimate(flops=flops, bytes_accessed=10**6, transcendentals=0),
        compiler_params=pltpu.CompilerParams(vmem_limit_bytes=32 * 2**20),
    )(*near, *(pltpu.with_memory_space_constraint(x, pltpu.HBM) for x in far))


def scratch_for(*arrays):
    scratch = []
    for x in arrays:
        space = pltpu.SMEM if x.dtype == jnp.int32 else pltpu.VMEM
        scratch.append(space(x.shape, x.dtype))
    return scratch, pltpu.SemaphoreType.DMA((len(arrays),))


def paired_blocks(grad_out, spec_saved, w1, w2, b1, mode_counts, assignment):
    length, width = grad_out.shape[2:]
    n_rows = assignment.shape[0]
    q = spec_saved.shape[3] // (NB * BS)
    rows = 2 * NB * q
    forward, inverse = lon_tables(KM, length)

    def by_part(table):
        table = table.reshape(2, NB, 2, q, length).transpose(0, 2, 1, 3, 4)
        return table.reshape(2 * rows, length).astype(BF16)

    inverse = jnp.asarray(by_part(inverse))
    forward = jnp.asarray(by_part(forward).T)

    def swap(chunks):
        pairs = [[(i, i ^ (2 * swap_at(j, i % 2))) for i in range(2 * NB)] for j in range(1, NB)]
        return [lax.ppermute(chunk, "lat", p) for chunk, p in zip(chunks, pairs)]

    field = grad_out.reshape(length, width)
    shape = jax.ShapeDtypeStruct
    far = (mode_counts, assignment, field, inverse, spec_saved[0])
    scratch, sems = scratch_for(*far)
    sent = call(
        functools.partial(analyse_kernel, q),
        (shape((rows, width), BF16),) * NB,
        scratch + [pltpu.VMEM((NB, rows, width), BF16), sems, pltpu.SemaphoreType.DMA((2, 4))],
        (),
        far,
    )
    received = [sent[0], *swap(sent[1:])]
    far = (mode_counts, assignment, w1[0], w2[0], b1[0], forward)
    scratch, _ = scratch_for(*far)
    far = (*far, field)
    wide = 2 * LANES
    mat1, turned1, turned2, bias, field, forward, latitudes = call(
        functools.partial(ready_kernel, q),
        (
            shape((wide, wide), BF16),
            shape((wide, wide), BF16),
            shape((wide, wide), BF16),
            shape((1, wide), F32),
            shape(field.shape, BF16),
            shape(forward.shape, BF16),
            shape((1, LANES), jnp.int32),
        ),
        scratch + [pltpu.SemaphoreType.DMA((len(far),))],
        (),
        far,
        2 * 10**9,
    )
    own = call(
        join_kernel,
        shape((NB, rows, width), BF16),
        [],
        (*received, bias),
        (),
    )
    other = lax.ppermute(own, "lat", [(i, i ^ 1) for i in range(2 * NB)])
    vectors = shape((NB * rows, wide), BF16)
    slopes = shape((NB * rows, wide), F32)
    by_pair = pltpu.VMEM((NB, rows, wide), F32)
    points0, hidden0, slope0 = call(
        own_kernel,
        (vectors, vectors, slopes),
        [by_pair],
        (*received, mat1, bias),
        (),
        2 * 10**9,
    )
    packed = shape((rows + rows // 2 + 4, LANES), BF16)
    scratch, sems = scratch_for(latitudes)
    both = shape((2, NB * rows, wide), BF16)
    tail = -(-packed.shape[0] // 24) * 8
    bundle = shape((FIELD_ROWS + tail, width), BF16)
    *chunks, bundle, points1, hidden1, grad_pre, grad_y = call(
        filter_kernel,
        (packed,) * (NB - 1) + (bundle, vectors, vectors, both, both),
        scratch
        + [
            pltpu.VMEM((n_rows, rows, wide), F32),
            by_pair,
            pltpu.VMEM((NB * rows, wide), F32),
            pltpu.VMEM(((n_rows + 1) * rows, LANES), F32),
            pltpu.VMEM(((n_rows + 1) * rows, LANES), F32),
            sems,
        ],
        (*received, other, slope0, mat1, turned1, turned2, bias, field, latitudes),
        (),
    )
    backs = swap(chunks)
    matrix = shape((2, BS // 2, BS), F32)
    gw1, gw2, gb1 = call(
        products_kernel,
        (matrix, matrix, shape((2, BS // 2), F32)),
        [],
        (points0, hidden0, points1, hidden1, grad_pre, grad_y),
        (),
        2 * 10**9,
    )
    three = call(join_kernel, shape((NB - 1, *packed.shape), BF16), [], backs, ())
    three = turn(three, "section")
    bundle = turn(bundle, "section")
    shifted = call(
        functools.partial(compose_kernel, lax.axis_size("section") - 1),
        shape((length, width), BF16),
        [
            by_pair,
            pltpu.VMEM((length, width), BF16),
            pltpu.SemaphoreType.DMA((width // LANES,)),
        ],
        (three, bundle, forward),
        (),
        out_specs=HBM,
    )
    shifted = shifted[None, None]
    return shifted, gw1.swapaxes(1, 2)[None], gw2.swapaxes(1, 2)[None], gb1[None]


def apply_mat(vec, mat):
    return jnp.einsum("kpi,ipj->kpj", vec, mat, preferred_element_type=F32)


def adjoint_mat(vec, mat):
    return jnp.einsum("kpj,ipj->kpi", vec, mat, preferred_element_type=F32)


def outer_sum(left, right):
    return jnp.einsum("kpi,kpj->ipj", left, right, preferred_element_type=F32)


def split_blocks(grad_out, spec_saved, w1, w2, b1, mode_counts, assignment):
    rows_dev = grad_out.shape[1]
    length = grad_out.shape[2]
    width = grad_out.shape[3]
    n_rows = assignment.shape[0]
    pairs_dev = spec_saved.shape[3] // BS
    forward, inverse = (jnp.asarray(t.astype(BF16)) for t in lon_tables(KM, length))
    cosine, sine = (jnp.asarray(t.astype(BF16))[:, assignment] for t in lat_waves(n_rows))
    table = jnp.stack(
        [jnp.stack([cosine, sine], axis=-1), jnp.stack([-sine, cosine], axis=-1)], axis=1
    )
    lat_pos = lax.axis_index("lat")
    lat_count = lax.axis_size("lat")
    own_lat = lax.dynamic_slice_in_dim(assignment, lat_pos * rows_dev, rows_dev)
    active = (jnp.arange(KM, dtype=jnp.int32)[None, :] < mode_counts[own_lat][:, None]).astype(F32)
    cotan = grad_out[0]
    spectral = jnp.einsum(
        "cml,rlni->rcmni",
        inverse,
        cotan.reshape(rows_dev, length, NB, BS),
        preferred_element_type=F32,
    )
    spectral = (spectral * active[:, None, :, None, None]).astype(BF16)
    spectral = spectral.reshape(rows_dev, 2, KM * NB * BS)
    pencil = lax.all_to_all(spectral, "lat", split_axis=2, concat_axis=0, tiled=True)
    pencil = pencil.reshape(n_rows, 2, pairs_dev, BS)
    grad_y = jnp.einsum("kerc,rcpi->kepi", table, pencil, preferred_element_type=F32).astype(BF16)
    saved = spec_saved[0].reshape(n_rows, 2, pairs_dev, BS)
    pair_ids = lat_pos * pairs_dev + jnp.arange(pairs_dev, dtype=jnp.int32)
    owner = (pair_ids % NB)[:, None] == jnp.arange(NB, dtype=jnp.int32)[None, :]
    owner = owner.astype(F32)
    first = jnp.take(w1[0].reshape(2, BS, NB, BS), pair_ids % NB, axis=2)
    second = jnp.take(w2[0].reshape(2, BS, NB, BS), pair_ids % NB, axis=2)
    shift_b = jnp.take(b1[0].reshape(2, NB, BS), pair_ids % NB, axis=1).astype(F32)
    v_r = saved[:, 0]
    v_i = saved[:, 1]
    pre_r = apply_mat(v_r, first[0]) - apply_mat(v_i, first[1]) + shift_b[0][None]
    pre_i = apply_mat(v_i, first[0]) + apply_mat(v_r, first[1]) + shift_b[1][None]
    hid_r = jax.nn.silu(pre_r).astype(BF16)
    hid_i = jax.nn.silu(pre_i).astype(BF16)
    dy_r = grad_y[:, 0]
    dy_i = grad_y[:, 1]
    dh_r = adjoint_mat(dy_r, second[0]) + adjoint_mat(dy_i, second[1])
    dh_i = adjoint_mat(dy_i, second[0]) - adjoint_mat(dy_r, second[1])
    dp_r = (dh_r * silu_slope(pre_r)).astype(BF16)
    dp_i = (dh_i * silu_slope(pre_i)).astype(BF16)
    gw2 = jnp.stack(
        [
            outer_sum(hid_r, dy_r) + outer_sum(hid_i, dy_i),
            outer_sum(hid_r, dy_i) - outer_sum(hid_i, dy_r),
        ]
    )
    gw1 = jnp.stack(
        [outer_sum(v_r, dp_r) + outer_sum(v_i, dp_i), outer_sum(v_r, dp_i) - outer_sum(v_i, dp_r)]
    )
    gb1 = jnp.stack([jnp.sum(dp_r.astype(F32), axis=0), jnp.sum(dp_i.astype(F32), axis=0)])
    dv_r = adjoint_mat(dp_r, first[0]) + adjoint_mat(dp_i, first[1])
    dv_i = adjoint_mat(dp_i, first[0]) - adjoint_mat(dp_r, first[1])
    grad_v = jnp.stack([dv_r, dv_i], axis=1).astype(BF16)
    grad_u = jnp.einsum("kerc,kepi->rcpi", table, grad_v, preferred_element_type=F32).astype(BF16)
    grad_u = grad_u.reshape(n_rows, 2, pairs_dev * BS)
    back = lax.all_to_all(grad_u, "lat", split_axis=0, concat_axis=2, tiled=True)
    back = back.reshape(rows_dev, 2, KM, NB, BS) * active[:, None, :, None, None].astype(BF16)
    mixed = jnp.einsum("cml,rcmni->rlni", forward, back, preferred_element_type=F32)
    mixed = mixed.reshape(rows_dev, length, width).astype(BF16)
    block_w1 = jnp.einsum("pn,cipj->cinj", owner, gw1).reshape(1, 2, BS, width)
    block_w2 = jnp.einsum("pn,cipj->cinj", owner, gw2).reshape(1, 2, BS, width)
    block_b1 = jnp.einsum("pn,cpj->cnj", owner, gb1).reshape(1, 2, width)
    columns = width // lat_count
    full_w1, full_w2, full_b1 = lax.psum((block_w1, block_w2, block_b1), "lat")
    sum_w1 = lax.dynamic_slice_in_dim(full_w1, lat_pos * columns, columns, 3)
    sum_w2 = lax.dynamic_slice_in_dim(full_w2, lat_pos * columns, columns, 3)
    sum_b1 = lax.dynamic_slice_in_dim(full_b1, lat_pos * columns, columns, 2)
    whole = (cotan.astype(F32) + mixed.astype(F32)).astype(BF16)
    received = from_behind(whole[None], "section", -1)
    return (received, sum_w1, sum_w2, sum_b1)


def per_device(grad_out, spec_saved, w1, w2, b1, mode_counts, assignment):
    n_dev = lax.axis_size("lat")
    pairs_dev = spec_saved.shape[3] // BS
    paired = n_dev == 2 * NB and grad_out.shape[1] == 1 and pairs_dev % NB == 0
    body = paired_blocks if paired else split_blocks
    return body(grad_out, spec_saved, w1, w2, b1, mode_counts, assignment)


def solution(mesh):
    return jax.shard_map(
        per_device,
        mesh=mesh,
        in_specs=(
            P("section", "lat", None, None),
            P("section", None, None, "lat"),
            P("section", None, None, None),
            P("section", None, None, None),
            P("section", None, None),
            P(),
            P(),
        ),
        out_specs=(
            P("section", "lat", None, None),
            P("section", None, None, "lat"),
            P("section", None, None, "lat"),
            P("section", None, "lat"),
        ),
        check_vma=False,
    )
```

```python
import functools
import math

import jax
import jax.numpy as jnp
import numpy as np
from jax import lax
from jax.experimental import pallas as pl
from jax.experimental.pallas import tpu as pltpu
from jax.sharding import PartitionSpec as P

NB = 4
BS = 96
KM = 72
LANES = 128
F32 = jnp.float32
BF16 = jnp.bfloat16


def from_behind(value, axis, by):
    length = lax.axis_size(axis)
    pairs = [(i, i + by) for i in range(length) if 0 <= i + by < length]
    return lax.ppermute(value, axis, pairs)


def turn(value, axis):
    length = lax.axis_size(axis)
    return lax.ppermute(value, axis, [(i, (i - 1) % length) for i in range(length)])


def halves_of_turn(value, axis):
    length = lax.axis_size(axis)
    if length % 2:
        return [turn(value, axis)] * 2
    to_even = [(i, i ^ 1) for i in range(length)]
    to_odd = [(i, i - 1) for i in range(2, length)] + [(0, 0), (1, length - 1)]
    return [lax.ppermute(value, axis, pairs) for pairs in (to_even, to_odd)]


def lon_tables(n_modes, length):
    modes = np.arange(n_modes)
    phase = modes[:, None] * np.arange(length)[None, :] % length
    angle = phase * (2.0 * math.pi / length)
    forward = np.stack([np.cos(angle), -np.sin(angle)]) / math.sqrt(length)
    weight = np.where(modes == 0, 1.0, 2.0)[None, :, None]
    return forward, forward * weight


def lat_waves(n_rows):
    freqs = np.arange(n_rows)
    angle = (freqs[:, None] * freqs[None, :] % n_rows) * (2.0 * math.pi / n_rows)
    factor = 1.0 / math.sqrt(n_rows)
    return np.cos(angle) * factor, np.sin(angle) * factor


def silu_slope(pre):
    sig = jax.nn.sigmoid(pre)
    return sig * (1.0 + pre * (1.0 - sig))


def window(x, start):
    low = start // LANES * LANES
    shift = start - low
    if shift == 0:
        return x[:, low : low + LANES]
    if shift + BS <= LANES:
        return pltpu.roll(x[:, low : low + LANES], LANES - shift, 1)
    return pltpu.roll(x[:, low : low + 2 * LANES], 2 * LANES - shift, 1)[:, :LANES]


def dense(parts):
    lane = lax.broadcasted_iota(jnp.int32, parts[0].shape, 1)
    first = pltpu.roll(parts[1], 96, 1)
    second = pltpu.roll(parts[2], 64, 1)
    third = pltpu.roll(parts[3], 32, 1)
    return jnp.concatenate(
        [
            jnp.where(lane < 96, parts[0], first),
            jnp.where(lane < 64, first, second),
            jnp.where(lane < 32, second, third),
        ],
        axis=1,
    )


def dot(a, b, contract):
    return lax.dot_general(a, b, ((contract[:1], contract[1:]), ((), ())), preferred_element_type=F32)


def mode_numbers(shape, axis, q):
    number = lax.broadcasted_iota(jnp.int32, shape, axis)
    second = number >= NB * q
    number = jnp.where(second, number - NB * q, number)
    mode = number
    for z in range(1, NB):
        mode = jnp.where(number >= z * q, number + z * q, mode)
    return jnp.where(second, mode + q, mode)


def eight_points(x, sign):
    root = float(np.float32(1.0 / math.sqrt(8.0)).astype(BF16))

    def add(a, b):
        return a[0] + b[0], a[1] + b[1]

    def sub(a, b):
        return a[0] - b[0], a[1] - b[1]

    def times_i(a, by):
        return (-a[1], a[0]) if by > 0 else (a[1], -a[0])

    def scale(a, by):
        return a[0] * by, a[1] * by

    def four(a, b, c, d):
        total, far, other, near = add(a, c), sub(a, c), add(b, d), sub(b, d)
        near = times_i(near, sign)
        return add(total, other), add(far, near), sub(total, other), sub(far, near)

    even = [scale(a, root) for a in four(*x[0::2])]
    odd = four(*x[1::2])
    turned = [
        scale(odd[0], root),
        scale(add(odd[1], times_i(odd[1], sign)), 0.25),
        scale(times_i(odd[2], sign), root),
        scale(sub(times_i(odd[3], sign), odd[3]), 0.25),
    ]
    return [add(a, b) for a, b in zip(even, turned)] + [sub(a, b) for a, b in zip(even, turned)]


def fetch(sems, sources, targets):
    copies = [
        pltpu.make_async_copy(source, target, sems.at[i])
        for i, (source, target) in enumerate(zip(sources, targets))
    ]
    for copy in copies:
        copy.start()
    return copies


def fetch_parts(sems, source, target, parts):
    return fetch(sems, [source.at[part] for part in parts], [target.at[part] for part in parts])


def columns(width):
    return [(slice(None), pl.ds(i, LANES)) for i in range(0, width, LANES)]


def wait(copies):
    for copy in copies:
        copy.wait()


def partner(d):
    return jnp.bitwise_xor(lax.axis_index("lat") // 2, d)


def analyse_kernel(q, *refs):
    hbm, outs, held = refs[:5], refs[5:9], refs[9:14]
    by_block, few, sems = refs[14:]
    counts, assign, field, table, saved = held
    early = fetch_parts(sems.at[0], hbm[4], saved, [pl.ds(k, 2) for k in range(0, 2 * NB, 2)])
    late = fetch_parts(sems.at[1], hbm[2], field, columns(field.shape[1]))
    late += fetch(few, hbm[:2] + hbm[3:4], held[:2] + held[3:4])
    wait(early + late)
    parts = [saved[:, c, :].astype(F32) for c in range(2)]
    points = [
        [
            jnp.concatenate([window(part, (mm * NB + n) * BS) for mm in range(q)], axis=0)
            for part in parts
        ]
        for n in range(NB)
    ]
    rows = by_block.shape[1]
    spectral = jnp.dot(table[...], field[...], preferred_element_type=F32)
    active = counts[assign[lax.axis_index("lat")]]
    held_modes = mode_numbers((rows, spectral.shape[1]), 0, q) < active
    spectra = [jnp.where(held_modes, spectral[c * rows : (c + 1) * rows], 0.0) for c in range(2)]
    for n in range(NB):
        pieces = [window(spectrum, n * BS) for spectrum in spectra]
        by_block[n] = dense(pieces + points[n]).astype(BF16)
    for d, out in enumerate(outs):
        out[...] = by_block[partner(d)]


def ready_kernel(q, *refs):
    hbm, (mat1, turned1, turned2, bias, own_table, latitudes) = refs[:6], refs[6:12]
    counts, assign, w1, w2, b1, table, sems = refs[12:]
    copies = fetch(sems, hbm, (counts, assign, w1, w2, b1, table))
    wait(copies)
    lane = lax.broadcasted_iota(jnp.int32, latitudes.shape, 1)
    line = jnp.zeros(latitudes.shape, jnp.int32)
    for r in range(2 * NB):
        line = jnp.where(lane == r, assign[r], line)
    latitudes[...] = line
    active = counts[assign[lax.axis_index("lat")]]
    rows = table.shape[1] // 2
    held_modes = mode_numbers((table.shape[0], rows), 1, q) < active
    for c in range(2):
        part = table[:, c * rows : (c + 1) * rows].astype(F32)
        own_table[:, c * rows : (c + 1) * rows] = jnp.where(held_modes, part, 0.0).astype(BF16)
    block = lax.axis_index("lat") // 2

    def pick(x):
        value = window(x, 0)
        for n in range(1, NB):
            value = jnp.where(block == n, window(x, n * BS), value)
        lane = lax.broadcasted_iota(jnp.int32, value.shape, 1)
        return jnp.where(lane < BS, value, 0.0)

    gap = jnp.zeros((LANES - BS, 2 * LANES), F32)
    for source, mat, turned in ((w1, mat1, turned1), (w2, None, turned2)):
        real, imag = (pick(source[c].astype(F32)) for c in range(2))
        whole = [
            jnp.concatenate([real, imag], axis=1),
            gap,
            jnp.concatenate([-imag, real], axis=1),
            gap,
        ]
        whole = jnp.concatenate(whole, axis=0)
        turned[...] = whole.T.astype(BF16)
        if mat is not None:
            mat[...] = whole.astype(BF16)
    shift_b = pick(b1[...].astype(F32))
    bias[...] = jnp.concatenate([shift_b[0:1], shift_b[1:2]], axis=1)


ORDER = (0, 3, 2, 1)


def join_kernel(*refs):
    out = refs[-1]
    for i in range(out.shape[0]):
        out[i] = refs[i][...]


def pack(band):
    rows = band.shape[0]
    tail = rows // 2 + 4
    left, right = band[:, :LANES], pltpu.roll(band[:, LANES:], 96, 1)
    lane = lax.broadcasted_iota(jnp.int32, left.shape, 1)
    upper = jnp.where(lane < 96, left, right)
    lower = pltpu.roll(right[rows - tail :], 64, 1)
    lower = jnp.where(lane[:tail] < 64, right[:tail], lower)
    return jnp.concatenate([upper, lower], axis=0)


def unpack(packed, rows):
    tail = rows // 2 + 4
    upper, lower = packed[:rows], packed[rows:]
    rest = jnp.concatenate([lower, pltpu.roll(lower, 64, 1)[2 * tail - rows :]], axis=0)
    lane = lax.broadcasted_iota(jnp.int32, upper.shape, 1)
    right = jnp.where(lane < 32, pltpu.roll(upper, 32, 1), pltpu.roll(rest, 32, 1))
    return [upper, right]


def silu_points(chunks, mat, bias, by_pair, points, hidden, slope):
    for d, chunk in enumerate(chunks):
        parts = [window(chunk, j * BS) for j in (2, 3)]
        by_pair[partner(d)] = jnp.concatenate(parts, axis=1)
    v = by_pair[...].reshape(points.shape).astype(BF16)
    pre = dot(v, mat[...], (1, 0)) + bias[...]
    sig = jax.nn.sigmoid(pre)
    points[...] = v
    hidden[...] = (pre * sig).astype(BF16)
    slope[...] = sig * (1.0 + pre * (1.0 - sig))


def own_kernel(*refs):
    mat1, bias, _, points, hidden, slope, by_pair = refs[NB:]
    chunks = [refs[i][...].astype(F32) for i in ORDER]
    silu_points(chunks, mat1, bias, by_pair, points, hidden, slope)


def filter_kernel(*refs):
    owns, (other, slope_own, mat1, turned1, turned2, bias, latitudes) = refs[:4], refs[4:11]
    outs, (points, hidden, grad_pre, grad_y) = refs[11:15], refs[15:19]
    assign, by_lat, by_pair, slope, real, imag, sems = refs[19:]
    copies = fetch(sems, (latitudes,), (assign,))
    core = lax.rem(lax.axis_index("lat"), 2)
    sides = [[owns[i][...].astype(F32) for i in ORDER], [other[i].astype(F32) for i in ORDER]]
    silu_points(sides[1], mat1, bias, by_pair, points, hidden, slope)
    spectra = [
        [jnp.concatenate([window(chunk, j * BS) for j in range(2)], axis=1) for chunk in chunks]
        for chunks in sides
    ]
    wait(copies)
    for side, rows in zip((core, 1 - core), spectra):
        for d, row in enumerate(rows):
            by_lat[assign[0, 2 * partner(d) + side]] = row
    n_rows, rows, _ = by_lat.shape
    half = rows * n_rows // 2
    waves = eight_points([(by_lat[r][:, :LANES], by_lat[r][:, LANES:]) for r in range(n_rows)], -1)
    step = rows + 1
    for k, wave in enumerate(waves):
        real[k * step : k * step + rows] = wave[0]
        imag[k * step : k * step + rows] = wave[1]
    dy = [
        jnp.concatenate([ref[pl.ds(m, n_rows, stride=step), :] for m in range(rows)], axis=0)
        for ref in (real, imag)
    ]
    dy = jnp.concatenate(dy, axis=1).astype(BF16)
    dy = [jnp.where(core == side, dy[:half], dy[half:]) for side in range(2)]
    dh = dot(jnp.concatenate(dy, axis=0), turned2[...], (1, 0))
    dp = [(dh[:half] * slope_own[...]).astype(BF16), (dh[half:] * slope[...]).astype(BF16)]
    dv = dot(jnp.concatenate(dp, axis=0), turned1[...], (1, 0)).astype(BF16).astype(F32)
    for side in range(2):
        grad_y[side] = dy[side]
        grad_pre[side] = dp[side]
    step = n_rows + 1
    dv = [jnp.where(core == g, dv[:half], dv[half:]) for g in range(2)]
    for g in range(2):
        for i in range(rows // 2):
            m = g * rows // 2 + i
            real[m * step : m * step + n_rows] = dv[g][i * n_rows : (i + 1) * n_rows, :LANES]
            imag[m * step : m * step + n_rows] = dv[g][i * n_rows : (i + 1) * n_rows, LANES:]
    inner = [tuple(ref[pl.ds(k, rows, stride=step), :] for ref in (real, imag)) for k in range(n_rows)]
    for r, band in enumerate(eight_points(inner, 1)):
        by_lat[r] = jnp.concatenate(band, axis=1)
    for out, d in zip(outs, ORDER):
        out[...] = pack(by_lat[assign[0, 2 * partner(d) + core]]).astype(BF16)


def products_kernel(points0, hidden0, points1, hidden1, grad_pre, grad_y, gw1, gw2, gb1):
    core = lax.rem(lax.axis_index("lat"), 2)
    half = BS // 2
    for ref, grads, values in ((gw1, grad_pre, (points0, points1)), (gw2, grad_y, (hidden0, hidden1))):
        both = dot(grads[0], values[0][...], (0, 0)) + dot(grads[1], values[1][...], (0, 0))
        real = both[:BS, :LANES] + both[LANES : LANES + BS, LANES:]
        imag = both[LANES : LANES + BS, :LANES] - both[:BS, LANES:]
        for c, full in enumerate((real, imag)):
            ref[c] = jnp.where(core == 0, full[:half], full[half:])[:, :BS]
    sums = sum(jnp.sum(grad_pre[side].astype(F32), axis=0, keepdims=True) for side in range(2))
    for c in range(2):
        line = sums[:, c * LANES : (c + 1) * LANES]
        gb1[c : c + 1] = jnp.where(core == 0, line[:, :half], line[:, half:BS])


def compose_kernel(last, three, one, even, odd, table, out, by_block, result, sems):
    rows = by_block.shape[1]
    chunks = [one[...].astype(F32)] + [three[i].astype(F32) for i in range(3)]
    for d, chunk in zip(ORDER, chunks):
        by_block[partner(d)] = jnp.concatenate(unpack(chunk, rows), axis=1)
    parts = [
        dense([by_block[n, :, c * LANES : (c + 1) * LANES] for n in range(NB)]) for c in range(2)
    ]
    parts = jnp.concatenate(parts, axis=0).astype(BF16)
    none = lax.axis_index("section") == last
    copies = []
    for i, (_, tile) in enumerate(columns(out.shape[1])):
        mixed = jnp.dot(table[...], parts[:, i * LANES : (i + 1) * LANES], preferred_element_type=F32)
        field = jnp.where(lax.axis_index("section") % 2 == 1, odd[:, tile], even[:, tile])
        whole = field.astype(F32) + mixed.astype(BF16).astype(F32)
        result[:, tile] = jnp.where(none, 0.0, whole).astype(BF16)
        copies.append(pltpu.make_async_copy(result.at[:, tile], out.at[:, tile], sems.at[i]))
        copies[-1].start()
    wait(copies)


VMEM = pl.BlockSpec(memory_space=pltpu.VMEM)
HBM = pl.BlockSpec(memory_space=pltpu.HBM)


def call(kernel, outs, scratch, near, far, flops=10**5, out_specs=None):
    out_specs = out_specs or (tuple([VMEM] * len(outs)) if isinstance(outs, tuple) else VMEM)
    many = isinstance(outs, tuple)
    return pl.pallas_call(
        kernel,
        out_shape=outs,
        in_specs=[VMEM] * len(near) + [HBM] * len(far),
        out_specs=out_specs,
        scratch_shapes=scratch,
        cost_estimate=pl.CostEstimate(flops=flops, bytes_accessed=10**3, transcendentals=0),
        compiler_params=pltpu.CompilerParams(vmem_limit_bytes=32 * 2**20),
    )(*near, *(pltpu.with_memory_space_constraint(x, pltpu.HBM) for x in far))


def scratch_for(*arrays):
    scratch = []
    for x in arrays:
        space = pltpu.SMEM if x.dtype == jnp.int32 else pltpu.VMEM
        scratch.append(space(x.shape, x.dtype))
    return scratch, pltpu.SemaphoreType.DMA((len(arrays),))


def paired_blocks(grad_out, spec_saved, w1, w2, b1, mode_counts, assignment):
    length, width = grad_out.shape[2:]
    n_rows = assignment.shape[0]
    q = spec_saved.shape[3] // (NB * BS)
    rows = 2 * NB * q
    forward, inverse = lon_tables(KM, length)

    def by_part(table):
        table = table.reshape(2, NB, 2, q, length).transpose(0, 2, 1, 3, 4)
        return table.reshape(2 * rows, length).astype(BF16)

    inverse = jnp.asarray(by_part(inverse))
    forward = jnp.asarray(by_part(forward).T)

    def swap(chunks):
        pairs = [[(i, i ^ (2 * d)) for i in range(2 * NB)] for d in ORDER[1:]]
        return [lax.ppermute(chunk, "lat", p) for chunk, p in zip(chunks, pairs)]

    field = grad_out.reshape(length, width)
    shape = jax.ShapeDtypeStruct
    far = (mode_counts, assignment, field, inverse, spec_saved[0])
    scratch, sems = scratch_for(*far)
    sent = call(
        functools.partial(analyse_kernel, q),
        (shape((rows, width), BF16),) * NB,
        scratch + [pltpu.VMEM((NB, rows, width), BF16), sems, pltpu.SemaphoreType.DMA((2, 4))],
        (),
        far,
    )
    even_field, odd_field = halves_of_turn(field, "section")
    received = [sent[0], *swap([sent[d] for d in ORDER[1:]])]
    far = (mode_counts, assignment, w1[0], w2[0], b1[0], forward)
    scratch, _ = scratch_for(*far)
    wide = 2 * LANES
    mat1, turned1, turned2, bias, forward, latitudes = call(
        functools.partial(ready_kernel, q),
        (
            shape((wide, wide), BF16),
            shape((wide, wide), BF16),
            shape((wide, wide), BF16),
            shape((1, wide), F32),
            shape(forward.shape, BF16),
            shape((1, LANES), jnp.int32),
        ),
        scratch + [pltpu.SemaphoreType.DMA((len(far),))],
        (),
        far,
        2 * 10**9,
    )
    own = call(
        join_kernel,
        shape((NB, rows, width), BF16),
        [],
        (*received, bias),
        (),
    )
    other = lax.ppermute(own, "lat", [(i, i ^ 1) for i in range(2 * NB)])
    vectors = shape((NB * rows, wide), BF16)
    slopes = shape((NB * rows, wide), F32)
    by_pair = pltpu.VMEM((NB, rows, wide), F32)
    points0, hidden0, slope0 = call(
        own_kernel,
        (vectors, vectors, slopes),
        [by_pair],
        (*received, mat1, bias, own),
        (),
    )
    packed = shape((rows + rows // 2 + 4, LANES), BF16)
    scratch, sems = scratch_for(latitudes)
    both = shape((2, NB * rows, wide), BF16)
    own_chunk, *chunks, points1, hidden1, grad_pre, grad_y = call(
        filter_kernel,
        (packed,) * NB + (vectors, vectors, both, both),
        scratch
        + [
            pltpu.VMEM((n_rows, rows, wide), F32),
            by_pair,
            pltpu.VMEM((NB * rows, wide), F32),
            pltpu.VMEM(((n_rows + 1) * rows, LANES), F32),
            pltpu.VMEM(((n_rows + 1) * rows, LANES), F32),
            sems,
        ],
        (*received, other, slope0, mat1, turned1, turned2, bias, latitudes),
        (),
    )
    backs = swap(chunks)
    matrix = shape((2, BS // 2, BS), F32)
    gw1, gw2, gb1 = call(
        products_kernel,
        (matrix, matrix, shape((2, BS // 2), F32)),
        [],
        (points0, hidden0, points1, hidden1, grad_pre, grad_y),
        (),
        2 * 10**9,
    )
    three = call(join_kernel, shape((NB - 1, *packed.shape), BF16), [], (*backs, even_field), ())
    three = turn(three, "section")
    one = turn(own_chunk, "section")
    shifted = call(
        functools.partial(compose_kernel, lax.axis_size("section") - 1),
        shape((length, width), BF16),
        [
            by_pair,
            pltpu.VMEM((length, width), BF16),
            pltpu.SemaphoreType.DMA((width // LANES,)),
        ],
        (three, one, even_field, odd_field, forward),
        (),
        out_specs=HBM,
    )
    shifted = shifted[None, None]
    return shifted, gw1.swapaxes(1, 2)[None], gw2.swapaxes(1, 2)[None], gb1[None]


def apply_mat(vec, mat):
    return jnp.einsum("kpi,ipj->kpj", vec, mat, preferred_element_type=F32)


def adjoint_mat(vec, mat):
    return jnp.einsum("kpj,ipj->kpi", vec, mat, preferred_element_type=F32)


def outer_sum(left, right):
    return jnp.einsum("kpi,kpj->ipj", left, right, preferred_element_type=F32)


def split_blocks(grad_out, spec_saved, w1, w2, b1, mode_counts, assignment):
    rows_dev = grad_out.shape[1]
    length = grad_out.shape[2]
    width = grad_out.shape[3]
    n_rows = assignment.shape[0]
    pairs_dev = spec_saved.shape[3] // BS
    forward, inverse = (jnp.asarray(t.astype(BF16)) for t in lon_tables(KM, length))
    cosine, sine = (jnp.asarray(t.astype(BF16))[:, assignment] for t in lat_waves(n_rows))
    table = jnp.stack(
        [jnp.stack([cosine, sine], axis=-1), jnp.stack([-sine, cosine], axis=-1)], axis=1
    )
    lat_pos = lax.axis_index("lat")
    lat_count = lax.axis_size("lat")
    own_lat = lax.dynamic_slice_in_dim(assignment, lat_pos * rows_dev, rows_dev)
    active = (jnp.arange(KM, dtype=jnp.int32)[None, :] < mode_counts[own_lat][:, None]).astype(F32)
    cotan = grad_out[0]
    spectral = jnp.einsum(
        "cml,rlni->rcmni",
        inverse,
        cotan.reshape(rows_dev, length, NB, BS),
        preferred_element_type=F32,
    )
    spectral = (spectral * active[:, None, :, None, None]).astype(BF16)
    spectral = spectral.reshape(rows_dev, 2, KM * NB * BS)
    pencil = lax.all_to_all(spectral, "lat", split_axis=2, concat_axis=0, tiled=True)
    pencil = pencil.reshape(n_rows, 2, pairs_dev, BS)
    grad_y = jnp.einsum("kerc,rcpi->kepi", table, pencil, preferred_element_type=F32).astype(BF16)
    saved = spec_saved[0].reshape(n_rows, 2, pairs_dev, BS)
    pair_ids = lat_pos * pairs_dev + jnp.arange(pairs_dev, dtype=jnp.int32)
    owner = (pair_ids % NB)[:, None] == jnp.arange(NB, dtype=jnp.int32)[None, :]
    owner = owner.astype(F32)
    first = jnp.take(w1[0].reshape(2, BS, NB, BS), pair_ids % NB, axis=2)
    second = jnp.take(w2[0].reshape(2, BS, NB, BS), pair_ids % NB, axis=2)
    shift_b = jnp.take(b1[0].reshape(2, NB, BS), pair_ids % NB, axis=1).astype(F32)
    v_r = saved[:, 0]
    v_i = saved[:, 1]
    pre_r = apply_mat(v_r, first[0]) - apply_mat(v_i, first[1]) + shift_b[0][None]
    pre_i = apply_mat(v_i, first[0]) + apply_mat(v_r, first[1]) + shift_b[1][None]
    hid_r = jax.nn.silu(pre_r).astype(BF16)
    hid_i = jax.nn.silu(pre_i).astype(BF16)
    dy_r = grad_y[:, 0]
    dy_i = grad_y[:, 1]
    dh_r = adjoint_mat(dy_r, second[0]) + adjoint_mat(dy_i, second[1])
    dh_i = adjoint_mat(dy_i, second[0]) - adjoint_mat(dy_r, second[1])
    dp_r = (dh_r * silu_slope(pre_r)).astype(BF16)
    dp_i = (dh_i * silu_slope(pre_i)).astype(BF16)
    gw2 = jnp.stack(
        [
            outer_sum(hid_r, dy_r) + outer_sum(hid_i, dy_i),
            outer_sum(hid_r, dy_i) - outer_sum(hid_i, dy_r),
        ]
    )
    gw1 = jnp.stack(
        [outer_sum(v_r, dp_r) + outer_sum(v_i, dp_i), outer_sum(v_r, dp_i) - outer_sum(v_i, dp_r)]
    )
    gb1 = jnp.stack([jnp.sum(dp_r.astype(F32), axis=0), jnp.sum(dp_i.astype(F32), axis=0)])
    dv_r = adjoint_mat(dp_r, first[0]) + adjoint_mat(dp_i, first[1])
    dv_i = adjoint_mat(dp_i, first[0]) - adjoint_mat(dp_r, first[1])
    grad_v = jnp.stack([dv_r, dv_i], axis=1).astype(BF16)
    grad_u = jnp.einsum("kerc,kepi->rcpi", table, grad_v, preferred_element_type=F32).astype(BF16)
    grad_u = grad_u.reshape(n_rows, 2, pairs_dev * BS)
    back = lax.all_to_all(grad_u, "lat", split_axis=0, concat_axis=2, tiled=True)
    back = back.reshape(rows_dev, 2, KM, NB, BS) * active[:, None, :, None, None].astype(BF16)
    mixed = jnp.einsum("cml,rcmni->rlni", forward, back, preferred_element_type=F32)
    mixed = mixed.reshape(rows_dev, length, width).astype(BF16)
    block_w1 = jnp.einsum("pn,cipj->cinj", owner, gw1).reshape(1, 2, BS, width)
    block_w2 = jnp.einsum("pn,cipj->cinj", owner, gw2).reshape(1, 2, BS, width)
    block_b1 = jnp.einsum("pn,cpj->cnj", owner, gb1).reshape(1, 2, width)
    columns = width // lat_count
    full_w1, full_w2, full_b1 = lax.psum((block_w1, block_w2, block_b1), "lat")
    sum_w1 = lax.dynamic_slice_in_dim(full_w1, lat_pos * columns, columns, 3)
    sum_w2 = lax.dynamic_slice_in_dim(full_w2, lat_pos * columns, columns, 3)
    sum_b1 = lax.dynamic_slice_in_dim(full_b1, lat_pos * columns, columns, 2)
    whole = (cotan.astype(F32) + mixed.astype(F32)).astype(BF16)
    received = from_behind(whole[None], "section", -1)
    return (received, sum_w1, sum_w2, sum_b1)


def per_device(grad_out, spec_saved, w1, w2, b1, mode_counts, assignment):
    n_dev = lax.axis_size("lat")
    pairs_dev = spec_saved.shape[3] // BS
    paired = n_dev == 2 * NB and grad_out.shape[1] == 1 and pairs_dev % NB == 0
    body = paired_blocks if paired else split_blocks
    return body(grad_out, spec_saved, w1, w2, b1, mode_counts, assignment)


def solution(mesh):
    return jax.shard_map(
        per_device,
        mesh=mesh,
        in_specs=(
            P("section", "lat", None, None),
            P("section", None, None, "lat"),
            P("section", None, None, None),
            P("section", None, None, None),
            P("section", None, None),
            P(),
            P(),
        ),
        out_specs=(
            P("section", "lat", None, None),
            P("section", None, None, "lat"),
            P("section", None, None, "lat"),
            P("section", None, "lat"),
        ),
        check_vma=False,
    )
```

```python
import functools
import math

import jax
import jax.numpy as jnp
import numpy as np
from jax import lax
from jax.experimental import pallas as pl
from jax.experimental.pallas import tpu as pltpu
from jax.sharding import PartitionSpec as P

NB = 4
BS = 96
KM = 72
LANES = 128
F32 = jnp.float32
BF16 = jnp.bfloat16


def from_behind(value, axis, by):
    length = lax.axis_size(axis)
    pairs = [(i, i + by) for i in range(length) if 0 <= i + by < length]
    return lax.ppermute(value, axis, pairs)


def turn(value, axis):
    length = lax.axis_size(axis)
    return lax.ppermute(value, axis, [(i, (i - 1) % length) for i in range(length)])


def lon_tables(n_modes, length):
    modes = np.arange(n_modes)
    phase = modes[:, None] * np.arange(length)[None, :] % length
    angle = phase * (2.0 * math.pi / length)
    forward = np.stack([np.cos(angle), -np.sin(angle)]) / math.sqrt(length)
    weight = np.where(modes == 0, 1.0, 2.0)[None, :, None]
    return forward, forward * weight


def lat_waves(n_rows):
    freqs = np.arange(n_rows)
    angle = (freqs[:, None] * freqs[None, :] % n_rows) * (2.0 * math.pi / n_rows)
    factor = 1.0 / math.sqrt(n_rows)
    return np.cos(angle) * factor, np.sin(angle) * factor


def silu_slope(pre):
    sig = jax.nn.sigmoid(pre)
    return sig * (1.0 + pre * (1.0 - sig))


def window(x, start):
    low = start // LANES * LANES
    shift = start - low
    if shift == 0:
        return x[:, low : low + LANES]
    if shift + BS <= LANES:
        return pltpu.roll(x[:, low : low + LANES], LANES - shift, 1)
    return pltpu.roll(x[:, low : low + 2 * LANES], 2 * LANES - shift, 1)[:, :LANES]


def dense(parts):
    lane = lax.broadcasted_iota(jnp.int32, parts[0].shape, 1)
    first = pltpu.roll(parts[1], 96, 1)
    second = pltpu.roll(parts[2], 64, 1)
    third = pltpu.roll(parts[3], 32, 1)
    return jnp.concatenate(
        [
            jnp.where(lane < 96, parts[0], first),
            jnp.where(lane < 64, first, second),
            jnp.where(lane < 32, second, third),
        ],
        axis=1,
    )


def dot(a, b, contract):
    return lax.dot_general(a, b, ((contract[:1], contract[1:]), ((), ())), preferred_element_type=F32)


def mode_numbers(shape, axis, q):
    number = lax.broadcasted_iota(jnp.int32, shape, axis)
    second = number >= NB * q
    number = jnp.where(second, number - NB * q, number)
    mode = number
    for z in range(1, NB):
        mode = jnp.where(number >= z * q, number + z * q, mode)
    return jnp.where(second, mode + q, mode)


def eight_points(x, sign):
    root = float(np.float32(1.0 / math.sqrt(8.0)).astype(BF16))

    def add(a, b):
        return a[0] + b[0], a[1] + b[1]

    def sub(a, b):
        return a[0] - b[0], a[1] - b[1]

    def times_i(a, by):
        return (-a[1], a[0]) if by > 0 else (a[1], -a[0])

    def scale(a, by):
        return a[0] * by, a[1] * by

    def four(a, b, c, d):
        total, far, other, near = add(a, c), sub(a, c), add(b, d), sub(b, d)
        near = times_i(near, sign)
        return add(total, other), add(far, near), sub(total, other), sub(far, near)

    even = [scale(a, root) for a in four(*x[0::2])]
    odd = four(*x[1::2])
    turned = [
        scale(odd[0], root),
        scale(add(odd[1], times_i(odd[1], sign)), 0.25),
        scale(times_i(odd[2], sign), root),
        scale(sub(times_i(odd[3], sign), odd[3]), 0.25),
    ]
    return [add(a, b) for a, b in zip(even, turned)] + [sub(a, b) for a, b in zip(even, turned)]


def fetch(sems, sources, targets):
    copies = [
        pltpu.make_async_copy(source, target, sems.at[i])
        for i, (source, target) in enumerate(zip(sources, targets))
    ]
    for copy in copies:
        copy.start()
    return copies


def fetch_parts(sems, source, target, parts):
    return fetch(sems, [source.at[part] for part in parts], [target.at[part] for part in parts])


def columns(width):
    return [(slice(None), pl.ds(i, LANES)) for i in range(0, width, LANES)]


def wait(copies):
    for copy in copies:
        copy.wait()


def partner(d):
    return jnp.bitwise_xor(lax.axis_index("lat") // 2, d)


def analyse_kernel(q, *refs):
    hbm, outs, held = refs[:5], refs[5:9], refs[9:14]
    by_block, few, sems = refs[14:]
    counts, assign, field, table, saved = held
    early = fetch_parts(sems.at[0], hbm[4], saved, [pl.ds(k, 2) for k in range(0, 2 * NB, 2)])
    late = fetch_parts(sems.at[1], hbm[2], field, columns(field.shape[1]))
    late += fetch(few, hbm[:2] + hbm[3:4], held[:2] + held[3:4])
    wait(early + late)
    parts = [saved[:, c, :].astype(F32) for c in range(2)]
    width = field.shape[1]
    points = [
        jnp.concatenate([part[:, i : i + width] for i in range(0, part.shape[1], width)], axis=0)
        for part in parts
    ]
    rows = by_block.shape[1]
    spectral = jnp.dot(table[...], field[...], preferred_element_type=F32)
    active = counts[assign[lax.axis_index("lat")]]
    held_modes = mode_numbers((rows, LANES), 0, q) < active
    spectra = [
        jnp.concatenate(
            [
                jnp.where(held_modes, spectral[c * rows : (c + 1) * rows, i : i + LANES], 0.0)
                for i in range(0, width, LANES)
            ],
            axis=1,
        )
        for c in range(2)
    ]
    arrays = [array.astype(BF16) for array in spectra + points]
    for n in range(NB):
        by_block[n] = dense([window(array, n * BS) for array in arrays]).astype(BF16)
    for d, out in enumerate(outs):
        out[...] = by_block[partner(d)]


def ready_kernel(q, *refs):
    hbm, (mat1, turned1, turned2, bias, own_field, own_table, latitudes) = refs[:7], refs[7:14]
    counts, assign, w1, w2, b1, table, sems = refs[14:]
    copies = fetch(sems, hbm, (counts, assign, w1, w2, b1, table, own_field))
    wait(copies[:6])
    lane = lax.broadcasted_iota(jnp.int32, latitudes.shape, 1)
    line = jnp.zeros(latitudes.shape, jnp.int32)
    for r in range(2 * NB):
        line = jnp.where(lane == r, assign[r], line)
    latitudes[...] = line
    active = counts[assign[lax.axis_index("lat")]]
    rows = table.shape[1] // 2
    held_modes = mode_numbers((table.shape[0], rows), 1, q) < active
    for c in range(2):
        part = table[:, c * rows : (c + 1) * rows].astype(F32)
        own_table[:, c * rows : (c + 1) * rows] = jnp.where(held_modes, part, 0.0).astype(BF16)
    block = lax.axis_index("lat") // 2

    def pick(x):
        value = window(x, 0)
        for n in range(1, NB):
            value = jnp.where(block == n, window(x, n * BS), value)
        lane = lax.broadcasted_iota(jnp.int32, value.shape, 1)
        return jnp.where(lane < BS, value, 0.0)

    gap = jnp.zeros((LANES - BS, 2 * LANES), F32)
    for source, mat, turned in ((w1, mat1, turned1), (w2, None, turned2)):
        real, imag = (pick(source[c].astype(F32)) for c in range(2))
        whole = [
            jnp.concatenate([real, imag], axis=1),
            gap,
            jnp.concatenate([-imag, real], axis=1),
            gap,
        ]
        whole = jnp.concatenate(whole, axis=0)
        turned[...] = whole.T.astype(BF16)
        if mat is not None:
            mat[...] = whole.astype(BF16)
    shift_b = pick(b1[...].astype(F32))
    bias[...] = jnp.concatenate([shift_b[0:1], shift_b[1:2]], axis=1)
    wait(copies[6:])


ORDER = (0, 3, 2, 1)
FIELD_ROWS = 184


def join_kernel(*refs):
    out = refs[-1]
    for i in range(out.shape[0]):
        out[i] = refs[i][...]


def pack(band):
    rows = band.shape[0]
    tail = rows // 2 + 4
    left, right = band[:, :LANES], pltpu.roll(band[:, LANES:], 96, 1)
    lane = lax.broadcasted_iota(jnp.int32, left.shape, 1)
    upper = jnp.where(lane < 96, left, right)
    lower = pltpu.roll(right[rows - tail :], 64, 1)
    lower = jnp.where(lane[:tail] < 64, right[:tail], lower)
    return jnp.concatenate([upper, lower], axis=0)


def unpack(packed, rows):
    tail = rows // 2 + 4
    upper, lower = packed[:rows], packed[rows:]
    rest = jnp.concatenate([lower, pltpu.roll(lower, 64, 1)[2 * tail - rows :]], axis=0)
    lane = lax.broadcasted_iota(jnp.int32, upper.shape, 1)
    right = jnp.where(lane < 32, pltpu.roll(upper, 32, 1), pltpu.roll(rest, 32, 1))
    return [upper, right]


def silu_points(chunks, mat, bias, by_pair, points, hidden, slope):
    for d, chunk in enumerate(chunks):
        parts = [window(chunk, j * BS) for j in (2, 3)]
        by_pair[partner(d)] = jnp.concatenate(parts, axis=1)
    v = by_pair[...].reshape(points.shape).astype(BF16)
    pre = dot(v, mat[...], (1, 0)) + bias[...]
    sig = jax.nn.sigmoid(pre)
    points[...] = v
    hidden[...] = (pre * sig).astype(BF16)
    slope[...] = sig * (1.0 + pre * (1.0 - sig))


def own_kernel(*refs):
    mat1, bias, points, hidden, slope, by_pair = refs[NB:]
    chunks = [refs[i][...].astype(F32) for i in ORDER]
    silu_points(chunks, mat1, bias, by_pair, points, hidden, slope)


def filter_kernel(*refs):
    owns, (other, slope_own, mat1, turned1, turned2, bias, own_field) = refs[:4], refs[4:11]
    latitudes, outs, (bundle, points, hidden, grad_pre, grad_y) = refs[11], refs[12:15], refs[15:20]
    assign, by_lat, by_pair, slope, real, imag, sems = refs[20:]
    copies = fetch(sems, (latitudes,), (assign,))
    core = lax.rem(lax.axis_index("lat"), 2)
    sides = [[owns[i][...].astype(F32) for i in ORDER], [other[i].astype(F32) for i in ORDER]]
    silu_points(sides[1], mat1, bias, by_pair, points, hidden, slope)
    spectra = [
        [jnp.concatenate([window(chunk, j * BS) for j in range(2)], axis=1) for chunk in chunks]
        for chunks in sides
    ]
    wait(copies)
    for side, rows in zip((core, 1 - core), spectra):
        for d, row in enumerate(rows):
            by_lat[assign[0, 2 * partner(d) + side]] = row
    n_rows, rows, _ = by_lat.shape
    half = rows * n_rows // 2
    waves = eight_points([(by_lat[r][:, :LANES], by_lat[r][:, LANES:]) for r in range(n_rows)], -1)
    step = rows + 1
    for k, wave in enumerate(waves):
        real[k * step : k * step + rows] = wave[0]
        imag[k * step : k * step + rows] = wave[1]
    dy = [
        jnp.concatenate([ref[pl.ds(m, n_rows, stride=step), :] for m in range(rows)], axis=0)
        for ref in (real, imag)
    ]
    dy = jnp.concatenate(dy, axis=1).astype(BF16)
    dy = [jnp.where(core == side, dy[:half], dy[half:]) for side in range(2)]
    dh = dot(jnp.concatenate(dy, axis=0), turned2[...], (1, 0))
    dp = [(dh[:half] * slope_own[...]).astype(BF16), (dh[half:] * slope[...]).astype(BF16)]
    dv = dot(jnp.concatenate(dp, axis=0), turned1[...], (1, 0)).astype(BF16).astype(F32)
    for side in range(2):
        grad_y[side] = dy[side]
        grad_pre[side] = dp[side]
    step = n_rows + 1
    dv = [jnp.where(core == g, dv[:half], dv[half:]) for g in range(2)]
    for g in range(2):
        for i in range(rows // 2):
            m = g * rows // 2 + i
            real[m * step : m * step + n_rows] = dv[g][i * n_rows : (i + 1) * n_rows, :LANES]
            imag[m * step : m * step + n_rows] = dv[g][i * n_rows : (i + 1) * n_rows, LANES:]
    inner = [tuple(ref[pl.ds(k, rows, stride=step), :] for ref in (real, imag)) for k in range(n_rows)]
    for r, band in enumerate(eight_points(inner, 1)):
        by_lat[r] = jnp.concatenate(band, axis=1)
    for i, d in enumerate(ORDER):
        band = pack(by_lat[assign[0, 2 * partner(d) + core]])
        if d:
            outs[i - 1][...] = band.astype(BF16)
        else:
            tail = bundle.shape[0] - FIELD_ROWS
            band = jnp.concatenate([band, jnp.zeros((3 * tail - band.shape[0], LANES), F32)], axis=0)
            band = jnp.concatenate([band[j * tail : (j + 1) * tail] for j in range(3)], axis=1)
            lines = own_field[...].astype(F32)
            gap = jnp.zeros((FIELD_ROWS - lines.shape[0], lines.shape[1]), F32)
            bundle[...] = jnp.concatenate([lines, gap, band], axis=0).astype(BF16)


def products_kernel(points0, hidden0, points1, hidden1, grad_pre, grad_y, gw1, gw2, gb1):
    core = lax.rem(lax.axis_index("lat"), 2)
    half = BS // 2
    for ref, grads, values in ((gw1, grad_pre, (points0, points1)), (gw2, grad_y, (hidden0, hidden1))):
        both = dot(grads[0], values[0][...], (0, 0)) + dot(grads[1], values[1][...], (0, 0))
        real = both[:BS, :LANES] + both[LANES : LANES + BS, LANES:]
        imag = both[LANES : LANES + BS, :LANES] - both[:BS, LANES:]
        for c, full in enumerate((real, imag)):
            ref[c] = jnp.where(core == 0, full[:half], full[half:])[:, :BS]
    sums = sum(jnp.sum(grad_pre[side].astype(F32), axis=0, keepdims=True) for side in range(2))
    for c in range(2):
        line = sums[:, c * LANES : (c + 1) * LANES]
        gb1[c : c + 1] = jnp.where(core == 0, line[:, :half], line[:, half:BS])


def compose_kernel(last, three, bundle, table, out, by_block, result, sems):
    rows = by_block.shape[1]
    lines = bundle[...].astype(F32)
    own = lines[FIELD_ROWS:]
    own = jnp.concatenate([own[:, i * LANES : (i + 1) * LANES] for i in range(3)], axis=0)
    chunks = [own[: three.shape[1]]] + [three[i].astype(F32) for i in range(3)]
    for d, chunk in zip(ORDER, chunks):
        by_block[partner(d)] = jnp.concatenate(unpack(chunk, rows), axis=1)
    parts = [
        dense([by_block[n, :, c * LANES : (c + 1) * LANES] for n in range(NB)]) for c in range(2)
    ]
    parts = jnp.concatenate(parts, axis=0).astype(BF16)
    none = lax.axis_index("section") == last
    copies = []
    for i, (_, tile) in enumerate(columns(out.shape[1])):
        mixed = jnp.dot(table[...], parts[:, i * LANES : (i + 1) * LANES], preferred_element_type=F32)
        field = lines[: out.shape[0], i * LANES : (i + 1) * LANES]
        whole = field + mixed.astype(BF16).astype(F32)
        result[:, tile] = jnp.where(none, 0.0, whole).astype(BF16)
        copies.append(pltpu.make_async_copy(result.at[:, tile], out.at[:, tile], sems.at[i]))
        copies[-1].start()
    wait(copies)


VMEM = pl.BlockSpec(memory_space=pltpu.VMEM)
HBM = pl.BlockSpec(memory_space=pltpu.HBM)


def call(kernel, outs, scratch, near, far, flops=10**8, out_specs=None):
    out_specs = out_specs or (tuple([VMEM] * len(outs)) if isinstance(outs, tuple) else VMEM)
    many = isinstance(outs, tuple)
    return pl.pallas_call(
        kernel,
        out_shape=outs,
        in_specs=[VMEM] * len(near) + [HBM] * len(far),
        out_specs=out_specs,
        scratch_shapes=scratch,
        cost_estimate=pl.CostEstimate(flops=flops, bytes_accessed=10**6, transcendentals=0),
        compiler_params=pltpu.CompilerParams(vmem_limit_bytes=32 * 2**20),
    )(*near, *(pltpu.with_memory_space_constraint(x, pltpu.HBM) for x in far))


def scratch_for(*arrays):
    scratch = []
    for x in arrays:
        space = pltpu.SMEM if x.dtype == jnp.int32 else pltpu.VMEM
        scratch.append(space(x.shape, x.dtype))
    return scratch, pltpu.SemaphoreType.DMA((len(arrays),))


def paired_blocks(grad_out, spec_saved, w1, w2, b1, mode_counts, assignment):
    length, width = grad_out.shape[2:]
    n_rows = assignment.shape[0]
    q = spec_saved.shape[3] // (NB * BS)
    rows = 2 * NB * q
    forward, inverse = lon_tables(KM, length)

    def by_part(table):
        table = table.reshape(2, NB, 2, q, length).transpose(0, 2, 1, 3, 4)
        return table.reshape(2 * rows, length).astype(BF16)

    inverse = jnp.asarray(by_part(inverse))
    forward = jnp.asarray(by_part(forward).T)

    def swap(chunks):
        pairs = [[(i, i ^ (2 * d)) for i in range(2 * NB)] for d in ORDER[1:]]
        return [lax.ppermute(chunk, "lat", p) for chunk, p in zip(chunks, pairs)]

    field = grad_out.reshape(length, width)
    shape = jax.ShapeDtypeStruct
    far = (mode_counts, assignment, field, inverse, spec_saved[0])
    scratch, sems = scratch_for(*far)
    sent = call(
        functools.partial(analyse_kernel, q),
        (shape((rows, width), BF16),) * NB,
        scratch + [pltpu.VMEM((NB, rows, width), BF16), sems, pltpu.SemaphoreType.DMA((2, 4))],
        (),
        far,
    )
    received = [sent[0], *swap([sent[d] for d in ORDER[1:]])]
    far = (mode_counts, assignment, w1[0], w2[0], b1[0], forward)
    scratch, _ = scratch_for(*far)
    far = (*far, field)
    wide = 2 * LANES
    mat1, turned1, turned2, bias, field, forward, latitudes = call(
        functools.partial(ready_kernel, q),
        (
            shape((wide, wide), BF16),
            shape((wide, wide), BF16),
            shape((wide, wide), BF16),
            shape((1, wide), F32),
            shape(field.shape, BF16),
            shape(forward.shape, BF16),
            shape((1, LANES), jnp.int32),
        ),
        scratch + [pltpu.SemaphoreType.DMA((len(far),))],
        (),
        far,
        2 * 10**9,
    )
    own = call(
        join_kernel,
        shape((NB, rows, width), BF16),
        [],
        (*received, bias),
        (),
    )
    other = lax.ppermute(own, "lat", [(i, i ^ 1) for i in range(2 * NB)])
    vectors = shape((NB * rows, wide), BF16)
    slopes = shape((NB * rows, wide), F32)
    by_pair = pltpu.VMEM((NB, rows, wide), F32)
    points0, hidden0, slope0 = call(
        own_kernel,
        (vectors, vectors, slopes),
        [by_pair],
        (*received, mat1, bias),
        (),
        2 * 10**9,
    )
    packed = shape((rows + rows // 2 + 4, LANES), BF16)
    scratch, sems = scratch_for(latitudes)
    both = shape((2, NB * rows, wide), BF16)
    tail = -(-packed.shape[0] // 24) * 8
    bundle = shape((FIELD_ROWS + tail, width), BF16)
    *chunks, bundle, points1, hidden1, grad_pre, grad_y = call(
        filter_kernel,
        (packed,) * (NB - 1) + (bundle, vectors, vectors, both, both),
        scratch
        + [
            pltpu.VMEM((n_rows, rows, wide), F32),
            by_pair,
            pltpu.VMEM((NB * rows, wide), F32),
            pltpu.VMEM(((n_rows + 1) * rows, LANES), F32),
            pltpu.VMEM(((n_rows + 1) * rows, LANES), F32),
            sems,
        ],
        (*received, other, slope0, mat1, turned1, turned2, bias, field, latitudes),
        (),
    )
    backs = swap(chunks)
    matrix = shape((2, BS // 2, BS), F32)
    gw1, gw2, gb1 = call(
        products_kernel,
        (matrix, matrix, shape((2, BS // 2), F32)),
        [],
        (points0, hidden0, points1, hidden1, grad_pre, grad_y),
        (),
        2 * 10**9,
    )
    three = call(join_kernel, shape((NB - 1, *packed.shape), BF16), [], backs, ())
    three = turn(three, "section")
    bundle = turn(bundle, "section")
    shifted = call(
        functools.partial(compose_kernel, lax.axis_size("section") - 1),
        shape((length, width), BF16),
        [
            by_pair,
            pltpu.VMEM((length, width), BF16),
            pltpu.SemaphoreType.DMA((width // LANES,)),
        ],
        (three, bundle, forward),
        (),
        out_specs=HBM,
    )
    shifted = shifted[None, None]
    return shifted, gw1.swapaxes(1, 2)[None], gw2.swapaxes(1, 2)[None], gb1[None]


def apply_mat(vec, mat):
    return jnp.einsum("kpi,ipj->kpj", vec, mat, preferred_element_type=F32)


def adjoint_mat(vec, mat):
    return jnp.einsum("kpj,ipj->kpi", vec, mat, preferred_element_type=F32)


def outer_sum(left, right):
    return jnp.einsum("kpi,kpj->ipj", left, right, preferred_element_type=F32)


def split_blocks(grad_out, spec_saved, w1, w2, b1, mode_counts, assignment):
    rows_dev = grad_out.shape[1]
    length = grad_out.shape[2]
    width = grad_out.shape[3]
    n_rows = assignment.shape[0]
    pairs_dev = spec_saved.shape[3] // BS
    forward, inverse = (jnp.asarray(t.astype(BF16)) for t in lon_tables(KM, length))
    cosine, sine = (jnp.asarray(t.astype(BF16))[:, assignment] for t in lat_waves(n_rows))
    table = jnp.stack(
        [jnp.stack([cosine, sine], axis=-1), jnp.stack([-sine, cosine], axis=-1)], axis=1
    )
    lat_pos = lax.axis_index("lat")
    lat_count = lax.axis_size("lat")
    own_lat = lax.dynamic_slice_in_dim(assignment, lat_pos * rows_dev, rows_dev)
    active = (jnp.arange(KM, dtype=jnp.int32)[None, :] < mode_counts[own_lat][:, None]).astype(F32)
    cotan = grad_out[0]
    spectral = jnp.einsum(
        "cml,rlni->rcmni",
        inverse,
        cotan.reshape(rows_dev, length, NB, BS),
        preferred_element_type=F32,
    )
    spectral = (spectral * active[:, None, :, None, None]).astype(BF16)
    spectral = spectral.reshape(rows_dev, 2, KM * NB * BS)
    pencil = lax.all_to_all(spectral, "lat", split_axis=2, concat_axis=0, tiled=True)
    pencil = pencil.reshape(n_rows, 2, pairs_dev, BS)
    grad_y = jnp.einsum("kerc,rcpi->kepi", table, pencil, preferred_element_type=F32).astype(BF16)
    saved = spec_saved[0].reshape(n_rows, 2, pairs_dev, BS)
    pair_ids = lat_pos * pairs_dev + jnp.arange(pairs_dev, dtype=jnp.int32)
    owner = (pair_ids % NB)[:, None] == jnp.arange(NB, dtype=jnp.int32)[None, :]
    owner = owner.astype(F32)
    first = jnp.take(w1[0].reshape(2, BS, NB, BS), pair_ids % NB, axis=2)
    second = jnp.take(w2[0].reshape(2, BS, NB, BS), pair_ids % NB, axis=2)
    shift_b = jnp.take(b1[0].reshape(2, NB, BS), pair_ids % NB, axis=1).astype(F32)
    v_r = saved[:, 0]
    v_i = saved[:, 1]
    pre_r = apply_mat(v_r, first[0]) - apply_mat(v_i, first[1]) + shift_b[0][None]
    pre_i = apply_mat(v_i, first[0]) + apply_mat(v_r, first[1]) + shift_b[1][None]
    hid_r = jax.nn.silu(pre_r).astype(BF16)
    hid_i = jax.nn.silu(pre_i).astype(BF16)
    dy_r = grad_y[:, 0]
    dy_i = grad_y[:, 1]
    dh_r = adjoint_mat(dy_r, second[0]) + adjoint_mat(dy_i, second[1])
    dh_i = adjoint_mat(dy_i, second[0]) - adjoint_mat(dy_r, second[1])
    dp_r = (dh_r * silu_slope(pre_r)).astype(BF16)
    dp_i = (dh_i * silu_slope(pre_i)).astype(BF16)
    gw2 = jnp.stack(
        [
            outer_sum(hid_r, dy_r) + outer_sum(hid_i, dy_i),
            outer_sum(hid_r, dy_i) - outer_sum(hid_i, dy_r),
        ]
    )
    gw1 = jnp.stack(
        [outer_sum(v_r, dp_r) + outer_sum(v_i, dp_i), outer_sum(v_r, dp_i) - outer_sum(v_i, dp_r)]
    )
    gb1 = jnp.stack([jnp.sum(dp_r.astype(F32), axis=0), jnp.sum(dp_i.astype(F32), axis=0)])
    dv_r = adjoint_mat(dp_r, first[0]) + adjoint_mat(dp_i, first[1])
    dv_i = adjoint_mat(dp_i, first[0]) - adjoint_mat(dp_r, first[1])
    grad_v = jnp.stack([dv_r, dv_i], axis=1).astype(BF16)
    grad_u = jnp.einsum("kerc,kepi->rcpi", table, grad_v, preferred_element_type=F32).astype(BF16)
    grad_u = grad_u.reshape(n_rows, 2, pairs_dev * BS)
    back = lax.all_to_all(grad_u, "lat", split_axis=0, concat_axis=2, tiled=True)
    back = back.reshape(rows_dev, 2, KM, NB, BS) * active[:, None, :, None, None].astype(BF16)
    mixed = jnp.einsum("cml,rcmni->rlni", forward, back, preferred_element_type=F32)
    mixed = mixed.reshape(rows_dev, length, width).astype(BF16)
    block_w1 = jnp.einsum("pn,cipj->cinj", owner, gw1).reshape(1, 2, BS, width)
    block_w2 = jnp.einsum("pn,cipj->cinj", owner, gw2).reshape(1, 2, BS, width)
    block_b1 = jnp.einsum("pn,cpj->cnj", owner, gb1).reshape(1, 2, width)
    columns = width // lat_count
    full_w1, full_w2, full_b1 = lax.psum((block_w1, block_w2, block_b1), "lat")
    sum_w1 = lax.dynamic_slice_in_dim(full_w1, lat_pos * columns, columns, 3)
    sum_w2 = lax.dynamic_slice_in_dim(full_w2, lat_pos * columns, columns, 3)
    sum_b1 = lax.dynamic_slice_in_dim(full_b1, lat_pos * columns, columns, 2)
    whole = (cotan.astype(F32) + mixed.astype(F32)).astype(BF16)
    received = from_behind(whole[None], "section", -1)
    return (received, sum_w1, sum_w2, sum_b1)


def per_device(grad_out, spec_saved, w1, w2, b1, mode_counts, assignment):
    n_dev = lax.axis_size("lat")
    pairs_dev = spec_saved.shape[3] // BS
    paired = n_dev == 2 * NB and grad_out.shape[1] == 1 and pairs_dev % NB == 0
    body = paired_blocks if paired else split_blocks
    return body(grad_out, spec_saved, w1, w2, b1, mode_counts, assignment)


def solution(mesh):
    return jax.shard_map(
        per_device,
        mesh=mesh,
        in_specs=(
            P("section", "lat", None, None),
            P("section", None, None, "lat"),
            P("section", None, None, None),
            P("section", None, None, None),
            P("section", None, None),
            P(),
            P(),
        ),
        out_specs=(
            P("section", "lat", None, None),
            P("section", None, None, "lat"),
            P("section", None, None, "lat"),
            P("section", None, "lat"),
        ),
        check_vma=False,
    )
```

```python
import functools
import math

import jax
import jax.numpy as jnp
import numpy as np
from jax import lax
from jax.experimental import pallas as pl
from jax.experimental.pallas import tpu as pltpu
from jax.sharding import PartitionSpec as P

NB = 4
BS = 96
KM = 72
LANES = 128
F32 = jnp.float32
BF16 = jnp.bfloat16


def from_behind(value, axis, by):
    length = lax.axis_size(axis)
    pairs = [(i, i + by) for i in range(length) if 0 <= i + by < length]
    return lax.ppermute(value, axis, pairs)


def turn(value, axis):
    length = lax.axis_size(axis)
    return lax.ppermute(value, axis, [(i, (i - 1) % length) for i in range(length)])


def lon_tables(n_modes, length):
    modes = np.arange(n_modes)
    phase = modes[:, None] * np.arange(length)[None, :] % length
    angle = phase * (2.0 * math.pi / length)
    forward = np.stack([np.cos(angle), -np.sin(angle)]) / math.sqrt(length)
    weight = np.where(modes == 0, 1.0, 2.0)[None, :, None]
    return forward, forward * weight


def lat_waves(n_rows):
    freqs = np.arange(n_rows)
    angle = (freqs[:, None] * freqs[None, :] % n_rows) * (2.0 * math.pi / n_rows)
    factor = 1.0 / math.sqrt(n_rows)
    return np.cos(angle) * factor, np.sin(angle) * factor


def silu_slope(pre):
    sig = jax.nn.sigmoid(pre)
    return sig * (1.0 + pre * (1.0 - sig))


def window(x, start):
    low = start // LANES * LANES
    shift = start - low
    if shift == 0:
        return x[:, low : low + LANES]
    if shift + BS <= LANES:
        return pltpu.roll(x[:, low : low + LANES], LANES - shift, 1)
    return pltpu.roll(x[:, low : low + 2 * LANES], 2 * LANES - shift, 1)[:, :LANES]


def dense(parts):
    lane = lax.broadcasted_iota(jnp.int32, parts[0].shape, 1)
    first = pltpu.roll(parts[1], 96, 1)
    second = pltpu.roll(parts[2], 64, 1)
    third = pltpu.roll(parts[3], 32, 1)
    return jnp.concatenate(
        [
            jnp.where(lane < 96, parts[0], first),
            jnp.where(lane < 64, first, second),
            jnp.where(lane < 32, second, third),
        ],
        axis=1,
    )


def dot(a, b, contract):
    return lax.dot_general(a, b, ((contract[:1], contract[1:]), ((), ())), preferred_element_type=F32)


def mode_numbers(shape, axis, q):
    number = lax.broadcasted_iota(jnp.int32, shape, axis)
    second = number >= NB * q
    number = jnp.where(second, number - NB * q, number)
    mode = number
    for z in range(1, NB):
        mode = jnp.where(number >= z * q, number + z * q, mode)
    return jnp.where(second, mode + q, mode)


def eight_points(x, sign):
    root = float(np.float32(1.0 / math.sqrt(8.0)).astype(BF16))

    def add(a, b):
        return a[0] + b[0], a[1] + b[1]

    def sub(a, b):
        return a[0] - b[0], a[1] - b[1]

    def times_i(a, by):
        return (-a[1], a[0]) if by > 0 else (a[1], -a[0])

    def scale(a, by):
        return a[0] * by, a[1] * by

    def four(a, b, c, d):
        total, far, other, near = add(a, c), sub(a, c), add(b, d), sub(b, d)
        near = times_i(near, sign)
        return add(total, other), add(far, near), sub(total, other), sub(far, near)

    even = [scale(a, root) for a in four(*x[0::2])]
    odd = four(*x[1::2])
    turned = [
        scale(odd[0], root),
        scale(add(odd[1], times_i(odd[1], sign)), 0.25),
        scale(times_i(odd[2], sign), root),
        scale(sub(times_i(odd[3], sign), odd[3]), 0.25),
    ]
    return [add(a, b) for a, b in zip(even, turned)] + [sub(a, b) for a, b in zip(even, turned)]


def fetch(sems, sources, targets):
    copies = [
        pltpu.make_async_copy(source, target, sems.at[i])
        for i, (source, target) in enumerate(zip(sources, targets))
    ]
    for copy in copies:
        copy.start()
    return copies


def fetch_parts(sems, source, target, parts):
    return fetch(sems, [source.at[part] for part in parts], [target.at[part] for part in parts])


def columns(width):
    return [(slice(None), pl.ds(i, LANES)) for i in range(0, width, LANES)]


def wait(copies):
    for copy in copies:
        copy.wait()


def partner(d):
    return jnp.bitwise_xor(lax.axis_index("lat") // 2, d)


def analyse_kernel(q, *refs):
    hbm, outs, held = refs[:5], refs[5:9], refs[9:14]
    by_block, few, sems = refs[14:]
    counts, assign, field, table, saved = held
    early = fetch_parts(sems.at[0], hbm[4], saved, [pl.ds(k, 2) for k in range(0, 2 * NB, 2)])
    late = fetch_parts(sems.at[1], hbm[2], field, columns(field.shape[1]))
    late += fetch(few, hbm[:2] + hbm[3:4], held[:2] + held[3:4])
    wait(early + late)
    parts = [saved[:, c, :].astype(F32) for c in range(2)]
    width = field.shape[1]
    points = [
        jnp.concatenate([part[:, i : i + width] for i in range(0, part.shape[1], width)], axis=0)
        for part in parts
    ]
    rows = by_block.shape[1]
    spectral = jnp.dot(table[...], field[...], preferred_element_type=F32)
    active = counts[assign[lax.axis_index("lat")]]
    held_modes = mode_numbers((rows, LANES), 0, q) < active
    spectra = [
        jnp.concatenate(
            [
                jnp.where(held_modes, spectral[c * rows : (c + 1) * rows, i : i + LANES], 0.0)
                for i in range(0, width, LANES)
            ],
            axis=1,
        )
        for c in range(2)
    ]
    arrays = [array.astype(BF16) for array in spectra + points]
    for n in range(NB):
        by_block[n] = dense([window(array, n * BS) for array in arrays]).astype(BF16)
    for d, out in enumerate(outs):
        out[...] = by_block[partner(d)]


def ready_kernel(q, *refs):
    hbm, (mat1, turned1, turned2, bias, own_field, own_table, latitudes) = refs[:7], refs[7:14]
    counts, assign, w1, w2, b1, table, sems = refs[14:]
    copies = fetch(sems, hbm, (counts, assign, w1, w2, b1, table, own_field))
    wait(copies[:6])
    lane = lax.broadcasted_iota(jnp.int32, latitudes.shape, 1)
    line = jnp.zeros(latitudes.shape, jnp.int32)
    for r in range(2 * NB):
        line = jnp.where(lane == r, assign[r], line)
    latitudes[...] = line
    active = counts[assign[lax.axis_index("lat")]]
    rows = table.shape[1] // 2
    held_modes = mode_numbers((table.shape[0], rows), 1, q) < active
    for c in range(2):
        part = table[:, c * rows : (c + 1) * rows].astype(F32)
        own_table[:, c * rows : (c + 1) * rows] = jnp.where(held_modes, part, 0.0).astype(BF16)
    block = lax.axis_index("lat") // 2

    def pick(x):
        value = window(x, 0)
        for n in range(1, NB):
            value = jnp.where(block == n, window(x, n * BS), value)
        lane = lax.broadcasted_iota(jnp.int32, value.shape, 1)
        return jnp.where(lane < BS, value, 0.0)

    gap = jnp.zeros((LANES - BS, 2 * LANES), F32)
    for source, mat, turned in ((w1, mat1, turned1), (w2, None, turned2)):
        real, imag = (pick(source[c].astype(F32)) for c in range(2))
        whole = [
            jnp.concatenate([real, imag], axis=1),
            gap,
            jnp.concatenate([-imag, real], axis=1),
            gap,
        ]
        whole = jnp.concatenate(whole, axis=0)
        turned[...] = whole.T.astype(BF16)
        if mat is not None:
            mat[...] = whole.astype(BF16)
    shift_b = pick(b1[...].astype(F32))
    bias[...] = jnp.concatenate([shift_b[0:1], shift_b[1:2]], axis=1)
    wait(copies[6:])


ORDER = (0, 3, 2, 1)
FIELD_ROWS = 184


def join_kernel(*refs):
    out = refs[-1]
    for i in range(out.shape[0]):
        out[i] = refs[i][...]


def pack(band):
    rows = band.shape[0]
    tail = rows // 2 + 4
    left, right = band[:, :LANES], pltpu.roll(band[:, LANES:], 96, 1)
    lane = lax.broadcasted_iota(jnp.int32, left.shape, 1)
    upper = jnp.where(lane < 96, left, right)
    lower = pltpu.roll(right[rows - tail :], 64, 1)
    lower = jnp.where(lane[:tail] < 64, right[:tail], lower)
    return jnp.concatenate([upper, lower], axis=0)


def unpack(packed, rows):
    tail = rows // 2 + 4
    upper, lower = packed[:rows], packed[rows:]
    rest = jnp.concatenate([lower, pltpu.roll(lower, 64, 1)[2 * tail - rows :]], axis=0)
    lane = lax.broadcasted_iota(jnp.int32, upper.shape, 1)
    right = jnp.where(lane < 32, pltpu.roll(upper, 32, 1), pltpu.roll(rest, 32, 1))
    return [upper, right]


def silu_points(chunks, mat, bias, by_pair, points, hidden, slope):
    for d, chunk in enumerate(chunks):
        parts = [window(chunk, j * BS) for j in (2, 3)]
        by_pair[partner(d)] = jnp.concatenate(parts, axis=1)
    v = by_pair[...].reshape(points.shape).astype(BF16)
    pre = dot(v, mat[...], (1, 0)) + bias[...]
    sig = jax.nn.sigmoid(pre)
    points[...] = v
    hidden[...] = (pre * sig).astype(BF16)
    slope[...] = sig * (1.0 + pre * (1.0 - sig))


def own_kernel(*refs):
    mat1, bias, points, hidden, slope, by_pair = refs[NB:]
    chunks = [refs[i][...].astype(F32) for i in ORDER]
    silu_points(chunks, mat1, bias, by_pair, points, hidden, slope)


def filter_kernel(*refs):
    owns, (other, slope_own, mat1, turned1, turned2, bias, own_field) = refs[:4], refs[4:11]
    latitudes, outs, (bundle, points, hidden, grad_pre, grad_y) = refs[11], refs[12:15], refs[15:20]
    assign, by_lat, by_pair, slope, real, imag, sems = refs[20:]
    copies = fetch(sems, (latitudes,), (assign,))
    core = lax.rem(lax.axis_index("lat"), 2)
    sides = [[owns[i][...].astype(F32) for i in ORDER], [other[i].astype(F32) for i in ORDER]]
    silu_points(sides[1], mat1, bias, by_pair, points, hidden, slope)
    spectra = [
        [jnp.concatenate([window(chunk, j * BS) for j in range(2)], axis=1) for chunk in chunks]
        for chunks in sides
    ]
    wait(copies)
    for side, rows in zip((core, 1 - core), spectra):
        for d, row in enumerate(rows):
            by_lat[assign[0, 2 * partner(d) + side]] = row
    n_rows, rows, _ = by_lat.shape
    half = rows * n_rows // 2
    waves = eight_points([(by_lat[r][:, :LANES], by_lat[r][:, LANES:]) for r in range(n_rows)], -1)
    step = rows + 1
    for k, wave in enumerate(waves):
        real[k * step : k * step + rows] = wave[0]
        imag[k * step : k * step + rows] = wave[1]
    dy = [
        jnp.concatenate([ref[pl.ds(m, n_rows, stride=step), :] for m in range(rows)], axis=0)
        for ref in (real, imag)
    ]
    dy = jnp.concatenate(dy, axis=1).astype(BF16)
    dy = [jnp.where(core == side, dy[:half], dy[half:]) for side in range(2)]
    dh = dot(jnp.concatenate(dy, axis=0), turned2[...], (1, 0))
    dp = [(dh[:half] * slope_own[...]).astype(BF16), (dh[half:] * slope[...]).astype(BF16)]
    dv = dot(jnp.concatenate(dp, axis=0), turned1[...], (1, 0)).astype(BF16).astype(F32)
    for side in range(2):
        grad_y[side] = dy[side]
        grad_pre[side] = dp[side]
    step = n_rows + 1
    dv = [jnp.where(core == g, dv[:half], dv[half:]) for g in range(2)]
    for g in range(2):
        for i in range(rows // 2):
            m = g * rows // 2 + i
            real[m * step : m * step + n_rows] = dv[g][i * n_rows : (i + 1) * n_rows, :LANES]
            imag[m * step : m * step + n_rows] = dv[g][i * n_rows : (i + 1) * n_rows, LANES:]
    inner = [tuple(ref[pl.ds(k, rows, stride=step), :] for ref in (real, imag)) for k in range(n_rows)]
    for r, band in enumerate(eight_points(inner, 1)):
        by_lat[r] = jnp.concatenate(band, axis=1)
    for i, d in enumerate(ORDER):
        band = pack(by_lat[assign[0, 2 * partner(d) + core]])
        if d:
            outs[i - 1][...] = band.astype(BF16)
        else:
            tail = bundle.shape[0] - FIELD_ROWS
            band = jnp.concatenate([band, jnp.zeros((3 * tail - band.shape[0], LANES), F32)], axis=0)
            band = jnp.concatenate([band[j * tail : (j + 1) * tail] for j in range(3)], axis=1)
            lines = own_field[...].astype(F32)
            gap = jnp.zeros((FIELD_ROWS - lines.shape[0], lines.shape[1]), F32)
            bundle[...] = jnp.concatenate([lines, gap, band], axis=0).astype(BF16)


def products_kernel(points0, hidden0, points1, hidden1, grad_pre, grad_y, gw1, gw2, gb1):
    core = lax.rem(lax.axis_index("lat"), 2)
    half = BS // 2
    for ref, grads, values in ((gw1, grad_pre, (points0, points1)), (gw2, grad_y, (hidden0, hidden1))):
        both = dot(grads[0], values[0][...], (0, 0)) + dot(grads[1], values[1][...], (0, 0))
        real = both[:BS, :LANES] + both[LANES : LANES + BS, LANES:]
        imag = both[LANES : LANES + BS, :LANES] - both[:BS, LANES:]
        for c, full in enumerate((real, imag)):
            ref[c] = jnp.where(core == 0, full[:half], full[half:])[:, :BS]
    sums = sum(jnp.sum(grad_pre[side].astype(F32), axis=0, keepdims=True) for side in range(2))
    for c in range(2):
        line = sums[:, c * LANES : (c + 1) * LANES]
        gb1[c : c + 1] = jnp.where(core == 0, line[:, :half], line[:, half:BS])


def compose_kernel(last, three, bundle, table, out, by_block, result, sems):
    rows = by_block.shape[1]
    lines = bundle[...].astype(F32)
    own = lines[FIELD_ROWS:]
    own = jnp.concatenate([own[:, i * LANES : (i + 1) * LANES] for i in range(3)], axis=0)
    chunks = [own[: three.shape[1]]] + [three[i].astype(F32) for i in range(3)]
    for d, chunk in zip(ORDER, chunks):
        by_block[partner(d)] = jnp.concatenate(unpack(chunk, rows), axis=1)
    blocks = [by_block[n].astype(BF16) for n in range(NB)]
    parts = [
        dense([block[:, c * LANES : (c + 1) * LANES] for block in blocks]).astype(F32)
        for c in range(2)
    ]
    parts = jnp.concatenate(parts, axis=0).astype(BF16)
    none = lax.axis_index("section") == last
    copies = []
    for i, (_, tile) in enumerate(columns(out.shape[1])):
        mixed = jnp.dot(table[...], parts[:, i * LANES : (i + 1) * LANES], preferred_element_type=F32)
        field = lines[: out.shape[0], i * LANES : (i + 1) * LANES]
        whole = field + mixed.astype(BF16).astype(F32)
        result[:, tile] = jnp.where(none, 0.0, whole).astype(BF16)
        copies.append(pltpu.make_async_copy(result.at[:, tile], out.at[:, tile], sems.at[i]))
        copies[-1].start()
    wait(copies)


VMEM = pl.BlockSpec(memory_space=pltpu.VMEM)
HBM = pl.BlockSpec(memory_space=pltpu.HBM)


def call(kernel, outs, scratch, near, far, flops=10**8, out_specs=None):
    out_specs = out_specs or (tuple([VMEM] * len(outs)) if isinstance(outs, tuple) else VMEM)
    many = isinstance(outs, tuple)
    return pl.pallas_call(
        kernel,
        out_shape=outs,
        in_specs=[VMEM] * len(near) + [HBM] * len(far),
        out_specs=out_specs,
        scratch_shapes=scratch,
        cost_estimate=pl.CostEstimate(flops=flops, bytes_accessed=10**6, transcendentals=0),
        compiler_params=pltpu.CompilerParams(vmem_limit_bytes=32 * 2**20),
    )(*near, *(pltpu.with_memory_space_constraint(x, pltpu.HBM) for x in far))


def scratch_for(*arrays):
    scratch = []
    for x in arrays:
        space = pltpu.SMEM if x.dtype == jnp.int32 else pltpu.VMEM
        scratch.append(space(x.shape, x.dtype))
    return scratch, pltpu.SemaphoreType.DMA((len(arrays),))


def paired_blocks(grad_out, spec_saved, w1, w2, b1, mode_counts, assignment):
    length, width = grad_out.shape[2:]
    n_rows = assignment.shape[0]
    q = spec_saved.shape[3] // (NB * BS)
    rows = 2 * NB * q
    forward, inverse = lon_tables(KM, length)

    def by_part(table):
        table = table.reshape(2, NB, 2, q, length).transpose(0, 2, 1, 3, 4)
        return table.reshape(2 * rows, length).astype(BF16)

    inverse = jnp.asarray(by_part(inverse))
    forward = jnp.asarray(by_part(forward).T)

    def swap(chunks):
        pairs = [[(i, i ^ (2 * d)) for i in range(2 * NB)] for d in ORDER[1:]]
        return [lax.ppermute(chunk, "lat", p) for chunk, p in zip(chunks, pairs)]

    field = grad_out.reshape(length, width)
    shape = jax.ShapeDtypeStruct
    far = (mode_counts, assignment, field, inverse, spec_saved[0])
    scratch, sems = scratch_for(*far)
    sent = call(
        functools.partial(analyse_kernel, q),
        (shape((rows, width), BF16),) * NB,
        scratch + [pltpu.VMEM((NB, rows, width), BF16), sems, pltpu.SemaphoreType.DMA((2, 4))],
        (),
        far,
    )
    received = [sent[0], *swap([sent[d] for d in ORDER[1:]])]
    far = (mode_counts, assignment, w1[0], w2[0], b1[0], forward)
    scratch, _ = scratch_for(*far)
    far = (*far, field)
    wide = 2 * LANES
    mat1, turned1, turned2, bias, field, forward, latitudes = call(
        functools.partial(ready_kernel, q),
        (
            shape((wide, wide), BF16),
            shape((wide, wide), BF16),
            shape((wide, wide), BF16),
            shape((1, wide), F32),
            shape(field.shape, BF16),
            shape(forward.shape, BF16),
            shape((1, LANES), jnp.int32),
        ),
        scratch + [pltpu.SemaphoreType.DMA((len(far),))],
        (),
        far,
        2 * 10**9,
    )
    own = call(
        join_kernel,
        shape((NB, rows, width), BF16),
        [],
        (*received, bias),
        (),
    )
    other = lax.ppermute(own, "lat", [(i, i ^ 1) for i in range(2 * NB)])
    vectors = shape((NB * rows, wide), BF16)
    slopes = shape((NB * rows, wide), F32)
    by_pair = pltpu.VMEM((NB, rows, wide), F32)
    points0, hidden0, slope0 = call(
        own_kernel,
        (vectors, vectors, slopes),
        [by_pair],
        (*received, mat1, bias),
        (),
        2 * 10**9,
    )
    packed = shape((rows + rows // 2 + 4, LANES), BF16)
    scratch, sems = scratch_for(latitudes)
    both = shape((2, NB * rows, wide), BF16)
    tail = -(-packed.shape[0] // 24) * 8
    bundle = shape((FIELD_ROWS + tail, width), BF16)
    *chunks, bundle, points1, hidden1, grad_pre, grad_y = call(
        filter_kernel,
        (packed,) * (NB - 1) + (bundle, vectors, vectors, both, both),
        scratch
        + [
            pltpu.VMEM((n_rows, rows, wide), F32),
            by_pair,
            pltpu.VMEM((NB * rows, wide), F32),
            pltpu.VMEM(((n_rows + 1) * rows, LANES), F32),
            pltpu.VMEM(((n_rows + 1) * rows, LANES), F32),
            sems,
        ],
        (*received, other, slope0, mat1, turned1, turned2, bias, field, latitudes),
        (),
    )
    backs = swap(chunks)
    matrix = shape((2, BS // 2, BS), F32)
    gw1, gw2, gb1 = call(
        products_kernel,
        (matrix, matrix, shape((2, BS // 2), F32)),
        [],
        (points0, hidden0, points1, hidden1, grad_pre, grad_y),
        (),
        2 * 10**9,
    )
    three = call(join_kernel, shape((NB - 1, *packed.shape), BF16), [], backs, ())
    three = turn(three, "section")
    bundle = turn(bundle, "section")
    shifted = call(
        functools.partial(compose_kernel, lax.axis_size("section") - 1),
        shape((length, width), BF16),
        [
            by_pair,
            pltpu.VMEM((length, width), BF16),
            pltpu.SemaphoreType.DMA((width // LANES,)),
        ],
        (three, bundle, forward),
        (),
        out_specs=HBM,
    )
    shifted = shifted[None, None]
    return shifted, gw1.swapaxes(1, 2)[None], gw2.swapaxes(1, 2)[None], gb1[None]


def apply_mat(vec, mat):
    return jnp.einsum("kpi,ipj->kpj", vec, mat, preferred_element_type=F32)


def adjoint_mat(vec, mat):
    return jnp.einsum("kpj,ipj->kpi", vec, mat, preferred_element_type=F32)


def outer_sum(left, right):
    return jnp.einsum("kpi,kpj->ipj", left, right, preferred_element_type=F32)


def split_blocks(grad_out, spec_saved, w1, w2, b1, mode_counts, assignment):
    rows_dev = grad_out.shape[1]
    length = grad_out.shape[2]
    width = grad_out.shape[3]
    n_rows = assignment.shape[0]
    pairs_dev = spec_saved.shape[3] // BS
    forward, inverse = (jnp.asarray(t.astype(BF16)) for t in lon_tables(KM, length))
    cosine, sine = (jnp.asarray(t.astype(BF16))[:, assignment] for t in lat_waves(n_rows))
    table = jnp.stack(
        [jnp.stack([cosine, sine], axis=-1), jnp.stack([-sine, cosine], axis=-1)], axis=1
    )
    lat_pos = lax.axis_index("lat")
    lat_count = lax.axis_size("lat")
    own_lat = lax.dynamic_slice_in_dim(assignment, lat_pos * rows_dev, rows_dev)
    active = (jnp.arange(KM, dtype=jnp.int32)[None, :] < mode_counts[own_lat][:, None]).astype(F32)
    cotan = grad_out[0]
    spectral = jnp.einsum(
        "cml,rlni->rcmni",
        inverse,
        cotan.reshape(rows_dev, length, NB, BS),
        preferred_element_type=F32,
    )
    spectral = (spectral * active[:, None, :, None, None]).astype(BF16)
    spectral = spectral.reshape(rows_dev, 2, KM * NB * BS)
    pencil = lax.all_to_all(spectral, "lat", split_axis=2, concat_axis=0, tiled=True)
    pencil = pencil.reshape(n_rows, 2, pairs_dev, BS)
    grad_y = jnp.einsum("kerc,rcpi->kepi", table, pencil, preferred_element_type=F32).astype(BF16)
    saved = spec_saved[0].reshape(n_rows, 2, pairs_dev, BS)
    pair_ids = lat_pos * pairs_dev + jnp.arange(pairs_dev, dtype=jnp.int32)
    owner = (pair_ids % NB)[:, None] == jnp.arange(NB, dtype=jnp.int32)[None, :]
    owner = owner.astype(F32)
    first = jnp.take(w1[0].reshape(2, BS, NB, BS), pair_ids % NB, axis=2)
    second = jnp.take(w2[0].reshape(2, BS, NB, BS), pair_ids % NB, axis=2)
    shift_b = jnp.take(b1[0].reshape(2, NB, BS), pair_ids % NB, axis=1).astype(F32)
    v_r = saved[:, 0]
    v_i = saved[:, 1]
    pre_r = apply_mat(v_r, first[0]) - apply_mat(v_i, first[1]) + shift_b[0][None]
    pre_i = apply_mat(v_i, first[0]) + apply_mat(v_r, first[1]) + shift_b[1][None]
    hid_r = jax.nn.silu(pre_r).astype(BF16)
    hid_i = jax.nn.silu(pre_i).astype(BF16)
    dy_r = grad_y[:, 0]
    dy_i = grad_y[:, 1]
    dh_r = adjoint_mat(dy_r, second[0]) + adjoint_mat(dy_i, second[1])
    dh_i = adjoint_mat(dy_i, second[0]) - adjoint_mat(dy_r, second[1])
    dp_r = (dh_r * silu_slope(pre_r)).astype(BF16)
    dp_i = (dh_i * silu_slope(pre_i)).astype(BF16)
    gw2 = jnp.stack(
        [
            outer_sum(hid_r, dy_r) + outer_sum(hid_i, dy_i),
            outer_sum(hid_r, dy_i) - outer_sum(hid_i, dy_r),
        ]
    )
    gw1 = jnp.stack(
        [outer_sum(v_r, dp_r) + outer_sum(v_i, dp_i), outer_sum(v_r, dp_i) - outer_sum(v_i, dp_r)]
    )
    gb1 = jnp.stack([jnp.sum(dp_r.astype(F32), axis=0), jnp.sum(dp_i.astype(F32), axis=0)])
    dv_r = adjoint_mat(dp_r, first[0]) + adjoint_mat(dp_i, first[1])
    dv_i = adjoint_mat(dp_i, first[0]) - adjoint_mat(dp_r, first[1])
    grad_v = jnp.stack([dv_r, dv_i], axis=1).astype(BF16)
    grad_u = jnp.einsum("kerc,kepi->rcpi", table, grad_v, preferred_element_type=F32).astype(BF16)
    grad_u = grad_u.reshape(n_rows, 2, pairs_dev * BS)
    back = lax.all_to_all(grad_u, "lat", split_axis=0, concat_axis=2, tiled=True)
    back = back.reshape(rows_dev, 2, KM, NB, BS) * active[:, None, :, None, None].astype(BF16)
    mixed = jnp.einsum("cml,rcmni->rlni", forward, back, preferred_element_type=F32)
    mixed = mixed.reshape(rows_dev, length, width).astype(BF16)
    block_w1 = jnp.einsum("pn,cipj->cinj", owner, gw1).reshape(1, 2, BS, width)
    block_w2 = jnp.einsum("pn,cipj->cinj", owner, gw2).reshape(1, 2, BS, width)
    block_b1 = jnp.einsum("pn,cpj->cnj", owner, gb1).reshape(1, 2, width)
    columns = width // lat_count
    full_w1, full_w2, full_b1 = lax.psum((block_w1, block_w2, block_b1), "lat")
    sum_w1 = lax.dynamic_slice_in_dim(full_w1, lat_pos * columns, columns, 3)
    sum_w2 = lax.dynamic_slice_in_dim(full_w2, lat_pos * columns, columns, 3)
    sum_b1 = lax.dynamic_slice_in_dim(full_b1, lat_pos * columns, columns, 2)
    whole = (cotan.astype(F32) + mixed.astype(F32)).astype(BF16)
    received = from_behind(whole[None], "section", -1)
    return (received, sum_w1, sum_w2, sum_b1)


def per_device(grad_out, spec_saved, w1, w2, b1, mode_counts, assignment):
    n_dev = lax.axis_size("lat")
    pairs_dev = spec_saved.shape[3] // BS
    paired = n_dev == 2 * NB and grad_out.shape[1] == 1 and pairs_dev % NB == 0
    body = paired_blocks if paired else split_blocks
    return body(grad_out, spec_saved, w1, w2, b1, mode_counts, assignment)


def solution(mesh):
    return jax.shard_map(
        per_device,
        mesh=mesh,
        in_specs=(
            P("section", "lat", None, None),
            P("section", None, None, "lat"),
            P("section", None, None, None),
            P("section", None, None, None),
            P("section", None, None),
            P(),
            P(),
        ),
        out_specs=(
            P("section", "lat", None, None),
            P("section", None, None, "lat"),
            P("section", None, None, "lat"),
            P("section", None, "lat"),
        ),
        check_vma=False,
    )
```

```python
import functools
import math

import jax
import jax.numpy as jnp
import numpy as np
from jax import lax
from jax.experimental import pallas as pl
from jax.experimental.pallas import tpu as pltpu
from jax.sharding import PartitionSpec as P

NB = 4
BS = 96
KM = 72
LANES = 128
F32 = jnp.float32
BF16 = jnp.bfloat16


def from_behind(value, axis, by):
    length = lax.axis_size(axis)
    pairs = [(i, i + by) for i in range(length) if 0 <= i + by < length]
    return lax.ppermute(value, axis, pairs)


def turn(value, axis):
    length = lax.axis_size(axis)
    return lax.ppermute(value, axis, [(i, (i - 1) % length) for i in range(length)])


def lon_tables(n_modes, length):
    modes = np.arange(n_modes)
    phase = modes[:, None] * np.arange(length)[None, :] % length
    angle = phase * (2.0 * math.pi / length)
    forward = np.stack([np.cos(angle), -np.sin(angle)]) / math.sqrt(length)
    weight = np.where(modes == 0, 1.0, 2.0)[None, :, None]
    return forward, forward * weight


def lat_waves(n_rows):
    freqs = np.arange(n_rows)
    angle = (freqs[:, None] * freqs[None, :] % n_rows) * (2.0 * math.pi / n_rows)
    factor = 1.0 / math.sqrt(n_rows)
    return np.cos(angle) * factor, np.sin(angle) * factor


def silu_slope(pre):
    sig = jax.nn.sigmoid(pre)
    return sig * (1.0 + pre * (1.0 - sig))


def window(x, start):
    low = start // LANES * LANES
    shift = start - low
    if shift == 0:
        return x[:, low : low + LANES]
    if shift + BS <= LANES:
        return pltpu.roll(x[:, low : low + LANES], LANES - shift, 1)
    return pltpu.roll(x[:, low : low + 2 * LANES], 2 * LANES - shift, 1)[:, :LANES]


def dense(parts):
    lane = lax.broadcasted_iota(jnp.int32, parts[0].shape, 1)
    first = pltpu.roll(parts[1], 96, 1)
    second = pltpu.roll(parts[2], 64, 1)
    third = pltpu.roll(parts[3], 32, 1)
    return jnp.concatenate(
        [
            jnp.where(lane < 96, parts[0], first),
            jnp.where(lane < 64, first, second),
            jnp.where(lane < 32, second, third),
        ],
        axis=1,
    )


def dot(a, b, contract):
    return lax.dot_general(a, b, ((contract[:1], contract[1:]), ((), ())), preferred_element_type=F32)


def mode_numbers(shape, axis, q):
    number = lax.broadcasted_iota(jnp.int32, shape, axis)
    second = number >= NB * q
    number = jnp.where(second, number - NB * q, number)
    mode = number
    for z in range(1, NB):
        mode = jnp.where(number >= z * q, number + z * q, mode)
    return jnp.where(second, mode + q, mode)


def eight_points(x, sign):
    root = float(np.float32(1.0 / math.sqrt(8.0)).astype(BF16))

    def add(a, b):
        return a[0] + b[0], a[1] + b[1]

    def sub(a, b):
        return a[0] - b[0], a[1] - b[1]

    def times_i(a, by):
        return (-a[1], a[0]) if by > 0 else (a[1], -a[0])

    def scale(a, by):
        return a[0] * by, a[1] * by

    def four(a, b, c, d):
        total, far, other, near = add(a, c), sub(a, c), add(b, d), sub(b, d)
        near = times_i(near, sign)
        return add(total, other), add(far, near), sub(total, other), sub(far, near)

    even = [scale(a, root) for a in four(*x[0::2])]
    odd = four(*x[1::2])
    turned = [
        scale(odd[0], root),
        scale(add(odd[1], times_i(odd[1], sign)), 0.25),
        scale(times_i(odd[2], sign), root),
        scale(sub(times_i(odd[3], sign), odd[3]), 0.25),
    ]
    return [add(a, b) for a, b in zip(even, turned)] + [sub(a, b) for a, b in zip(even, turned)]


def fetch(sems, sources, targets):
    copies = [
        pltpu.make_async_copy(source, target, sems.at[i])
        for i, (source, target) in enumerate(zip(sources, targets))
    ]
    for copy in copies:
        copy.start()
    return copies


def fetch_parts(sems, source, target, parts):
    return fetch(sems, [source.at[part] for part in parts], [target.at[part] for part in parts])


def columns(width):
    return [(slice(None), pl.ds(i, LANES)) for i in range(0, width, LANES)]


def wait(copies):
    for copy in copies:
        copy.wait()


def partner(d):
    return jnp.bitwise_xor(lax.axis_index("lat") // 2, d)


def analyse_kernel(q, *refs):
    hbm, outs, held = refs[:5], refs[5:9], refs[9:14]
    by_block, few, sems = refs[14:]
    counts, assign, field, table, saved = held
    early = fetch_parts(sems.at[0], hbm[4], saved, [pl.ds(k, 2) for k in range(0, 2 * NB, 2)])
    late = fetch_parts(sems.at[1], hbm[2], field, columns(field.shape[1]))
    late += fetch(few, hbm[:2] + hbm[3:4], held[:2] + held[3:4])
    wait(early + late)
    parts = [saved[:, c, :].astype(F32) for c in range(2)]
    width = field.shape[1]
    points = [
        jnp.concatenate([part[:, i : i + width] for i in range(0, part.shape[1], width)], axis=0)
        for part in parts
    ]
    rows = by_block.shape[1]
    spectral = jnp.dot(table[...], field[...], preferred_element_type=F32)
    active = counts[assign[lax.axis_index("lat")]]
    held_modes = mode_numbers((rows, LANES), 0, q) < active
    spectra = [
        jnp.concatenate(
            [
                jnp.where(held_modes, spectral[c * rows : (c + 1) * rows, i : i + LANES], 0.0)
                for i in range(0, width, LANES)
            ],
            axis=1,
        )
        for c in range(2)
    ]
    arrays = [array.astype(BF16) for array in spectra + points]
    for n in range(NB):
        by_block[n] = dense([window(array, n * BS) for array in arrays]).astype(BF16)
    for d, out in enumerate(outs):
        out[...] = by_block[partner(d)]


def ready_kernel(q, *refs):
    hbm, (mat1, turned1, turned2, bias, own_field, own_table, latitudes) = refs[:7], refs[7:14]
    counts, assign, w1, w2, b1, table, sems = refs[14:]
    copies = fetch(sems, hbm, (counts, assign, w1, w2, b1, table, own_field))
    wait(copies[:6])
    lane = lax.broadcasted_iota(jnp.int32, latitudes.shape, 1)
    line = jnp.zeros(latitudes.shape, jnp.int32)
    for r in range(2 * NB):
        line = jnp.where(lane == r, assign[r], line)
    latitudes[...] = line
    active = counts[assign[lax.axis_index("lat")]]
    rows = table.shape[1] // 2
    held_modes = mode_numbers((table.shape[0], rows), 1, q) < active
    for c in range(2):
        part = table[:, c * rows : (c + 1) * rows].astype(F32)
        own_table[:, c * rows : (c + 1) * rows] = jnp.where(held_modes, part, 0.0).astype(BF16)
    block = lax.axis_index("lat") // 2

    def pick(x):
        value = window(x, 0)
        for n in range(1, NB):
            value = jnp.where(block == n, window(x, n * BS), value)
        lane = lax.broadcasted_iota(jnp.int32, value.shape, 1)
        return jnp.where(lane < BS, value, 0.0)

    gap = jnp.zeros((LANES - BS, 2 * LANES), F32)
    for source, mat, turned in ((w1, mat1, turned1), (w2, None, turned2)):
        real, imag = (pick(source[c].astype(F32)) for c in range(2))
        whole = [
            jnp.concatenate([real, imag], axis=1),
            gap,
            jnp.concatenate([-imag, real], axis=1),
            gap,
        ]
        whole = jnp.concatenate(whole, axis=0)
        turned[...] = whole.T.astype(BF16)
        if mat is not None:
            mat[...] = whole.astype(BF16)
    shift_b = pick(b1[...].astype(F32))
    bias[...] = jnp.concatenate([shift_b[0:1], shift_b[1:2]], axis=1)
    wait(copies[6:])


ORDER = (0, 3, 2, 1)
FIELD_ROWS = 184


def join_kernel(*refs):
    out = refs[-1]
    for i in range(out.shape[0]):
        out[i] = refs[i][...]


def pack(band):
    rows = band.shape[0]
    tail = rows // 2 + 4
    left, right = band[:, :LANES], pltpu.roll(band[:, LANES:], 96, 1)
    lane = lax.broadcasted_iota(jnp.int32, left.shape, 1)
    upper = jnp.where(lane < 96, left, right)
    lower = pltpu.roll(right[rows - tail :], 64, 1)
    lower = jnp.where(lane[:tail] < 64, right[:tail], lower)
    return jnp.concatenate([upper, lower], axis=0)


def unpack(packed, rows):
    tail = rows // 2 + 4
    upper, lower = packed[:rows], packed[rows:]
    rest = jnp.concatenate([lower, pltpu.roll(lower, 64, 1)[2 * tail - rows :]], axis=0)
    lane = lax.broadcasted_iota(jnp.int32, upper.shape, 1)
    right = jnp.where(lane < 32, pltpu.roll(upper, 32, 1), pltpu.roll(rest, 32, 1))
    return [upper, right]


def silu_points(chunks, mat, bias, by_pair, points, hidden, slope):
    for d, chunk in enumerate(chunks):
        parts = [window(chunk, j * BS) for j in (2, 3)]
        by_pair[partner(d)] = jnp.concatenate(parts, axis=1)
    v = by_pair[...].reshape(points.shape).astype(BF16)
    pre = dot(v, mat[...], (1, 0)) + bias[...]
    sig = jax.nn.sigmoid(pre)
    points[...] = v
    hidden[...] = (pre * sig).astype(BF16)
    slope[...] = sig * (1.0 + pre * (1.0 - sig))


def own_kernel(*refs):
    mat1, bias, points, hidden, slope, by_pair = refs[NB:]
    chunks = [refs[i][...].astype(F32) for i in ORDER]
    silu_points(chunks, mat1, bias, by_pair, points, hidden, slope)


def row_spectrum(chunk):
    return jnp.concatenate([window(chunk, j * BS) for j in range(2)], axis=1)


def filter_kernel(*refs):
    owns, (other, slope_own, mat1, turned1, turned2, bias, own_field) = refs[:4], refs[4:11]
    latitudes, outs, (bundle, points, hidden, grad_pre, grad_y) = refs[11], refs[12:15], refs[15:20]
    assign, by_lat, by_pair, slope, real, imag, sems = refs[20:]
    copies = fetch(sems, (latitudes,), (assign,))
    core = lax.rem(lax.axis_index("lat"), 2)
    sides = [[owns[i][...].astype(F32) for i in ORDER], [other[i].astype(F32) for i in ORDER]]
    silu_points(sides[1], mat1, bias, by_pair, points, hidden, slope)
    spectra = [
        [row_spectrum((chunk * 1.0).astype(BF16)) for chunk in chunks]
        for chunks in sides
    ]
    wait(copies)
    for side, rows in zip((core, 1 - core), spectra):
        for d, row in enumerate(rows):
            by_lat[assign[0, 2 * partner(d) + side]] = row.astype(F32)
    n_rows, rows, _ = by_lat.shape
    half = rows * n_rows // 2
    waves = eight_points([(by_lat[r][:, :LANES], by_lat[r][:, LANES:]) for r in range(n_rows)], -1)
    step = rows + 1
    for k, wave in enumerate(waves):
        real[k * step : k * step + rows] = wave[0]
        imag[k * step : k * step + rows] = wave[1]
    dy = [
        jnp.concatenate([ref[pl.ds(m, n_rows, stride=step), :] for m in range(rows)], axis=0)
        for ref in (real, imag)
    ]
    dy = jnp.concatenate(dy, axis=1).astype(BF16)
    dy = [jnp.where(core == side, dy[:half], dy[half:]) for side in range(2)]
    dh = dot(jnp.concatenate(dy, axis=0), turned2[...], (1, 0))
    dp = [(dh[:half] * slope_own[...]).astype(BF16), (dh[half:] * slope[...]).astype(BF16)]
    dv = dot(jnp.concatenate(dp, axis=0), turned1[...], (1, 0)).astype(BF16).astype(F32)
    for side in range(2):
        grad_y[side] = dy[side]
        grad_pre[side] = dp[side]
    step = n_rows + 1
    dv = [jnp.where(core == g, dv[:half], dv[half:]) for g in range(2)]
    for g in range(2):
        for i in range(rows // 2):
            m = g * rows // 2 + i
            real[m * step : m * step + n_rows] = dv[g][i * n_rows : (i + 1) * n_rows, :LANES]
            imag[m * step : m * step + n_rows] = dv[g][i * n_rows : (i + 1) * n_rows, LANES:]
    inner = [tuple(ref[pl.ds(k, rows, stride=step), :] for ref in (real, imag)) for k in range(n_rows)]
    for r, band in enumerate(eight_points(inner, 1)):
        by_lat[r] = jnp.concatenate(band, axis=1)
    for i, d in enumerate(ORDER):
        band = pack(by_lat[assign[0, 2 * partner(d) + core]])
        if d:
            outs[i - 1][...] = band.astype(BF16)
        else:
            tail = bundle.shape[0] - FIELD_ROWS
            band = jnp.concatenate([band, jnp.zeros((3 * tail - band.shape[0], LANES), F32)], axis=0)
            band = jnp.concatenate([band[j * tail : (j + 1) * tail] for j in range(3)], axis=1)
            lines = own_field[...].astype(F32)
            gap = jnp.zeros((FIELD_ROWS - lines.shape[0], lines.shape[1]), F32)
            bundle[...] = jnp.concatenate([lines, gap, band], axis=0).astype(BF16)


def products_kernel(points0, hidden0, points1, hidden1, grad_pre, grad_y, gw1, gw2, gb1):
    core = lax.rem(lax.axis_index("lat"), 2)
    half = BS // 2
    for ref, grads, values in ((gw1, grad_pre, (points0, points1)), (gw2, grad_y, (hidden0, hidden1))):
        both = dot(grads[0], values[0][...], (0, 0)) + dot(grads[1], values[1][...], (0, 0))
        real = both[:BS, :LANES] + both[LANES : LANES + BS, LANES:]
        imag = both[LANES : LANES + BS, :LANES] - both[:BS, LANES:]
        for c, full in enumerate((real, imag)):
            ref[c] = jnp.where(core == 0, full[:half], full[half:])[:, :BS]
    sums = sum(jnp.sum(grad_pre[side].astype(F32), axis=0, keepdims=True) for side in range(2))
    for c in range(2):
        line = sums[:, c * LANES : (c + 1) * LANES]
        gb1[c : c + 1] = jnp.where(core == 0, line[:, :half], line[:, half:BS])


def compose_kernel(last, three, bundle, table, out, by_block, result, sems):
    rows = by_block.shape[1]
    lines = bundle[...].astype(F32)
    own = lines[FIELD_ROWS:]
    own = jnp.concatenate([own[:, i * LANES : (i + 1) * LANES] for i in range(3)], axis=0)
    chunks = [own[: three.shape[1]]] + [three[i].astype(F32) for i in range(3)]
    for d, chunk in zip(ORDER, chunks):
        by_block[partner(d)] = jnp.concatenate(unpack(chunk, rows), axis=1)
    parts = [
        dense([by_block[n, :, c * LANES : (c + 1) * LANES] for n in range(NB)]) for c in range(2)
    ]
    parts = jnp.concatenate(parts, axis=0).astype(BF16)
    none = lax.axis_index("section") == last
    copies = []
    for i, (_, tile) in enumerate(columns(out.shape[1])):
        mixed = jnp.dot(table[...], parts[:, i * LANES : (i + 1) * LANES], preferred_element_type=F32)
        field = lines[: out.shape[0], i * LANES : (i + 1) * LANES]
        whole = field + mixed.astype(BF16).astype(F32)
        result[:, tile] = jnp.where(none, 0.0, whole).astype(BF16)
        copies.append(pltpu.make_async_copy(result.at[:, tile], out.at[:, tile], sems.at[i]))
        copies[-1].start()
    wait(copies)


VMEM = pl.BlockSpec(memory_space=pltpu.VMEM)
HBM = pl.BlockSpec(memory_space=pltpu.HBM)


def call(kernel, outs, scratch, near, far, flops=10**8, out_specs=None):
    out_specs = out_specs or (tuple([VMEM] * len(outs)) if isinstance(outs, tuple) else VMEM)
    many = isinstance(outs, tuple)
    return pl.pallas_call(
        kernel,
        out_shape=outs,
        in_specs=[VMEM] * len(near) + [HBM] * len(far),
        out_specs=out_specs,
        scratch_shapes=scratch,
        cost_estimate=pl.CostEstimate(flops=flops, bytes_accessed=10**6, transcendentals=0),
        compiler_params=pltpu.CompilerParams(vmem_limit_bytes=32 * 2**20),
    )(*near, *(pltpu.with_memory_space_constraint(x, pltpu.HBM) for x in far))


def scratch_for(*arrays):
    scratch = []
    for x in arrays:
        space = pltpu.SMEM if x.dtype == jnp.int32 else pltpu.VMEM
        scratch.append(space(x.shape, x.dtype))
    return scratch, pltpu.SemaphoreType.DMA((len(arrays),))


def paired_blocks(grad_out, spec_saved, w1, w2, b1, mode_counts, assignment):
    length, width = grad_out.shape[2:]
    n_rows = assignment.shape[0]
    q = spec_saved.shape[3] // (NB * BS)
    rows = 2 * NB * q
    forward, inverse = lon_tables(KM, length)

    def by_part(table):
        table = table.reshape(2, NB, 2, q, length).transpose(0, 2, 1, 3, 4)
        return table.reshape(2 * rows, length).astype(BF16)

    inverse = jnp.asarray(by_part(inverse))
    forward = jnp.asarray(by_part(forward).T)

    def swap(chunks):
        pairs = [[(i, i ^ (2 * d)) for i in range(2 * NB)] for d in ORDER[1:]]
        return [lax.ppermute(chunk, "lat", p) for chunk, p in zip(chunks, pairs)]

    field = grad_out.reshape(length, width)
    shape = jax.ShapeDtypeStruct
    far = (mode_counts, assignment, field, inverse, spec_saved[0])
    scratch, sems = scratch_for(*far)
    sent = call(
        functools.partial(analyse_kernel, q),
        (shape((rows, width), BF16),) * NB,
        scratch + [pltpu.VMEM((NB, rows, width), BF16), sems, pltpu.SemaphoreType.DMA((2, 4))],
        (),
        far,
    )
    received = [sent[0], *swap([sent[d] for d in ORDER[1:]])]
    far = (mode_counts, assignment, w1[0], w2[0], b1[0], forward)
    scratch, _ = scratch_for(*far)
    far = (*far, field)
    wide = 2 * LANES
    mat1, turned1, turned2, bias, field, forward, latitudes = call(
        functools.partial(ready_kernel, q),
        (
            shape((wide, wide), BF16),
            shape((wide, wide), BF16),
            shape((wide, wide), BF16),
            shape((1, wide), F32),
            shape(field.shape, BF16),
            shape(forward.shape, BF16),
            shape((1, LANES), jnp.int32),
        ),
        scratch + [pltpu.SemaphoreType.DMA((len(far),))],
        (),
        far,
        2 * 10**9,
    )
    own = call(
        join_kernel,
        shape((NB, rows, width), BF16),
        [],
        (*received, bias),
        (),
    )
    other = lax.ppermute(own, "lat", [(i, i ^ 1) for i in range(2 * NB)])
    vectors = shape((NB * rows, wide), BF16)
    slopes = shape((NB * rows, wide), F32)
    by_pair = pltpu.VMEM((NB, rows, wide), F32)
    points0, hidden0, slope0 = call(
        own_kernel,
        (vectors, vectors, slopes),
        [by_pair],
        (*received, mat1, bias),
        (),
        2 * 10**9,
    )
    packed = shape((rows + rows // 2 + 4, LANES), BF16)
    scratch, sems = scratch_for(latitudes)
    both = shape((2, NB * rows, wide), BF16)
    tail = -(-packed.shape[0] // 24) * 8
    bundle = shape((FIELD_ROWS + tail, width), BF16)
    *chunks, bundle, points1, hidden1, grad_pre, grad_y = call(
        filter_kernel,
        (packed,) * (NB - 1) + (bundle, vectors, vectors, both, both),
        scratch
        + [
            pltpu.VMEM((n_rows, rows, wide), F32),
            by_pair,
            pltpu.VMEM((NB * rows, wide), F32),
            pltpu.VMEM(((n_rows + 1) * rows, LANES), F32),
            pltpu.VMEM(((n_rows + 1) * rows, LANES), F32),
            sems,
        ],
        (*received, other, slope0, mat1, turned1, turned2, bias, field, latitudes),
        (),
    )
    backs = swap(chunks)
    matrix = shape((2, BS // 2, BS), F32)
    gw1, gw2, gb1 = call(
        products_kernel,
        (matrix, matrix, shape((2, BS // 2), F32)),
        [],
        (points0, hidden0, points1, hidden1, grad_pre, grad_y),
        (),
        2 * 10**9,
    )
    three = call(join_kernel, shape((NB - 1, *packed.shape), BF16), [], backs, ())
    three = turn(three, "section")
    bundle = turn(bundle, "section")
    shifted = call(
        functools.partial(compose_kernel, lax.axis_size("section") - 1),
        shape((length, width), BF16),
        [
            by_pair,
            pltpu.VMEM((length, width), BF16),
            pltpu.SemaphoreType.DMA((width // LANES,)),
        ],
        (three, bundle, forward),
        (),
        out_specs=HBM,
    )
    shifted = shifted[None, None]
    return shifted, gw1.swapaxes(1, 2)[None], gw2.swapaxes(1, 2)[None], gb1[None]


def apply_mat(vec, mat):
    return jnp.einsum("kpi,ipj->kpj", vec, mat, preferred_element_type=F32)


def adjoint_mat(vec, mat):
    return jnp.einsum("kpj,ipj->kpi", vec, mat, preferred_element_type=F32)


def outer_sum(left, right):
    return jnp.einsum("kpi,kpj->ipj", left, right, preferred_element_type=F32)


def split_blocks(grad_out, spec_saved, w1, w2, b1, mode_counts, assignment):
    rows_dev = grad_out.shape[1]
    length = grad_out.shape[2]
    width = grad_out.shape[3]
    n_rows = assignment.shape[0]
    pairs_dev = spec_saved.shape[3] // BS
    forward, inverse = (jnp.asarray(t.astype(BF16)) for t in lon_tables(KM, length))
    cosine, sine = (jnp.asarray(t.astype(BF16))[:, assignment] for t in lat_waves(n_rows))
    table = jnp.stack(
        [jnp.stack([cosine, sine], axis=-1), jnp.stack([-sine, cosine], axis=-1)], axis=1
    )
    lat_pos = lax.axis_index("lat")
    lat_count = lax.axis_size("lat")
    own_lat = lax.dynamic_slice_in_dim(assignment, lat_pos * rows_dev, rows_dev)
    active = (jnp.arange(KM, dtype=jnp.int32)[None, :] < mode_counts[own_lat][:, None]).astype(F32)
    cotan = grad_out[0]
    spectral = jnp.einsum(
        "cml,rlni->rcmni",
        inverse,
        cotan.reshape(rows_dev, length, NB, BS),
        preferred_element_type=F32,
    )
    spectral = (spectral * active[:, None, :, None, None]).astype(BF16)
    spectral = spectral.reshape(rows_dev, 2, KM * NB * BS)
    pencil = lax.all_to_all(spectral, "lat", split_axis=2, concat_axis=0, tiled=True)
    pencil = pencil.reshape(n_rows, 2, pairs_dev, BS)
    grad_y = jnp.einsum("kerc,rcpi->kepi", table, pencil, preferred_element_type=F32).astype(BF16)
    saved = spec_saved[0].reshape(n_rows, 2, pairs_dev, BS)
    pair_ids = lat_pos * pairs_dev + jnp.arange(pairs_dev, dtype=jnp.int32)
    owner = (pair_ids % NB)[:, None] == jnp.arange(NB, dtype=jnp.int32)[None, :]
    owner = owner.astype(F32)
    first = jnp.take(w1[0].reshape(2, BS, NB, BS), pair_ids % NB, axis=2)
    second = jnp.take(w2[0].reshape(2, BS, NB, BS), pair_ids % NB, axis=2)
    shift_b = jnp.take(b1[0].reshape(2, NB, BS), pair_ids % NB, axis=1).astype(F32)
    v_r = saved[:, 0]
    v_i = saved[:, 1]
    pre_r = apply_mat(v_r, first[0]) - apply_mat(v_i, first[1]) + shift_b[0][None]
    pre_i = apply_mat(v_i, first[0]) + apply_mat(v_r, first[1]) + shift_b[1][None]
    hid_r = jax.nn.silu(pre_r).astype(BF16)
    hid_i = jax.nn.silu(pre_i).astype(BF16)
    dy_r = grad_y[:, 0]
    dy_i = grad_y[:, 1]
    dh_r = adjoint_mat(dy_r, second[0]) + adjoint_mat(dy_i, second[1])
    dh_i = adjoint_mat(dy_i, second[0]) - adjoint_mat(dy_r, second[1])
    dp_r = (dh_r * silu_slope(pre_r)).astype(BF16)
    dp_i = (dh_i * silu_slope(pre_i)).astype(BF16)
    gw2 = jnp.stack(
        [
            outer_sum(hid_r, dy_r) + outer_sum(hid_i, dy_i),
            outer_sum(hid_r, dy_i) - outer_sum(hid_i, dy_r),
        ]
    )
    gw1 = jnp.stack(
        [outer_sum(v_r, dp_r) + outer_sum(v_i, dp_i), outer_sum(v_r, dp_i) - outer_sum(v_i, dp_r)]
    )
    gb1 = jnp.stack([jnp.sum(dp_r.astype(F32), axis=0), jnp.sum(dp_i.astype(F32), axis=0)])
    dv_r = adjoint_mat(dp_r, first[0]) + adjoint_mat(dp_i, first[1])
    dv_i = adjoint_mat(dp_i, first[0]) - adjoint_mat(dp_r, first[1])
    grad_v = jnp.stack([dv_r, dv_i], axis=1).astype(BF16)
    grad_u = jnp.einsum("kerc,kepi->rcpi", table, grad_v, preferred_element_type=F32).astype(BF16)
    grad_u = grad_u.reshape(n_rows, 2, pairs_dev * BS)
    back = lax.all_to_all(grad_u, "lat", split_axis=0, concat_axis=2, tiled=True)
    back = back.reshape(rows_dev, 2, KM, NB, BS) * active[:, None, :, None, None].astype(BF16)
    mixed = jnp.einsum("cml,rcmni->rlni", forward, back, preferred_element_type=F32)
    mixed = mixed.reshape(rows_dev, length, width).astype(BF16)
    block_w1 = jnp.einsum("pn,cipj->cinj", owner, gw1).reshape(1, 2, BS, width)
    block_w2 = jnp.einsum("pn,cipj->cinj", owner, gw2).reshape(1, 2, BS, width)
    block_b1 = jnp.einsum("pn,cpj->cnj", owner, gb1).reshape(1, 2, width)
    columns = width // lat_count
    full_w1, full_w2, full_b1 = lax.psum((block_w1, block_w2, block_b1), "lat")
    sum_w1 = lax.dynamic_slice_in_dim(full_w1, lat_pos * columns, columns, 3)
    sum_w2 = lax.dynamic_slice_in_dim(full_w2, lat_pos * columns, columns, 3)
    sum_b1 = lax.dynamic_slice_in_dim(full_b1, lat_pos * columns, columns, 2)
    whole = (cotan.astype(F32) + mixed.astype(F32)).astype(BF16)
    received = from_behind(whole[None], "section", -1)
    return (received, sum_w1, sum_w2, sum_b1)


def per_device(grad_out, spec_saved, w1, w2, b1, mode_counts, assignment):
    n_dev = lax.axis_size("lat")
    pairs_dev = spec_saved.shape[3] // BS
    paired = n_dev == 2 * NB and grad_out.shape[1] == 1 and pairs_dev % NB == 0
    body = paired_blocks if paired else split_blocks
    return body(grad_out, spec_saved, w1, w2, b1, mode_counts, assignment)


def solution(mesh):
    return jax.shard_map(
        per_device,
        mesh=mesh,
        in_specs=(
            P("section", "lat", None, None),
            P("section", None, None, "lat"),
            P("section", None, None, None),
            P("section", None, None, None),
            P("section", None, None),
            P(),
            P(),
        ),
        out_specs=(
            P("section", "lat", None, None),
            P("section", None, None, "lat"),
            P("section", None, None, "lat"),
            P("section", None, "lat"),
        ),
        check_vma=False,
    )
```
